32 devices in a mesh: seq: 4 (over y, core), cp: 8 (over z, x).
Axes of the slice: x: 2, y: 2, z: 4, core: 2. Of those that a mesh axis runs over, the one named last changes fastest.
Arguments:
- query: bfloat16 [4096, 4608], P(('seq', 'cp')), may hold values from -6 to 6
- key_proj: bfloat16 [4096, 4608], P(('seq', 'cp')), may hold values from -6 to 6
- value_proj: bfloat16 [4096, 4608], P(('seq', 'cp')), may hold values from -6 to 6
- featurizer: float32 [3, 7, 288], replicated, may hold values from -2 to 2
- rates: float32 [16, 4608], replicated, may hold values from 6.1035156e-05 to 0.25
- residues: float32 [16, 4608], replicated, may hold values from -5 to 5
- skip: float32 [4608], replicated, may hold values from -4 to 4
Outputs:
- operator_out: bfloat16 [4096, 4608], P(('seq', 'cp'))
The draws below stay inside these ranges and needn't reach their ends.
All inputs are finite; a program needn't handle non-finite values.
Results may differ from the reference program's by a relative error of at most 0.0064.
Values may be sent and summed in bfloat16 or wider, within the bound.
No kernel may reach another device: no remote copies, remote signals or barrier semaphores. Data moves between devices by JAX's collectives and lax.ppermute only.
A program may use at most 128 MiB of HBM per device.

```python
import math
import jax
import jax.numpy as jnp
from jax import lax

DW = 4608
TAPS = 7
MODES = 16
NGROUPS = 288
TOKENS = 4096


def steps_of(rng, shape, split, smallest, largest):
    gain = 1.0
    for axis_at, shards_of in split:
        steps = jax.random.uniform(jax.random.fold_in(jax.random.fold_in(rng, 6), axis_at), (shards_of,), jnp.float32, smallest / len(split), largest / len(split))
        gain = gain * jnp.repeat(jnp.exp(steps), shape[axis_at] // shards_of).reshape((-1,) + (1,) * (len(shape) - 1 - axis_at))
    return gain


def bell_draw(key, extent, width, limit, cuts=(), kind=jnp.bfloat16):
    entries = jax.random.normal(key, extent, jnp.float32) * width
    if len(cuts) > 0:
        entries = steps_of(key, extent, cuts, -0.22, 0.18) * entries
    return jnp.clip(entries, min=-limit, max=limit).astype(kind)


def setup_inputs(seed: int = 0) -> dict:
    keys = jax.random.split(jax.random.key(seed), 8)
    query = bell_draw(keys[0], (TOKENS, DW), 1.0, 6.0, ((0, 32),))
    key_proj = bell_draw(keys[1], (TOKENS, DW), 1.0, 6.0, ((0, 32),))
    value_proj = bell_draw(keys[2], (TOKENS, DW), 1.0, 6.0, ((0, 32),))
    featurizer = bell_draw(keys[3], (3, TAPS, NGROUPS), TAPS ** -0.5, 2.0, (), jnp.float32)
    rates = jnp.clip(jnp.exp(jax.random.uniform(keys[4], (MODES, DW), jnp.float32, math.log(6.103515625e-05), math.log(0.25))), 6.103515625e-05, 0.25)
    residues = bell_draw(keys[5], (MODES, DW), 1.0, 5.0, (), jnp.float32)
    skip = bell_draw(keys[6], (DW,), 1.0, 4.0, (), jnp.float32)
    return {"query": query, "key_proj": key_proj, "value_proj": value_proj, "featurizer": featurizer, "rates": rates, "residues": residues, "skip": skip}


precise = lax.Precision.HIGHEST

def mode_terms(decay_rate, residue_part):
    mode_count = decay_rate.shape[1]
    return residue_part * jnp.sqrt(-jnp.expm1(-2.0 * decay_rate) / mode_count)

def short_conv(extended, tap_table, row_count):
    tap_count = tap_table.shape[0]
    running = jnp.zeros((row_count, extended.shape[1]), jnp.float32)
    for lag_index in range(tap_count):
        first_row = tap_count - 1 - lag_index
        running = running + tap_table[lag_index][None, :] * extended[first_row:first_row + row_count].astype(jnp.float32)
    return running

def link_blocks(earlier, later):
    return (earlier[0] * later[0], later[0] * earlier[1] + later[1])

def modal_local(signal, decay_rate, mode_coef, block_len):
    row_count, chan_count = signal.shape
    block_count = row_count // block_len
    blocks = signal.reshape(block_count, block_len, chan_count)
    offsets = jnp.arange(block_len, dtype=jnp.float32)
    falloff = jnp.exp(-decay_rate[None, :, :] * offsets[:, None, None])
    kernel = lax.optimization_barrier(jnp.sum(mode_coef[None] * falloff, axis=2))
    lag_table = jnp.arange(block_len, dtype=jnp.int32)[:, None] - jnp.arange(block_len, dtype=jnp.int32)[None, :]
    toeplitz = jnp.where((lag_table >= 0)[:, :, None], kernel[jnp.maximum(lag_table, 0)], 0.0)
    within = jnp.einsum('ijc,bjc->bic', toeplitz, blocks, precision=precise)
    block_state = jnp.einsum('jcr,bjc->bcr', falloff[::-1], blocks, precision=precise)
    factor = jnp.broadcast_to(jnp.exp(-decay_rate * block_len)[None], block_state.shape)
    _, through = lax.associative_scan(link_blocks, (factor, block_state))
    entering = jnp.concatenate([jnp.zeros_like(through[:1]), through[:-1]], axis=0)
    leading = mode_coef[None] * falloff * jnp.exp(-decay_rate)[None]
    carried = jnp.einsum('icr,bcr->bic', leading, entering, precision=precise)
    return ((within + carried).reshape(row_count, chan_count), through[-1])

def reference(query, key_proj, value_proj, featurizer, rates, residues, skip):
    row_count, feature_width = query.shape
    tap_count = featurizer.shape[1]
    filters = jnp.repeat(featurizer, feature_width // featurizer.shape[2], axis=2)
    chan_block = math.gcd(feature_width, 128)
    block_total = feature_width // chan_block

    def per_block(block_index):
        col_start = block_index * chan_block
        tap_part = lax.dynamic_slice_in_dim(filters, col_start, chan_block, 2)
        featured = []
        for member, source in enumerate((query, key_proj, value_proj)):
            columns = lax.dynamic_slice_in_dim(source, col_start, chan_block, 1)
            extended = jnp.concatenate([jnp.zeros((tap_count - 1, chan_block), columns.dtype), columns], axis=0)
            featured.append(short_conv(extended, tap_part[member], row_count))
        gate_half = featured[0].astype(jnp.bfloat16)
        gate = lax.optimization_barrier(gate_half).astype(jnp.float32)
        signal_half = (featured[1] * featured[2]).astype(jnp.bfloat16)
        signal = lax.optimization_barrier(signal_half).astype(jnp.float32)
        decay_rate = lax.dynamic_slice_in_dim(rates, col_start, chan_block, 1).T
        residue_part = lax.dynamic_slice_in_dim(residues, col_start, chan_block, 1).T
        mode_coef = mode_terms(decay_rate, residue_part)
        convolved, _ = modal_local(signal, decay_rate, mode_coef, 16)
        skip_part = lax.dynamic_slice_in_dim(skip, col_start, chan_block, 0)
        convolved = convolved + skip_part[None, :] * signal
        conv_half = lax.optimization_barrier(convolved.astype(jnp.bfloat16))
        return (gate * conv_half.astype(jnp.float32)).astype(jnp.bfloat16)
    stacked = lax.map(per_block, jnp.arange(block_total, dtype=jnp.int32))
    return stacked.transpose(1, 0, 2).reshape(row_count, feature_width)
```

```python
import functools
import math

import jax
import jax.numpy as jnp
from jax import lax
from jax.experimental import pallas as pl
from jax.experimental.pallas import tpu as pltpu
from jax.sharding import PartitionSpec as P

LANES = 128
ROWS = 8
TILES = 4
CHUNK = TILES * LANES
f32 = jnp.float32
bf16 = jnp.bfloat16


def params(limit=32 * 2**20):
    return pltpu.CompilerParams(vmem_limit_bytes=limit)


def put_tile(scratch, group, slot, tile):
    scratch[pl.ds((group * ROWS + slot) * ROWS, ROWS), :] = tile


def get_row(scratch, group, row):
    return scratch[pl.ds(group * ROWS * ROWS + row, ROWS, stride=ROWS), :]


def lanes_of(value, tile):
    return value[:, tile * LANES : (tile + 1) * LANES]


def stage_tokens(source, scratch):
    half_groups = source.shape[0] // ROWS // 2
    for pair in range(half_groups):
        block = source[pl.ds(pair * 2 * ROWS, 2 * ROWS), :].astype(f32)
        for part in range(2):
            group = pair * 2 + part
            half, within = group // half_groups, group % half_groups
            for tile in range(TILES):
                piece = lanes_of(block, tile)[part * ROWS : (part + 1) * ROWS]
                put_tile(scratch, within + 1, half * TILES + tile, piece)
                if half == 0 and within == half_groups - 1:
                    put_tile(scratch, 0, TILES + tile, piece)


def stage_table(table, scratch):
    for group in range(table.shape[0] // ROWS):
        for tile in range(TILES):
            piece = lanes_of(table, tile)[group * ROWS : (group + 1) * ROWS]
            put_tile(scratch, group, tile, piece)
            put_tile(scratch, group, TILES + tile, piece)


def fir(taps, now, past):
    total = taps[0] * now
    for lag in range(1, len(taps)):
        total = total + taps[lag] * past[-lag]
    return total


def rounded(value):
    return value.astype(bf16).astype(f32)


def pack_kernel(key_ref, value_ref, query_ref, out_ref):
    tails = [ref[...].astype(f32)[ROWS:] for ref in (key_ref, value_ref, query_ref)]
    out_ref[...] = jnp.concatenate(tails, axis=0).astype(bf16)


def chunk_taps(feat_ref, members, scratch):
    taps, width = feat_ref.shape[-2:]
    share = CHUNK // width
    group = lax.broadcasted_iota(jnp.int32, (width, CHUNK), 0)
    channel = lax.broadcasted_iota(jnp.int32, (width, CHUNK), 1)
    pick = (group == channel // share).astype(f32).astype(bf16)
    for position, member in enumerate(members):
        rest = feat_ref[member]
        wide = jnp.zeros((taps, CHUNK), f32)
        for _ in range(3):
            term = rest.astype(bf16)
            rest = rest - term.astype(f32)
            wide = wide + jnp.dot(term, pick, preferred_element_type=f32)
        wide = jnp.concatenate([wide, jnp.zeros((ROWS - taps, CHUNK), f32)], axis=0)
        for tile in range(TILES):
            put_tile(scratch, position, tile, lanes_of(wide, tile))
            put_tile(scratch, position, TILES + tile, lanes_of(wide, tile))
    return [
        [get_row(scratch, position, lag) for lag in range(taps)] for position in range(len(members))
    ]


def first_half():
    return lax.broadcasted_iota(jnp.int32, (ROWS, LANES), 0) < TILES


def power(base, exponent):
    result = None
    while exponent:
        if exponent & 1:
            result = base if result is None else result * base
        base = base * base
        exponent >>= 1
    return result


def signal_kernel(key_ref, value_ref, feat_ref, rate_ref, u_ref, decay_ref, tap_ref, state_ref, *scratches):
    key_scr, value_scr, table_scr = scratches
    modes = rate_ref.shape[0]
    steps = u_ref.shape[0]
    top = first_half()
    for ref, scr in ((key_ref, key_scr), (value_ref, value_scr)):
        stage_tokens(ref, scr)
        for tile in range(TILES):
            put_tile(scr, 0, tile, jnp.zeros((ROWS, LANES), f32))
    taps = chunk_taps(feat_ref, (1, 2), table_scr)
    for member in range(2):
        for lag, tap in enumerate(taps[member]):
            tap_ref[member * ROWS + lag] = tap
    reach = len(taps[0]) - 1
    stage_table(rate_ref[...], table_scr)
    for mode in range(modes):
        decay_ref[mode] = jnp.exp(-get_row(table_scr, mode // ROWS, mode % ROWS))
    decay = [decay_ref[mode] for mode in range(modes)]

    def eight(group, carry, opening=False):
        state, past = carry
        state = list(state)
        past = [list(past[0]), list(past[1])]
        for row in range(ROWS):
            parts = []
            for member, scr in enumerate((key_scr, value_scr)):
                now = get_row(scr, group + 1, row)
                parts.append(fir(taps[member], now, past[member]))
                past[member] = past[member][1:] + [now]
            u = rounded(parts[0] * parts[1])
            if opening and row < reach:
                u = jnp.where(top, 0.0, u)
            u_ref[group * ROWS + row] = u
            if opening and row == 0:
                state = [u for _ in range(modes)]
            else:
                state = [decay[mode] * state[mode] + u for mode in range(modes)]
        return tuple(state), (tuple(past[0]), tuple(past[1]))

    past = tuple(
        tuple(get_row(scr, 0, ROWS - reach + row) for row in range(reach)) for scr in (key_scr, value_scr)
    )
    carry = eight(0, ((None,) * modes, past), True)
    state, _ = lax.fori_loop(1, steps // ROWS, eight, carry)
    for mode in range(modes):
        through = power(decay[mode], steps) * state[mode]
        state_ref[mode] = pltpu.roll(through, TILES, 0) + state[mode]


def head_kernel(key_ref, value_ref, halo_ref, decay_ref, tap_ref, state_ref, out_ref, head_ref, *scratches, tokens):
    key_scr, value_scr, total_scr = scratches
    chunks, modes = state_ref.shape[:2]
    pieces, piece_rows = out_ref.shape[:2]
    reach = tap_ref.shape[1] // 2 - 2
    top = first_half()
    for chunk in range(chunks):
        span = slice(chunk * CHUNK, (chunk + 1) * CHUNK)
        halo = halo_ref[:, span].astype(f32)
        for member, (ref, scr) in enumerate(((key_ref, key_scr), (value_ref, value_scr))):
            block = ref[:, span].astype(f32)
            for tile in range(TILES):
                before = lanes_of(halo, tile)[member * ROWS : (member + 1) * ROWS]
                after = lanes_of(block, tile)[:ROWS]
                for slot in (tile, TILES + tile):
                    put_tile(scr, 0, slot, before)
                    put_tile(scr, 1, slot, after)
        taps = [[tap_ref[chunk, member * ROWS + lag] for lag in range(reach + 1)] for member in range(2)]
        signals = []
        for row in range(reach):
            parts = []
            for member, scr in enumerate((key_scr, value_scr)):
                seen = [
                    get_row(scr, 1, row - lag) if lag <= row else get_row(scr, 0, ROWS + row - lag)
                    for lag in range(reach + 1)
                ]
                parts.append(fir(taps[member], seen[0], seen[:0:-1]))
            signals.append(jnp.where(top, rounded(parts[0] * parts[1]), 0.0))
            head_ref[chunk, row] = signals[-1]
        for row in range(reach, ROWS):
            head_ref[chunk, row] = jnp.zeros((ROWS, LANES), f32)
        for mode in range(modes):
            decay = decay_ref[chunk, mode]
            head = signals[0]
            for row in range(1, reach):
                head = decay * head + signals[row]
            head = power(decay, tokens - reach) * head
            total = state_ref[chunk, mode] + pltpu.roll(head, TILES, 0)
            total_scr[mode, chunk * TILES : (chunk + 1) * TILES, :] = total[TILES:]
    split = pieces // modes
    for mode in range(modes):
        for part in range(split):
            rows = total_scr[mode, part * piece_rows : (part + 1) * piece_rows, :]
            out_ref[mode * split + part] = rows.astype(out_ref.dtype)


def local_kernel(u_ref, head_ref, decay_ref, coef_ref, skip_ref, y_ref, lead_ref, mid_ref, table_scr):
    steps = u_ref.shape[0]
    modes = decay_ref.shape[0]
    stage_table(coef_ref[...], table_scr)
    for mode in range(modes):
        lead_ref[mode] = get_row(table_scr, mode // ROWS, mode % ROWS)
    coef = [lead_ref[mode] for mode in range(modes)]
    skip_tile = jnp.broadcast_to(skip_ref[...], (ROWS, CHUNK))
    stage_table(skip_tile, table_scr)
    skip = get_row(table_scr, 0, 0)
    decay = [decay_ref[mode] for mode in range(modes)]

    def eight(group, state, opening=False):
        state = list(state)
        for row in range(ROWS):
            u = u_ref[group * ROWS + row]
            if opening:
                u = u + head_ref[row]
            if opening and row == 0:
                state = [u for _ in range(modes)]
            else:
                state = [decay[mode] * state[mode] + u for mode in range(modes)]
            terms = [skip * u] + [coef[mode] * state[mode] for mode in range(modes)]
            while len(terms) > 1:
                terms = [sum(terms[at + 1 : at + 2], terms[at]) for at in range(0, len(terms), 2)]
            y_ref[group * ROWS + row] = terms[0]
        return tuple(state)

    state = eight(0, (None,) * modes, True)
    state = lax.fori_loop(1, steps // ROWS, eight, state)
    for mode in range(modes):
        mid_ref[mode] = pltpu.roll(state[mode], TILES, 0)


def gate_kernel(query_ref, halo_ref, feat_ref, gate_ref, query_scr, table_scr):
    steps = gate_ref.shape[0]
    stage_tokens(query_ref, query_scr)
    halo = halo_ref[...].astype(f32)[2 * ROWS :]
    for tile in range(TILES):
        put_tile(query_scr, 0, tile, lanes_of(halo, tile))
    (taps,) = chunk_taps(feat_ref, (0,), table_scr)
    reach = len(taps) - 1

    def eight(group, past):
        past = list(past)
        for row in range(ROWS):
            now = get_row(query_scr, group + 1, row)
            gate_ref[group * ROWS + row] = rounded(fir(taps, now, past))
            past = past[1:] + [now]
        return tuple(past)

    past = tuple(get_row(query_scr, 0, ROWS - reach + row) for row in range(reach))
    lax.fori_loop(0, steps // ROWS, eight, past)


def prefix_kernel(piece_ref, rate_ref, out_ref, table_scr, *, tokens, axes):
    devices, piece_rows = piece_ref.shape[:2]
    split = devices // rate_ref.shape[0]
    mine = lax.axis_index(axes)
    mode, part = mine // split, mine % split
    group = pl.multiple_of(mode // ROWS * ROWS, ROWS)
    first = pl.multiple_of(part * piece_rows * LANES, LANES)
    rows = rate_ref[pl.ds(group, ROWS), pl.ds(first, piece_rows * LANES)]
    here = lax.broadcasted_iota(jnp.int32, rows.shape, 0) == mode - group
    rate = jnp.sum(jnp.where(here, rows, 0.0), axis=0, keepdims=True)
    for row in range(piece_rows):
        table_scr[row : row + 1, :] = lanes_of(rate, row)
    through = jnp.exp(-float(tokens) * table_scr[:piece_rows, :])

    def lap(source, entering):
        out_ref[source] = entering.astype(out_ref.dtype)
        return through * entering + piece_ref[source].astype(f32)

    lax.fori_loop(0, devices, lap, jnp.zeros((piece_rows, LANES), f32))


def final_kernel(piece_ref, decay_ref, lead_ref, mid_ref, y_ref, gate_ref, out_ref, total_scr, enter_scr, out_scr):
    chunk = pl.program_id(0)
    modes = decay_ref.shape[0]
    steps = y_ref.shape[0]
    top = first_half()

    @pl.when(chunk == 0)
    def _():
        pieces, piece_rows = piece_ref.shape[:2]
        split = pieces // modes
        for mode in range(modes):
            for part in range(split):
                rows = piece_ref[mode * split + part].astype(f32)
                total_scr[mode, part * piece_rows : (part + 1) * piece_rows, :] = rows
        for at in range(enter_scr.shape[0]):
            for mode in range(modes):
                rows = total_scr[mode, at * TILES : (at + 1) * TILES, :]
                enter_scr[at, mode, :TILES, :] = rows
                enter_scr[at, mode, TILES:, :] = rows

    decay = [decay_ref[mode] for mode in range(modes)]
    state = []
    for mode in range(modes):
        enter = enter_scr[chunk, mode]
        later = power(decay[mode], steps) * enter + mid_ref[mode]
        state.append(lead_ref[mode] * jnp.where(top, enter, later))

    def eight(group, state):
        state = list(state)
        for row in range(ROWS):
            state = [decay[mode] * state[mode] for mode in range(modes)]
            terms = state
            while len(terms) > 1:
                terms = [sum(terms[at + 1 : at + 2], terms[at]) for at in range(0, len(terms), 2)]
            at = group * ROWS + row
            value = gate_ref[at] * rounded(y_ref[at] + terms[0])
            out_scr[pl.ds(group * ROWS * ROWS + row, ROWS, stride=ROWS), :] = value
        return tuple(state)

    lax.fori_loop(0, steps // ROWS, eight, tuple(state))
    half_groups = steps // ROWS
    for pair in range(half_groups):
        for tile in range(TILES):
            parts = []
            for group in (pair * 2, pair * 2 + 1):
                half, within = group // half_groups, group % half_groups
                slot = (within * ROWS + half * TILES + tile) * ROWS
                parts.append(out_scr[pl.ds(slot, ROWS), :])
            out_ref[pl.ds(pair * 2 * ROWS, 2 * ROWS), tile * LANES : (tile + 1) * LANES] = jnp.concatenate(
                parts, axis=0
            ).astype(bf16)


def cost(flops, moved):
    return pl.CostEstimate(flops=int(flops), bytes_accessed=int(moved), transcendentals=0)


def local(query, key_proj, value_proj, featurizer, rates, residues, skip, *, axes):
    tokens, width = query.shape
    modes = rates.shape[0]
    members, taps, groups = featurizer.shape
    devices = math.prod(lax.axis_size(axis) for axis in axes)
    chunks = width // CHUNK
    steps = tokens // 2
    tiles = width // LANES
    split = devices // modes
    even = devices % modes == 0 and tiles % split == 0
    shape = jax.ShapeDtypeStruct
    vmem = pltpu.VMEM
    elements = tokens * width

    def blocks(*dims):
        return pl.BlockSpec((None, *dims), lambda at: (at,) + (0,) * len(dims))

    columns = lambda rows: pl.BlockSpec((rows, CHUNK), lambda at: (0, at))
    whole = lambda *dims: pl.BlockSpec(dims, lambda at: (0,) * len(dims))
    tail = pl.BlockSpec((2 * ROWS, width), lambda at: (tokens // (2 * ROWS) - 1, 0))
    front = pl.BlockSpec((2 * ROWS, width), lambda at: (0, 0))
    vectors = lambda count: shape((chunks, count, ROWS, LANES), f32)

    feat = featurizer.reshape(members, taps, chunks, groups // chunks).transpose(2, 0, 1, 3)
    feat_block = blocks(members, taps, groups // chunks)

    packed = pl.pallas_call(
        pack_kernel,
        grid=(1,),
        in_specs=[tail] * 3,
        out_specs=whole(3 * ROWS, width),
        out_shape=shape((3 * ROWS, width), bf16),
        compiler_params=params(),
        name="pack",
    )(key_proj, value_proj, query)
    halo = lax.ppermute(packed, axes, [(at, at + 1) for at in range(devices - 1)])

    stage = vmem(((steps // ROWS + 1) * ROWS * ROWS, LANES), f32)
    table = vmem((2 * ROWS * ROWS, LANES), f32)
    u, decay, wide_taps, state = pl.pallas_call(
        signal_kernel,
        grid=(chunks,),
        in_specs=[columns(tokens)] * 2 + [feat_block, columns(modes)],
        out_specs=[blocks(n, ROWS, LANES) for n in (steps, modes, 2 * ROWS, modes)],
        out_shape=[vectors(n) for n in (steps, modes, 2 * ROWS, modes)],
        scratch_shapes=[stage, stage, table],
        compiler_params=params(),
        cost_estimate=cost(60 * elements, 10 * elements),
        name="signal",
    )(key_proj, value_proj, feat, rates)

    pieces = (modes * split, tiles // split, LANES) if even else (modes, tiles, LANES)
    flat = (modes, width)
    small = vmem((2 * ROWS * ROWS, LANES), f32)
    left, head = pl.pallas_call(
        functools.partial(head_kernel, tokens=tokens),
        grid=(1,),
        in_specs=[front, front, whole(3 * ROWS, width)]
        + [whole(chunks, n, ROWS, LANES) for n in (modes, 2 * ROWS, modes)],
        out_specs=[whole(*pieces), whole(chunks, ROWS, ROWS, LANES)],
        out_shape=[shape(pieces, bf16), vectors(ROWS)],
        scratch_shapes=[small, small, vmem((modes, tiles, LANES), f32)],
        compiler_params=params(),
        name="head",
    )(key_proj, value_proj, halo, decay, wide_taps, state)

    def swap(value):
        return lax.all_to_all(value, axes, split_axis=0, concat_axis=0, tiled=True)

    if even:
        theirs = swap(left)
        entering = pl.pallas_call(
            functools.partial(prefix_kernel, tokens=tokens, axes=axes),
            grid=(1,),
            in_specs=[whole(*pieces), whole(modes, width)],
            out_specs=whole(*pieces),
            out_shape=shape(pieces, bf16),
            scratch_shapes=[vmem((-(-pieces[1] // ROWS) * ROWS, LANES), f32)],
            compiler_params=params(),
            name="prefix",
        )(theirs, rates)
        entered = swap(entering)
    else:
        share = modes * width // devices
        theirs = swap(left.reshape(devices, share))
        mine = lax.axis_index(axes)
        through = jnp.exp(-float(tokens) * lax.dynamic_slice_in_dim(rates.reshape(-1), mine * share, share))
        _, entering = lax.scan(
            lambda so_far, piece: (through * so_far + piece.astype(f32), so_far.astype(bf16)),
            jnp.zeros((share,), f32),
            theirs,
        )
        entered = swap(entering).reshape(pieces)

    coef = residues * jnp.sqrt(-jnp.expm1(-2.0 * rates) / modes)
    y, lead, mid = pl.pallas_call(
        local_kernel,
        grid=(chunks,),
        in_specs=[blocks(n, ROWS, LANES) for n in (steps, ROWS, modes)] + [columns(modes), columns(1)],
        out_specs=[blocks(n, ROWS, LANES) for n in (steps, modes, modes)],
        out_shape=[vectors(n) for n in (steps, modes, modes)],
        scratch_shapes=[table],
        compiler_params=params(),
        cost_estimate=cost(66 * elements, 8 * elements),
        name="within",
    )(u, head, decay, coef, skip[None, :])

    gate = pl.pallas_call(
        gate_kernel,
        grid=(chunks,),
        in_specs=[columns(tokens), columns(3 * ROWS), feat_block],
        out_specs=blocks(steps, ROWS, LANES),
        out_shape=vectors(steps),
        scratch_shapes=[stage, table],
        compiler_params=params(),
        cost_estimate=cost(14 * elements, 6 * elements),
        name="gate",
    )(query, halo, feat)

    return pl.pallas_call(
        final_kernel,
        grid=(chunks,),
        in_specs=[whole(*pieces)] + [blocks(n, ROWS, LANES) for n in (modes, modes, modes, steps, steps)],
        out_specs=columns(tokens),
        out_shape=shape((tokens, width), bf16),
        scratch_shapes=[
            vmem((modes, tiles, LANES), f32),
            vmem((chunks, modes, ROWS, LANES), f32),
            vmem((steps * ROWS, LANES), f32),
        ],
        compiler_params=params(),
        cost_estimate=cost(40 * elements, 10 * elements),
        name="final",
    )(entered, decay, lead, mid, y, gate)


def solution(mesh):
    axes = tuple(mesh.axis_names)
    placed = (P(axes, None),) * 3 + (P(),) * 4
    return jax.shard_map(
        functools.partial(local, axes=axes),
        mesh=mesh,
        in_specs=placed,
        out_specs=P(axes, None),
        check_vma=False,
    )
```

```python
import functools
import math

import jax
import jax.numpy as jnp
from jax import lax
from jax.experimental import pallas as pl
from jax.experimental.pallas import tpu as pltpu
from jax.sharding import PartitionSpec as P

LANES = 128
ROWS = 8
TILES = 4
CHUNK = TILES * LANES
f32 = jnp.float32
bf16 = jnp.bfloat16


def params(limit=56 * 2**20):
    return pltpu.CompilerParams(vmem_limit_bytes=limit)


def put_tile(scratch, group, slot, tile):
    scratch[pl.ds((group * ROWS + slot) * ROWS, ROWS), :] = tile


def get_row(scratch, group, row):
    return scratch[pl.ds(group * ROWS * ROWS + row, ROWS, stride=ROWS), :]


def lanes_of(value, tile):
    return value[:, tile * LANES : (tile + 1) * LANES]


def stage_tokens(source, scratch):
    half_groups = source.shape[0] // ROWS // 2
    for pair in range(half_groups):
        block = source[pl.ds(pair * 2 * ROWS, 2 * ROWS), :].astype(f32)
        for part in range(2):
            group = pair * 2 + part
            half, within = group // half_groups, group % half_groups
            for tile in range(TILES):
                piece = lanes_of(block, tile)[part * ROWS : (part + 1) * ROWS]
                put_tile(scratch, within + 1, half * TILES + tile, piece)
                if half == 0 and within == half_groups - 1:
                    put_tile(scratch, 0, TILES + tile, piece)


def stage_table(table, scratch):
    for group in range(table.shape[0] // ROWS):
        for tile in range(TILES):
            piece = lanes_of(table, tile)[group * ROWS : (group + 1) * ROWS]
            put_tile(scratch, group, tile, piece)
            put_tile(scratch, group, TILES + tile, piece)


def fir(taps, now, past):
    total = taps[0] * now
    for lag in range(1, len(taps)):
        total = total + taps[lag] * past[-lag]
    return total


def rounded(value):
    return value.astype(bf16).astype(f32)


def pack_kernel(key_ref, value_ref, query_ref, out_ref):
    tails = [ref[...].astype(f32)[ROWS:] for ref in (key_ref, value_ref, query_ref)]
    out_ref[...] = jnp.concatenate(tails, axis=0).astype(bf16)


def widened(group_taps):
    count = group_taps.shape[-1]
    group = lax.broadcasted_iota(jnp.int32, (count, LANES), 0)
    lane = lax.broadcasted_iota(jnp.int32, (count, LANES), 1)
    pick = (group == lane // (LANES // count)).astype(f32).astype(bf16)
    wide, rest = None, group_taps
    for _ in range(3):
        term = rest.astype(bf16)
        rest = rest - term.astype(f32)
        part = jnp.dot(term, pick, preferred_element_type=f32)
        wide = part if wide is None else wide + part
    return [wide[at : at + ROWS] for at in range(0, wide.shape[0], ROWS)]


def first_half():
    return lax.broadcasted_iota(jnp.int32, (ROWS, LANES), 0) < TILES


def power(base, exponent):
    result = None
    while exponent:
        if exponent & 1:
            result = base if result is None else result * base
        base = base * base
        exponent >>= 1
    return result


def signal_kernel(key_ref, value_ref, feat_ref, rate_ref, u_ref, decay_ref, tap_ref, state_ref, *scratches):
    key_scr, value_scr, table_scr = scratches
    modes = rate_ref.shape[0]
    steps = u_ref.shape[0]
    top = first_half()
    for ref, scr in ((key_ref, key_scr), (value_ref, value_scr)):
        stage_tokens(ref, scr)
        for tile in range(TILES):
            put_tile(scr, 0, tile, jnp.zeros((ROWS, LANES), f32))
    reach = tap_ref.shape[0] // 2 - 1
    both = widened(feat_ref[(reach + 1) * ROWS :, :])
    taps = (both[: reach + 1], both[reach + 1 :])
    for lag, tap in enumerate(both):
        tap_ref[lag] = tap
    stage_table(rate_ref[...], table_scr)
    for mode in range(modes):
        decay_ref[mode] = jnp.exp(-get_row(table_scr, mode // ROWS, mode % ROWS))
    decay = [decay_ref[mode] for mode in range(modes)]

    def eight(group, carry, opening=False):
        state, past = carry
        state = list(state)
        past = [list(past[0]), list(past[1])]
        for row in range(ROWS):
            parts = []
            for member, scr in enumerate((key_scr, value_scr)):
                now = get_row(scr, group + 1, row)
                parts.append(fir(taps[member], now, past[member]))
                past[member] = past[member][1:] + [now]
            u = rounded(parts[0] * parts[1])
            if opening and row < reach:
                u = jnp.where(top, 0.0, u)
            u_ref[group * ROWS + row] = u
            if opening and row == 0:
                state = [u for _ in range(modes)]
            else:
                state = [decay[mode] * state[mode] + u for mode in range(modes)]
        return tuple(state), (tuple(past[0]), tuple(past[1]))

    past = tuple(
        tuple(get_row(scr, 0, ROWS - reach + row) for row in range(reach)) for scr in (key_scr, value_scr)
    )
    carry = eight(0, ((None,) * modes, past), True)
    for group in range(1, steps // ROWS):
        carry = eight(group, carry)
    state, _ = carry
    for mode in range(modes):
        through = power(decay[mode], steps) * state[mode]
        state_ref[mode] = pltpu.roll(through, TILES, 0) + state[mode]


def head_kernel(key_ref, value_ref, halo_ref, decay_ref, tap_ref, state_ref, out_ref, head_ref, *scratches, tokens):
    key_scr, value_scr, total_scr = scratches
    chunks, modes = state_ref.shape[:2]
    pieces, piece_rows = out_ref.shape[:2]
    reach = tap_ref.shape[1] // 2 - 1
    top = first_half()
    for chunk in range(chunks):
        span = slice(chunk * CHUNK, (chunk + 1) * CHUNK)
        halo = halo_ref[:, span].astype(f32)
        for member, (ref, scr) in enumerate(((key_ref, key_scr), (value_ref, value_scr))):
            block = ref[:, span].astype(f32)
            for tile in range(TILES):
                before = lanes_of(halo, tile)[member * ROWS : (member + 1) * ROWS]
                after = lanes_of(block, tile)[:ROWS]
                for slot in (tile, TILES + tile):
                    put_tile(scr, 0, slot, before)
                    put_tile(scr, 1, slot, after)
        taps = [
            [tap_ref[chunk, member * (reach + 1) + lag] for lag in range(reach + 1)] for member in range(2)
        ]
        signals = []
        for row in range(reach):
            parts = []
            for member, scr in enumerate((key_scr, value_scr)):
                seen = [
                    get_row(scr, 1, row - lag) if lag <= row else get_row(scr, 0, ROWS + row - lag)
                    for lag in range(reach + 1)
                ]
                parts.append(fir(taps[member], seen[0], seen[:0:-1]))
            signals.append(jnp.where(top, rounded(parts[0] * parts[1]), 0.0))
            head_ref[chunk, row] = signals[-1]
        for row in range(reach, ROWS):
            head_ref[chunk, row] = jnp.zeros((ROWS, LANES), f32)
        for mode in range(modes):
            decay = decay_ref[chunk, mode]
            head = signals[0]
            for row in range(1, reach):
                head = decay * head + signals[row]
            head = power(decay, tokens - reach) * head
            total = state_ref[chunk, mode] + pltpu.roll(head, TILES, 0)
            total_scr[mode, chunk * TILES : (chunk + 1) * TILES, :] = total[TILES:]
    split = pieces // modes
    for mode in range(modes):
        for part in range(split):
            rows = total_scr[mode, part * piece_rows : (part + 1) * piece_rows, :]
            out_ref[mode * split + part] = rows.astype(out_ref.dtype)


def local_kernel(u_ref, head_ref, decay_ref, coef_ref, skip_ref, y_ref, lead_ref, mid_ref, table_scr):
    steps = u_ref.shape[0]
    modes = decay_ref.shape[0]
    stage_table(coef_ref[...], table_scr)
    for mode in range(modes):
        lead_ref[mode] = get_row(table_scr, mode // ROWS, mode % ROWS)
    coef = [lead_ref[mode] for mode in range(modes)]
    skip_tile = jnp.broadcast_to(skip_ref[...], (ROWS, CHUNK))
    stage_table(skip_tile, table_scr)
    skip = get_row(table_scr, 0, 0)
    decay = [decay_ref[mode] for mode in range(modes)]

    def eight(group, state, opening=False):
        state = list(state)
        for row in range(ROWS):
            u = u_ref[group * ROWS + row]
            if opening:
                u = u + head_ref[row]
            if opening and row == 0:
                state = [u for _ in range(modes)]
            else:
                state = [decay[mode] * state[mode] + u for mode in range(modes)]
            terms = [skip * u] + [coef[mode] * state[mode] for mode in range(modes)]
            while len(terms) > 1:
                terms = [sum(terms[at + 1 : at + 2], terms[at]) for at in range(0, len(terms), 2)]
            y_ref[group * ROWS + row] = terms[0]
        return tuple(state)

    state = eight(0, (None,) * modes, True)
    for group in range(1, steps // ROWS):
        state = eight(group, state)
    for mode in range(modes):
        mid_ref[mode] = pltpu.roll(state[mode], TILES, 0)


def gate_kernel(query_ref, halo_ref, feat_ref, gate_ref, query_scr):
    steps = gate_ref.shape[0]
    stage_tokens(query_ref, query_scr)
    halo = halo_ref[...].astype(f32)[2 * ROWS :]
    for tile in range(TILES):
        put_tile(query_scr, 0, tile, lanes_of(halo, tile))
    reach = feat_ref.shape[0] // (3 * ROWS) - 1
    taps = widened(feat_ref[: (reach + 1) * ROWS, :])

    def eight(group, past):
        past = list(past)
        for row in range(ROWS):
            now = get_row(query_scr, group + 1, row)
            gate_ref[group * ROWS + row] = rounded(fir(taps, now, past))
            past = past[1:] + [now]
        return tuple(past)

    past = tuple(get_row(query_scr, 0, ROWS - reach + row) for row in range(reach))
    for group in range(steps // ROWS):
        past = eight(group, past)


def prefix_kernel(piece_ref, rate_ref, out_ref, table_scr, *, tokens, axes):
    devices, piece_rows = piece_ref.shape[:2]
    split = devices // rate_ref.shape[0]
    mine = lax.axis_index(axes)
    mode, part = mine // split, mine % split
    group = pl.multiple_of(mode // ROWS * ROWS, ROWS)
    first = pl.multiple_of(part * piece_rows * LANES, LANES)
    rows = rate_ref[pl.ds(group, ROWS), pl.ds(first, piece_rows * LANES)]
    here = lax.broadcasted_iota(jnp.int32, rows.shape, 0) == mode - group
    rate = jnp.sum(jnp.where(here, rows, 0.0), axis=0, keepdims=True)
    for row in range(piece_rows):
        table_scr[row : row + 1, :] = lanes_of(rate, row)
    through = jnp.exp(-float(tokens) * table_scr[:piece_rows, :])

    def lap(source, entering):
        out_ref[source] = entering.astype(out_ref.dtype)
        return through * entering + piece_ref[source].astype(f32)

    lax.fori_loop(0, devices, lap, jnp.zeros((piece_rows, LANES), f32))


def final_kernel(piece_ref, decay_ref, lead_ref, mid_ref, y_ref, gate_ref, out_ref, total_scr, enter_scr, out_scr):
    chunk = pl.program_id(0)
    modes = decay_ref.shape[0]
    steps = y_ref.shape[0]
    top = first_half()

    @pl.when(chunk == 0)
    def _():
        pieces, piece_rows = piece_ref.shape[:2]
        split = pieces // modes
        for mode in range(modes):
            for part in range(split):
                rows = piece_ref[mode * split + part].astype(f32)
                total_scr[mode, part * piece_rows : (part + 1) * piece_rows, :] = rows
        for at in range(enter_scr.shape[0]):
            for mode in range(modes):
                rows = total_scr[mode, at * TILES : (at + 1) * TILES, :]
                enter_scr[at, mode, :TILES, :] = rows
                enter_scr[at, mode, TILES:, :] = rows

    decay = [decay_ref[mode] for mode in range(modes)]
    state = []
    for mode in range(modes):
        enter = enter_scr[chunk, mode]
        later = power(decay[mode], steps) * enter + mid_ref[mode]
        state.append(lead_ref[mode] * jnp.where(top, enter, later))

    def eight(group, state):
        state = list(state)
        for row in range(ROWS):
            state = [decay[mode] * state[mode] for mode in range(modes)]
            terms = state
            while len(terms) > 1:
                terms = [sum(terms[at + 1 : at + 2], terms[at]) for at in range(0, len(terms), 2)]
            at = group * ROWS + row
            value = gate_ref[at] * rounded(y_ref[at] + terms[0])
            out_scr[pl.ds(group * ROWS * ROWS + row, ROWS, stride=ROWS), :] = value
        return tuple(state)

    for group in range(steps // ROWS):
        state = eight(group, state)
    half_groups = steps // ROWS
    for pair in range(half_groups):
        for tile in range(TILES):
            parts = []
            for group in (pair * 2, pair * 2 + 1):
                half, within = group // half_groups, group % half_groups
                slot = (within * ROWS + half * TILES + tile) * ROWS
                parts.append(out_scr[pl.ds(slot, ROWS), :])
            out_ref[pl.ds(pair * 2 * ROWS, 2 * ROWS), tile * LANES : (tile + 1) * LANES] = jnp.concatenate(
                parts, axis=0
            ).astype(bf16)


def cost(flops, moved):
    return pl.CostEstimate(flops=int(flops), bytes_accessed=int(moved), transcendentals=0)


def local(query, key_proj, value_proj, featurizer, rates, residues, skip, *, axes):
    tokens, width = query.shape
    modes = rates.shape[0]
    members, taps, groups = featurizer.shape
    devices = math.prod(lax.axis_size(axis) for axis in axes)
    chunks = width // CHUNK
    steps = tokens // 2
    tiles = width // LANES
    split = devices // modes
    even = devices % modes == 0 and tiles % split == 0
    shape = jax.ShapeDtypeStruct
    vmem = pltpu.VMEM
    elements = tokens * width

    def blocks(*dims):
        return pl.BlockSpec((None, *dims), lambda at: (at,) + (0,) * len(dims))

    columns = lambda rows: pl.BlockSpec((rows, CHUNK), lambda at: (0, at))
    whole = lambda *dims: pl.BlockSpec(dims, lambda at: (0,) * len(dims))
    tail = pl.BlockSpec((2 * ROWS, width), lambda at: (tokens // (2 * ROWS) - 1, 0))
    front = pl.BlockSpec((2 * ROWS, width), lambda at: (0, 0))
    vectors = lambda count: shape((chunks, count, ROWS, LANES), f32)

    feat = featurizer.reshape(members, taps, chunks, 1, TILES, groups // tiles).transpose(2, 0, 1, 3, 4, 5)
    feat = jnp.broadcast_to(feat, (chunks, members, taps, 2, TILES, groups // tiles))
    feat = feat.reshape(chunks, members * taps * ROWS, groups // tiles)
    feat_block = blocks(members * taps * ROWS, groups // tiles)

    packed = pl.pallas_call(
        pack_kernel,
        grid=(1,),
        in_specs=[tail] * 3,
        out_specs=whole(3 * ROWS, width),
        out_shape=shape((3 * ROWS, width), bf16),
        compiler_params=params(),
        name="pack",
    )(key_proj, value_proj, query)
    halo = lax.ppermute(packed, axes, [(at, at + 1) for at in range(devices - 1)])

    stage = vmem(((steps // ROWS + 1) * ROWS * ROWS, LANES), f32)
    table = vmem((2 * ROWS * ROWS, LANES), f32)
    u, decay, wide_taps, state = pl.pallas_call(
        signal_kernel,
        grid=(chunks,),
        in_specs=[columns(tokens)] * 2 + [feat_block, columns(modes)],
        out_specs=[blocks(n, ROWS, LANES) for n in (steps, modes, 2 * taps, modes)],
        out_shape=[vectors(n) for n in (steps, modes, 2 * taps, modes)],
        scratch_shapes=[stage, stage, table],
        compiler_params=params(),
        cost_estimate=cost(60 * elements, 10 * elements),
        name="signal",
    )(key_proj, value_proj, feat, rates)

    pieces = (modes * split, tiles // split, LANES) if even else (modes, tiles, LANES)
    flat = (modes, width)
    small = vmem((2 * ROWS * ROWS, LANES), f32)
    left, head = pl.pallas_call(
        functools.partial(head_kernel, tokens=tokens),
        grid=(1,),
        in_specs=[front, front, whole(3 * ROWS, width)]
        + [whole(chunks, n, ROWS, LANES) for n in (modes, 2 * taps, modes)],
        out_specs=[whole(*pieces), whole(chunks, ROWS, ROWS, LANES)],
        out_shape=[shape(pieces, bf16), vectors(ROWS)],
        scratch_shapes=[small, small, vmem((modes, tiles, LANES), f32)],
        compiler_params=params(),
        name="head",
    )(key_proj, value_proj, halo, decay, wide_taps, state)

    left, halo_late = lax.optimization_barrier((left, halo))
    gate = pl.pallas_call(
        gate_kernel,
        grid=(chunks,),
        in_specs=[columns(tokens), columns(3 * ROWS), feat_block],
        out_specs=blocks(steps, ROWS, LANES),
        out_shape=vectors(steps),
        scratch_shapes=[stage],
        compiler_params=params(),
        cost_estimate=cost(14 * elements, 6 * elements),
        name="gate",
    )(query, halo_late, feat)

    def swap(value):
        return lax.all_to_all(value, axes, split_axis=0, concat_axis=0, tiled=True)

    if even:
        theirs, gate = lax.optimization_barrier((swap(left), gate))
        entering = pl.pallas_call(
            functools.partial(prefix_kernel, tokens=tokens, axes=axes),
            grid=(1,),
            in_specs=[whole(*pieces), whole(modes, width)],
            out_specs=whole(*pieces),
            out_shape=shape(pieces, bf16),
            scratch_shapes=[vmem((-(-pieces[1] // ROWS) * ROWS, LANES), f32)],
            compiler_params=params(),
            name="prefix",
        )(theirs, rates)
    else:
        share = modes * width // devices
        theirs, gate = lax.optimization_barrier((swap(left.reshape(devices, share)), gate))
        mine = lax.axis_index(axes)
        through = jnp.exp(-float(tokens) * lax.dynamic_slice_in_dim(rates.reshape(-1), mine * share, share))
        _, entering = lax.scan(
            lambda so_far, piece: (through * so_far + piece.astype(f32), so_far.astype(bf16)),
            jnp.zeros((share,), f32),
            theirs,
        )

    entering, u_late = lax.optimization_barrier((entering, u))
    entered = swap(entering).reshape(pieces)
    coef = residues * jnp.sqrt(-jnp.expm1(-2.0 * rates) / modes)
    y, lead, mid = pl.pallas_call(
        local_kernel,
        grid=(chunks,),
        in_specs=[blocks(n, ROWS, LANES) for n in (steps, ROWS, modes)] + [columns(modes), columns(1)],
        out_specs=[blocks(n, ROWS, LANES) for n in (steps, modes, modes)],
        out_shape=[vectors(n) for n in (steps, modes, modes)],
        scratch_shapes=[table],
        compiler_params=params(),
        cost_estimate=cost(66 * elements, 8 * elements),
        name="within",
    )(u_late, head, decay, coef, skip[None, :])

    return pl.pallas_call(
        final_kernel,
        grid=(chunks,),
        in_specs=[whole(*pieces)] + [blocks(n, ROWS, LANES) for n in (modes, modes, modes, steps, steps)],
        out_specs=columns(tokens),
        out_shape=shape((tokens, width), bf16),
        scratch_shapes=[
            vmem((modes, tiles, LANES), f32),
            vmem((chunks, modes, ROWS, LANES), f32),
            vmem((steps * ROWS, LANES), f32),
        ],
        compiler_params=params(),
        cost_estimate=cost(40 * elements, 10 * elements),
        name="final",
    )(entered, decay, lead, mid, y, gate)


def solution(mesh):
    axes = tuple(mesh.axis_names)
    placed = (P(axes, None),) * 3 + (P(),) * 4
    return jax.shard_map(
        functools.partial(local, axes=axes),
        mesh=mesh,
        in_specs=placed,
        out_specs=P(axes, None),
        check_vma=False,
    )
```

```python
import functools
import math

import jax
import jax.numpy as jnp
from jax import lax
from jax.experimental import pallas as pl
from jax.experimental.pallas import tpu as pltpu
from jax.sharding import PartitionSpec as P

LANES = 128
ROWS = 8
TILES = 4
CHUNK = TILES * LANES
LAP = 16
f32 = jnp.float32
bf16 = jnp.bfloat16


def put_tile(scratch, group, slot, tile):
    scratch[pl.ds((group * ROWS + slot) * ROWS, ROWS), :] = tile


def get_row(scratch, group, row):
    return scratch[pl.ds(group * ROWS * ROWS + row, ROWS, stride=ROWS), :]


def lanes_of(value, tile):
    return value[:, tile * LANES : (tile + 1) * LANES]


def stage_tokens(source, scratch):
    half_groups = source.shape[0] // ROWS // 2
    for pair in range(half_groups):
        block = source[pl.ds(pair * 2 * ROWS, 2 * ROWS), :].astype(f32)
        for part in range(2):
            group = pair * 2 + part
            half, within = group // half_groups, group % half_groups
            for tile in range(TILES):
                piece = lanes_of(block, tile)[part * ROWS : (part + 1) * ROWS]
                put_tile(scratch, within + 1, half * TILES + tile, piece)
                if half == 0 and within == half_groups - 1:
                    put_tile(scratch, 0, TILES + tile, piece)


def stage_table(table, scratch):
    for group in range(table.shape[0] // ROWS):
        for tile in range(TILES):
            piece = lanes_of(table, tile)[group * ROWS : (group + 1) * ROWS]
            put_tile(scratch, group, tile, piece)
            put_tile(scratch, group, TILES + tile, piece)


def fir(taps, now, past):
    total = taps[0] * now
    for lag in range(1, len(taps)):
        total = total + taps[lag] * past[-lag]
    return total


def rounded(value):
    return value.astype(bf16).astype(f32)


def lag_taps(rows, scratch, group):
    for tile in range(TILES):
        put_tile(scratch, group, tile, lanes_of(rows, tile))
        put_tile(scratch, group, TILES + tile, lanes_of(rows, tile))


def widened(group_taps):
    count = group_taps.shape[-1]
    group = lax.broadcasted_iota(jnp.int32, (count, CHUNK), 0)
    lane = lax.broadcasted_iota(jnp.int32, (count, CHUNK), 1)
    pick = (group == lane // (CHUNK // count)).astype(f32).astype(bf16)
    parts, rest = [], group_taps
    for _ in range(3):
        term = rest.astype(bf16)
        rest = rest - term.astype(f32)
        parts.append(jnp.dot(term, pick, preferred_element_type=f32))
    return parts[0] + parts[1] + parts[2]


def first_half():
    return lax.broadcasted_iota(jnp.int32, (ROWS, LANES), 0) < TILES


def power(base, exponent):
    result = None
    while exponent:
        if exponent & 1:
            result = base if result is None else result * base
        base = base * base
        exponent >>= 1
    return result


def tree(terms):
    while len(terms) > 1:
        terms = [sum(terms[at + 1 : at + 2], terms[at]) for at in range(0, len(terms), 2)]
    return terms[0]


def span(at):
    return pl.ds(pl.multiple_of(at * CHUNK, CHUNK), CHUNK)


def laps(steps, body, carry):
    def lap(number, carry):
        for part in range(LAP // ROWS):
            carry = body(number * (LAP // ROWS) + part, carry)
        return carry

    return lax.fori_loop(0, steps // LAP, lap, carry)


def pack_kernel(key_ref, value_ref, query_ref, out_ref, sem):
    tokens = key_ref.shape[0]
    copies = [
        pltpu.make_async_copy(
            ref.at[pl.ds(tokens - 2 * ROWS, 2 * ROWS)], out_ref.at[pl.ds(at * 2 * ROWS, 2 * ROWS)], sem.at[at]
        )
        for at, ref in enumerate((key_ref, value_ref, query_ref))
    ]
    for copy in copies:
        copy.start()
    for copy in copies:
        copy.wait()


def signal_kernel(key_ref, value_ref, feat_ref, rate_ref, u_ref, decay_ref, pair_ref, *scratches):
    key_buf, value_buf, feat_buf, rate_buf, u_buf, decay_buf, pair_buf = scratches[:7]
    wide_scr, key_scr, value_scr, table_scr, in_sem, small_sem, out_sem, last_sem = scratches[7:]
    chunks, steps = u_buf.shape[:2]
    modes = rate_buf.shape[0]
    reach = feat_buf.shape[2] - 2
    top = first_half()

    def fetch(at):
        return [
            pltpu.make_async_copy(ref.at[:, span(at)], buf.at[at], in_sem.at[member, at])
            for member, (ref, buf) in enumerate(((key_ref, key_buf), (value_ref, value_buf)))
        ]

    def send(at):
        return pltpu.make_async_copy(u_buf.at[at], u_ref.at[at], out_sem.at[at])

    small = [
        pltpu.make_async_copy(feat_ref, feat_buf, small_sem.at[0]),
        pltpu.make_async_copy(rate_ref, rate_buf, small_sem.at[1]),
    ]
    for copy in small:
        copy.start()
    for at in range(chunks):
        for copy in fetch(at):
            copy.start()
    small[0].wait()
    for member in range(2):
        rows = feat_buf[:, member + 1].reshape(chunks * ROWS, feat_buf.shape[-1])
        wide_scr[:, member] = widened(rows).reshape(chunks, ROWS, CHUNK)
    small[1].wait()

    def chunk(at, _):
        stage_table(rate_buf[:, span(at)], table_scr)
        decay = []
        for mode in range(modes):
            decay.append(jnp.exp(-get_row(table_scr, mode // ROWS, mode % ROWS)))
            decay_buf[at, mode] = decay[mode]
        taps = []
        for member in range(2):
            lag_taps(wide_scr[at, member], table_scr, member + 2)
            taps.append([get_row(table_scr, member + 2, lag) for lag in range(reach + 1)])
        for copy in fetch(at):
            copy.wait()
        for buf, scr in ((key_buf, key_scr), (value_buf, value_scr)):
            stage_tokens(buf.at[at], scr)
            for tile in range(TILES):
                put_tile(scr, 0, tile, jnp.zeros((ROWS, LANES), f32))

        def eight(group, carry):
            state, past = carry
            state = list(state)
            past = [list(past[0]), list(past[1])]
            for row in range(ROWS):
                parts = []
                for member, scr in enumerate((key_scr, value_scr)):
                    now = get_row(scr, group + 1, row)
                    parts.append(fir(taps[member], now, past[member]))
                    past[member] = past[member][1:] + [now]
                u = rounded(parts[0] * parts[1])
                if row < reach:
                    u = jnp.where(jnp.logical_and(top, group == 0), 0.0, u)
                u_buf[at, group * ROWS + row] = u
                state = [decay[mode] * state[mode] + u for mode in range(modes)]
            return tuple(state), (tuple(past[0]), tuple(past[1]))

        past = tuple(
            tuple(get_row(scr, 0, ROWS - reach + row) for row in range(reach)) for scr in (key_scr, value_scr)
        )
        state, _ = laps(steps, eight, ((jnp.zeros((ROWS, LANES), f32),) * modes, past))
        send(at).start()
        for mode in range(modes // 2):
            whole = []
            for one in (mode, mode + modes // 2):
                whole.append(state[one] + pltpu.roll(power(decay[one], steps) * state[one], TILES, 0))
            pair_buf[at, mode] = jnp.where(top, pltpu.roll(whole[0], TILES, 0), whole[1])
            pair_buf[at, modes // 2 + mode] = jnp.where(top, decay[mode], decay[mode + modes // 2])
        for lag in range(reach + 1):
            pair_buf[at, modes + lag] = jnp.where(top, taps[0][lag], taps[1][lag])
        return 0

    lax.fori_loop(0, chunks, chunk, 0)
    last = [
        pltpu.make_async_copy(decay_buf, decay_ref, last_sem.at[0]),
        pltpu.make_async_copy(pair_buf, pair_ref, last_sem.at[1]),
    ]
    for copy in last:
        copy.start()
    for at in range(chunks):
        send(at).wait()
    for copy in last:
        copy.wait()


def head_kernel(key_ref, value_ref, halo_ref, pair_ref, out_ref, head_ref, *scratches, tokens, reach):
    front_buf, halo_buf, pair_buf, out_buf, head_buf, token_scr, total_scr, in_sem, pair_sem, out_sem = scratches
    chunks = pair_buf.shape[0]
    pieces, piece_rows = out_buf.shape[:2]
    modes = total_scr.shape[0]
    half = modes // 2
    top = first_half()
    copies = [
        pltpu.make_async_copy(halo_ref.at[pl.ds(0, 4 * ROWS)], halo_buf, in_sem.at[0]),
        pltpu.make_async_copy(key_ref.at[pl.ds(0, 2 * ROWS)], front_buf.at[0], in_sem.at[1]),
        pltpu.make_async_copy(value_ref.at[pl.ds(0, 2 * ROWS)], front_buf.at[1], in_sem.at[2]),
    ]
    pairs = [
        pltpu.make_async_copy(pair_ref.at[chunk], pair_buf.at[chunk], pair_sem.at[chunk]) for chunk in range(chunks)
    ]
    for copy in copies + pairs:
        copy.start()
    for copy in copies:
        copy.wait()
    for chunk in range(chunks):
        pairs[chunk].wait()
        lanes = slice(chunk * CHUNK, (chunk + 1) * CHUNK)
        for member in range(2):
            before = halo_buf[member * 2 * ROWS : (member + 1) * 2 * ROWS, lanes].astype(f32)[ROWS:]
            after = front_buf[member, :, lanes].astype(f32)[:ROWS]
            for tile in range(TILES):
                put_tile(token_scr, 0, member * TILES + tile, lanes_of(before, tile))
                put_tile(token_scr, 1, member * TILES + tile, lanes_of(after, tile))
        taps = [pair_buf[chunk, modes + lag] for lag in range(reach + 1)]
        seen = [get_row(token_scr, 0, ROWS - reach + row) for row in range(reach)]
        signals = []
        for row in range(reach):
            now = get_row(token_scr, 1, row)
            both = fir(taps, now, seen)
            seen = seen[1:] + [now]
            signals.append(rounded(both * pltpu.roll(both, TILES, 0)))
            head_buf[chunk, row] = jnp.where(top, signals[-1], 0.0)
        for row in range(reach, ROWS):
            head_buf[chunk, row] = jnp.zeros((ROWS, LANES), f32)
        for mode in range(half):
            decay = pair_buf[chunk, half + mode]
            head = signals[0]
            for row in range(1, reach):
                head = decay * head + signals[row]
            total = pair_buf[chunk, mode] + power(decay, tokens - reach) * head
            rows = slice(chunk * TILES, (chunk + 1) * TILES)
            total_scr[mode, rows, :] = total[:TILES]
            total_scr[half + mode, rows, :] = total[TILES:]
    split = pieces // modes
    for mode in range(modes):
        for part in range(split):
            rows = total_scr[mode, part * piece_rows : (part + 1) * piece_rows, :]
            out_buf[mode * split + part] = rows.astype(out_buf.dtype)
    outs = [
        pltpu.make_async_copy(out_buf, out_ref, out_sem.at[0]),
        pltpu.make_async_copy(head_buf, head_ref, out_sem.at[1]),
    ]
    for copy in outs:
        copy.start()
    for copy in outs:
        copy.wait()


def local_kernel(u_ref, head_ref, decay_ref, coef_ref, skip_ref, y_ref, enter_ref, *scratches):
    u_buf, head_buf, decay_buf, coef_buf, skip_buf, y_buf, enter_buf, table_scr = scratches[:8]
    in_sem, small_sem, out_sem = scratches[8:]
    chunks, steps = u_buf.shape[:2]
    modes = decay_buf.shape[1]
    top = first_half()

    def fetch(at):
        return [
            pltpu.make_async_copy(ref.at[at], buf.at[at], in_sem.at[member, at])
            for member, (ref, buf) in enumerate(((u_ref, u_buf), (decay_ref, decay_buf)))
        ]

    def send(at):
        return [
            pltpu.make_async_copy(buf.at[at], ref.at[at], out_sem.at[member, at])
            for member, (ref, buf) in enumerate(((y_ref, y_buf), (enter_ref, enter_buf)))
        ]

    small = [
        pltpu.make_async_copy(ref, buf, small_sem.at[at])
        for at, (ref, buf) in enumerate(((head_ref, head_buf), (coef_ref, coef_buf), (skip_ref, skip_buf)))
    ]
    for copy in small:
        copy.start()
    for at in range(chunks):
        for copy in fetch(at):
            copy.start()
    for copy in small:
        copy.wait()

    def chunk(at, _):
        stage_table(coef_buf[:, span(at)], table_scr)
        coef = [get_row(table_scr, mode // ROWS, mode % ROWS) for mode in range(modes)]
        lag_taps(jnp.broadcast_to(skip_buf[:, span(at)], (ROWS, CHUNK)), table_scr, modes // ROWS)
        skip = get_row(table_scr, modes // ROWS, 0)
        for copy in fetch(at):
            copy.wait()
        for row in range(ROWS):
            u_buf[at, row] = u_buf[at, row] + head_buf[at, row]
        decay = [decay_buf[at, mode] for mode in range(modes)]

        def eight(group, state):
            state = list(state)
            for row in range(ROWS):
                u = u_buf[at, group * ROWS + row]
                state = [decay[mode] * state[mode] + u for mode in range(modes)]
                y_buf[at, group * ROWS + row] = tree(
                    [skip * u] + [coef[mode] * state[mode] for mode in range(modes)]
                )
            return tuple(state)

        state = laps(steps, eight, (jnp.zeros((ROWS, LANES), f32),) * modes)
        for mode in range(modes):
            middle = pltpu.roll(state[mode], TILES, 0)
            enter_buf[at, mode] = coef[mode] * jnp.where(top, 1.0, power(decay[mode], steps))
            enter_buf[at, modes + mode] = jnp.where(top, 0.0, coef[mode] * middle)
        for copy in send(at):
            copy.start()
        return 0

    lax.fori_loop(0, chunks, chunk, 0)
    for at in range(chunks):
        for copy in send(at):
            copy.wait()


def gate_kernel(query_ref, halo_ref, feat_ref, gate_ref, *scratches):
    query_buf, halo_buf, feat_buf, gate_buf, wide_scr, query_scr, table_scr, in_sem, small_sem, out_sem = scratches
    chunks, steps = gate_buf.shape[0], gate_buf.shape[1] // ROWS
    reach = feat_buf.shape[2] - 2

    def fetch(at):
        return pltpu.make_async_copy(query_ref.at[:, span(at)], query_buf.at[at], in_sem.at[at])

    def send(at):
        return pltpu.make_async_copy(gate_buf.at[at], gate_ref.at[at], out_sem.at[at])

    small = [
        pltpu.make_async_copy(feat_ref, feat_buf, small_sem.at[0]),
        pltpu.make_async_copy(halo_ref.at[pl.ds(4 * ROWS, 2 * ROWS)], halo_buf, small_sem.at[1]),
    ]
    for copy in small:
        copy.start()
    for at in range(chunks):
        fetch(at).start()
    for copy in small:
        copy.wait()
    wide_scr[...] = widened(feat_buf[:, 0].reshape(chunks * ROWS, feat_buf.shape[-1])).reshape(chunks, ROWS, CHUNK)

    def chunk(at, _):
        lag_taps(wide_scr[at], table_scr, 0)
        taps = [get_row(table_scr, 0, lag) for lag in range(reach + 1)]
        fetch(at).wait()
        stage_tokens(query_buf.at[at], query_scr)
        halo = halo_buf[:, span(at)].astype(f32)[ROWS:]
        for tile in range(TILES):
            put_tile(query_scr, 0, tile, lanes_of(halo, tile))

        def eight(group, past):
            past = list(past)
            found = []
            for row in range(ROWS):
                now = get_row(query_scr, group + 1, row)
                found.append(fir(taps, now, past))
                past = past[1:] + [now]
            rows = jnp.concatenate(found, axis=0).astype(bf16)
            gate_buf[at, pl.ds(pl.multiple_of(group * ROWS * ROWS, ROWS * ROWS), ROWS * ROWS), :] = rows
            return tuple(past)

        past = tuple(get_row(query_scr, 0, ROWS - reach + row) for row in range(reach))
        laps(steps, eight, past)
        send(at).start()
        return 0

    lax.fori_loop(0, chunks, chunk, 0)
    for at in range(chunks):
        send(at).wait()


def prefix_kernel(piece_ref, rate_ref, out_ref, table_scr, *, tokens, axes):
    devices, piece_rows = piece_ref.shape[:2]
    split = devices // rate_ref.shape[0]
    mine = lax.axis_index(axes)
    mode, part = mine // split, mine % split
    group = pl.multiple_of(mode // ROWS * ROWS, ROWS)
    first = pl.multiple_of(part * piece_rows * LANES, LANES)
    rows = rate_ref[pl.ds(group, ROWS), pl.ds(first, piece_rows * LANES)]
    here = lax.broadcasted_iota(jnp.int32, rows.shape, 0) == mode - group
    rate = jnp.sum(jnp.where(here, rows, 0.0), axis=0, keepdims=True)
    for row in range(piece_rows):
        table_scr[row : row + 1, :] = lanes_of(rate, row)
    through = jnp.exp(-float(tokens) * table_scr[:piece_rows, :])

    def lap(source, entering):
        out_ref[source] = entering.astype(out_ref.dtype)
        return through * entering + piece_ref[source].astype(f32)

    lax.fori_loop(0, devices, lap, jnp.zeros((piece_rows, LANES), f32))


def final_kernel(piece_ref, decay_ref, enter_ref, y_ref, gate_ref, out_ref, *scratches):
    piece_buf, decay_buf, enter_buf, y_buf, gate_buf, out_buf, total_scr, state_scr, out_scr = scratches[:9]
    piece_sem, in_sem, out_sem = scratches[9:]
    chunks, modes = decay_buf.shape[:2]
    steps = y_buf.shape[1]
    half_groups = steps // ROWS

    def fetch(at):
        sources = ((decay_ref, decay_buf), (enter_ref, enter_buf), (y_ref, y_buf), (gate_ref, gate_buf))
        return [
            pltpu.make_async_copy(ref.at[at], buf.at[at], in_sem.at[member, at])
            for member, (ref, buf) in enumerate(sources)
        ]

    def send(at):
        return pltpu.make_async_copy(out_buf.at[at], out_ref.at[:, span(at)], out_sem.at[at])

    piece_copy = pltpu.make_async_copy(piece_ref, piece_buf, piece_sem.at[0])
    piece_copy.start()
    for at in range(chunks):
        for copy in fetch(at):
            copy.start()
    piece_copy.wait()
    pieces, piece_rows = piece_buf.shape[:2]
    split = pieces // modes
    for mode in range(modes):
        for part in range(split):
            rows = piece_buf[mode * split + part].astype(f32)
            total_scr[mode, part * piece_rows : (part + 1) * piece_rows, :] = rows
    for at in range(chunks):
        for mode in range(modes):
            rows = total_scr[mode, at * TILES : (at + 1) * TILES, :]
            state_scr[at, mode, :TILES, :] = rows
            state_scr[at, mode, TILES:, :] = rows

    def chunk(at, _):
        for copy in fetch(at):
            copy.wait()
        decay = [decay_buf[at, mode] for mode in range(modes)]
        state = tuple(
            enter_buf[at, mode] * state_scr[at, mode] + enter_buf[at, modes + mode] for mode in range(modes)
        )

        def eight(group, state):
            first = pl.multiple_of(group * ROWS * ROWS, ROWS * ROWS)
            gates = gate_buf[at, pl.ds(first, ROWS * ROWS), :].astype(f32)
            for row in range(ROWS):
                state = [decay[mode] * state[mode] for mode in range(modes)]
                conv = rounded(y_buf[at, group * ROWS + row] + tree(state))
                value = gates[row * ROWS : (row + 1) * ROWS] * conv
                out_scr[pl.ds(first + row, ROWS, stride=ROWS), :] = value
            return tuple(state)

        laps(steps, eight, state)
        for pair in range(half_groups):
            for tile in range(TILES):
                parts = []
                for group in (pair * 2, pair * 2 + 1):
                    half, within = group // half_groups, group % half_groups
                    slot = (within * ROWS + half * TILES + tile) * ROWS
                    parts.append(out_scr[pl.ds(slot, ROWS), :])
                rows = jnp.concatenate(parts, axis=0).astype(bf16)
                out_buf[at, pl.ds(pair * 2 * ROWS, 2 * ROWS), tile * LANES : (tile + 1) * LANES] = rows
        send(at).start()
        return 0

    lax.fori_loop(0, chunks, chunk, 0)
    for at in range(chunks):
        send(at).wait()


def cost(flops, moved):
    return pl.CostEstimate(flops=int(flops), bytes_accessed=int(moved), transcendentals=0)


def local(query, key_proj, value_proj, featurizer, rates, residues, skip, *, axes):
    tokens, width = query.shape
    modes = rates.shape[0]
    members, taps, groups = featurizer.shape
    devices = math.prod(lax.axis_size(axis) for axis in axes)
    chunks = width // CHUNK
    steps = tokens // 2
    tiles = width // LANES
    split = devices // modes
    even = devices % modes == 0 and tiles % split == 0
    shape = jax.ShapeDtypeStruct
    vmem = pltpu.VMEM
    dma = pltpu.SemaphoreType.DMA
    elements = tokens * width
    there = pl.BlockSpec(memory_space=pl.ANY)

    def call(kernel, inputs, outputs, scratches, name, **more):
        return pl.pallas_call(
            kernel,
            in_specs=[there] * len(inputs),
            out_specs=[there] * len(outputs),
            out_shape=outputs,
            scratch_shapes=scratches,
            compiler_params=pltpu.CompilerParams(vmem_limit_bytes=60 * 2**20),
            name=name,
            **more,
        )(*inputs)

    def vectors(count, kind=f32):
        return (chunks, count, ROWS, LANES), kind

    (packed,) = call(
        pack_kernel,
        (key_proj, value_proj, query),
        [shape((members * 2 * ROWS, width), bf16)],
        [dma((members,))],
        "pack",
    )
    halo = lax.ppermute(packed, axes, [(at, at + 1) for at in range(devices - 1)])

    feat = featurizer.reshape(members, taps, chunks, groups // chunks).transpose(2, 0, 1, 3)
    feat = jnp.pad(feat, ((0, 0), (0, 0), (0, ROWS - taps), (0, 0)))
    tokens_buf = vmem((chunks, tokens, CHUNK), bf16)
    feat_buf = vmem(feat.shape, f32)
    stage = vmem(((steps // ROWS + 1) * ROWS * ROWS, LANES), f32)
    pairs = vectors(modes + taps)
    u, decay, pair = call(
        signal_kernel,
        (key_proj, value_proj, feat, rates),
        [shape(*vectors(steps)), shape(*vectors(modes)), shape(*pairs)],
        [tokens_buf, tokens_buf, feat_buf, vmem((modes, width), f32)]
        + [vmem(*vectors(steps)), vmem(*vectors(modes)), vmem(*pairs)]
        + [vmem((chunks, 2, ROWS, CHUNK), f32), stage, stage, vmem((4 * ROWS * ROWS, LANES), f32)]
        + [dma((2, chunks)), dma((2,)), dma((chunks,)), dma((2,))],
        "signal",
        cost_estimate=cost(60 * elements, 10 * elements),
    )

    pieces = (modes * split, tiles // split, LANES) if even else (modes, tiles, LANES)
    left, head = call(
        functools.partial(head_kernel, tokens=tokens, reach=taps - 1),
        (key_proj, value_proj, halo, pair),
        [shape(pieces, bf16), shape(*vectors(ROWS))],
        [vmem((2, 2 * ROWS, width), bf16), vmem((4 * ROWS, width), bf16), vmem(*pairs)]
        + [vmem(pieces, bf16), vmem(*vectors(ROWS)), vmem((2 * ROWS * ROWS, LANES), f32)]
        + [vmem((modes, tiles, LANES), f32), dma((3,)), dma((chunks,)), dma((2,))],
        "head",
    )
    left, halo_late = lax.optimization_barrier((left, halo))

    gate_shape = ((chunks, steps * ROWS, LANES), bf16)
    (gate,) = call(
        gate_kernel,
        (query, halo_late, feat),
        [shape(*gate_shape)],
        [tokens_buf, vmem((2 * ROWS, width), bf16), feat_buf, vmem(*gate_shape)]
        + [vmem((chunks, ROWS, CHUNK), f32), stage, vmem((ROWS * ROWS, LANES), f32)]
        + [dma((chunks,)), dma((2,)), dma((chunks,))],
        "gate",
        cost_estimate=cost(14 * elements, 4 * elements),
    )

    def swap(value):
        return lax.all_to_all(value, axes, split_axis=0, concat_axis=0, tiled=True)

    if even:
        theirs, gate = lax.optimization_barrier((swap(left), gate))
        entering = pl.pallas_call(
            functools.partial(prefix_kernel, tokens=tokens, axes=axes),
            out_shape=shape(pieces, bf16),
            scratch_shapes=[vmem((-(-pieces[1] // ROWS) * ROWS, LANES), f32)],
            compiler_params=pltpu.CompilerParams(vmem_limit_bytes=60 * 2**20),
            name="prefix",
        )(theirs, rates)
    else:
        share = modes * width // devices
        theirs, gate = lax.optimization_barrier((swap(left.reshape(devices, share)), gate))
        mine = lax.axis_index(axes)
        through = jnp.exp(-float(tokens) * lax.dynamic_slice_in_dim(rates.reshape(-1), mine * share, share))
        _, entering = lax.scan(
            lambda so_far, piece: (through * so_far + piece.astype(f32), so_far.astype(bf16)),
            jnp.zeros((share,), f32),
            theirs,
        )

    entering, u_late = lax.optimization_barrier((entering, u))
    entered = swap(entering).reshape(pieces)
    coef = residues * jnp.sqrt(-jnp.expm1(-2.0 * rates) / modes)
    y, enter = call(
        local_kernel,
        (u_late, head, decay, coef, skip[None, :]),
        [shape(*vectors(steps)), shape(*vectors(2 * modes))],
        [vmem(*vectors(steps)), vmem(*vectors(ROWS)), vmem(*vectors(modes)), vmem((modes, width), f32)]
        + [vmem((1, width), f32), vmem(*vectors(steps)), vmem(*vectors(2 * modes))]
        + [vmem((3 * ROWS * ROWS, LANES), f32), dma((2, chunks)), dma((3,)), dma((2, chunks))],
        "within",
        cost_estimate=cost(66 * elements, 8 * elements),
    )

    (out,) = call(
        final_kernel,
        (entered, decay, enter, y, gate),
        [shape((tokens, width), bf16)],
        [vmem(pieces, bf16), vmem(*vectors(modes)), vmem(*vectors(2 * modes)), vmem(*vectors(steps))]
        + [vmem(*gate_shape), tokens_buf, vmem((modes, tiles, LANES), f32), vmem(*vectors(modes))]
        + [vmem((steps * ROWS, LANES), f32), dma((1,)), dma((4, chunks)), dma((chunks,))],
        "final",
        cost_estimate=cost(40 * elements, 10 * elements),
    )
    return out


def solution(mesh):
    axes = tuple(mesh.axis_names)
    placed = (P(axes, None),) * 3 + (P(),) * 4
    return jax.shard_map(
        functools.partial(local, axes=axes),
        mesh=mesh,
        in_specs=placed,
        out_specs=P(axes, None),
        check_vma=False,
    )
```

```python
import functools
import math

import jax
import jax.numpy as jnp
from jax import lax
from jax.experimental import pallas as pl
from jax.experimental.pallas import tpu as pltpu
from jax.sharding import PartitionSpec as P

LANES = 128
ROWS = 8
TILES = 4
CHUNK = TILES * LANES
LAP = 16
BLOCK = LAP * ROWS
AHEAD = 3
f32 = jnp.float32
bf16 = jnp.bfloat16


def put_tile(scratch, group, slot, tile):
    scratch[pl.ds((group * ROWS + slot) * ROWS, ROWS), :] = tile


def get_row(scratch, group, row):
    return scratch[pl.ds(group * ROWS * ROWS + row, ROWS, stride=ROWS), :]


def lanes_of(value, tile):
    return value[:, tile * LANES : (tile + 1) * LANES]


def place(row, step=1):
    return pl.ds(pl.multiple_of(row * ROWS, ROWS), step * ROWS)


def spread(row_of):
    slot = lax.broadcasted_iota(jnp.int32, (ROWS, LANES), 0) % TILES
    result = jnp.broadcast_to(row_of(TILES - 1), (ROWS, LANES))
    for tile in range(TILES - 1):
        result = jnp.where(slot == tile, jnp.broadcast_to(row_of(tile), (ROWS, LANES)), result)
    return result


def spread_rows(ref, at, rows):
    def one(row):
        return spread(lambda tile: ref[row : row + 1, pl.ds(pl.multiple_of((at * TILES + tile) * LANES, LANES), LANES)])

    return [one(row) for row in rows]


def relayout():
    row = lax.broadcasted_iota(jnp.int32, (BLOCK, BLOCK), 0)
    column = lax.broadcasted_iota(jnp.int32, (BLOCK, BLOCK), 1)
    same = jnp.logical_and(row // ROWS == column % LAP, row % ROWS == column // LAP)
    return same.astype(f32).astype(bf16)


def block_of(buf, at, number, steps):
    return jnp.concatenate(
        [
            buf[at, pl.ds(pl.multiple_of(half * steps + number * LAP, LAP), LAP), tile * LANES : (tile + 1) * LANES]
            for half in range(2)
            for tile in range(TILES)
        ],
        axis=0,
    )


def move_block(bufs, scrs, at, slot, number, steps, matrix):
    wide = jnp.concatenate([block_of(buf, at, number, steps) for buf in bufs], axis=1)
    moved = jnp.dot(matrix, wide, preferred_element_type=f32)
    rows = pl.ds(pl.multiple_of(number * BLOCK, BLOCK), BLOCK)
    for position, scr in enumerate(scrs):
        scr[slot, rows, :] = lanes_of(moved, position)


def fir(taps, now, past):
    total = taps[0] * now
    for lag in range(1, len(taps)):
        total = total + taps[lag] * past[-lag]
    return total


def rounded(value):
    return value.astype(bf16).astype(f32)


def widened(group_taps):
    count = group_taps.shape[-1]
    group = lax.broadcasted_iota(jnp.int32, (count, CHUNK), 0)
    lane = lax.broadcasted_iota(jnp.int32, (count, CHUNK), 1)
    pick = (group == lane // (CHUNK // count)).astype(f32).astype(bf16)
    parts, rest = [], group_taps
    for _ in range(3):
        term = rest.astype(bf16)
        rest = rest - term.astype(f32)
        parts.append(jnp.dot(term, pick, preferred_element_type=f32))
    return parts[0] + parts[1] + parts[2]


def chunk_taps(wide_scr, at, member):
    def one(lag):
        return spread(lambda tile: wide_scr[at, member, lag : lag + 1, tile * LANES : (tile + 1) * LANES])

    return one


def first_half():
    return lax.broadcasted_iota(jnp.int32, (ROWS, LANES), 0) < TILES


def power(base, exponent):
    result = None
    while exponent:
        if exponent & 1:
            result = base if result is None else result * base
        base = base * base
        exponent >>= 1
    return result


def tree(terms):
    while len(terms) > 1:
        terms = [sum(terms[at + 1 : at + 2], terms[at]) for at in range(0, len(terms), 2)]
    return terms[0]


def span(at):
    return pl.ds(pl.multiple_of(at * CHUNK, CHUNK), CHUNK)


def start_all(copies):
    for copy in copies:
        copy.start()


def wait_all(copies):
    for copy in copies:
        copy.wait()


def over_chunks(chunks, fetch, body):
    for at in range(min(AHEAD, chunks)):
        start_all(fetch(at))

    def one(at, _):
        @pl.when(at + AHEAD < chunks)
        def _():
            start_all(fetch(at + AHEAD))

        body(at)
        return 0

    return lambda: lax.fori_loop(0, chunks, one, 0)


def pack_kernel(key_ref, value_ref, query_ref, out_ref, in_buf, out_buf, in_sem, out_sem):
    tokens = key_ref.shape[0]
    copies = [
        pltpu.make_async_copy(ref.at[pl.ds(tokens - 2 * ROWS, 2 * ROWS)], in_buf.at[at], in_sem.at[at])
        for at, ref in enumerate((key_ref, value_ref, query_ref))
    ]
    start_all(copies)
    wait_all(copies)
    tails = [in_buf[at].astype(f32)[ROWS:] for at in range(len(copies))]
    out_buf[...] = jnp.concatenate(tails, axis=0).astype(bf16)
    last = pltpu.make_async_copy(out_buf, out_ref, out_sem.at[0])
    last.start()
    last.wait()


def signal_kernel(key_ref, value_ref, feat_ref, rate_ref, u_ref, decay_ref, pair_ref, *scratches):
    key_buf, value_buf, feat_buf, rate_buf, u_buf, decay_buf, pair_buf = scratches[:7]
    wide_scr, key_scr, value_scr, in_sem, small_sem, out_sem = scratches[7:]
    chunks, steps = u_buf.shape[0], u_buf.shape[1] // ROWS
    modes = rate_buf.shape[0]
    reach = feat_buf.shape[2] - 1
    top = first_half()
    matrix = relayout()
    bufs, scrs = (key_buf, value_buf), (key_scr, value_scr)

    def fetch(at):
        return [
            pltpu.make_async_copy(ref.at[:, span(at)], buf.at[at], in_sem.at[member, at])
            for member, (ref, buf) in enumerate(((key_ref, key_buf), (value_ref, value_buf)))
        ]

    def send(at):
        sources = ((u_buf, u_ref), (decay_buf, decay_ref), (pair_buf, pair_ref))
        return [
            pltpu.make_async_copy(buf.at[at], ref.at[at], out_sem.at[member, at])
            for member, (buf, ref) in enumerate(sources)
        ]

    small = [
        pltpu.make_async_copy(feat_ref, feat_buf, small_sem.at[0]),
        pltpu.make_async_copy(rate_ref, rate_buf, small_sem.at[1]),
    ]
    start_all(small)

    def chunk(at):
        @pl.when(at + 1 < chunks)
        def _():
            wait_all(fetch(at + 1))

        decay = [jnp.exp(-rate) for rate in spread_rows(rate_buf, at, range(modes))]
        for mode in range(modes):
            decay_buf[at, mode] = decay[mode]
        taps = [[chunk_taps(wide_scr, at, member)(lag) for lag in range(reach + 1)] for member in range(2)]
        slot, later = at % 2, jnp.minimum(at + 1, chunks - 1)

        def lap(number, carry):
            state, past = carry
            state = list(state)
            past = [list(past[0]), list(past[1])]
            move_block(bufs, scrs, later, 1 - slot, number, steps, matrix)
            opening = jnp.logical_and(top, number == 0)
            for row in range(0, LAP, 2):
                found = []
                for step in (row, row + 1):
                    parts = []
                    for member, scr in enumerate(scrs):
                        now = scr[slot, place(number * LAP + step), :]
                        parts.append(fir(taps[member], now, past[member]))
                        past[member] = past[member][1:] + [now]
                    u = parts[0] * parts[1]
                    found.append(jnp.where(opening, 0.0, u) if step < reach else u)
                both = jnp.concatenate(found, axis=0).astype(bf16)
                u_buf[at, place(number * LAP + row, 2), :] = both
                both = both.astype(f32)
                for u in (both[:ROWS], both[ROWS:]):
                    state = [decay[mode] * state[mode] + u for mode in range(modes)]
            return tuple(state), (tuple(past[0]), tuple(past[1]))

        past = tuple(
            tuple(pltpu.roll(scr[slot, place(steps - reach + row), :], TILES, 0) for row in range(reach))
            for scr in scrs
        )
        zero = jnp.zeros((ROWS, LANES), f32)
        state, _ = lax.fori_loop(0, steps // LAP, lap, ((zero,) * modes, past))
        for mode in range(modes // 2):
            whole = []
            for one in (mode, mode + modes // 2):
                whole.append(state[one] + pltpu.roll(power(decay[one], steps) * state[one], TILES, 0))
            pair_buf[at, mode] = jnp.where(top, pltpu.roll(whole[0], TILES, 0), whole[1])
            pair_buf[at, modes // 2 + mode] = jnp.where(top, decay[mode], decay[mode + modes // 2])
        for lag in range(reach + 1):
            pair_buf[at, modes + lag] = jnp.where(top, taps[0][lag], taps[1][lag])
        start_all(send(at))

    run = over_chunks(chunks, fetch, chunk)
    small[0].wait()
    count = feat_buf.shape[-1]
    for member in range(2):
        rows = [feat_buf[at, member + 1] for at in range(chunks)]
        rows = [jnp.concatenate([row, jnp.zeros((ROWS - reach - 1, count), f32)], axis=0) for row in rows]
        wide = widened(jnp.concatenate(rows, axis=0))
        wide_scr[:, member] = wide.reshape(chunks, ROWS, CHUNK)
    small[1].wait()
    wait_all(fetch(0))
    for number in range(steps // LAP):
        move_block(bufs, scrs, 0, 0, number, steps, matrix)
    run()
    for at in range(chunks):
        wait_all(send(at))


def head_kernel(key_ref, value_ref, halo_ref, pair_ref, out_ref, head_ref, *scratches, tokens, reach):
    front_buf, pair_buf, out_buf, head_buf, token_scr, total_scr, in_sem, pair_sem, out_sem = scratches
    chunks = pair_buf.shape[0]
    pieces, piece_rows = out_buf.shape[:2]
    modes = total_scr.shape[0]
    half = modes // 2
    top = first_half()
    copies = [
        pltpu.make_async_copy(key_ref.at[pl.ds(0, 2 * ROWS)], front_buf.at[0], in_sem.at[0]),
        pltpu.make_async_copy(value_ref.at[pl.ds(0, 2 * ROWS)], front_buf.at[1], in_sem.at[1]),
    ]
    pairs = [
        pltpu.make_async_copy(pair_ref.at[chunk], pair_buf.at[chunk], pair_sem.at[chunk]) for chunk in range(chunks)
    ]
    start_all(copies + pairs)
    wait_all(copies)
    nothing = jnp.zeros((ROWS, LANES), f32)
    for chunk in range(chunks):
        pairs[chunk].wait()
        lanes = slice(chunk * CHUNK, (chunk + 1) * CHUNK)
        halo = halo_ref[:, lanes].astype(f32)
        for member in range(2):
            before = halo[member * ROWS : (member + 1) * ROWS]
            after = front_buf[member, :, lanes].astype(f32)[:ROWS]
            for tile in range(TILES):
                put_tile(token_scr, 0, member * TILES + tile, lanes_of(before, tile))
                put_tile(token_scr, 1, member * TILES + tile, lanes_of(after, tile))
        taps = [pair_buf[chunk, modes + lag] for lag in range(reach + 1)]
        seen = [get_row(token_scr, 0, ROWS - reach + row) for row in range(reach)]
        signals = []
        for row in range(reach):
            now = get_row(token_scr, 1, row)
            both = fir(taps, now, seen)
            seen = seen[1:] + [now]
            signals.append(rounded(both * pltpu.roll(both, TILES, 0)))
        kept = [jnp.where(top, one, 0.0) for one in signals] + [nothing] * (ROWS - reach)
        head_buf[chunk] = jnp.concatenate(kept, axis=0).astype(bf16)
        for mode in range(half):
            decay = pair_buf[chunk, half + mode]
            head = signals[0]
            for row in range(1, reach):
                head = decay * head + signals[row]
            total = pair_buf[chunk, mode] + power(decay, tokens - reach) * head
            rows = slice(chunk * TILES, (chunk + 1) * TILES)
            total_scr[mode, rows, :] = total[:TILES]
            total_scr[half + mode, rows, :] = total[TILES:]
    split = pieces // modes
    for mode in range(modes):
        for part in range(split):
            rows = total_scr[mode, part * piece_rows : (part + 1) * piece_rows, :]
            out_buf[mode * split + part] = rows.astype(out_buf.dtype)
    outs = [
        pltpu.make_async_copy(out_buf, out_ref, out_sem.at[0]),
        pltpu.make_async_copy(head_buf, head_ref, out_sem.at[1]),
    ]
    start_all(outs)
    wait_all(outs)


def local_kernel(u_ref, head_ref, decay_ref, coef_ref, skip_ref, y_ref, enter_ref, *scratches):
    u_buf, head_buf, decay_buf, coef_buf, skip_buf, y_buf, enter_buf = scratches[:7]
    in_sem, small_sem, out_sem = scratches[7:]
    chunks, steps = u_buf.shape[0], u_buf.shape[1] // ROWS
    modes = decay_buf.shape[1]
    top = first_half()

    def fetch(at):
        return [
            pltpu.make_async_copy(ref.at[at], buf.at[at], in_sem.at[member, at])
            for member, (ref, buf) in enumerate(((u_ref, u_buf), (decay_ref, decay_buf)))
        ]

    def send(at):
        return [
            pltpu.make_async_copy(buf.at[at], ref.at[at], out_sem.at[member, at])
            for member, (ref, buf) in enumerate(((y_ref, y_buf), (enter_ref, enter_buf)))
        ]

    small = [
        pltpu.make_async_copy(ref, buf, small_sem.at[at])
        for at, (ref, buf) in enumerate(((head_ref, head_buf), (coef_ref, coef_buf), (skip_ref, skip_buf)))
    ]
    start_all(small)

    def chunk(at):
        coef = spread_rows(coef_buf, at, range(modes))
        (skip,) = spread_rows(skip_buf, at, range(1))
        wait_all(fetch(at))
        front = slice(0, ROWS * ROWS)
        u_buf[at, front] = (u_buf[at, front].astype(f32) + head_buf[at].astype(f32)).astype(bf16)
        decay = [decay_buf[at, mode] for mode in range(modes)]

        def lap(number, state):
            state = list(state)
            for row in range(0, LAP, 2):
                both = u_buf[at, place(number * LAP + row, 2), :].astype(f32)
                for step, u in ((row, both[:ROWS]), (row + 1, both[ROWS:])):
                    state = [decay[mode] * state[mode] + u for mode in range(modes)]
                    y_buf[at, number * LAP + step] = tree(
                        [skip * u] + [coef[mode] * state[mode] for mode in range(modes)]
                    )
            return tuple(state)

        state = lax.fori_loop(0, steps // LAP, lap, (jnp.zeros((ROWS, LANES), f32),) * modes)
        for mode in range(modes):
            middle = pltpu.roll(state[mode], TILES, 0)
            enter_buf[at, mode] = coef[mode] * jnp.where(top, 1.0, power(decay[mode], steps))
            enter_buf[at, modes + mode] = jnp.where(top, 0.0, coef[mode] * middle)
        start_all(send(at))

    run = over_chunks(chunks, fetch, chunk)
    wait_all(small)
    run()
    for at in range(chunks):
        wait_all(send(at))


def gate_kernel(query_ref, halo_ref, feat_ref, gate_ref, *scratches):
    query_buf, halo_buf, feat_buf, gate_buf, wide_scr, query_scr, halo_scr = scratches[:7]
    in_sem, small_sem, out_sem = scratches[7:]
    chunks, steps = gate_buf.shape[0], gate_buf.shape[1] // ROWS
    reach = feat_buf.shape[2] - 1
    top = first_half()
    matrix = relayout()

    def fetch(at):
        return [pltpu.make_async_copy(query_ref.at[:, span(at)], query_buf.at[at], in_sem.at[at])]

    def send(at):
        return pltpu.make_async_copy(gate_buf.at[at], gate_ref.at[at], out_sem.at[at])

    small = [
        pltpu.make_async_copy(feat_ref, feat_buf, small_sem.at[0]),
        pltpu.make_async_copy(halo_ref, halo_buf, small_sem.at[1]),
    ]
    start_all(small)

    def chunk(at):
        @pl.when(at + 1 < chunks)
        def _():
            wait_all(fetch(at + 1))

        taps = [chunk_taps(wide_scr, at, 0)(lag) for lag in range(reach + 1)]
        slot, later = at % 2, jnp.minimum(at + 1, chunks - 1)
        halo = halo_buf[:, span(at)].astype(f32)[2 * ROWS :]
        for tile in range(TILES):
            put_tile(halo_scr, 0, tile, lanes_of(halo, tile))
            put_tile(halo_scr, 0, TILES + tile, lanes_of(halo, tile))

        def lap(number, past):
            past = list(past)
            move_block((query_buf,), (query_scr,), later, 1 - slot, number, steps, matrix)
            found = []
            for row in range(LAP):
                now = query_scr[slot, place(number * LAP + row), :]
                found.append(fir(taps, now, past))
                past = past[1:] + [now]
            gate_buf[at, place(number * LAP, LAP), :] = jnp.concatenate(found, axis=0).astype(bf16)
            return tuple(past)

        past = tuple(
            jnp.where(
                top,
                get_row(halo_scr, 0, ROWS - reach + row),
                pltpu.roll(query_scr[slot, place(steps - reach + row), :], TILES, 0),
            )
            for row in range(reach)
        )
        lax.fori_loop(0, steps // LAP, lap, past)
        send(at).start()

    run = over_chunks(chunks, fetch, chunk)
    wait_all(small)
    count = feat_buf.shape[-1]
    rows = [feat_buf[at, 0] for at in range(chunks)]
    rows = [jnp.concatenate([row, jnp.zeros((ROWS - reach - 1, count), f32)], axis=0) for row in rows]
    wide_scr[:, 0] = widened(jnp.concatenate(rows, axis=0)).reshape(chunks, ROWS, CHUNK)
    wait_all(fetch(0))
    for number in range(steps // LAP):
        move_block((query_buf,), (query_scr,), 0, 0, number, steps, matrix)
    run()
    for at in range(chunks):
        send(at).wait()


def prefix_kernel(piece_ref, rate_ref, out_ref, rate_buf, out_buf, table_scr, sem, *, tokens, axes):
    devices, piece_rows = piece_ref.shape[:2]
    split = devices // rate_ref.shape[0]
    mine = lax.axis_index(axes)
    mode, part = mine // split, mine % split
    group = pl.multiple_of(mode // ROWS * ROWS, ROWS)
    first_copy = pltpu.make_async_copy(rate_ref.at[pl.ds(group, ROWS)], rate_buf, sem.at[0])
    first_copy.start()
    first_copy.wait()
    first = pl.multiple_of(part * piece_rows * LANES, LANES)
    rows = rate_buf[:, pl.ds(first, piece_rows * LANES)]
    here = lax.broadcasted_iota(jnp.int32, rows.shape, 0) == mode - group
    rate = jnp.sum(jnp.where(here, rows, 0.0), axis=0, keepdims=True)
    for row in range(piece_rows):
        table_scr[row : row + 1, :] = lanes_of(rate, row)
    through = jnp.exp(-float(tokens) * table_scr[:piece_rows, :])

    def lap(number, entering):
        for part in range(4):
            source = number * 4 + part
            out_buf[source] = entering.astype(out_buf.dtype)
            entering = through * entering + piece_ref[source].astype(f32)
        return entering

    lax.fori_loop(0, devices // 4, lap, jnp.zeros((piece_rows, LANES), f32))
    last = pltpu.make_async_copy(out_buf, out_ref, sem.at[1])
    last.start()
    last.wait()


def final_kernel(piece_ref, decay_ref, enter_ref, y_ref, gate_ref, out_ref, *scratches):
    decay_buf, enter_buf, y_buf, gate_buf, out_buf, total_scr, state_scr, value_scr = scratches[:8]
    in_sem, out_sem = scratches[8:]
    chunks, modes = decay_buf.shape[:2]
    steps = y_buf.shape[1]
    count = steps // LAP
    matrix = relayout()

    def fetch(at):
        sources = ((decay_ref, decay_buf), (enter_ref, enter_buf), (y_ref, y_buf), (gate_ref, gate_buf))
        return [
            pltpu.make_async_copy(ref.at[at], buf.at[at], in_sem.at[member, at])
            for member, (ref, buf) in enumerate(sources)
        ]

    def send(at):
        return pltpu.make_async_copy(out_buf.at[at], out_ref.at[:, span(at)], out_sem.at[at])

    def settle(number):
        at, within = number // count, number % count
        moved = lax.dot_general(
            matrix, value_scr[number % 2], (((0,), (0,)), ((), ())), preferred_element_type=f32
        ).astype(bf16)
        for half in range(2):
            for tile in range(TILES):
                slot = half * TILES + tile
                rows = pl.ds(pl.multiple_of(half * steps + within * LAP, LAP), LAP)
                out_buf[at, rows, tile * LANES : (tile + 1) * LANES] = moved[slot * LAP : (slot + 1) * LAP]

    def chunk(at):
        wait_all(fetch(at))
        decay = [decay_buf[at, mode] for mode in range(modes)]
        state = tuple(
            enter_buf[at, mode] * state_scr[at, mode] + enter_buf[at, modes + mode] for mode in range(modes)
        )

        def lap(number, state):
            settle(jnp.maximum(at * count + number - 1, 0))
            found = []
            for row in range(0, LAP, 2):
                gates = gate_buf[at, place(number * LAP + row, 2), :].astype(f32)
                sums = []
                for step in (row, row + 1):
                    state = [decay[mode] * state[mode] for mode in range(modes)]
                    sums.append(y_buf[at, number * LAP + step] + tree(state))
                found.append((gates * rounded(jnp.concatenate(sums, axis=0))).astype(bf16))
            value_scr[(at * count + number) % 2] = jnp.concatenate(found, axis=0)
            return tuple(state)

        lax.fori_loop(0, count, lap, state)

        @pl.when(at > 0)
        def _():
            send(at - 1).start()

    run = over_chunks(chunks, fetch, chunk)
    value_scr[...] = jnp.zeros(value_scr.shape, bf16)
    pieces, piece_rows = piece_ref.shape[:2]
    split = pieces // modes
    for mode in range(modes):
        for part in range(split):
            rows = piece_ref[mode * split + part].astype(f32)
            total_scr[mode, part * piece_rows : (part + 1) * piece_rows, :] = rows
    for at in range(chunks):
        for mode in range(modes):
            rows = total_scr[mode, at * TILES : (at + 1) * TILES, :]
            state_scr[at, mode, :TILES, :] = rows
            state_scr[at, mode, TILES:, :] = rows
    run()
    settle(chunks * count - 1)
    send(chunks - 1).start()
    for at in range(chunks):
        send(at).wait()


def cost(flops, moved):
    return pl.CostEstimate(flops=int(flops), bytes_accessed=int(moved), transcendentals=0)


def local(query, key_proj, value_proj, featurizer, rates, residues, skip, *, axes):
    tokens, width = query.shape
    modes = rates.shape[0]
    members, taps, groups = featurizer.shape
    devices = math.prod(lax.axis_size(axis) for axis in axes)
    chunks = width // CHUNK
    steps = tokens // 2
    tiles = width // LANES
    split = devices // modes
    even = devices % modes == 0 and tiles % split == 0
    shape = jax.ShapeDtypeStruct
    vmem = pltpu.VMEM
    dma = pltpu.SemaphoreType.DMA
    elements = tokens * width
    there = pl.BlockSpec(memory_space=pltpu.HBM)

    def call(kernel, inputs, outputs, scratches, name, near=(), **more):
        inputs = [
            value if at in near else pltpu.with_memory_space_constraint(value, pltpu.HBM)
            for at, value in enumerate(inputs)
        ]
        return pl.pallas_call(
            kernel,
            in_specs=[pl.BlockSpec(memory_space=vmem) if at in near else there for at in range(len(inputs))],
            out_specs=[there] * len(outputs),
            out_shape=[pltpu.HBM(one.shape, one.dtype) for one in outputs],
            scratch_shapes=scratches,
            compiler_params=pltpu.CompilerParams(vmem_limit_bytes=32 * 2**20),
            name=name,
            **more,
        )(*inputs)

    def vectors(count, kind=f32):
        return (chunks, count, ROWS, LANES), kind

    packed_shape = ((members * ROWS, width), bf16)
    (packed,) = call(
        pack_kernel,
        (key_proj, value_proj, query),
        [shape(*packed_shape)],
        [vmem((members, 2 * ROWS, width), bf16), vmem(*packed_shape), dma((members,)), dma((1,))],
        "pack",
    )
    halo = lax.ppermute(packed, axes, [(at, at + 1) for at in range(devices - 1)])

    feat = featurizer.reshape(members, taps, chunks, groups // chunks).transpose(2, 0, 1, 3)
    tokens_buf = vmem((chunks, tokens, CHUNK), bf16)
    feat_buf = vmem(feat.shape, f32)
    moved = vmem((2, steps * ROWS, LANES), f32)
    pairs = vectors(modes + taps)
    flat = ((chunks, steps * ROWS, LANES), bf16)
    u, decay, pair = call(
        signal_kernel,
        (key_proj, value_proj, feat, rates),
        [shape(*flat), shape(*vectors(modes)), shape(*pairs)],
        [tokens_buf, tokens_buf, feat_buf, vmem((modes, width), f32)]
        + [vmem(*flat), vmem(*vectors(modes)), vmem(*pairs)]
        + [vmem((chunks, 2, ROWS, CHUNK), f32), moved, moved]
        + [dma((2, chunks)), dma((2,)), dma((3, chunks))],
        "signal",
        cost_estimate=cost(60 * elements, 10 * elements),
    )

    pieces = (modes * split, tiles // split, LANES) if even else (modes, tiles, LANES)
    front = ((chunks, ROWS * ROWS, LANES), bf16)
    left, head = call(
        functools.partial(head_kernel, tokens=tokens, reach=taps - 1),
        (key_proj, value_proj, halo, pair),
        [shape(pieces, bf16), shape(*front)],
        [vmem((2, 2 * ROWS, width), bf16), vmem(*pairs)]
        + [vmem(pieces, bf16), vmem(*front), vmem((2 * ROWS * ROWS, LANES), f32)]
        + [vmem((modes, tiles, LANES), f32), dma((2,)), dma((chunks,)), dma((2,))],
        "head",
        near=(2,),
    )
    left, halo_late, rates_late, skip_late = lax.optimization_barrier((left, halo, rates, skip))
    coef = residues * jnp.sqrt(-jnp.expm1(-2.0 * rates_late) / modes)
    skip_row = skip_late[None, :]
    (gate,) = call(
        gate_kernel,
        (query, halo_late, feat),
        [shape(*flat)],
        [tokens_buf, vmem(*packed_shape), feat_buf, vmem(*flat)]
        + [vmem((chunks, 1, ROWS, CHUNK), f32), moved, vmem((ROWS * ROWS, LANES), f32)]
        + [dma((chunks,)), dma((2,)), dma((chunks,))],
        "gate",
        cost_estimate=cost(14 * elements, 4 * elements),
    )

    def swap(value):
        return lax.all_to_all(value, axes, split_axis=0, concat_axis=0, tiled=True)

    share = modes * width // devices
    theirs = swap(left if even else left.reshape(devices, share))
    theirs, gate, coef, skip_row = lax.optimization_barrier((theirs, gate, coef, skip_row))
    if even:
        (entering,) = call(
            functools.partial(prefix_kernel, tokens=tokens, axes=axes),
            (theirs, rates),
            [shape(pieces, bf16)],
            [vmem((ROWS, width), f32), vmem(pieces, bf16)]
            + [vmem((-(-pieces[1] // ROWS) * ROWS, LANES), f32), dma((2,))],
            "prefix",
            near=(0,),
        )
    else:
        mine = lax.axis_index(axes)
        through = jnp.exp(-float(tokens) * lax.dynamic_slice_in_dim(rates.reshape(-1), mine * share, share))
        _, entering = lax.scan(
            lambda so_far, piece: (through * so_far + piece.astype(f32), so_far.astype(bf16)),
            jnp.zeros((share,), f32),
            theirs,
        )

    entering, u_late = lax.optimization_barrier((entering, u))
    entered = swap(entering).reshape(pieces)
    y, enter = call(
        local_kernel,
        (u_late, head, decay, coef, skip_row),
        [shape(*vectors(steps)), shape(*vectors(2 * modes))],
        [vmem(*flat), vmem(*front), vmem(*vectors(modes)), vmem((modes, width), f32)]
        + [vmem((1, width), f32), vmem(*vectors(steps)), vmem(*vectors(2 * modes))]
        + [dma((2, chunks)), dma((3,)), dma((2, chunks))],
        "within",
        cost_estimate=cost(66 * elements, 8 * elements),
    )

    (out,) = call(
        final_kernel,
        (entered, decay, enter, y, gate),
        [shape((tokens, width), bf16)],
        [vmem(*vectors(modes)), vmem(*vectors(2 * modes)), vmem(*vectors(steps))]
        + [vmem(*flat), tokens_buf, vmem((modes, tiles, LANES), f32), vmem(*vectors(modes))]
        + [vmem((2, BLOCK, LANES), bf16), dma((4, chunks)), dma((chunks,))],
        "final",
        near=(0,),
        cost_estimate=cost(40 * elements, 10 * elements),
    )
    return out


def solution(mesh):
    axes = tuple(mesh.axis_names)
    placed = (P(axes, None),) * 3 + (P(),) * 4
    return jax.shard_map(
        functools.partial(local, axes=axes),
        mesh=mesh,
        in_specs=placed,
        out_specs=P(axes, None),
        check_vma=False,
    )
```

```python
import functools
import math

import jax
import jax.numpy as jnp
from jax import lax
from jax.experimental import pallas as pl
from jax.experimental.pallas import tpu as pltpu
from jax.sharding import PartitionSpec as P

LANES = 128
ROWS = 8
TILES = 4
CHUNK = TILES * LANES
AHEAD = 3
f32 = jnp.float32
bf16 = jnp.bfloat16


def put_tile(scratch, group, slot, tile):
    scratch[pl.ds((group * ROWS + slot) * ROWS, ROWS), :] = tile


def get_row(scratch, group, row):
    return scratch[pl.ds(group * ROWS * ROWS + row, ROWS, stride=ROWS), :]


def lanes_of(value, tile):
    return value[:, tile * LANES : (tile + 1) * LANES]


def tile_lanes(tile):
    return pl.ds(pl.multiple_of(tile * LANES, LANES), LANES)


def span(at):
    return pl.ds(pl.multiple_of(at * CHUNK, CHUNK), CHUNK)


def wide(row):
    return jnp.broadcast_to(row, (ROWS, LANES))


def sublane():
    return lax.broadcasted_iota(jnp.int32, (ROWS, LANES), 0)


def spread(row_of):
    slot = sublane() % TILES
    result = wide(row_of(TILES - 1))
    for tile in range(TILES - 1):
        result = jnp.where(slot == tile, wide(row_of(tile)), result)
    return result


def spread_rows(ref, at, rows):
    def one(row):
        return spread(lambda tile: ref[row : row + 1, tile_lanes(at * TILES + tile)])

    return [one(row) for row in rows]


def rounded(value):
    return value.astype(bf16).astype(f32)


def tiles_of(block):
    block = block.astype(f32)
    return [block[at : at + ROWS] for at in range(0, block.shape[0], ROWS)]


def shifted(now, last, by):
    turned = pltpu.roll(now, by, 0)
    return jnp.where(sublane() < by, last, turned), turned


def fir_step(tile, taps, past):
    one, kept = shifted(tile, past[0], 1)
    nested = taps[6] * tile
    after = [kept]
    for level in (4, 2, 0):
        moved, kept = shifted(nested, past[1 + level // 2], 2)
        after.insert(1, kept)
        nested = taps[level] * tile + taps[level + 1] * one + moved
    return nested, after


def fir_start():
    return [jnp.zeros((ROWS, LANES), f32)] * 4


def chunk_taps(wide_ref, at, member, tile, count):
    return [wide(wide_ref[at, member, lag : lag + 1, tile_lanes(tile)]) for lag in range(count)]


def widened(feat_ref, member, out_ref, position):
    chunks, _, taps, count = feat_ref.shape
    rows = [feat_ref[at, member] for at in range(chunks)]
    rows = [jnp.concatenate([row, jnp.zeros((ROWS - taps, count), f32)], axis=0) for row in rows]
    group = lax.broadcasted_iota(jnp.int32, (count, CHUNK), 0)
    lane = lax.broadcasted_iota(jnp.int32, (count, CHUNK), 1)
    pick = (group == lane // (CHUNK // count)).astype(f32).astype(bf16)
    parts, rest = [], jnp.concatenate(rows, axis=0)
    for _ in range(3):
        term = rest.astype(bf16)
        rest = rest - term.astype(f32)
        parts.append(jnp.dot(term, pick, preferred_element_type=f32))
    out_ref[:, position] = (parts[0] + parts[1] + parts[2]).reshape(chunks, ROWS, CHUNK)


def power(base, exponent):
    result = None
    while exponent:
        if exponent & 1:
            result = base if result is None else result * base
        base = base * base
        exponent >>= 1
    return result


def tree(terms):
    while len(terms) > 1:
        terms = [sum(terms[at + 1 : at + 2], terms[at]) for at in range(0, len(terms), 2)]
    return terms[0]


def start_all(copies):
    for copy in copies:
        copy.start()


def wait_all(copies):
    for copy in copies:
        copy.wait()


def begin(chunks, fetch):
    for at in range(min(AHEAD, chunks)):
        start_all(fetch(at))


def over_chunks(chunks, fetch, body, send):
    def one(at, _):
        @pl.when(at + AHEAD < chunks)
        def _():
            start_all(fetch(at + AHEAD))

        wait_all(fetch(at))
        body(at)
        start_all(send(at))
        return 0

    lax.fori_loop(0, chunks, one, 0)
    for at in range(chunks):
        wait_all(send(at))


def columns_in(pairs, sem):
    def fetch(at):
        return [
            pltpu.make_async_copy(ref.at[:, span(at)], buf.at[at], sem.at[member, at])
            for member, (ref, buf) in enumerate(pairs)
        ]

    return fetch


def columns_out(ref, buf, sem):
    return lambda at: [pltpu.make_async_copy(buf.at[at], ref.at[:, span(at)], sem.at[0, at])]


def pack_kernel(key_ref, value_ref, query_ref, out_ref, in_buf, in_sem):
    tokens = key_ref.shape[0]
    copies = [
        pltpu.make_async_copy(ref.at[pl.ds(tokens - 2 * ROWS, 2 * ROWS)], in_buf.at[at], in_sem.at[at])
        for at, ref in enumerate((key_ref, value_ref, query_ref))
    ]
    start_all(copies)
    wait_all(copies)
    tails = [in_buf[at].astype(f32)[ROWS:] for at in range(len(copies))]
    out_ref[...] = jnp.concatenate(tails, axis=0).astype(bf16)


def signal_kernel(key_ref, value_ref, feat_ref, rate_ref, u_ref, wide_ref, state_ref, *scratches):
    key_buf, value_buf, u_buf, power_scr, in_sem, out_sem = scratches
    chunks, tokens = u_buf.shape[:2]
    modes = rate_ref.shape[0]
    count = feat_ref.shape[2]
    fetch = columns_in(((key_ref, key_buf), (value_ref, value_buf)), in_sem)
    begin(chunks, fetch)
    for member in range(2):
        widened(feat_ref, member + 1, wide_ref, member)

    def chunk(at):
        through = jnp.exp(-rate_ref[:, span(at)])
        for level in range(4):
            power_scr[level] = through
            through = through * through

        def tile(number, _):
            lanes = tile_lanes(number)
            taps = [chunk_taps(wide_ref, at, member, number, count) for member in range(2)]
            past = [fir_start(), fir_start()]
            for pair in range(tokens // (2 * ROWS)):
                rows = slice(pair * 2 * ROWS, (pair + 1) * 2 * ROWS)
                sources = [tiles_of(buf[at, rows, lanes]) for buf in (key_buf, value_buf)]
                found = []
                for part in range(2):
                    both = []
                    for member in range(2):
                        value, past[member] = fir_step(sources[member][part], taps[member], past[member])
                        both.append(value)
                    u = both[0] * both[1]
                    if pair == 0 and part == 0:
                        u = jnp.where(sublane() < count - 1, 0.0, u)
                    found.append(u)
                u_buf[at, rows, lanes] = jnp.concatenate(found, axis=0).astype(bf16)
            return 0

        lax.fori_loop(0, TILES, tile, 0)

        def gather(number, _):
            lanes = tile_lanes(number)
            decay = [wide(power_scr[3, mode : mode + 1, lanes]) for mode in range(modes)]
            state = None
            for pair in range(tokens // (2 * ROWS)):
                for u in tiles_of(u_buf[at, pair * 2 * ROWS : (pair + 1) * 2 * ROWS, lanes]):
                    if state is None:
                        state = [u] * modes
                    else:
                        state = [decay[mode] * state[mode] + u for mode in range(modes)]
            for mode in range(modes):
                whole = state[mode]
                for level in (2, 1, 0):
                    factor = wide(power_scr[level, mode : mode + 1, lanes])
                    whole = factor * whole + pltpu.roll(whole, ROWS - (1 << level), 0)
                state_ref[mode, pl.ds(at * TILES + number, 1), :] = whole[:1]
            return 0

        lax.fori_loop(0, TILES, gather, 0)

    over_chunks(chunks, fetch, chunk, columns_out(u_ref, u_buf, out_sem))


def head_kernel(key_ref, value_ref, halo_ref, rate_ref, wide_ref, state_ref, out_ref, head_ref, *scratches, tokens, reach):
    front_buf, rate_scr, token_scr, total_scr, in_sem = scratches
    modes, tiles = state_ref.shape[:2]
    pieces, piece_rows = out_ref.shape[:2]
    copies = [
        pltpu.make_async_copy(ref.at[pl.ds(0, 2 * ROWS)], front_buf.at[member], in_sem.at[member])
        for member, ref in enumerate((key_ref, value_ref))
    ]
    start_all(copies)
    for group in range(modes // ROWS):
        for tile in range(tiles):
            rows = pl.ds((group * tiles + tile) * ROWS, ROWS)
            rate_scr[rows, :] = rate_ref[group * ROWS : (group + 1) * ROWS, tile * LANES : (tile + 1) * LANES]
    wait_all(copies)

    def one(tile, _):
        lanes = tile_lanes(tile)
        halo = tiles_of(halo_ref[:, lanes])
        parts = []
        for member in range(2):
            taps = chunk_taps(wide_ref, tile // TILES, member, tile % TILES, reach + 1)
            _, past = fir_step(halo[member], taps, fir_start())
            value, _ = fir_step(tiles_of(front_buf[member, :, lanes])[0], taps, past)
            parts.append(value)
        u = jnp.where(sublane() < reach, rounded(parts[0] * parts[1]), 0.0)
        token_scr[pl.ds(pl.multiple_of(tile * ROWS, ROWS), ROWS), :] = u
        head_ref[:, lanes] = jnp.concatenate([u, jnp.zeros((ROWS, LANES), f32)], axis=0).astype(bf16)
        return 0

    lax.fori_loop(0, tiles, one, 0)
    signals = [token_scr[pl.ds(row, tiles, stride=ROWS), :] for row in range(reach)]
    split = pieces // modes
    for mode in range(modes):
        start = mode // ROWS * tiles * ROWS + mode % ROWS
        decay = jnp.exp(-rate_scr[pl.ds(start, tiles, stride=ROWS), :])
        head = signals[0]
        for row in range(1, reach):
            head = decay * head + signals[row]
        total_scr[mode] = state_ref[mode] + power(decay, tokens - reach) * head
        for part in range(split):
            rows = total_scr[mode, part * piece_rows : (part + 1) * piece_rows, :]
            out_ref[mode * split + part] = rows.astype(out_ref.dtype)


def gate_kernel(query_ref, halo_ref, feat_ref, rate_ref, coef_ref, gate_ref, lead_ref, *scratches):
    query_buf, halo_buf, gate_buf, lead_buf, wide_scr, in_sem, small_sem, out_sem, lead_sem = scratches
    chunks, tokens = gate_buf.shape[:2]
    modes = rate_ref.shape[0]
    count = feat_ref.shape[2]
    fetch = columns_in(((query_ref, query_buf),), in_sem)
    halo_copy = pltpu.make_async_copy(halo_ref, halo_buf, small_sem.at[0])
    halo_copy.start()
    begin(chunks, fetch)
    widened(feat_ref, 0, wide_scr, 0)
    halo_copy.wait()
    steps = (sublane() + 1).astype(f32)

    def send(at):
        return [
            pltpu.make_async_copy(gate_buf.at[at], gate_ref.at[:, span(at)], out_sem.at[0, at]),
            pltpu.make_async_copy(lead_buf.at[at], lead_ref.at[at], lead_sem.at[at]),
        ]

    def chunk(at):
        def tile(number, _):
            lanes = tile_lanes(number)
            all_lanes = tile_lanes(at * TILES + number)
            taps = chunk_taps(wide_scr, at, 0, number, count)
            _, past = fir_step(tiles_of(halo_buf[:, all_lanes])[2], taps, fir_start())
            for pair in range(tokens // (2 * ROWS)):
                rows = slice(pair * 2 * ROWS, (pair + 1) * 2 * ROWS)
                found = []
                for source in tiles_of(query_buf[at, rows, lanes]):
                    value, past = fir_step(source, taps, past)
                    found.append(value)
                gate_buf[at, rows, lanes] = jnp.concatenate(found, axis=0).astype(bf16)
            for mode in range(modes):
                rate = wide(rate_ref[mode : mode + 1, all_lanes])
                coef = wide(coef_ref[mode : mode + 1, all_lanes])
                lead_buf[at, number * modes + mode] = coef * jnp.exp(-rate * steps)
            return 0

        lax.fori_loop(0, TILES, tile, 0)

    over_chunks(chunks, fetch, chunk, send)


def prefix_kernel(piece_ref, rate_ref, out_ref, table_scr, *, tokens, axes):
    devices, piece_rows = piece_ref.shape[:2]
    split = devices // rate_ref.shape[0]
    mine = lax.axis_index(axes)
    mode, part = mine // split, mine % split
    group = pl.multiple_of(mode // ROWS * ROWS, ROWS)
    first = pl.multiple_of(part * piece_rows * LANES, LANES)
    rows = rate_ref[pl.ds(group, ROWS), pl.ds(first, piece_rows * LANES)]
    here = lax.broadcasted_iota(jnp.int32, rows.shape, 0) == mode - group
    rate = jnp.sum(jnp.where(here, rows, 0.0), axis=0, keepdims=True)
    for row in range(piece_rows):
        table_scr[row : row + 1, :] = lanes_of(rate, row)
    through = jnp.exp(-float(tokens) * table_scr[:piece_rows, :])

    def lap(number, entering):
        for step in range(4):
            source = number * 4 + step
            out_ref[source] = entering.astype(out_ref.dtype)
            entering = through * entering + piece_ref[source].astype(f32)
        return entering

    lax.fori_loop(0, devices // 4, lap, jnp.zeros((piece_rows, LANES), f32))


def local_kernel(u_ref, head_ref, rate_ref, coef_ref, skip_ref, y_ref, mid_ref, *scratches):
    u_buf, y_buf, mid_buf, token_scr, sum_scr, in_sem, out_sem, mid_sem = scratches
    chunks, tokens = u_buf.shape[:2]
    modes = rate_ref.shape[0]
    half_groups = tokens // ROWS // 2
    fetch = columns_in(((u_ref, u_buf),), in_sem)
    begin(chunks, fetch)

    def send(at):
        return [
            pltpu.make_async_copy(y_buf.at[at], y_ref.at[:, span(at)], out_sem.at[0, at]),
            pltpu.make_async_copy(mid_buf.at[at], mid_ref.at[at], mid_sem.at[at]),
        ]

    def chunk(at):
        front = u_buf[at, : 2 * ROWS].astype(f32) + head_ref[:, span(at)].astype(f32)
        u_buf[at, : 2 * ROWS] = front.astype(bf16)
        for pair in range(half_groups):
            block = u_buf[at, pair * 2 * ROWS : (pair + 1) * 2 * ROWS, :].astype(f32)
            for part in range(2):
                group = pair * 2 + part
                half, within = group // half_groups, group % half_groups
                for tile in range(TILES):
                    piece = lanes_of(block, tile)[part * ROWS : (part + 1) * ROWS]
                    put_tile(token_scr, within, half * TILES + tile, piece)
        (skip,) = spread_rows(skip_ref, at, range(1))
        for first in range(0, modes, ROWS):
            some = range(first, first + ROWS)
            coef = spread_rows(coef_ref, at, some)
            decay = [jnp.exp(-rate) for rate in spread_rows(rate_ref, at, some)]

            def eight(group, state):
                state = list(state)
                for row in range(ROWS):
                    u = get_row(token_scr, group, row)
                    state = [factor * one + u for factor, one in zip(decay, state)]
                    terms = [factor * one for factor, one in zip(coef, state)]
                    place = pl.ds(group * ROWS * ROWS + row, ROWS, stride=ROWS)
                    so_far = skip * u if first == 0 else sum_scr[place, :]
                    sum_scr[place, :] = so_far + tree(terms)
                return tuple(state)

            state = lax.fori_loop(0, half_groups, eight, (jnp.zeros((ROWS, LANES), f32),) * ROWS)
            for at_mode, one in zip(some, state):
                mid_buf[at, at_mode] = one
        for group in range(2 * half_groups):
            half, within = group // half_groups, group % half_groups
            for tile in range(TILES):
                slot = (within * ROWS + half * TILES + tile) * ROWS
                rows = slice(group * ROWS, (group + 1) * ROWS)
                y_buf[at, rows, tile * LANES : (tile + 1) * LANES] = sum_scr[pl.ds(slot, ROWS), :]

    over_chunks(chunks, fetch, chunk, send)


def final_kernel(piece_ref, rate_ref, lead_ref, mid_ref, y_ref, gate_ref, out_ref, *scratches):
    lead_buf, mid_buf, y_buf, gate_buf, out_buf, total_scr, power_scr, in_sem, wide_sem, out_sem = scratches
    chunks, modes = mid_buf.shape[:2]
    tokens = y_buf.shape[1]
    columns = columns_in(((y_ref, y_buf), (gate_ref, gate_buf)), in_sem)

    def fetch(at):
        return columns(at) + [
            pltpu.make_async_copy(ref.at[at], buf.at[at], wide_sem.at[member, at])
            for member, (ref, buf) in enumerate(((lead_ref, lead_buf), (mid_ref, mid_buf)))
        ]

    begin(chunks, fetch)
    pieces, piece_rows = piece_ref.shape[:2]
    split = pieces // modes
    for mode in range(modes):
        for part in range(split):
            rows = piece_ref[mode * split + part].astype(f32)
            total_scr[mode, part * piece_rows : (part + 1) * piece_rows, :] = rows

    def chunk(at):
        power_scr[...] = jnp.exp(-float(ROWS) * rate_ref[:, span(at)])

        def tile(number, _):
            lanes = tile_lanes(number)
            decay = [wide(power_scr[mode : mode + 1, lanes]) for mode in range(modes)]
            state = [
                lead_buf[at, number * modes + mode] * wide(total_scr[mode, pl.ds(at * TILES + number, 1), :])
                for mode in range(modes)
            ]
            for pair in range(tokens // (2 * ROWS)):
                rows = slice(pair * 2 * ROWS, (pair + 1) * 2 * ROWS)
                gates = gate_buf[at, rows, lanes].astype(f32)
                sums = []
                for part in range(2):
                    if pair == tokens // (4 * ROWS) and part == 0:
                        state = [
                            one + lead_buf[at, number * modes + mode] * wide(mid_buf[at, mode, pl.ds(number, 1), :])
                            for mode, one in enumerate(state)
                        ]
                    here = slice((pair * 2 + part) * ROWS, (pair * 2 + part + 1) * ROWS)
                    sums.append(y_buf[at, here, lanes] + tree(state))
                    state = [factor * one for factor, one in zip(decay, state)]
                out_buf[at, rows, lanes] = (gates * rounded(jnp.concatenate(sums, axis=0))).astype(bf16)
            return 0

        lax.fori_loop(0, TILES, tile, 0)

    over_chunks(chunks, fetch, chunk, columns_out(out_ref, out_buf, out_sem))


def cost(flops, moved):
    return pl.CostEstimate(flops=int(flops), bytes_accessed=int(moved), transcendentals=0)


def local(query, key_proj, value_proj, featurizer, rates, residues, skip, *, axes):
    tokens, width = query.shape
    modes = rates.shape[0]
    members, taps, groups = featurizer.shape
    devices = math.prod(lax.axis_size(axis) for axis in axes)
    chunks = width // CHUNK
    tiles = width // LANES
    split = devices // modes
    even = devices % modes == 0 and tiles % split == 0
    vmem = pltpu.VMEM
    far = pltpu.HBM
    near = jax.ShapeDtypeStruct
    dma = pltpu.SemaphoreType.DMA
    elements = tokens * width

    def call(kernel, inputs, outputs, scratches, name, close=(), **more):
        inputs = [
            value if at in close else pltpu.with_memory_space_constraint(value, far)
            for at, value in enumerate(inputs)
        ]
        beside, there = pl.BlockSpec(memory_space=vmem), pl.BlockSpec(memory_space=far)
        return pl.pallas_call(
            kernel,
            in_specs=[beside if at in close else there for at in range(len(inputs))],
            out_specs=[beside if isinstance(one, near) else there for one in outputs],
            out_shape=outputs,
            scratch_shapes=scratches,
            compiler_params=pltpu.CompilerParams(vmem_limit_bytes=32 * 2**20),
            name=name,
            **more,
        )(*inputs)

    (packed,) = call(
        pack_kernel,
        (key_proj, value_proj, query),
        [near((members * ROWS, width), bf16)],
        [vmem((members, 2 * ROWS, width), bf16), dma((members,))],
        "pack",
    )
    halo = lax.ppermute(packed, axes, [(at, at + 1) for at in range(devices - 1)])

    feat = featurizer.reshape(members, taps, chunks, groups // chunks).transpose(2, 0, 1, 3)
    half_buf, whole_buf = vmem((chunks, tokens, CHUNK), bf16), vmem((chunks, tokens, CHUNK), f32)
    u, wide_taps, state = call(
        signal_kernel,
        (key_proj, value_proj, feat, rates),
        [far((tokens, width), bf16), near((chunks, 2, ROWS, CHUNK), f32), near((modes, tiles, LANES), f32)],
        [half_buf, half_buf, half_buf, vmem((4, modes, CHUNK), f32), dma((2, chunks)), dma((1, chunks))],
        "signal",
        close=(2, 3),
        cost_estimate=cost(60 * elements, 10 * elements),
    )

    pieces = (modes * split, tiles // split, LANES) if even else (modes, tiles, LANES)
    left, head = call(
        functools.partial(head_kernel, tokens=tokens, reach=taps - 1),
        (key_proj, value_proj, halo, rates, wide_taps, state),
        [near(pieces, bf16), near((2 * ROWS, width), bf16)],
        [vmem((2, 2 * ROWS, width), bf16), vmem((modes * tiles, LANES), f32)]
        + [vmem((tiles * ROWS, LANES), f32), vmem((modes, tiles, LANES), f32), dma((2,))],
        "head",
        close=(2, 3, 4, 5),
    )
    left, halo_late, rates_late, skip_late = lax.optimization_barrier((left, halo, rates, skip))
    coef = residues * jnp.sqrt(-jnp.expm1(-2.0 * rates_late) / modes)
    skip_row = skip_late[None, :]
    gate, lead = call(
        gate_kernel,
        (query, halo_late, feat, rates, coef),
        [far((tokens, width), bf16), far((chunks, TILES * modes, ROWS, LANES), f32)],
        [half_buf, vmem((members * ROWS, width), bf16), half_buf]
        + [vmem((chunks, TILES * modes, ROWS, LANES), f32), vmem((chunks, 1, ROWS, CHUNK), f32)]
        + [dma((1, chunks)), dma((1,)), dma((1, chunks)), dma((chunks,))],
        "gate",
        close=(2, 3, 4),
        cost_estimate=cost(30 * elements, 8 * elements),
    )

    def swap(value):
        return lax.all_to_all(value, axes, split_axis=0, concat_axis=0, tiled=True)

    share = modes * width // devices
    theirs = swap(left if even else left.reshape(devices, share))
    theirs, gate, lead, coef, skip_row = lax.optimization_barrier((theirs, gate, lead, coef, skip_row))
    if even:
        (entering,) = call(
            functools.partial(prefix_kernel, tokens=tokens, axes=axes),
            (theirs, rates),
            [near(pieces, bf16)],
            [vmem((-(-pieces[1] // ROWS) * ROWS, LANES), f32)],
            "prefix",
            close=(0, 1),
        )
    else:
        mine = lax.axis_index(axes)
        through = jnp.exp(-float(tokens) * lax.dynamic_slice_in_dim(rates.reshape(-1), mine * share, share))
        _, entering = lax.scan(
            lambda so_far, piece: (through * so_far + piece.astype(f32), so_far.astype(bf16)),
            jnp.zeros((share,), f32),
            theirs,
        )

    entering, u_late = lax.optimization_barrier((entering, u))
    entered = swap(entering).reshape(pieces)
    stage = vmem((tokens // ROWS // 2 * ROWS * ROWS, LANES), f32)
    y, mid = call(
        local_kernel,
        (u_late, head, rates, coef, skip_row),
        [far((tokens, width), f32), far((chunks, modes, ROWS, LANES), f32)],
        [half_buf, whole_buf, vmem((chunks, modes, ROWS, LANES), f32), stage, stage]
        + [dma((1, chunks)), dma((1, chunks)), dma((chunks,))],
        "within",
        close=(1, 2, 3, 4),
        cost_estimate=cost(66 * elements, 8 * elements),
    )

    (out,) = call(
        final_kernel,
        (entered, rates, lead, mid, y, gate),
        [far((tokens, width), bf16)],
        [vmem((chunks, TILES * modes, ROWS, LANES), f32), vmem((chunks, modes, ROWS, LANES), f32)]
        + [whole_buf, half_buf, half_buf, vmem((modes, tiles, LANES), f32), vmem((modes, CHUNK), f32)]
        + [dma((2, chunks)), dma((2, chunks)), dma((1, chunks))],
        "final",
        close=(0, 1),
        cost_estimate=cost(40 * elements, 10 * elements),
    )
    return out


def solution(mesh):
    axes = tuple(mesh.axis_names)
    placed = (P(axes, None),) * 3 + (P(),) * 4
    return jax.shard_map(
        functools.partial(local, axes=axes),
        mesh=mesh,
        in_specs=placed,
        out_specs=P(axes, None),
        check_vma=False,
    )
```

```python
import functools
import math

import jax
import jax.numpy as jnp
from jax import lax
from jax.experimental import pallas as pl
from jax.experimental.pallas import tpu as pltpu
from jax.sharding import PartitionSpec as P

LANES = 128
ROWS = 8
TILES = 4
CHUNK = TILES * LANES
AHEAD = 3
f32 = jnp.float32
bf16 = jnp.bfloat16


def put_tile(scratch, group, slot, tile):
    scratch[pl.ds((group * ROWS + slot) * ROWS, ROWS), :] = tile


def get_row(scratch, group, row):
    return scratch[pl.ds(group * ROWS * ROWS + row, ROWS, stride=ROWS), :]


def lanes_of(value, tile):
    return value[:, tile * LANES : (tile + 1) * LANES]


def tile_lanes(tile):
    return pl.ds(pl.multiple_of(tile * LANES, LANES), LANES)


def span(at):
    return pl.ds(pl.multiple_of(at * CHUNK, CHUNK), CHUNK)


def wide(row):
    return jnp.broadcast_to(row, (ROWS, LANES))


def sublane():
    return lax.broadcasted_iota(jnp.int32, (ROWS, LANES), 0)


def spread(row_of):
    slot = sublane() % TILES
    result = wide(row_of(TILES - 1))
    for tile in range(TILES - 1):
        result = jnp.where(slot == tile, wide(row_of(tile)), result)
    return result


def spread_rows(ref, at, rows):
    def one(row):
        return spread(lambda tile: ref[row : row + 1, tile_lanes(at * TILES + tile)])

    return [one(row) for row in rows]


def rounded(value):
    return value.astype(bf16).astype(f32)


def tiles_of(block):
    block = block.astype(f32)
    return [block[at : at + ROWS] for at in range(0, block.shape[0], ROWS)]


def fir(column, taps, first):
    total = taps[0] * column[pl.ds(first, ROWS), :]
    for lag in range(1, len(taps)):
        total = total + taps[lag] * column[pl.ds(first - lag, ROWS), :]
    return total


def lay_column(column, source, lanes):
    for pair in range(source.shape[0] // (2 * ROWS)):
        rows = slice(pair * 2 * ROWS, (pair + 1) * 2 * ROWS)
        column[pl.ds(ROWS + pair * 2 * ROWS, 2 * ROWS), :] = source[rows, lanes].astype(f32)


def chunk_taps(wide_ref, at, member, tile, count):
    return [wide(wide_ref[at, member, lag : lag + 1, tile_lanes(tile)]) for lag in range(count)]


def widened(feat_ref, member, out_ref, position):
    chunks, _, taps, count = feat_ref.shape
    rows = [feat_ref[at, member] for at in range(chunks)]
    rows = [jnp.concatenate([row, jnp.zeros((ROWS - taps, count), f32)], axis=0) for row in rows]
    group = lax.broadcasted_iota(jnp.int32, (count, CHUNK), 0)
    lane = lax.broadcasted_iota(jnp.int32, (count, CHUNK), 1)
    pick = (group == lane // (CHUNK // count)).astype(f32).astype(bf16)
    parts, rest = [], jnp.concatenate(rows, axis=0)
    for _ in range(3):
        term = rest.astype(bf16)
        rest = rest - term.astype(f32)
        parts.append(jnp.dot(term, pick, preferred_element_type=f32))
    out_ref[:, position] = (parts[0] + parts[1] + parts[2]).reshape(chunks, ROWS, CHUNK)


def power(base, exponent):
    result = None
    while exponent:
        if exponent & 1:
            result = base if result is None else result * base
        base = base * base
        exponent >>= 1
    return result


def tree(terms):
    while len(terms) > 1:
        terms = [sum(terms[at + 1 : at + 2], terms[at]) for at in range(0, len(terms), 2)]
    return terms[0]


def start_all(copies):
    for copy in copies:
        copy.start()


def wait_all(copies):
    for copy in copies:
        copy.wait()


def begin(chunks, fetch):
    for at in range(min(AHEAD, chunks)):
        start_all(fetch(at))


def over_chunks(chunks, fetch, body, send):
    def one(at, _):
        @pl.when(at + AHEAD < chunks)
        def _():
            start_all(fetch(at + AHEAD))

        wait_all(fetch(at))
        body(at)
        start_all(send(at))
        return 0

    lax.fori_loop(0, chunks, one, 0)
    for at in range(chunks):
        wait_all(send(at))


def columns_in(pairs, sem):
    def fetch(at):
        return [
            pltpu.make_async_copy(ref.at[:, span(at)], buf.at[at], sem.at[member, at])
            for member, (ref, buf) in enumerate(pairs)
        ]

    return fetch


def columns_out(ref, buf, sem):
    return lambda at: [pltpu.make_async_copy(buf.at[at], ref.at[:, span(at)], sem.at[0, at])]


def pack_kernel(key_ref, value_ref, query_ref, out_ref, in_buf, in_sem):
    tokens = key_ref.shape[0]
    copies = [
        pltpu.make_async_copy(ref.at[pl.ds(tokens - 2 * ROWS, 2 * ROWS)], in_buf.at[at], in_sem.at[at])
        for at, ref in enumerate((key_ref, value_ref, query_ref))
    ]
    start_all(copies)
    wait_all(copies)
    tails = [in_buf[at].astype(f32)[ROWS:] for at in range(len(copies))]
    out_ref[...] = jnp.concatenate(tails, axis=0).astype(bf16)


def signal_kernel(key_ref, value_ref, feat_ref, rate_ref, u_ref, wide_ref, state_ref, *scratches):
    key_buf, value_buf, u_buf, power_scr, *columns, in_sem, out_sem = scratches
    chunks, tokens = u_buf.shape[:2]
    modes = rate_ref.shape[0]
    count = feat_ref.shape[2]
    fetch = columns_in(((key_ref, key_buf), (value_ref, value_buf)), in_sem)
    begin(chunks, fetch)
    for member in range(2):
        widened(feat_ref, member + 1, wide_ref, member)

    def chunk(at):
        through = jnp.exp(-rate_ref[:, span(at)])
        for level in range(4):
            power_scr[level] = through
            through = through * through

        def tile(number, _):
            lanes = tile_lanes(number)
            taps = [chunk_taps(wide_ref, at, member, number, count) for member in range(2)]
            for column, buf in zip(columns, (key_buf, value_buf)):
                column[pl.ds(0, ROWS), :] = jnp.zeros((ROWS, LANES), f32)
                lay_column(column, buf.at[at], lanes)
            for pair in range(tokens // (2 * ROWS)):
                found = []
                for first in (pair * 2 * ROWS + ROWS, pair * 2 * ROWS + 2 * ROWS):
                    u = fir(columns[0], taps[0], first) * fir(columns[1], taps[1], first)
                    found.append(jnp.where(sublane() < count - 1, 0.0, u) if first == ROWS else u)
                rows = slice(pair * 2 * ROWS, (pair + 1) * 2 * ROWS)
                u_buf[at, rows, lanes] = jnp.concatenate(found, axis=0).astype(bf16)
            return 0

        lax.fori_loop(0, TILES, tile, 0)

        def gather(number, _):
            lanes = tile_lanes(number)
            decay = [wide(power_scr[3, mode : mode + 1, lanes]) for mode in range(modes)]
            state = None
            for pair in range(tokens // (2 * ROWS)):
                for u in tiles_of(u_buf[at, pair * 2 * ROWS : (pair + 1) * 2 * ROWS, lanes]):
                    if state is None:
                        state = [u] * modes
                    else:
                        state = [decay[mode] * state[mode] + u for mode in range(modes)]
            for mode in range(modes):
                whole = state[mode]
                for level in (2, 1, 0):
                    factor = wide(power_scr[level, mode : mode + 1, lanes])
                    whole = factor * whole + pltpu.roll(whole, ROWS - (1 << level), 0)
                state_ref[mode, pl.ds(at * TILES + number, 1), :] = whole[:1]
            return 0

        lax.fori_loop(0, TILES, gather, 0)

    over_chunks(chunks, fetch, chunk, columns_out(u_ref, u_buf, out_sem))


def head_kernel(key_ref, value_ref, halo_ref, rate_ref, wide_ref, state_ref, out_ref, head_ref, *scratches, tokens, reach):
    front_buf, rate_scr, column_scr, token_scr, total_scr, in_sem = scratches
    modes, tiles = state_ref.shape[:2]
    pieces, piece_rows = out_ref.shape[:2]
    copies = [
        pltpu.make_async_copy(ref.at[pl.ds(0, 2 * ROWS)], front_buf.at[member], in_sem.at[member])
        for member, ref in enumerate((key_ref, value_ref))
    ]
    start_all(copies)
    for group in range(modes // ROWS):
        for tile in range(tiles):
            rows = pl.ds((group * tiles + tile) * ROWS, ROWS)
            rate_scr[rows, :] = rate_ref[group * ROWS : (group + 1) * ROWS, tile * LANES : (tile + 1) * LANES]
    wait_all(copies)

    def some(chunk, _):
        for number in range(TILES):
            lanes = tile_lanes(chunk * TILES + number)
            halo = halo_ref[:, lanes].astype(f32)
            parts = []
            for member in range(2):
                taps = chunk_taps(wide_ref, chunk, member, number, reach + 1)
                column = column_scr.at[number, member]
                column[pl.ds(0, ROWS), :] = halo[member * ROWS : (member + 1) * ROWS]
                column[pl.ds(ROWS, ROWS), :] = front_buf[member, :, lanes].astype(f32)[:ROWS]
                parts.append(fir(column, taps, ROWS))
            u = jnp.where(sublane() < reach, rounded(parts[0] * parts[1]), 0.0)
            token_scr[pl.ds(pl.multiple_of((chunk * TILES + number) * ROWS, ROWS), ROWS), :] = u
            head_ref[:, lanes] = jnp.concatenate([u, jnp.zeros((ROWS, LANES), f32)], axis=0).astype(bf16)
        return 0

    lax.fori_loop(0, tiles // TILES, some, 0)
    signals = [token_scr[pl.ds(row, tiles, stride=ROWS), :] for row in range(reach)]
    split = pieces // modes
    for mode in range(modes):
        start = mode // ROWS * tiles * ROWS + mode % ROWS
        decay = jnp.exp(-rate_scr[pl.ds(start, tiles, stride=ROWS), :])
        head = signals[0]
        for row in range(1, reach):
            head = decay * head + signals[row]
        total_scr[mode] = state_ref[mode] + power(decay, tokens - reach) * head
        for part in range(split):
            rows = total_scr[mode, part * piece_rows : (part + 1) * piece_rows, :]
            out_ref[mode * split + part] = rows.astype(out_ref.dtype)


def gate_kernel(query_ref, halo_ref, feat_ref, gate_ref, *scratches):
    query_buf, halo_buf, gate_buf, wide_scr, column, in_sem, small_sem, out_sem = scratches
    chunks, tokens = gate_buf.shape[:2]
    count = feat_ref.shape[2]
    fetch = columns_in(((query_ref, query_buf),), in_sem)
    halo_copy = pltpu.make_async_copy(halo_ref, halo_buf, small_sem.at[0])
    halo_copy.start()
    begin(chunks, fetch)
    widened(feat_ref, 0, wide_scr, 0)
    halo_copy.wait()

    def chunk(at):
        def tile(number, _):
            lanes = tile_lanes(number)
            taps = chunk_taps(wide_scr, at, 0, number, count)
            halo = halo_buf[:, tile_lanes(at * TILES + number)].astype(f32)
            column[pl.ds(0, ROWS), :] = halo[2 * ROWS :]
            lay_column(column, query_buf.at[at], lanes)
            for pair in range(tokens // (2 * ROWS)):
                first = pair * 2 * ROWS + ROWS
                found = [fir(column, taps, first), fir(column, taps, first + ROWS)]
                rows = slice(pair * 2 * ROWS, (pair + 1) * 2 * ROWS)
                gate_buf[at, rows, lanes] = jnp.concatenate(found, axis=0).astype(bf16)
            return 0

        lax.fori_loop(0, TILES, tile, 0)

    over_chunks(chunks, fetch, chunk, columns_out(gate_ref, gate_buf, out_sem))


def prefix_kernel(piece_ref, rate_ref, coef_ref, out_ref, table_scr, *, tokens, axes):
    devices, piece_rows = piece_ref.shape[:2]
    split = devices // rate_ref.shape[0]
    mine = lax.axis_index(axes)
    mode, part = mine // split, mine % split
    group = pl.multiple_of(mode // ROWS * ROWS, ROWS)
    first = pl.multiple_of(part * piece_rows * LANES, LANES)

    def mine_of(ref):
        rows = ref[pl.ds(group, ROWS), pl.ds(first, piece_rows * LANES)]
        here = lax.broadcasted_iota(jnp.int32, rows.shape, 0) == mode - group
        row = jnp.sum(jnp.where(here, rows, 0.0), axis=0, keepdims=True)
        for number in range(piece_rows):
            table_scr[number : number + 1, :] = lanes_of(row, number)
        return table_scr[:piece_rows, :]

    coef = mine_of(coef_ref)
    through = jnp.exp(-float(tokens) * mine_of(rate_ref))

    def lap(number, entering):
        for step in range(4):
            source = number * 4 + step
            out_ref[source] = (coef * entering).astype(out_ref.dtype)
            entering = through * entering + piece_ref[source].astype(f32)
        return entering

    lax.fori_loop(0, devices // 4, lap, jnp.zeros((piece_rows, LANES), f32))


def local_kernel(u_ref, head_ref, rate_ref, coef_ref, skip_ref, y_ref, mid_ref, *scratches):
    u_buf, y_buf, mid_buf, token_scr, vector_scr, part_scr, sum_scr, in_sem, out_sem, mid_sem = scratches
    chunks, tokens = u_buf.shape[:2]
    modes = rate_ref.shape[0]
    half_groups = tokens // ROWS // 2
    fetch = columns_in(((u_ref, u_buf),), in_sem)
    begin(chunks, fetch)

    def send(at):
        return [
            pltpu.make_async_copy(y_buf.at[at], y_ref.at[:, span(at)], out_sem.at[0, at]),
            pltpu.make_async_copy(mid_buf.at[at], mid_ref.at[at], mid_sem.at[at]),
        ]

    def chunk(at):
        front = u_buf[at, : 2 * ROWS].astype(f32) + head_ref[:, span(at)].astype(f32)
        u_buf[at, : 2 * ROWS] = front.astype(bf16)
        for pair in range(half_groups):
            block = u_buf[at, pair * 2 * ROWS : (pair + 1) * 2 * ROWS, :].astype(f32)
            for part in range(2):
                group = pair * 2 + part
                half, within = group // half_groups, group % half_groups
                for tile in range(TILES):
                    piece = lanes_of(block, tile)[part * ROWS : (part + 1) * ROWS]
                    put_tile(token_scr, within, half * TILES + tile, piece)
        (skip,) = spread_rows(skip_ref, at, range(1))
        for first in range(0, modes, ROWS):
            some = range(first, first + ROWS)
            coef = spread_rows(coef_ref, at, some)
            decay = [jnp.exp(-rate) for rate in spread_rows(rate_ref, at, some)]

            def eight(group, state):
                state = list(state)
                for row in range(ROWS):
                    strided = pl.ds(group * ROWS * ROWS + row, ROWS, stride=ROWS)
                    dense = pl.ds(pl.multiple_of((group * ROWS + row) * ROWS, ROWS), ROWS)
                    if first == 0:
                        u = token_scr[strided, :]
                        vector_scr[dense, :] = u
                        so_far = skip * u
                    else:
                        u = vector_scr[dense, :]
                        so_far = part_scr[dense, :]
                    state = [factor * one + u for factor, one in zip(decay, state)]
                    value = so_far + tree([factor * one for factor, one in zip(coef, state)])
                    if first + ROWS < modes:
                        part_scr[dense, :] = value
                    else:
                        sum_scr[strided, :] = value
                return tuple(state)

            state = lax.fori_loop(0, half_groups, eight, (jnp.zeros((ROWS, LANES), f32),) * ROWS)
            for at_mode, factor, one in zip(some, coef, state):
                mid_buf[at, at_mode] = factor * one
        for group in range(2 * half_groups):
            half, within = group // half_groups, group % half_groups
            for tile in range(TILES):
                slot = (within * ROWS + half * TILES + tile) * ROWS
                rows = slice(group * ROWS, (group + 1) * ROWS)
                y_buf[at, rows, tile * LANES : (tile + 1) * LANES] = sum_scr[pl.ds(slot, ROWS), :]

    over_chunks(chunks, fetch, chunk, send)


def final_kernel(piece_ref, rate_ref, mid_ref, y_ref, gate_ref, out_ref, *scratches):
    mid_buf, y_buf, gate_buf, out_buf, total_scr, power_scr, lead_scr, in_sem, mid_sem, out_sem = scratches
    chunks, modes = mid_buf.shape[:2]
    tokens = y_buf.shape[1]
    columns = columns_in(((y_ref, y_buf), (gate_ref, gate_buf)), in_sem)

    def fetch(at):
        return columns(at) + [pltpu.make_async_copy(mid_ref.at[at], mid_buf.at[at], mid_sem.at[at])]

    begin(chunks, fetch)
    pieces, piece_rows = piece_ref.shape[:2]
    split = pieces // modes
    for mode in range(modes):
        for part in range(split):
            rows = piece_ref[mode * split + part].astype(f32)
            total_scr[mode, part * piece_rows : (part + 1) * piece_rows, :] = rows
    bits = [(sublane() >> level) % 2 == 1 for level in range(3)]

    def chunk(at):
        through = jnp.exp(-rate_ref[:, span(at)])
        for level in range(4):
            power_scr[level] = through
            through = through * through

        def tile(number, _):
            lanes = tile_lanes(number)
            state = []
            for mode in range(modes):
                rows = [wide(power_scr[level, mode : mode + 1, lanes]) for level in range(3)]
                lead = rows[0]
                for bit, row in zip(bits, rows):
                    lead = lead * jnp.where(bit, row, 1.0)
                lead_scr[mode] = lead
                state.append(lead * wide(total_scr[mode, pl.ds(at * TILES + number, 1), :]))
            decay = [wide(power_scr[3, mode : mode + 1, lanes]) for mode in range(modes)]
            for pair in range(tokens // (2 * ROWS)):
                rows = slice(pair * 2 * ROWS, (pair + 1) * 2 * ROWS)
                gates = gate_buf[at, rows, lanes].astype(f32)
                sums = []
                for part in range(2):
                    if pair == tokens // (4 * ROWS) and part == 0:
                        state = [
                            one + lead_scr[mode] * wide(mid_buf[at, mode, pl.ds(number, 1), :])
                            for mode, one in enumerate(state)
                        ]
                    here = slice((pair * 2 + part) * ROWS, (pair * 2 + part + 1) * ROWS)
                    sums.append(y_buf[at, here, lanes] + tree(state))
                    state = [factor * one for factor, one in zip(decay, state)]
                out_buf[at, rows, lanes] = (gates * rounded(jnp.concatenate(sums, axis=0))).astype(bf16)
            return 0

        lax.fori_loop(0, TILES, tile, 0)

    over_chunks(chunks, fetch, chunk, columns_out(out_ref, out_buf, out_sem))


def cost(flops, moved):
    return pl.CostEstimate(flops=int(flops), bytes_accessed=int(moved), transcendentals=0)


def local(query, key_proj, value_proj, featurizer, rates, residues, skip, *, axes):
    tokens, width = query.shape
    modes = rates.shape[0]
    members, taps, groups = featurizer.shape
    devices = math.prod(lax.axis_size(axis) for axis in axes)
    chunks = width // CHUNK
    tiles = width // LANES
    split = devices // modes
    even = devices % modes == 0 and tiles % split == 0
    vmem = pltpu.VMEM
    far = pltpu.HBM
    near = jax.ShapeDtypeStruct
    dma = pltpu.SemaphoreType.DMA
    elements = tokens * width

    def call(kernel, inputs, outputs, scratches, name, close=(), **more):
        inputs = [
            value if at in close else pltpu.with_memory_space_constraint(value, far)
            for at, value in enumerate(inputs)
        ]
        beside, there = pl.BlockSpec(memory_space=vmem), pl.BlockSpec(memory_space=far)
        return pl.pallas_call(
            kernel,
            in_specs=[beside if at in close else there for at in range(len(inputs))],
            out_specs=[beside if isinstance(one, near) else there for one in outputs],
            out_shape=outputs,
            scratch_shapes=scratches,
            compiler_params=pltpu.CompilerParams(vmem_limit_bytes=32 * 2**20),
            name=name,
            **more,
        )(*inputs)

    (packed,) = call(
        pack_kernel,
        (key_proj, value_proj, query),
        [near((members * ROWS, width), bf16)],
        [vmem((members, 2 * ROWS, width), bf16), dma((members,))],
        "pack",
    )
    halo = lax.ppermute(packed, axes, [(at, at + 1) for at in range(devices - 1)])

    feat = featurizer.reshape(members, taps, chunks, groups // chunks).transpose(2, 0, 1, 3)
    column = vmem((ROWS + tokens, LANES), f32)
    half_buf, whole_buf = vmem((chunks, tokens, CHUNK), bf16), vmem((chunks, tokens, CHUNK), f32)
    u, wide_taps, state = call(
        signal_kernel,
        (key_proj, value_proj, feat, rates),
        [far((tokens, width), bf16), near((chunks, 2, ROWS, CHUNK), f32), near((modes, tiles, LANES), f32)],
        [half_buf, half_buf, half_buf, vmem((4, modes, CHUNK), f32), column, column]
        + [dma((2, chunks)), dma((1, chunks))],
        "signal",
        close=(2, 3),
        cost_estimate=cost(60 * elements, 10 * elements),
    )

    pieces = (modes * split, tiles // split, LANES) if even else (modes, tiles, LANES)
    left, head = call(
        functools.partial(head_kernel, tokens=tokens, reach=taps - 1),
        (key_proj, value_proj, halo, rates, wide_taps, state),
        [near(pieces, bf16), near((2 * ROWS, width), bf16)],
        [vmem((2, 2 * ROWS, width), bf16), vmem((modes * tiles, LANES), f32), vmem((TILES, 2, 2 * ROWS, LANES), f32)]
        + [vmem((tiles * ROWS, LANES), f32), vmem((modes, tiles, LANES), f32), dma((2,))],
        "head",
        close=(2, 3, 4, 5),
    )
    left, halo_late, rates_late, skip_late = lax.optimization_barrier((left, halo, rates, skip))
    coef = residues * jnp.sqrt(-jnp.expm1(-2.0 * rates_late) / modes)
    skip_row = skip_late[None, :]
    (gate,) = call(
        gate_kernel,
        (query, halo_late, feat),
        [far((tokens, width), bf16)],
        [half_buf, vmem((members * ROWS, width), bf16), half_buf, vmem((chunks, 1, ROWS, CHUNK), f32), column]
        + [dma((1, chunks)), dma((1,)), dma((1, chunks))],
        "gate",
        close=(2,),
        cost_estimate=cost(14 * elements, 4 * elements),
    )

    def swap(value):
        return lax.all_to_all(value, axes, split_axis=0, concat_axis=0, tiled=True)

    share = modes * width // devices
    theirs = swap(left if even else left.reshape(devices, share))
    theirs, gate, coef, skip_row = lax.optimization_barrier((theirs, gate, coef, skip_row))
    if even:
        (entering,) = call(
            functools.partial(prefix_kernel, tokens=tokens, axes=axes),
            (theirs, rates, coef),
            [near(pieces, bf16)],
            [vmem((-(-pieces[1] // ROWS) * ROWS, LANES), f32)],
            "prefix",
            close=(0, 1, 2),
        )
    else:
        mine = lax.axis_index(axes)
        through = jnp.exp(-float(tokens) * lax.dynamic_slice_in_dim(rates.reshape(-1), mine * share, share))
        factor = lax.dynamic_slice_in_dim(coef.reshape(-1), mine * share, share)
        _, entering = lax.scan(
            lambda so_far, piece: (through * so_far + piece.astype(f32), (factor * so_far).astype(bf16)),
            jnp.zeros((share,), f32),
            theirs,
        )

    entering, u_late = lax.optimization_barrier((entering, u))
    entered = swap(entering).reshape(pieces)
    stage = vmem((tokens // ROWS // 2 * ROWS * ROWS, LANES), f32)
    y, mid = call(
        local_kernel,
        (u_late, head, rates, coef, skip_row),
        [far((tokens, width), f32), far((chunks, modes, ROWS, LANES), f32)],
        [half_buf, whole_buf, vmem((chunks, modes, ROWS, LANES), f32)] + [stage] * 4
        + [dma((1, chunks)), dma((1, chunks)), dma((chunks,))],
        "within",
        close=(1, 2, 3, 4),
        cost_estimate=cost(66 * elements, 8 * elements),
    )

    (out,) = call(
        final_kernel,
        (entered, rates, mid, y, gate),
        [far((tokens, width), bf16)],
        [vmem((chunks, modes, ROWS, LANES), f32), whole_buf, half_buf, half_buf]
        + [vmem((modes, tiles, LANES), f32), vmem((4, modes, CHUNK), f32), vmem((modes, ROWS, LANES), f32)]
        + [dma((2, chunks)), dma((chunks,)), dma((1, chunks))],
        "final",
        close=(0, 1),
        cost_estimate=cost(40 * elements, 10 * elements),
    )
    return out


def solution(mesh):
    axes = tuple(mesh.axis_names)
    placed = (P(axes, None),) * 3 + (P(),) * 4
    return jax.shard_map(
        functools.partial(local, axes=axes),
        mesh=mesh,
        in_specs=placed,
        out_specs=P(axes, None),
        check_vma=False,
    )
```

```python
import functools
import math

import jax
import jax.numpy as jnp
from jax import lax
from jax.experimental import pallas as pl
from jax.experimental.pallas import tpu as pltpu
from jax.sharding import PartitionSpec as P

LANES = 128
ROWS = 8
TILES = 4
CHUNK = TILES * LANES
AHEAD = 3
f32 = jnp.float32
bf16 = jnp.bfloat16


def put_tile(scratch, group, slot, tile):
    scratch[pl.ds((group * ROWS + slot) * ROWS, ROWS), :] = tile


def get_row(scratch, group, row):
    return scratch[pl.ds(group * ROWS * ROWS + row, ROWS, stride=ROWS), :]


def lanes_of(value, tile):
    return value[:, tile * LANES : (tile + 1) * LANES]


def tile_lanes(tile):
    return pl.ds(pl.multiple_of(tile * LANES, LANES), LANES)


def span(at):
    return pl.ds(pl.multiple_of(at * CHUNK, CHUNK), CHUNK)


def wide(row):
    return jnp.broadcast_to(row, (ROWS, LANES))


def sublane():
    return lax.broadcasted_iota(jnp.int32, (ROWS, LANES), 0)


def spread(row_of):
    slot = sublane() % TILES
    result = wide(row_of(TILES - 1))
    for tile in range(TILES - 1):
        result = jnp.where(slot == tile, wide(row_of(tile)), result)
    return result


def spread_rows(ref, at, rows):
    def one(row):
        return spread(lambda tile: ref[row : row + 1, tile_lanes(at * TILES + tile)])

    return [one(row) for row in rows]


def rounded(value):
    return value.astype(bf16).astype(f32)


def tiles_of(block):
    block = block.astype(f32)
    return [block[at : at + ROWS] for at in range(0, block.shape[0], ROWS)]


def fir(column, taps, first, count):
    half = ROWS // 2
    top = sublane() < half

    def seen(start, lags):
        return [column[pl.ds(start - lag, ROWS), :] for lag in range(lags)]

    def far_part(rows):
        total = taps[half] * rows[0]
        for lag in range(half + 1, len(taps)):
            total = total + taps[lag] * rows[lag - half]
        return pltpu.roll(total, half, 0)

    before = far_part(seen(first - ROWS, len(taps) - half))
    results = []
    for start in range(first, first + count * ROWS, ROWS):
        rows = seen(start, half)
        now = far_part(rows)
        total = taps[0] * rows[0]
        for lag in range(1, half):
            total = total + taps[lag] * rows[lag]
        results.append(total + jnp.where(top, before, now))
        before = now
    return results


def lay_column(column, source, lanes):
    for pair in range(source.shape[0] // (2 * ROWS)):
        rows = slice(pair * 2 * ROWS, (pair + 1) * 2 * ROWS)
        column[pl.ds((pair + 1) * 2 * ROWS, 2 * ROWS), :] = source[rows, lanes].astype(f32)


def chunk_taps(wide_ref, at, member, tile, count):
    return [wide(wide_ref[at, member, lag : lag + 1, tile_lanes(tile)]) for lag in range(count)]


def widened(feat_ref, member, out_ref, position):
    chunks, _, taps, count = feat_ref.shape
    rows = [feat_ref[at, member] for at in range(chunks)]
    rows = [jnp.concatenate([row, jnp.zeros((ROWS - taps, count), f32)], axis=0) for row in rows]
    group = lax.broadcasted_iota(jnp.int32, (count, CHUNK), 0)
    lane = lax.broadcasted_iota(jnp.int32, (count, CHUNK), 1)
    pick = (group == lane // (CHUNK // count)).astype(f32).astype(bf16)
    parts, rest = [], jnp.concatenate(rows, axis=0)
    for _ in range(3):
        term = rest.astype(bf16)
        rest = rest - term.astype(f32)
        parts.append(jnp.dot(term, pick, preferred_element_type=f32))
    out_ref[:, position] = (parts[0] + parts[1] + parts[2]).reshape(chunks, ROWS, CHUNK)


def power(base, exponent):
    result = None
    while exponent:
        if exponent & 1:
            result = base if result is None else result * base
        base = base * base
        exponent >>= 1
    return result


def tree(terms):
    while len(terms) > 1:
        terms = [sum(terms[at + 1 : at + 2], terms[at]) for at in range(0, len(terms), 2)]
    return terms[0]


def start_all(copies):
    for copy in copies:
        copy.start()


def wait_all(copies):
    for copy in copies:
        copy.wait()


def begin(chunks, fetch):
    for at in range(min(AHEAD, chunks)):
        start_all(fetch(at))


def over_chunks(chunks, fetch, body, send):
    def one(at, _):
        @pl.when(at + AHEAD < chunks)
        def _():
            start_all(fetch(at + AHEAD))

        wait_all(fetch(at))
        body(at)
        start_all(send(at))
        return 0

    lax.fori_loop(0, chunks, one, 0)
    for at in range(chunks):
        wait_all(send(at))


def columns_in(pairs, sem):
    def fetch(at):
        return [
            pltpu.make_async_copy(ref.at[:, span(at)], buf.at[at], sem.at[member, at])
            for member, (ref, buf) in enumerate(pairs)
        ]

    return fetch


def columns_out(ref, buf, sem):
    return lambda at: [pltpu.make_async_copy(buf.at[at], ref.at[:, span(at)], sem.at[0, at])]


def pack_kernel(key_ref, value_ref, query_ref, out_ref, in_buf, in_sem):
    tokens = key_ref.shape[0]
    copies = [
        pltpu.make_async_copy(ref.at[pl.ds(tokens - 2 * ROWS, 2 * ROWS)], in_buf.at[at], in_sem.at[at])
        for at, ref in enumerate((key_ref, value_ref, query_ref))
    ]
    start_all(copies)
    wait_all(copies)
    tails = [in_buf[at].astype(f32)[ROWS:] for at in range(len(copies))]
    out_ref[...] = jnp.concatenate(tails, axis=0).astype(bf16)


def signal_kernel(key_ref, value_ref, feat_ref, rate_ref, u_ref, wide_ref, state_ref, *scratches):
    key_buf, value_buf, u_buf, power_scr, *columns, in_sem, out_sem = scratches
    chunks, tokens = u_buf.shape[:2]
    modes = rate_ref.shape[0]
    count = feat_ref.shape[2]
    fetch = columns_in(((key_ref, key_buf), (value_ref, value_buf)), in_sem)
    begin(chunks, fetch)
    for member in range(2):
        widened(feat_ref, member + 1, wide_ref, member)

    def chunk(at):
        through = jnp.exp(-rate_ref[:, span(at)])
        for level in range(4):
            power_scr[level] = through
            through = through * through

        def tile(number, _):
            lanes = tile_lanes(number)
            taps = [chunk_taps(wide_ref, at, member, number, count) for member in range(2)]
            parts = []
            for member, (column, buf) in enumerate(zip(columns, (key_buf, value_buf))):
                column[pl.ds(0, 2 * ROWS), :] = jnp.zeros((2 * ROWS, LANES), f32)
                lay_column(column, buf.at[at], lanes)
                parts.append(fir(column, taps[member], 2 * ROWS, tokens // ROWS))
            found = [one * other for one, other in zip(*parts)]
            found[0] = jnp.where(sublane() < count - 1, 0.0, found[0])
            for pair in range(tokens // (2 * ROWS)):
                rows = slice(pair * 2 * ROWS, (pair + 1) * 2 * ROWS)
                u_buf[at, rows, lanes] = jnp.concatenate(found[pair * 2 : pair * 2 + 2], axis=0).astype(bf16)
            return 0

        lax.fori_loop(0, TILES, tile, 0)

        def gather(number, _):
            lanes = tile_lanes(number)
            decay = [wide(power_scr[3, mode : mode + 1, lanes]) for mode in range(modes)]
            state = None
            for pair in range(tokens // (2 * ROWS)):
                for u in tiles_of(u_buf[at, pair * 2 * ROWS : (pair + 1) * 2 * ROWS, lanes]):
                    if state is None:
                        state = [u] * modes
                    else:
                        state = [decay[mode] * state[mode] + u for mode in range(modes)]
            for mode in range(modes):
                whole = state[mode]
                for level in (2, 1, 0):
                    factor = wide(power_scr[level, mode : mode + 1, lanes])
                    whole = factor * whole + pltpu.roll(whole, ROWS - (1 << level), 0)
                state_ref[mode, pl.ds(at * TILES + number, 1), :] = whole[:1]
            return 0

        lax.fori_loop(0, TILES, gather, 0)

    over_chunks(chunks, fetch, chunk, columns_out(u_ref, u_buf, out_sem))


def head_kernel(key_ref, value_ref, halo_ref, rate_ref, wide_ref, state_ref, out_ref, head_ref, *scratches, tokens, reach):
    front_buf, rate_scr, column_scr, token_scr, total_scr, in_sem = scratches
    modes, tiles = state_ref.shape[:2]
    pieces, piece_rows = out_ref.shape[:2]
    copies = [
        pltpu.make_async_copy(ref.at[pl.ds(0, 2 * ROWS)], front_buf.at[member], in_sem.at[member])
        for member, ref in enumerate((key_ref, value_ref))
    ]
    start_all(copies)
    for group in range(modes // ROWS):
        for tile in range(tiles):
            rows = pl.ds((group * tiles + tile) * ROWS, ROWS)
            rate_scr[rows, :] = rate_ref[group * ROWS : (group + 1) * ROWS, tile * LANES : (tile + 1) * LANES]
    wait_all(copies)

    def some(chunk, _):
        for number in range(TILES):
            lanes = tile_lanes(chunk * TILES + number)
            halo = halo_ref[:, lanes].astype(f32)
            parts = []
            for member in range(2):
                taps = chunk_taps(wide_ref, chunk, member, number, reach + 1)
                column = column_scr.at[number, member]
                column[pl.ds(0, ROWS), :] = jnp.zeros((ROWS, LANES), f32)
                column[pl.ds(ROWS, ROWS), :] = halo[member * ROWS : (member + 1) * ROWS]
                column[pl.ds(2 * ROWS, ROWS), :] = front_buf[member, :, lanes].astype(f32)[:ROWS]
                parts += fir(column, taps, 2 * ROWS, 1)
            u = jnp.where(sublane() < reach, rounded(parts[0] * parts[1]), 0.0)
            token_scr[pl.ds(pl.multiple_of((chunk * TILES + number) * ROWS, ROWS), ROWS), :] = u
            head_ref[:, lanes] = jnp.concatenate([u, jnp.zeros((ROWS, LANES), f32)], axis=0).astype(bf16)
        return 0

    lax.fori_loop(0, tiles // TILES, some, 0)
    signals = [token_scr[pl.ds(row, tiles, stride=ROWS), :] for row in range(reach)]
    split = pieces // modes
    for mode in range(modes):
        start = mode // ROWS * tiles * ROWS + mode % ROWS
        decay = jnp.exp(-rate_scr[pl.ds(start, tiles, stride=ROWS), :])
        head = signals[0]
        for row in range(1, reach):
            head = decay * head + signals[row]
        total_scr[mode] = state_ref[mode] + power(decay, tokens - reach) * head
        for part in range(split):
            rows = total_scr[mode, part * piece_rows : (part + 1) * piece_rows, :]
            out_ref[mode * split + part] = rows.astype(out_ref.dtype)


def gate_kernel(query_ref, halo_ref, feat_ref, gate_ref, *scratches):
    query_buf, halo_buf, gate_buf, wide_scr, column, in_sem, small_sem, out_sem = scratches
    chunks, tokens = gate_buf.shape[:2]
    count = feat_ref.shape[2]
    fetch = columns_in(((query_ref, query_buf),), in_sem)
    halo_copy = pltpu.make_async_copy(halo_ref, halo_buf, small_sem.at[0])
    halo_copy.start()
    begin(chunks, fetch)
    widened(feat_ref, 0, wide_scr, 0)
    halo_copy.wait()

    def chunk(at):
        def tile(number, _):
            lanes = tile_lanes(number)
            taps = chunk_taps(wide_scr, at, 0, number, count)
            halo = halo_buf[:, tile_lanes(at * TILES + number)].astype(f32)
            column[pl.ds(0, ROWS), :] = jnp.zeros((ROWS, LANES), f32)
            column[pl.ds(ROWS, ROWS), :] = halo[2 * ROWS :]
            lay_column(column, query_buf.at[at], lanes)
            found = fir(column, taps, 2 * ROWS, tokens // ROWS)
            for pair in range(tokens // (2 * ROWS)):
                rows = slice(pair * 2 * ROWS, (pair + 1) * 2 * ROWS)
                gate_buf[at, rows, lanes] = jnp.concatenate(found[pair * 2 : pair * 2 + 2], axis=0).astype(bf16)
            return 0

        lax.fori_loop(0, TILES, tile, 0)

    over_chunks(chunks, fetch, chunk, columns_out(gate_ref, gate_buf, out_sem))


def prefix_kernel(piece_ref, rate_ref, coef_ref, out_ref, table_scr, *, tokens, axes):
    devices, piece_rows = piece_ref.shape[:2]
    split = devices // rate_ref.shape[0]
    mine = lax.axis_index(axes)
    mode, part = mine // split, mine % split
    group = pl.multiple_of(mode // ROWS * ROWS, ROWS)
    first = pl.multiple_of(part * piece_rows * LANES, LANES)

    def mine_of(ref):
        rows = ref[pl.ds(group, ROWS), pl.ds(first, piece_rows * LANES)]
        here = lax.broadcasted_iota(jnp.int32, rows.shape, 0) == mode - group
        row = jnp.sum(jnp.where(here, rows, 0.0), axis=0, keepdims=True)
        for number in range(piece_rows):
            table_scr[number : number + 1, :] = lanes_of(row, number)
        return table_scr[:piece_rows, :]

    coef = mine_of(coef_ref)
    through = jnp.exp(-float(tokens) * mine_of(rate_ref))

    def lap(number, entering):
        for step in range(4):
            source = number * 4 + step
            out_ref[source] = (coef * entering).astype(out_ref.dtype)
            entering = through * entering + piece_ref[source].astype(f32)
        return entering

    lax.fori_loop(0, devices // 4, lap, jnp.zeros((piece_rows, LANES), f32))


def local_kernel(u_ref, head_ref, rate_ref, coef_ref, skip_ref, *rest, first, last):
    y_ref, mid_ref, u_buf, y_buf, mid_buf, token_scr, sum_scr, in_sem, out_sem, mid_sem = rest[-10:]
    tokens = u_buf.shape[1]
    modes = rate_ref.shape[0]
    half_groups = tokens // ROWS // 2
    take = columns_in(((u_ref, u_buf),), in_sem)
    give = columns_out(y_ref, y_buf, out_sem)

    def fetch(number):
        return take(number + first)

    def send(number):
        at = number + first
        return give(at) + [pltpu.make_async_copy(mid_buf.at[at], mid_ref.at[at], mid_sem.at[at])]

    begin(last - first, fetch)

    def chunk(number):
        at = number + first
        front = u_buf[at, : 2 * ROWS].astype(f32) + head_ref[:, span(at)].astype(f32)
        u_buf[at, : 2 * ROWS] = front.astype(bf16)
        for pair in range(half_groups):
            block = u_buf[at, pair * 2 * ROWS : (pair + 1) * 2 * ROWS, :].astype(f32)
            for part in range(2):
                group = pair * 2 + part
                half, within = group // half_groups, group % half_groups
                for tile in range(TILES):
                    piece = lanes_of(block, tile)[part * ROWS : (part + 1) * ROWS]
                    put_tile(token_scr, within, half * TILES + tile, piece)
        (skip,) = spread_rows(skip_ref, at, range(1))
        coef = spread_rows(coef_ref, at, range(modes))
        decay = [jnp.exp(-rate) for rate in spread_rows(rate_ref, at, range(modes))]

        def eight(group, state):
            state = list(state)
            for row in range(ROWS):
                u = get_row(token_scr, group, row)
                state = [factor * one + u for factor, one in zip(decay, state)]
                terms = [factor * one for factor, one in zip([skip] + coef, [u] + state)]
                sum_scr[pl.ds(group * ROWS * ROWS + row, ROWS, stride=ROWS), :] = tree(terms)
            return tuple(state)

        state = lax.fori_loop(0, half_groups, eight, (jnp.zeros((ROWS, LANES), f32),) * modes)
        for mode, (factor, one) in enumerate(zip(coef, state)):
            mid_buf[at, mode] = factor * one
        for group in range(2 * half_groups):
            half, within = group // half_groups, group % half_groups
            for tile in range(TILES):
                slot = (within * ROWS + half * TILES + tile) * ROWS
                rows = slice(group * ROWS, (group + 1) * ROWS)
                y_buf[at, rows, tile * LANES : (tile + 1) * LANES] = sum_scr[pl.ds(slot, ROWS), :]

    over_chunks(last - first, fetch, chunk, send)


def final_kernel(piece_ref, rate_ref, mid_ref, y_ref, gate_ref, out_ref, *scratches):
    mid_buf, y_buf, gate_buf, out_buf, total_scr, power_scr, lead_scr, in_sem, mid_sem, out_sem = scratches
    chunks, modes = mid_buf.shape[:2]
    tokens = y_buf.shape[1]
    columns = columns_in(((y_ref, y_buf), (gate_ref, gate_buf)), in_sem)

    def fetch(at):
        return columns(at) + [pltpu.make_async_copy(mid_ref.at[at], mid_buf.at[at], mid_sem.at[at])]

    begin(chunks, fetch)
    pieces, piece_rows = piece_ref.shape[:2]
    split = pieces // modes
    for mode in range(modes):
        for part in range(split):
            rows = piece_ref[mode * split + part].astype(f32)
            total_scr[mode, part * piece_rows : (part + 1) * piece_rows, :] = rows
    bits = [(sublane() >> level) % 2 == 1 for level in range(3)]

    def chunk(at):
        through = jnp.exp(-rate_ref[:, span(at)])
        for level in range(4):
            power_scr[level] = through
            through = through * through

        def tile(number, _):
            lanes = tile_lanes(number)
            state = []
            for mode in range(modes):
                rows = [wide(power_scr[level, mode : mode + 1, lanes]) for level in range(3)]
                lead = rows[0]
                for bit, row in zip(bits, rows):
                    lead = lead * jnp.where(bit, row, 1.0)
                lead_scr[mode] = lead
                state.append(lead * wide(total_scr[mode, pl.ds(at * TILES + number, 1), :]))
            decay = [wide(power_scr[3, mode : mode + 1, lanes]) for mode in range(modes)]
            for pair in range(tokens // (2 * ROWS)):
                rows = slice(pair * 2 * ROWS, (pair + 1) * 2 * ROWS)
                gates = gate_buf[at, rows, lanes].astype(f32)
                sums = []
                for part in range(2):
                    if pair == tokens // (4 * ROWS) and part == 0:
                        state = [
                            one + lead_scr[mode] * wide(mid_buf[at, mode, pl.ds(number, 1), :])
                            for mode, one in enumerate(state)
                        ]
                    here = slice((pair * 2 + part) * ROWS, (pair * 2 + part + 1) * ROWS)
                    sums.append(y_buf[at, here, lanes] + tree(state))
                    state = [factor * one for factor, one in zip(decay, state)]
                out_buf[at, rows, lanes] = (gates * rounded(jnp.concatenate(sums, axis=0))).astype(bf16)
            return 0

        lax.fori_loop(0, TILES, tile, 0)

    over_chunks(chunks, fetch, chunk, columns_out(out_ref, out_buf, out_sem))


def cost(flops, moved):
    return pl.CostEstimate(flops=int(flops), bytes_accessed=int(moved), transcendentals=0)


def local(query, key_proj, value_proj, featurizer, rates, residues, skip, *, axes):
    tokens, width = query.shape
    modes = rates.shape[0]
    members, taps, groups = featurizer.shape
    devices = math.prod(lax.axis_size(axis) for axis in axes)
    chunks = width // CHUNK
    tiles = width // LANES
    split = devices // modes
    even = devices % modes == 0 and tiles % split == 0
    vmem = pltpu.VMEM
    far = pltpu.HBM
    near = jax.ShapeDtypeStruct
    dma = pltpu.SemaphoreType.DMA
    elements = tokens * width

    def call(kernel, inputs, outputs, scratches, name, close=(), **more):
        inputs = [
            value if at in close else pltpu.with_memory_space_constraint(value, far)
            for at, value in enumerate(inputs)
        ]
        beside, there = pl.BlockSpec(memory_space=vmem), pl.BlockSpec(memory_space=far)
        return pl.pallas_call(
            kernel,
            in_specs=[beside if at in close else there for at in range(len(inputs))],
            out_specs=[beside if isinstance(one, near) else there for one in outputs],
            out_shape=outputs,
            scratch_shapes=scratches,
            compiler_params=pltpu.CompilerParams(vmem_limit_bytes=32 * 2**20),
            name=name,
            **more,
        )(*inputs)

    (packed,) = call(
        pack_kernel,
        (key_proj, value_proj, query),
        [near((members * ROWS, width), bf16)],
        [vmem((members, 2 * ROWS, width), bf16), dma((members,))],
        "pack",
    )
    halo = lax.ppermute(packed, axes, [(at, at + 1) for at in range(devices - 1)])

    feat = featurizer.reshape(members, taps, chunks, groups // chunks).transpose(2, 0, 1, 3)
    column = vmem((2 * ROWS + tokens, LANES), f32)
    half_buf, whole_buf = vmem((chunks, tokens, CHUNK), bf16), vmem((chunks, tokens, CHUNK), f32)
    u, wide_taps, state = call(
        signal_kernel,
        (key_proj, value_proj, feat, rates),
        [far((tokens, width), bf16), near((chunks, 2, ROWS, CHUNK), f32), near((modes, tiles, LANES), f32)],
        [half_buf, half_buf, half_buf, vmem((4, modes, CHUNK), f32), column, column]
        + [dma((2, chunks)), dma((1, chunks))],
        "signal",
        close=(2, 3),
        cost_estimate=cost(60 * elements, 10 * elements),
    )

    pieces = (modes * split, tiles // split, LANES) if even else (modes, tiles, LANES)
    left, head = call(
        functools.partial(head_kernel, tokens=tokens, reach=taps - 1),
        (key_proj, value_proj, halo, rates, wide_taps, state),
        [near(pieces, bf16), near((2 * ROWS, width), bf16)],
        [vmem((2, 2 * ROWS, width), bf16), vmem((modes * tiles, LANES), f32), vmem((TILES, 2, 3 * ROWS, LANES), f32)]
        + [vmem((tiles * ROWS, LANES), f32), vmem((modes, tiles, LANES), f32), dma((2,))],
        "head",
        close=(2, 3, 4, 5),
    )
    left, halo_late, rates_late, skip_late, u_late = lax.optimization_barrier((left, halo, rates, skip, u))
    coef = residues * jnp.sqrt(-jnp.expm1(-2.0 * rates_late) / modes)
    skip_row = skip_late[None, :]
    (gate,) = call(
        gate_kernel,
        (query, halo_late, feat),
        [far((tokens, width), bf16)],
        [half_buf, vmem((members * ROWS, width), bf16), half_buf, vmem((chunks, 1, ROWS, CHUNK), f32), column]
        + [dma((1, chunks)), dma((1,)), dma((1, chunks))],
        "gate",
        close=(2,),
        cost_estimate=cost(14 * elements, 4 * elements),
    )

    stage = vmem((tokens // ROWS // 2 * ROWS * ROWS, LANES), f32)

    def within(u, head, y, mid, first, last):
        before = () if y is None else (y, mid)
        return call(
            functools.partial(local_kernel, first=first, last=last),
            (u, head, rates, coef, skip_row, *before),
            [far((tokens, width), f32), far((chunks, modes, ROWS, LANES), f32)],
            [half_buf, whole_buf, vmem((chunks, modes, ROWS, LANES), f32), stage, stage]
            + [dma((1, chunks)), dma((1, chunks)), dma((chunks,))],
            "within",
            close=(1, 2, 3, 4),
            cost_estimate=cost(7 * (last - first) * tokens * CHUNK * 10, (last - first) * tokens * CHUNK * 8),
            input_output_aliases={5 + at: at for at in range(len(before))},
        )

    early = chunks // 3
    y, mid = within(u_late, head, None, None, 0, early)

    def swap(value):
        return lax.all_to_all(value, axes, split_axis=0, concat_axis=0, tiled=True)

    share = modes * width // devices
    theirs = swap(left if even else left.reshape(devices, share))
    theirs, gate, coef, skip_row, y, mid = lax.optimization_barrier((theirs, gate, coef, skip_row, y, mid))
    if even:
        (entering,) = call(
            functools.partial(prefix_kernel, tokens=tokens, axes=axes),
            (theirs, rates, coef),
            [near(pieces, bf16)],
            [vmem((-(-pieces[1] // ROWS) * ROWS, LANES), f32)],
            "prefix",
            close=(0, 1, 2),
        )
    else:
        mine = lax.axis_index(axes)
        through = jnp.exp(-float(tokens) * lax.dynamic_slice_in_dim(rates.reshape(-1), mine * share, share))
        factor = lax.dynamic_slice_in_dim(coef.reshape(-1), mine * share, share)
        _, entering = lax.scan(
            lambda so_far, piece: (through * so_far + piece.astype(f32), (factor * so_far).astype(bf16)),
            jnp.zeros((share,), f32),
            theirs,
        )

    entering, u_late = lax.optimization_barrier((entering, u))
    entered = swap(entering).reshape(pieces)
    y, mid = within(u_late, head, y, mid, early, chunks)

    (out,) = call(
        final_kernel,
        (entered, rates, mid, y, gate),
        [far((tokens, width), bf16)],
        [vmem((chunks, modes, ROWS, LANES), f32), whole_buf, half_buf, half_buf]
        + [vmem((modes, tiles, LANES), f32), vmem((4, modes, CHUNK), f32), vmem((modes, ROWS, LANES), f32)]
        + [dma((2, chunks)), dma((chunks,)), dma((1, chunks))],
        "final",
        close=(0, 1),
        cost_estimate=cost(40 * elements, 10 * elements),
    )
    return out


def solution(mesh):
    axes = tuple(mesh.axis_names)
    placed = (P(axes, None),) * 3 + (P(),) * 4
    return jax.shard_map(
        functools.partial(local, axes=axes),
        mesh=mesh,
        in_specs=placed,
        out_specs=P(axes, None),
        check_vma=False,
    )
```

```python
import functools
import math

import jax
import jax.numpy as jnp
from jax import lax
from jax.experimental import pallas as pl
from jax.experimental.pallas import tpu as pltpu
from jax.sharding import PartitionSpec as P

LANES = 128
ROWS = 8
TILES = 4
CHUNK = TILES * LANES
AHEAD = 2
f32 = jnp.float32
bf16 = jnp.bfloat16


def put_tile(scratch, group, slot, tile):
    scratch[pl.ds((group * ROWS + slot) * ROWS, ROWS), :] = tile


def get_row(scratch, group, row):
    return scratch[pl.ds(group * ROWS * ROWS + row, ROWS, stride=ROWS), :]


def lanes_of(value, tile):
    return value[:, tile * LANES : (tile + 1) * LANES]


def tile_lanes(tile):
    return pl.ds(pl.multiple_of(tile * LANES, LANES), LANES)


def span(at):
    return pl.ds(pl.multiple_of(at * CHUNK, CHUNK), CHUNK)


def wide(row):
    return jnp.broadcast_to(row, (ROWS, LANES))


def sublane():
    return lax.broadcasted_iota(jnp.int32, (ROWS, LANES), 0)


def spread(row_of):
    slot = sublane() % TILES
    result = wide(row_of(TILES - 1))
    for tile in range(TILES - 1):
        result = jnp.where(slot == tile, wide(row_of(tile)), result)
    return result


def spread_rows(ref, at, rows):
    def one(row):
        return spread(lambda tile: ref[row : row + 1, tile_lanes(at * TILES + tile)])

    return [one(row) for row in rows]


def rounded(value):
    return value.astype(bf16).astype(f32)


def tiles_of(block):
    block = block.astype(f32)
    return [block[at : at + ROWS] for at in range(0, block.shape[0], ROWS)]


def fir(column, taps, first):
    total = taps[0] * column[pl.ds(first, ROWS), :]
    for lag in range(1, len(taps)):
        total = total + taps[lag] * column[pl.ds(first - lag, ROWS), :]
    return total


def lay_column(column, source, lanes):
    for pair in range(source.shape[0] // (2 * ROWS)):
        rows = slice(pair * 2 * ROWS, (pair + 1) * 2 * ROWS)
        column[pl.ds(ROWS + pair * 2 * ROWS, 2 * ROWS), :] = source[rows, lanes].astype(f32)


def chunk_taps(wide_ref, at, member, tile, count):
    return [wide(wide_ref[at, member, lag : lag + 1, tile_lanes(tile)]) for lag in range(count)]


def widened(feat_ref, member, out_ref, position):
    chunks, _, taps, count = feat_ref.shape
    rows = [feat_ref[at, member] for at in range(chunks)]
    rows = [jnp.concatenate([row, jnp.zeros((ROWS - taps, count), f32)], axis=0) for row in rows]
    group = lax.broadcasted_iota(jnp.int32, (count, CHUNK), 0)
    lane = lax.broadcasted_iota(jnp.int32, (count, CHUNK), 1)
    pick = (group == lane // (CHUNK // count)).astype(f32).astype(bf16)
    parts, rest = [], jnp.concatenate(rows, axis=0)
    for _ in range(3):
        term = rest.astype(bf16)
        rest = rest - term.astype(f32)
        parts.append(jnp.dot(term, pick, preferred_element_type=f32))
    out_ref[:, position] = (parts[0] + parts[1] + parts[2]).reshape(chunks, ROWS, CHUNK)


def power(base, exponent):
    result = None
    while exponent:
        if exponent & 1:
            result = base if result is None else result * base
        base = base * base
        exponent >>= 1
    return result


def tree(terms):
    while len(terms) > 1:
        terms = [sum(terms[at + 1 : at + 2], terms[at]) for at in range(0, len(terms), 2)]
    return terms[0]


def start_all(copies):
    for copy in copies:
        copy.start()


def wait_all(copies):
    for copy in copies:
        copy.wait()


def begin(chunks, fetch):
    for at in range(min(AHEAD, chunks)):
        start_all(fetch(at))


def over_chunks(chunks, fetch, body, send, last=True):
    def one(at, _):
        @pl.when(at + AHEAD < chunks)
        def _():
            start_all(fetch(at + AHEAD))

        wait_all(fetch(at))
        body(at)
        start_all(send(at))
        return 0

    lax.fori_loop(0, chunks, one, 0)
    if last:
        for at in range(chunks):
            wait_all(send(at))


def columns_in(pairs, sem):
    def fetch(at):
        return [
            pltpu.make_async_copy(ref.at[:, span(at)], buf.at[at], sem.at[member, at])
            for member, (ref, buf) in enumerate(pairs)
        ]

    return fetch


def columns_out(ref, buf, sem):
    return lambda at: [pltpu.make_async_copy(buf.at[at], ref.at[:, span(at)], sem.at[0, at])]


def pack_kernel(key_ref, value_ref, query_ref, out_ref, in_buf, in_sem):
    tokens = key_ref.shape[0]
    copies = [
        pltpu.make_async_copy(ref.at[pl.ds(tokens - 2 * ROWS, 2 * ROWS)], in_buf.at[at], in_sem.at[at])
        for at, ref in enumerate((key_ref, value_ref, query_ref))
    ]
    start_all(copies)
    wait_all(copies)
    tails = [in_buf[at].astype(f32)[ROWS:] for at in range(len(copies))]
    out_ref[...] = jnp.concatenate(tails, axis=0).astype(bf16)


def signal_kernel(key_ref, value_ref, feat_ref, rate_ref, u_ref, wide_ref, state_ref, power_scr, last_scr, *columns):
    tokens, tiles = u_ref.shape[0], state_ref.shape[1]
    modes = rate_ref.shape[0]
    chunks = tiles // TILES
    count = feat_ref.shape[2]
    for member in range(2):
        widened(feat_ref, member + 1, wide_ref, member)
    for column in columns:
        column[pl.ds(0, ROWS), :] = jnp.zeros((ROWS, LANES), f32)
    last_scr[...] = jnp.zeros(last_scr.shape, f32)

    def powers(at, _):
        through = jnp.exp(-rate_ref[:, span(at)])
        for level in range(4):
            power_scr[level, :, span(at)] = through
            through = through * through
        return 0

    lax.fori_loop(0, chunks, powers, 0)

    def reduce(number):
        lanes = tile_lanes(number)
        for mode in range(modes):
            whole = last_scr[mode]
            for level in (2, 1, 0):
                factor = wide(power_scr[level, mode : mode + 1, lanes])
                whole = factor * whole + pltpu.roll(whole, ROWS - (1 << level), 0)
            state_ref[mode, pl.ds(number, 1), :] = whole[:1]

    def tile(number, _):
        lanes = tile_lanes(number)
        reduce(jnp.maximum(number - 1, 0))
        taps = [chunk_taps(wide_ref, number // TILES, member, number % TILES, count) for member in range(2)]
        for column, ref in zip(columns, (key_ref, value_ref)):
            lay_column(column, ref, lanes)
        decay = [wide(power_scr[3, mode : mode + 1, lanes]) for mode in range(modes)]
        state = None
        for pair in range(tokens // (2 * ROWS)):
            found = []
            for first in (pair * 2 * ROWS + ROWS, pair * 2 * ROWS + 2 * ROWS):
                u = fir(columns[0], taps[0], first) * fir(columns[1], taps[1], first)
                found.append(jnp.where(sublane() < count - 1, 0.0, u) if first == ROWS else u)
            both = jnp.concatenate(found, axis=0).astype(bf16)
            u_ref[pair * 2 * ROWS : (pair + 1) * 2 * ROWS, lanes] = both
            for u in tiles_of(both):
                if state is None:
                    state = [u] * modes
                else:
                    state = [factor * one + u for factor, one in zip(decay, state)]
        for mode in range(modes):
            last_scr[mode] = state[mode]
        return 0

    lax.fori_loop(0, tiles, tile, 0)
    reduce(tiles - 1)


def head_kernel(key_ref, value_ref, halo_ref, rate_ref, wide_ref, state_ref, out_ref, head_ref, *scratches, tokens, reach):
    rate_scr, column_scr, token_scr, total_scr = scratches
    modes, tiles = state_ref.shape[:2]
    pieces, piece_rows = out_ref.shape[:2]
    for group in range(modes // ROWS):
        for tile in range(tiles):
            rows = pl.ds((group * tiles + tile) * ROWS, ROWS)
            rate_scr[rows, :] = rate_ref[group * ROWS : (group + 1) * ROWS, tile * LANES : (tile + 1) * LANES]

    def some(chunk, _):
        for number in range(TILES):
            lanes = tile_lanes(chunk * TILES + number)
            halo = halo_ref[:, lanes].astype(f32)
            parts = []
            for member in range(2):
                taps = chunk_taps(wide_ref, chunk, member, number, reach + 1)
                column = column_scr.at[number, member]
                column[pl.ds(0, ROWS), :] = halo[member * ROWS : (member + 1) * ROWS]
                source = (key_ref, value_ref)[member]
                column[pl.ds(ROWS, ROWS), :] = source[: 2 * ROWS, lanes].astype(f32)[:ROWS]
                parts.append(fir(column, taps, ROWS))
            u = jnp.where(sublane() < reach, rounded(parts[0] * parts[1]), 0.0)
            token_scr[pl.ds(pl.multiple_of((chunk * TILES + number) * ROWS, ROWS), ROWS), :] = u
            head_ref[:, lanes] = jnp.concatenate([u, jnp.zeros((ROWS, LANES), f32)], axis=0).astype(bf16)
        return 0

    lax.fori_loop(0, tiles // TILES, some, 0)
    signals = [token_scr[pl.ds(row, tiles, stride=ROWS), :] for row in range(reach)]
    split = pieces // modes
    for mode in range(modes):
        start = mode // ROWS * tiles * ROWS + mode % ROWS
        decay = jnp.exp(-rate_scr[pl.ds(start, tiles, stride=ROWS), :])
        head = signals[0]
        for row in range(1, reach):
            head = decay * head + signals[row]
        total_scr[mode] = state_ref[mode] + power(decay, tokens - reach) * head
        for part in range(split):
            rows = total_scr[mode, part * piece_rows : (part + 1) * piece_rows, :]
            out_ref[mode * split + part] = rows.astype(out_ref.dtype)


def gate_kernel(query_ref, halo_ref, feat_ref, u_ref, head_ref, rate_ref, coef_ref, skip_ref, gate_ref, *rest, early):
    y_ref, mid_ref, query_buf, halo_buf, gate_buf, wide_scr, column, in_sem, small_sem, out_sem = rest[:10]
    inner = rest[10:]
    chunks, tokens = gate_buf.shape[:2]
    count = feat_ref.shape[2]
    fetch = columns_in(((query_ref, query_buf),), in_sem)
    halo_copy = pltpu.make_async_copy(halo_ref, halo_buf, small_sem.at[0])
    halo_copy.start()
    begin(chunks, fetch)
    local_fetch, local_chunk, local_send = local_parts(
        u_ref, head_ref, rate_ref, coef_ref, skip_ref, y_ref, mid_ref, *inner, first=0
    )
    begin(early, local_fetch)
    widened(feat_ref, 0, wide_scr, 0)
    halo_copy.wait()

    def chunk(at):
        def tile(number, _):
            lanes = tile_lanes(number)
            taps = chunk_taps(wide_scr, at, 0, number, count)
            halo = halo_buf[:, tile_lanes(at * TILES + number)].astype(f32)
            column[pl.ds(0, ROWS), :] = halo[2 * ROWS :]
            lay_column(column, query_buf.at[at], lanes)
            for pair in range(tokens // (2 * ROWS)):
                first = pair * 2 * ROWS + ROWS
                found = [fir(column, taps, first), fir(column, taps, first + ROWS)]
                rows = slice(pair * 2 * ROWS, (pair + 1) * 2 * ROWS)
                gate_buf[at, rows, lanes] = jnp.concatenate(found, axis=0).astype(bf16)
            return 0

        lax.fori_loop(0, TILES, tile, 0)

    give = columns_out(gate_ref, gate_buf, out_sem)
    over_chunks(chunks, fetch, chunk, give, last=False)
    over_chunks(early, local_fetch, local_chunk, local_send)
    for at in range(chunks):
        wait_all(give(at))


def prefix_kernel(piece_ref, rate_ref, coef_ref, out_ref, table_scr, *, tokens, axes):
    devices, piece_rows = piece_ref.shape[:2]
    split = devices // rate_ref.shape[0]
    mine = lax.axis_index(axes)
    mode, part = mine // split, mine % split
    group = pl.multiple_of(mode // ROWS * ROWS, ROWS)
    first = pl.multiple_of(part * piece_rows * LANES, LANES)

    def mine_of(ref):
        rows = ref[pl.ds(group, ROWS), pl.ds(first, piece_rows * LANES)]
        here = lax.broadcasted_iota(jnp.int32, rows.shape, 0) == mode - group
        row = jnp.sum(jnp.where(here, rows, 0.0), axis=0, keepdims=True)
        for number in range(piece_rows):
            table_scr[number : number + 1, :] = lanes_of(row, number)
        return table_scr[:piece_rows, :]

    coef = mine_of(coef_ref)
    through = jnp.exp(-float(tokens) * mine_of(rate_ref))

    def lap(number, entering):
        for step in range(4):
            source = number * 4 + step
            out_ref[source] = (coef * entering).astype(out_ref.dtype)
            entering = through * entering + piece_ref[source].astype(f32)
        return entering

    lax.fori_loop(0, devices // 4, lap, jnp.zeros((piece_rows, LANES), f32))


def local_kernel(u_ref, head_ref, rate_ref, coef_ref, skip_ref, *rest, first, last):
    fetch, chunk, send = local_parts(u_ref, head_ref, rate_ref, coef_ref, skip_ref, *rest[-10:], first=first)
    begin(last - first, fetch)
    over_chunks(last - first, fetch, chunk, send)


def local_parts(u_ref, head_ref, rate_ref, coef_ref, skip_ref, y_ref, mid_ref, *scratches, first):
    u_buf, y_buf, mid_buf, token_scr, sum_scr, in_sem, out_sem, mid_sem = scratches
    tokens = u_buf.shape[1]
    modes = rate_ref.shape[0]
    half_groups = tokens // ROWS // 2
    take = columns_in(((u_ref, u_buf),), in_sem)
    give = columns_out(y_ref, y_buf, out_sem)

    def fetch(number):
        return take(number + first)

    def send(number):
        at = number + first
        return give(at) + [pltpu.make_async_copy(mid_buf.at[at], mid_ref.at[at], mid_sem.at[at])]

    def chunk(number):
        at = number + first
        front = u_buf[at, : 2 * ROWS].astype(f32) + head_ref[:, span(at)].astype(f32)
        u_buf[at, : 2 * ROWS] = front.astype(bf16)
        for pair in range(half_groups):
            block = u_buf[at, pair * 2 * ROWS : (pair + 1) * 2 * ROWS, :].astype(f32)
            for part in range(2):
                group = pair * 2 + part
                half, within = group // half_groups, group % half_groups
                for tile in range(TILES):
                    piece = lanes_of(block, tile)[part * ROWS : (part + 1) * ROWS]
                    put_tile(token_scr, within, half * TILES + tile, piece)
        (skip,) = spread_rows(skip_ref, at, range(1))
        coef = spread_rows(coef_ref, at, range(modes))
        decay = [jnp.exp(-rate) for rate in spread_rows(rate_ref, at, range(modes))]

        def eight(group, state):
            state = list(state)
            for row in range(ROWS):
                u = get_row(token_scr, group, row)
                state = [factor * one + u for factor, one in zip(decay, state)]
                terms = [factor * one for factor, one in zip([skip] + coef, [u] + state)]
                sum_scr[pl.ds(group * ROWS * ROWS + row, ROWS, stride=ROWS), :] = tree(terms)
            return tuple(state)

        state = lax.fori_loop(0, half_groups, eight, (jnp.zeros((ROWS, LANES), f32),) * modes)
        for mode, (factor, one) in enumerate(zip(coef, state)):
            mid_buf[at, mode] = factor * one
        for group in range(2 * half_groups):
            half, within = group // half_groups, group % half_groups
            for tile in range(TILES):
                slot = (within * ROWS + half * TILES + tile) * ROWS
                rows = slice(group * ROWS, (group + 1) * ROWS)
                y_buf[at, rows, tile * LANES : (tile + 1) * LANES] = sum_scr[pl.ds(slot, ROWS), :]

    return fetch, chunk, send


def final_kernel(piece_ref, rate_ref, mid_ref, y_ref, gate_ref, out_ref, *scratches):
    mid_buf, y_buf, gate_buf, out_buf, total_scr, power_scr, lead_scr, in_sem, mid_sem, out_sem = scratches
    chunks, modes = mid_buf.shape[:2]
    tokens = y_buf.shape[1]
    columns = columns_in(((y_ref, y_buf), (gate_ref, gate_buf)), in_sem)

    def fetch(at):
        return columns(at) + [pltpu.make_async_copy(mid_ref.at[at], mid_buf.at[at], mid_sem.at[at])]

    begin(chunks, fetch)
    pieces, piece_rows = piece_ref.shape[:2]
    split = pieces // modes
    for mode in range(modes):
        for part in range(split):
            rows = piece_ref[mode * split + part].astype(f32)
            total_scr[mode, part * piece_rows : (part + 1) * piece_rows, :] = rows
    bits = [(sublane() >> level) % 2 == 1 for level in range(3)]

    def chunk(at):
        through = jnp.exp(-rate_ref[:, span(at)])
        for level in range(4):
            power_scr[level] = through
            through = through * through

        def tile(number, _):
            lanes = tile_lanes(number)
            state = []
            for mode in range(modes):
                rows = [wide(power_scr[level, mode : mode + 1, lanes]) for level in range(3)]
                lead = rows[0]
                for bit, row in zip(bits, rows):
                    lead = lead * jnp.where(bit, row, 1.0)
                lead_scr[mode] = lead
                state.append(lead * wide(total_scr[mode, pl.ds(at * TILES + number, 1), :]))
            decay = [wide(power_scr[3, mode : mode + 1, lanes]) for mode in range(modes)]
            for pair in range(tokens // (2 * ROWS)):
                rows = slice(pair * 2 * ROWS, (pair + 1) * 2 * ROWS)
                gates = gate_buf[at, rows, lanes].astype(f32)
                sums = []
                for part in range(2):
                    if pair == tokens // (4 * ROWS) and part == 0:
                        state = [
                            one + lead_scr[mode] * wide(mid_buf[at, mode, pl.ds(number, 1), :])
                            for mode, one in enumerate(state)
                        ]
                    here = slice((pair * 2 + part) * ROWS, (pair * 2 + part + 1) * ROWS)
                    sums.append(y_buf[at, here, lanes] + tree(state))
                    state = [factor * one for factor, one in zip(decay, state)]
                out_buf[at, rows, lanes] = (gates * rounded(jnp.concatenate(sums, axis=0))).astype(bf16)
            return 0

        lax.fori_loop(0, TILES, tile, 0)

    over_chunks(chunks, fetch, chunk, columns_out(out_ref, out_buf, out_sem))


def cost(flops, moved):
    return pl.CostEstimate(flops=int(flops), bytes_accessed=int(moved), transcendentals=0)


def local(query, key_proj, value_proj, featurizer, rates, residues, skip, *, axes):
    tokens, width = query.shape
    modes = rates.shape[0]
    members, taps, groups = featurizer.shape
    devices = math.prod(lax.axis_size(axis) for axis in axes)
    chunks = width // CHUNK
    tiles = width // LANES
    split = devices // modes
    even = devices % modes == 0 and tiles % split == 0
    vmem = pltpu.VMEM
    far = pltpu.HBM
    near = jax.ShapeDtypeStruct
    dma = pltpu.SemaphoreType.DMA
    elements = tokens * width

    def call(kernel, inputs, outputs, scratches, name, close=(), **more):
        inputs = [
            value if at in close else pltpu.with_memory_space_constraint(value, far)
            for at, value in enumerate(inputs)
        ]
        beside, there = pl.BlockSpec(memory_space=vmem), pl.BlockSpec(memory_space=far)
        return pl.pallas_call(
            kernel,
            in_specs=[beside if at in close else there for at in range(len(inputs))],
            out_specs=[beside if isinstance(one, near) else there for one in outputs],
            out_shape=outputs,
            scratch_shapes=scratches,
            compiler_params=pltpu.CompilerParams(vmem_limit_bytes=32 * 2**20),
            name=name,
            **more,
        )(*inputs)

    (packed,) = call(
        pack_kernel,
        (key_proj, value_proj, query),
        [near((members * ROWS, width), bf16)],
        [vmem((members, 2 * ROWS, width), bf16), dma((members,))],
        "pack",
    )
    halo = lax.ppermute(packed, axes, [(at, at + 1) for at in range(devices - 1)])

    feat = featurizer.reshape(members, taps, chunks, groups // chunks).transpose(2, 0, 1, 3)
    column = vmem((ROWS + tokens, LANES), f32)
    half_buf, whole_buf = vmem((chunks, tokens, CHUNK), bf16), vmem((chunks, tokens, CHUNK), f32)
    u, wide_taps, state = call(
        signal_kernel,
        (key_proj, value_proj, feat, rates),
        [near((tokens, width), bf16), near((chunks, 2, ROWS, CHUNK), f32), near((modes, tiles, LANES), f32)],
        [vmem((4, modes, width), f32), vmem((modes, ROWS, LANES), f32), column, column],
        "signal",
        close=range(4),
        cost_estimate=cost(60 * elements, 10 * elements),
    )

    pieces = (modes * split, tiles // split, LANES) if even else (modes, tiles, LANES)
    left, head = call(
        functools.partial(head_kernel, tokens=tokens, reach=taps - 1),
        (key_proj, value_proj, halo, rates, wide_taps, state),
        [near(pieces, bf16), near((2 * ROWS, width), bf16)],
        [vmem((modes * tiles, LANES), f32), vmem((TILES, 2, 2 * ROWS, LANES), f32)]
        + [vmem((tiles * ROWS, LANES), f32), vmem((modes, tiles, LANES), f32)],
        "head",
        close=range(6),
    )
    left, halo_late, rates_late, skip_late, u_late = lax.optimization_barrier((left, halo, rates, skip, u))
    coef = residues * jnp.sqrt(-jnp.expm1(-2.0 * rates_late) / modes)
    skip_row = skip_late[None, :]
    stage = vmem((tokens // ROWS // 2 * ROWS * ROWS, LANES), f32)
    local_shapes = [far((tokens, width), f32), far((chunks, modes, ROWS, LANES), f32)]
    local_scratches = [half_buf, whole_buf, vmem((chunks, modes, ROWS, LANES), f32), stage, stage]
    local_scratches += [dma((1, chunks)), dma((1, chunks)), dma((chunks,))]
    early = chunks * 2 // 9
    gate, y, mid = call(
        functools.partial(gate_kernel, early=early),
        (query, halo_late, feat, u_late, head, rates, coef, skip_row),
        [far((tokens, width), bf16)] + local_shapes,
        [half_buf, vmem((members * ROWS, width), bf16), half_buf, vmem((chunks, 1, ROWS, CHUNK), f32), column]
        + [dma((1, chunks)), dma((1,)), dma((1, chunks))]
        + local_scratches,
        "gate",
        close=(2, 4, 5, 6, 7),
        cost_estimate=cost(28 * elements, 6 * elements),
    )

    def swap(value):
        return lax.all_to_all(value, axes, split_axis=0, concat_axis=0, tiled=True)

    share = modes * width // devices
    theirs = swap(left if even else left.reshape(devices, share))
    theirs, gate, coef, skip_row, y, mid = lax.optimization_barrier((theirs, gate, coef, skip_row, y, mid))
    if even:
        (entering,) = call(
            functools.partial(prefix_kernel, tokens=tokens, axes=axes),
            (theirs, rates, coef),
            [near(pieces, bf16)],
            [vmem((-(-pieces[1] // ROWS) * ROWS, LANES), f32)],
            "prefix",
            close=(0, 1, 2),
        )
    else:
        mine = lax.axis_index(axes)
        through = jnp.exp(-float(tokens) * lax.dynamic_slice_in_dim(rates.reshape(-1), mine * share, share))
        factor = lax.dynamic_slice_in_dim(coef.reshape(-1), mine * share, share)
        _, entering = lax.scan(
            lambda so_far, piece: (through * so_far + piece.astype(f32), (factor * so_far).astype(bf16)),
            jnp.zeros((share,), f32),
            theirs,
        )

    entering, u_late = lax.optimization_barrier((entering, u))
    entered = swap(entering).reshape(pieces)
    y, mid = call(
        functools.partial(local_kernel, first=early, last=chunks),
        (u_late, head, rates, coef, skip_row, y, mid),
        local_shapes,
        local_scratches,
        "within",
        close=(1, 2, 3, 4),
        cost_estimate=cost(50 * elements, 8 * elements),
        input_output_aliases={5: 0, 6: 1},
    )

    (out,) = call(
        final_kernel,
        (entered, rates, mid, y, gate),
        [far((tokens, width), bf16)],
        [vmem((chunks, modes, ROWS, LANES), f32), whole_buf, half_buf, half_buf]
        + [vmem((modes, tiles, LANES), f32), vmem((4, modes, CHUNK), f32), vmem((modes, ROWS, LANES), f32)]
        + [dma((2, chunks)), dma((chunks,)), dma((1, chunks))],
        "final",
        close=(0, 1),
        cost_estimate=cost(40 * elements, 10 * elements),
    )
    return out


def solution(mesh):
    axes = tuple(mesh.axis_names)
    placed = (P(axes, None),) * 3 + (P(),) * 4
    return jax.shard_map(
        functools.partial(local, axes=axes),
        mesh=mesh,
        in_specs=placed,
        out_specs=P(axes, None),
        check_vma=False,
    )
```

```python
import functools
import math

import jax
import jax.numpy as jnp
from jax import lax
from jax.experimental import pallas as pl
from jax.experimental.pallas import tpu as pltpu
from jax.sharding import PartitionSpec as P

LANES = 128
ROWS = 8
TILES = 4
CHUNK = TILES * LANES
AHEAD = 2
f32 = jnp.float32
bf16 = jnp.bfloat16


def put_tile(scratch, group, slot, tile):
    scratch[pl.ds((group * ROWS + slot) * ROWS, ROWS), :] = tile


def get_row(scratch, group, row):
    return scratch[pl.ds(group * ROWS * ROWS + row, ROWS, stride=ROWS), :]


def lanes_of(value, tile):
    return value[:, tile * LANES : (tile + 1) * LANES]


def tile_lanes(tile):
    return pl.ds(pl.multiple_of(tile * LANES, LANES), LANES)


def span(at):
    return pl.ds(pl.multiple_of(at * CHUNK, CHUNK), CHUNK)


def wide(row):
    return jnp.broadcast_to(row, (ROWS, LANES))


def sublane():
    return lax.broadcasted_iota(jnp.int32, (ROWS, LANES), 0)


def spread(row_of):
    slot = sublane() % TILES
    result = wide(row_of(TILES - 1))
    for tile in range(TILES - 1):
        result = jnp.where(slot == tile, wide(row_of(tile)), result)
    return result


def spread_rows(ref, at, rows):
    def one(row):
        return spread(lambda tile: ref[row : row + 1, tile_lanes(at * TILES + tile)])

    return [one(row) for row in rows]


def rounded(value):
    return value.astype(bf16).astype(f32)


def tiles_of(block):
    block = block.astype(f32)
    return [block[at : at + ROWS] for at in range(0, block.shape[0], ROWS)]


def fir(column, taps, first):
    total = taps[0] * column[pl.ds(first, ROWS), :]
    for lag in range(1, len(taps)):
        total = total + taps[lag] * column[pl.ds(first - lag, ROWS), :]
    return total


def lay_column(column, source, lanes):
    for pair in range(source.shape[0] // (2 * ROWS)):
        rows = slice(pair * 2 * ROWS, (pair + 1) * 2 * ROWS)
        column[pl.ds(ROWS + pair * 2 * ROWS, 2 * ROWS), :] = source[rows, lanes].astype(f32)


def chunk_taps(wide_ref, at, member, tile, count):
    return [wide(wide_ref[at, member, lag : lag + 1, tile_lanes(tile)]) for lag in range(count)]


def widened(feat_ref, member, out_ref, position):
    chunks, _, taps, count = feat_ref.shape
    rows = [feat_ref[at, member] for at in range(chunks)]
    rows = [jnp.concatenate([row, jnp.zeros((ROWS - taps, count), f32)], axis=0) for row in rows]
    group = lax.broadcasted_iota(jnp.int32, (count, CHUNK), 0)
    lane = lax.broadcasted_iota(jnp.int32, (count, CHUNK), 1)
    pick = (group == lane // (CHUNK // count)).astype(f32).astype(bf16)
    parts, rest = [], jnp.concatenate(rows, axis=0)
    for _ in range(3):
        term = rest.astype(bf16)
        rest = rest - term.astype(f32)
        parts.append(jnp.dot(term, pick, preferred_element_type=f32))
    out_ref[:, position] = (parts[0] + parts[1] + parts[2]).reshape(chunks, ROWS, CHUNK)


def power(base, exponent):
    result = None
    while exponent:
        if exponent & 1:
            result = base if result is None else result * base
        base = base * base
        exponent >>= 1
    return result


def tree(terms):
    while len(terms) > 1:
        terms = [sum(terms[at + 1 : at + 2], terms[at]) for at in range(0, len(terms), 2)]
    return terms[0]


def start_all(copies):
    for copy in copies:
        copy.start()


def wait_all(copies):
    for copy in copies:
        copy.wait()


def begin(chunks, fetch):
    for at in range(min(AHEAD, chunks)):
        start_all(fetch(at))


def over_chunks(chunks, fetch, body, send, last=True):
    def one(at, _):
        @pl.when(at + AHEAD < chunks)
        def _():
            start_all(fetch(at + AHEAD))

        wait_all(fetch(at))
        body(at)
        start_all(send(at))
        return 0

    lax.fori_loop(0, chunks, one, 0)
    if last:
        for at in range(chunks):
            wait_all(send(at))


def columns_in(pairs, sem):
    def fetch(at):
        return [
            pltpu.make_async_copy(ref.at[:, span(at)], buf.at[at], sem.at[member, at])
            for member, (ref, buf) in enumerate(pairs)
        ]

    return fetch


def columns_out(ref, buf, sem):
    return lambda at: [pltpu.make_async_copy(buf.at[at], ref.at[:, span(at)], sem.at[0, at])]


def pack_kernel(key_ref, value_ref, query_ref, out_ref, in_buf, in_sem):
    tokens = key_ref.shape[0]
    copies = [
        pltpu.make_async_copy(ref.at[pl.ds(tokens - 2 * ROWS, 2 * ROWS)], in_buf.at[at], in_sem.at[at])
        for at, ref in enumerate((key_ref, value_ref, query_ref))
    ]
    start_all(copies)
    wait_all(copies)
    tails = [in_buf[at].astype(f32)[ROWS:] for at in range(len(copies))]
    out_ref[...] = jnp.concatenate(tails, axis=0).astype(bf16)


def signal_kernel(key_ref, value_ref, feat_ref, rate_ref, u_ref, wide_ref, state_ref, *scratches):
    u_buf, power_scr, last_scr, *columns, out_sem = scratches
    tokens, tiles = u_ref.shape[0], state_ref.shape[1]
    modes = rate_ref.shape[0]
    chunks = tiles // TILES
    count = feat_ref.shape[2]
    for member in range(2):
        widened(feat_ref, member + 1, wide_ref, member)
    for column in columns:
        column[pl.ds(0, ROWS), :] = jnp.zeros((ROWS, LANES), f32)
    last_scr[...] = jnp.zeros(last_scr.shape, f32)

    def powers(at, _):
        through = jnp.exp(-rate_ref[:, span(at)])
        for level in range(4):
            power_scr[level, :, span(at)] = through
            through = through * through
        return 0

    lax.fori_loop(0, chunks, powers, 0)

    def reduce(number):
        lanes = tile_lanes(number)
        for mode in range(modes):
            whole = last_scr[mode]
            for level in (2, 1, 0):
                factor = wide(power_scr[level, mode : mode + 1, lanes])
                whole = factor * whole + pltpu.roll(whole, ROWS - (1 << level), 0)
            state_ref[mode, pl.ds(number, 1), :] = whole[:1]

    def tile(number, _):
        lanes = tile_lanes(number)
        reduce(jnp.maximum(number - 1, 0))
        taps = [chunk_taps(wide_ref, number // TILES, member, number % TILES, count) for member in range(2)]
        for column, ref in zip(columns, (key_ref, value_ref)):
            lay_column(column, ref, lanes)
        decay = [wide(power_scr[3, mode : mode + 1, lanes]) for mode in range(modes)]
        state = None
        for pair in range(tokens // (2 * ROWS)):
            found = []
            for first in (pair * 2 * ROWS + ROWS, pair * 2 * ROWS + 2 * ROWS):
                u = fir(columns[0], taps[0], first) * fir(columns[1], taps[1], first)
                found.append(jnp.where(sublane() < count - 1, 0.0, u) if first == ROWS else u)
            both = jnp.concatenate(found, axis=0).astype(bf16)
            u_buf[pair * 2 * ROWS : (pair + 1) * 2 * ROWS, lanes] = both
            for u in tiles_of(both):
                if state is None:
                    state = [u] * modes
                else:
                    state = [factor * one + u for factor, one in zip(decay, state)]
        for mode in range(modes):
            last_scr[mode] = state[mode]
        return 0

    def send(at):
        return pltpu.make_async_copy(u_buf.at[:, span(at)], u_ref.at[:, span(at)], out_sem.at[at])

    def chunk(at, _):
        lax.fori_loop(at * TILES, (at + 1) * TILES, tile, 0)
        send(at).start()
        return 0

    lax.fori_loop(0, chunks, chunk, 0)
    reduce(tiles - 1)
    for at in range(chunks):
        send(at).wait()


def head_kernel(key_ref, value_ref, halo_ref, rate_ref, wide_ref, state_ref, out_ref, head_ref, *scratches, tokens, reach):
    rate_scr, column_scr, token_scr, total_scr = scratches
    modes, tiles = state_ref.shape[:2]
    for group in range(modes // ROWS):
        for tile in range(tiles):
            rows = pl.ds((group * tiles + tile) * ROWS, ROWS)
            rate_scr[rows, :] = rate_ref[group * ROWS : (group + 1) * ROWS, tile * LANES : (tile + 1) * LANES]

    def some(chunk, _):
        for number in range(TILES):
            lanes = tile_lanes(chunk * TILES + number)
            halo = halo_ref[:, lanes].astype(f32)
            parts = []
            for member in range(2):
                taps = chunk_taps(wide_ref, chunk, member, number, reach + 1)
                column = column_scr.at[number, member]
                column[pl.ds(0, ROWS), :] = halo[member * ROWS : (member + 1) * ROWS]
                source = (key_ref, value_ref)[member]
                column[pl.ds(ROWS, ROWS), :] = source[: 2 * ROWS, lanes].astype(f32)[:ROWS]
                parts.append(fir(column, taps, ROWS))
            u = jnp.where(sublane() < reach, rounded(parts[0] * parts[1]), 0.0)
            token_scr[pl.ds(pl.multiple_of((chunk * TILES + number) * ROWS, ROWS), ROWS), :] = u
            head_ref[:, lanes] = jnp.concatenate([u, jnp.zeros((ROWS, LANES), f32)], axis=0).astype(bf16)
        return 0

    lax.fori_loop(0, tiles // TILES, some, 0)
    signals = [token_scr[pl.ds(row, tiles, stride=ROWS), :] for row in range(reach)]
    for mode in range(modes):
        start = mode // ROWS * tiles * ROWS + mode % ROWS
        decay = jnp.exp(-rate_scr[pl.ds(start, tiles, stride=ROWS), :])
        head = signals[0]
        for row in range(1, reach):
            head = decay * head + signals[row]
        total_scr[mode * tiles : (mode + 1) * tiles, :] = state_ref[mode] + power(decay, tokens - reach) * head
    out_ref[...] = total_scr[...].astype(bf16)


def gate_kernel(query_ref, halo_ref, feat_ref, u_ref, head_ref, rate_ref, coef_ref, skip_ref, gate_ref, *rest, early):
    y_ref, mid_ref, query_buf, halo_buf, gate_buf, wide_scr, column, in_sem, small_sem, out_sem = rest[:10]
    inner = rest[10:]
    chunks, tokens = gate_buf.shape[:2]
    count = feat_ref.shape[2]
    fetch = columns_in(((query_ref, query_buf),), in_sem)
    halo_copy = pltpu.make_async_copy(halo_ref, halo_buf, small_sem.at[0])
    halo_copy.start()
    begin(chunks, fetch)
    local_fetch, local_chunk, local_send = local_parts(
        u_ref, head_ref, rate_ref, coef_ref, skip_ref, y_ref, mid_ref, *inner, first=0
    )
    begin(early, local_fetch)
    widened(feat_ref, 0, wide_scr, 0)
    halo_copy.wait()

    def chunk(at):
        def tile(number, _):
            lanes = tile_lanes(number)
            taps = chunk_taps(wide_scr, at, 0, number, count)
            halo = halo_buf[:, tile_lanes(at * TILES + number)].astype(f32)
            column[pl.ds(0, ROWS), :] = halo[2 * ROWS :]
            lay_column(column, query_buf.at[at], lanes)
            for pair in range(tokens // (2 * ROWS)):
                first = pair * 2 * ROWS + ROWS
                found = [fir(column, taps, first), fir(column, taps, first + ROWS)]
                rows = slice(pair * 2 * ROWS, (pair + 1) * 2 * ROWS)
                gate_buf[at, rows, lanes] = jnp.concatenate(found, axis=0).astype(bf16)
            return 0

        lax.fori_loop(0, TILES, tile, 0)

    give = columns_out(gate_ref, gate_buf, out_sem)
    over_chunks(chunks, fetch, chunk, give, last=False)
    over_chunks(early, local_fetch, local_chunk, local_send)
    for at in range(chunks):
        wait_all(give(at))


def carry_kernel(state_ref, rate_ref, coef_ref, out_ref, state_buf, rate_scr, through_scr, total_scr, sem, *, tokens, axes):
    devices, rows = state_buf.shape[:2]
    modes = rate_ref.shape[0]
    tiles = rows // modes
    mine = lax.axis_index(axes)

    def fetch(source):
        return pltpu.make_async_copy(state_ref.at[source], state_buf.at[source], sem.at[source])

    def begin_one(source, _):
        fetch(source).start()
        return 0

    lax.fori_loop(0, mine, begin_one, 0)

    def by_row(ref):
        for group in range(modes // ROWS):
            for tile in range(tiles):
                place = pl.ds((group * tiles + tile) * ROWS, ROWS)
                rate_scr[place, :] = ref[group * ROWS : (group + 1) * ROWS, tile * LANES : (tile + 1) * LANES]
        return [
            rate_scr[pl.ds(mode // ROWS * tiles * ROWS + mode % ROWS, tiles, stride=ROWS), :] for mode in range(modes)
        ]

    for mode, rate in enumerate(by_row(rate_ref)):
        through_scr[mode * tiles : (mode + 1) * tiles, :] = jnp.exp(-float(tokens) * rate)
    total_scr[...] = jnp.zeros(total_scr.shape, f32)

    def lap(source, _):
        fetch(source).wait()
        for first in range(0, rows, 2 * ROWS):
            part = slice(first, first + 2 * ROWS)
            total_scr[part, :] = through_scr[part, :] * total_scr[part, :] + state_buf[source, part, :].astype(f32)
        return 0

    lax.fori_loop(0, mine, lap, 0)
    for mode, coef in enumerate(by_row(coef_ref)):
        part = slice(mode * tiles, (mode + 1) * tiles)
        out_ref[part, :] = coef * total_scr[part, :]


def local_parts(u_ref, head_ref, rate_ref, coef_ref, skip_ref, y_ref, mid_ref, *scratches, first):
    u_buf, y_buf, mid_buf, token_scr, sum_scr, in_sem, out_sem, mid_sem = scratches
    tokens = u_buf.shape[1]
    modes = rate_ref.shape[0]
    half_groups = tokens // ROWS // 2
    take = columns_in(((u_ref, u_buf),), in_sem)
    give = columns_out(y_ref, y_buf, out_sem)

    def fetch(number):
        return take(number + first)

    def send(number):
        at = number + first
        return give(at) + [pltpu.make_async_copy(mid_buf.at[at], mid_ref.at[at], mid_sem.at[at])]

    def chunk(number):
        at = number + first
        front = u_buf[at, : 2 * ROWS].astype(f32) + head_ref[:, span(at)].astype(f32)
        u_buf[at, : 2 * ROWS] = front.astype(bf16)
        for pair in range(half_groups):
            block = u_buf[at, pair * 2 * ROWS : (pair + 1) * 2 * ROWS, :].astype(f32)
            for part in range(2):
                group = pair * 2 + part
                half, within = group // half_groups, group % half_groups
                for tile in range(TILES):
                    piece = lanes_of(block, tile)[part * ROWS : (part + 1) * ROWS]
                    put_tile(token_scr, within, half * TILES + tile, piece)
        (skip,) = spread_rows(skip_ref, at, range(1))
        coef = spread_rows(coef_ref, at, range(modes))
        decay = [jnp.exp(-rate) for rate in spread_rows(rate_ref, at, range(modes))]

        def eight(group, state):
            state = list(state)
            for row in range(ROWS):
                u = get_row(token_scr, group, row)
                state = [factor * one + u for factor, one in zip(decay, state)]
                terms = [factor * one for factor, one in zip([skip] + coef, [u] + state)]
                sum_scr[pl.ds(group * ROWS * ROWS + row, ROWS, stride=ROWS), :] = tree(terms)
            return tuple(state)

        state = lax.fori_loop(0, half_groups, eight, (jnp.zeros((ROWS, LANES), f32),) * modes)
        for mode, (factor, one) in enumerate(zip(coef, state)):
            mid_buf[at, mode] = factor * one
        for group in range(2 * half_groups):
            half, within = group // half_groups, group % half_groups
            for tile in range(TILES):
                slot = (within * ROWS + half * TILES + tile) * ROWS
                rows = slice(group * ROWS, (group + 1) * ROWS)
                y_buf[at, rows, tile * LANES : (tile + 1) * LANES] = sum_scr[pl.ds(slot, ROWS), :]

    return fetch, chunk, send


def final_kernel(piece_ref, rate_ref, mid_ref, y_ref, gate_ref, out_ref, *scratches):
    mid_buf, y_buf, gate_buf, out_buf, power_scr, lead_scr, in_sem, mid_sem, out_sem = scratches
    chunks, modes = mid_buf.shape[:2]
    tokens = y_buf.shape[1]
    columns = columns_in(((y_ref, y_buf), (gate_ref, gate_buf)), in_sem)

    def fetch(at):
        return columns(at) + [pltpu.make_async_copy(mid_ref.at[at], mid_buf.at[at], mid_sem.at[at])]

    begin(chunks, fetch)
    tiles = piece_ref.shape[0] // modes
    bits = [(sublane() >> level) % 2 == 1 for level in range(3)]

    def chunk(at):
        through = jnp.exp(-rate_ref[:, span(at)])
        for level in range(4):
            power_scr[level] = through
            through = through * through

        def tile(number, _):
            lanes = tile_lanes(number)
            state = []
            for mode in range(modes):
                rows = [wide(power_scr[level, mode : mode + 1, lanes]) for level in range(3)]
                lead = rows[0]
                for bit, row in zip(bits, rows):
                    lead = lead * jnp.where(bit, row, 1.0)
                lead_scr[mode] = lead
                state.append(lead * wide(piece_ref[pl.ds(mode * tiles + at * TILES + number, 1), :]))
            decay = [wide(power_scr[3, mode : mode + 1, lanes]) for mode in range(modes)]
            for pair in range(tokens // (2 * ROWS)):
                rows = slice(pair * 2 * ROWS, (pair + 1) * 2 * ROWS)
                gates = gate_buf[at, rows, lanes].astype(f32)
                sums = []
                for part in range(2):
                    if pair == tokens // (4 * ROWS) and part == 0:
                        state = [
                            one + lead_scr[mode] * wide(mid_buf[at, mode, pl.ds(number, 1), :])
                            for mode, one in enumerate(state)
                        ]
                    here = slice((pair * 2 + part) * ROWS, (pair * 2 + part + 1) * ROWS)
                    sums.append(y_buf[at, here, lanes] + tree(state))
                    state = [factor * one for factor, one in zip(decay, state)]
                out_buf[at, rows, lanes] = (gates * rounded(jnp.concatenate(sums, axis=0))).astype(bf16)
            return 0

        lax.fori_loop(0, TILES, tile, 0)

    over_chunks(chunks, fetch, chunk, columns_out(out_ref, out_buf, out_sem))


def cost(flops, moved):
    return pl.CostEstimate(flops=int(flops), bytes_accessed=int(moved), transcendentals=0)


def local(query, key_proj, value_proj, featurizer, rates, residues, skip, *, axes):
    tokens, width = query.shape
    modes = rates.shape[0]
    members, taps, groups = featurizer.shape
    devices = math.prod(lax.axis_size(axis) for axis in axes)
    chunks = width // CHUNK
    tiles = width // LANES
    vmem = pltpu.VMEM
    far = pltpu.HBM
    near = jax.ShapeDtypeStruct
    dma = pltpu.SemaphoreType.DMA
    elements = tokens * width

    def call(kernel, inputs, outputs, scratches, name, close=(), **more):
        inputs = [
            value if at in close else pltpu.with_memory_space_constraint(value, far)
            for at, value in enumerate(inputs)
        ]
        beside, there = pl.BlockSpec(memory_space=vmem), pl.BlockSpec(memory_space=far)
        return pl.pallas_call(
            kernel,
            in_specs=[beside if at in close else there for at in range(len(inputs))],
            out_specs=[beside if isinstance(one, near) else there for one in outputs],
            out_shape=outputs,
            scratch_shapes=scratches,
            compiler_params=pltpu.CompilerParams(vmem_limit_bytes=32 * 2**20),
            name=name,
            **more,
        )(*inputs)

    (packed,) = call(
        pack_kernel,
        (key_proj, value_proj, query),
        [near((members * ROWS, width), bf16)],
        [vmem((members, 2 * ROWS, width), bf16), dma((members,))],
        "pack",
    )
    halo = lax.ppermute(packed, axes, [(at, at + 1) for at in range(devices - 1)])

    feat = featurizer.reshape(members, taps, chunks, groups // chunks).transpose(2, 0, 1, 3)
    column = vmem((ROWS + tokens, LANES), f32)
    half_buf, whole_buf = vmem((chunks, tokens, CHUNK), bf16), vmem((chunks, tokens, CHUNK), f32)
    u, wide_taps, state = call(
        signal_kernel,
        (key_proj, value_proj, feat, rates),
        [far((tokens, width), bf16), near((chunks, 2, ROWS, CHUNK), f32), near((modes, tiles, LANES), f32)],
        [vmem((tokens, width), bf16), vmem((4, modes, width), f32), vmem((modes, ROWS, LANES), f32)]
        + [column, column, dma((chunks,))],
        "signal",
        close=range(4),
        cost_estimate=cost(60 * elements, 10 * elements),
    )

    flat = (modes * tiles, LANES)
    left, head = call(
        functools.partial(head_kernel, tokens=tokens, reach=taps - 1),
        (key_proj, value_proj, halo, rates, wide_taps, state),
        [near(flat, bf16), near((2 * ROWS, width), bf16)],
        [vmem((modes * tiles, LANES), f32), vmem((TILES, 2, 2 * ROWS, LANES), f32)]
        + [vmem((tiles * ROWS, LANES), f32), vmem(flat, f32)],
        "head",
        close=range(6),
    )
    left, halo_late, rates_late, skip_late = lax.optimization_barrier((left, halo, rates, skip))
    coef = residues * jnp.sqrt(-jnp.expm1(-2.0 * rates_late) / modes)
    skip_row = skip_late[None, :]
    stage = vmem((tokens // ROWS // 2 * ROWS * ROWS, LANES), f32)
    local_shapes = [far((tokens, width), f32), far((chunks, modes, ROWS, LANES), f32)]
    local_scratches = [half_buf, whole_buf, vmem((chunks, modes, ROWS, LANES), f32), stage, stage]
    local_scratches += [dma((1, chunks)), dma((1, chunks)), dma((chunks,))]
    gate, y, mid = call(
        functools.partial(gate_kernel, early=chunks),
        (query, halo_late, feat, u, head, rates, coef, skip_row),
        [far((tokens, width), bf16)] + local_shapes,
        [half_buf, vmem((members * ROWS, width), bf16), half_buf, vmem((chunks, 1, ROWS, CHUNK), f32), column]
        + [dma((1, chunks)), dma((1,)), dma((1, chunks))]
        + local_scratches,
        "gate",
        close=(2, 4, 5, 6, 7),
        cost_estimate=cost(28 * elements, 6 * elements),
    )

    if devices * flat[0] * LANES * 2 <= 8 * 2**20:
        gathered = lax.all_gather(left, axes)
        gathered, gate, y, mid = lax.optimization_barrier((gathered, gate, y, mid))
        (entered,) = call(
            functools.partial(carry_kernel, tokens=tokens, axes=axes),
            (gathered, rates, coef),
            [near(flat, f32)],
            [vmem((devices, *flat), bf16)] + [vmem(flat, f32)] * 3 + [dma((devices,))],
            "carry",
            close=(1, 2),
        )
    else:
        share = modes * width // devices
        first = lax.axis_index(axes) * share

        def swap(value):
            return lax.all_to_all(value, axes, split_axis=0, concat_axis=0, tiled=True)

        theirs = swap(left.reshape(devices, share))
        through = jnp.exp(-float(tokens) * lax.dynamic_slice_in_dim(rates.reshape(-1), first, share))
        factor = lax.dynamic_slice_in_dim(coef.reshape(-1), first, share)
        _, entering = lax.scan(
            lambda so_far, piece: (through * so_far + piece.astype(f32), (factor * so_far).astype(bf16)),
            jnp.zeros((share,), f32),
            theirs,
        )
        entered = swap(entering).reshape(flat).astype(f32)

    (out,) = call(
        final_kernel,
        (entered, rates, mid, y, gate),
        [far((tokens, width), bf16)],
        [vmem((chunks, modes, ROWS, LANES), f32), whole_buf, half_buf, half_buf]
        + [vmem((4, modes, CHUNK), f32), vmem((modes, ROWS, LANES), f32)]
        + [dma((2, chunks)), dma((chunks,)), dma((1, chunks))],
        "final",
        close=(0, 1),
        cost_estimate=cost(40 * elements, 10 * elements),
    )
    return out


def solution(mesh):
    axes = tuple(mesh.axis_names)
    placed = (P(axes, None),) * 3 + (P(),) * 4
    return jax.shard_map(
        functools.partial(local, axes=axes),
        mesh=mesh,
        in_specs=placed,
        out_specs=P(axes, None),
        check_vma=False,
    )
```

```python
import functools
import math

import jax
import jax.numpy as jnp
from jax import lax
from jax.experimental import pallas as pl
from jax.experimental.pallas import tpu as pltpu
from jax.sharding import PartitionSpec as P

LANES = 128
ROWS = 8
TILES = 4
CHUNK = TILES * LANES
AHEAD = 2
f32 = jnp.float32
bf16 = jnp.bfloat16


def put_tile(scratch, group, slot, tile):
    scratch[pl.ds((group * ROWS + slot) * ROWS, ROWS), :] = tile


def get_row(scratch, group, row):
    return scratch[pl.ds(group * ROWS * ROWS + row, ROWS, stride=ROWS), :]


def lanes_of(value, tile):
    return value[:, tile * LANES : (tile + 1) * LANES]


def tile_lanes(tile):
    return pl.ds(pl.multiple_of(tile * LANES, LANES), LANES)


def span(at):
    return pl.ds(pl.multiple_of(at * CHUNK, CHUNK), CHUNK)


def wide(row):
    return jnp.broadcast_to(row, (ROWS, LANES))


def sublane():
    return lax.broadcasted_iota(jnp.int32, (ROWS, LANES), 0)


def spread(row_of):
    slot = sublane() % TILES
    result = wide(row_of(TILES - 1))
    for tile in range(TILES - 1):
        result = jnp.where(slot == tile, wide(row_of(tile)), result)
    return result


def spread_rows(ref, at, rows):
    def one(row):
        return spread(lambda tile: ref[row : row + 1, tile_lanes(at * TILES + tile)])

    return [one(row) for row in rows]


def rounded(value):
    return value.astype(bf16).astype(f32)


def tiles_of(block):
    block = block.astype(f32)
    return [block[at : at + ROWS] for at in range(0, block.shape[0], ROWS)]


def fir(column, taps, first, count):
    half = ROWS // 2
    top = sublane() < half

    def seen(start, lags):
        return [column[pl.ds(start - lag, ROWS), :] for lag in range(lags)]

    def far_part(rows):
        total = taps[half] * rows[0]
        for lag in range(half + 1, len(taps)):
            total = total + taps[lag] * rows[lag - half]
        return pltpu.roll(total, half, 0)

    before = far_part(seen(first - ROWS, len(taps) - half))
    for start in range(first, first + count * ROWS, ROWS):
        rows = seen(start, half)
        now = far_part(rows)
        total = taps[0] * rows[0]
        for lag in range(1, half):
            total = total + taps[lag] * rows[lag]
        yield total + jnp.where(top, before, now)
        before = now


def lay_column(column, source, lanes):
    for pair in range(source.shape[0] // (2 * ROWS)):
        rows = slice(pair * 2 * ROWS, (pair + 1) * 2 * ROWS)
        column[pl.ds((pair + 1) * 2 * ROWS, 2 * ROWS), :] = source[rows, lanes].astype(f32)


def chunk_taps(wide_ref, at, member, tile, count):
    return [wide(wide_ref[at, member, lag : lag + 1, tile_lanes(tile)]) for lag in range(count)]


def widened(feat_ref, member, out_ref, position):
    chunks, _, taps, count = feat_ref.shape
    rows = [feat_ref[at, member] for at in range(chunks)]
    rows = [jnp.concatenate([row, jnp.zeros((ROWS - taps, count), f32)], axis=0) for row in rows]
    group = lax.broadcasted_iota(jnp.int32, (count, CHUNK), 0)
    lane = lax.broadcasted_iota(jnp.int32, (count, CHUNK), 1)
    pick = (group == lane // (CHUNK // count)).astype(f32).astype(bf16)
    parts, rest = [], jnp.concatenate(rows, axis=0)
    for _ in range(3):
        term = rest.astype(bf16)
        rest = rest - term.astype(f32)
        parts.append(jnp.dot(term, pick, preferred_element_type=f32))
    out_ref[:, position] = (parts[0] + parts[1] + parts[2]).reshape(chunks, ROWS, CHUNK)


def power(base, exponent):
    result = None
    while exponent:
        if exponent & 1:
            result = base if result is None else result * base
        base = base * base
        exponent >>= 1
    return result


def tree(terms):
    while len(terms) > 1:
        terms = [sum(terms[at + 1 : at + 2], terms[at]) for at in range(0, len(terms), 2)]
    return terms[0]


def start_all(copies):
    for copy in copies:
        copy.start()


def wait_all(copies):
    for copy in copies:
        copy.wait()


def begin(chunks, fetch):
    for at in range(min(AHEAD, chunks)):
        start_all(fetch(at))


def over_chunks(first, last, body, send):
    def one(at, _):
        body(at)
        start_all(send(at))
        return 0

    lax.fori_loop(first, last, one, 0)


def with_fetch(chunks, fetch, body):
    def one(at):
        @pl.when(at + AHEAD < chunks)
        def _():
            start_all(fetch(at + AHEAD))

        wait_all(fetch(at))
        body(at)

    return one


def columns_in(pairs, sem):
    def fetch(at):
        return [
            pltpu.make_async_copy(ref.at[:, span(at)], buf.at[at], sem.at[member, at])
            for member, (ref, buf) in enumerate(pairs)
        ]

    return fetch


def columns_out(ref, buf, sem):
    return lambda at: [pltpu.make_async_copy(buf.at[at], ref.at[:, span(at)], sem.at[0, at])]


def pack_kernel(key_ref, value_ref, query_ref, out_ref, in_buf, in_sem):
    tokens = key_ref.shape[0]
    copies = [
        pltpu.make_async_copy(ref.at[pl.ds(tokens - 2 * ROWS, 2 * ROWS)], in_buf.at[at], in_sem.at[at])
        for at, ref in enumerate((key_ref, value_ref, query_ref))
    ]
    start_all(copies)
    wait_all(copies)
    tails = [in_buf[at].astype(f32)[ROWS:] for at in range(len(copies))]
    out_ref[...] = jnp.concatenate(tails, axis=0).astype(bf16)


def signal_kernel(key_ref, value_ref, feat_ref, rate_ref, u_ref, wide_ref, state_ref, power_scr, last_scr, *columns):
    tokens, tiles = u_ref.shape[0], state_ref.shape[1]
    modes = rate_ref.shape[0]
    chunks = tiles // TILES
    count = feat_ref.shape[2]
    for member in range(2):
        widened(feat_ref, member + 1, wide_ref, member)
    for column in columns:
        column[pl.ds(0, 2 * ROWS), :] = jnp.zeros((2 * ROWS, LANES), f32)
    last_scr[...] = jnp.zeros(last_scr.shape, f32)

    def powers(at, _):
        through = jnp.exp(-rate_ref[:, span(at)])
        for level in range(4):
            power_scr[level, :, span(at)] = through
            through = through * through
        return 0

    lax.fori_loop(0, chunks, powers, 0)

    def reduce(number):
        lanes = tile_lanes(number)
        for mode in range(modes):
            whole = last_scr[mode]
            for level in (2, 1, 0):
                factor = wide(power_scr[level, mode : mode + 1, lanes])
                whole = factor * whole + pltpu.roll(whole, ROWS - (1 << level), 0)
            state_ref[mode, pl.ds(number, 1), :] = whole[:1]

    def tile(number, _):
        lanes = tile_lanes(number)
        reduce(jnp.maximum(number - 1, 0))
        taps = [chunk_taps(wide_ref, number // TILES, member, number % TILES, count) for member in range(2)]
        for column, ref in zip(columns, (key_ref, value_ref)):
            lay_column(column, ref, lanes)
        decay = [wide(power_scr[3, mode : mode + 1, lanes]) for mode in range(modes)]
        state = None
        parts = [fir(column, some, 2 * ROWS, tokens // ROWS) for column, some in zip(columns, taps)]
        for pair in range(tokens // (2 * ROWS)):
            found = [next(parts[0]) * next(parts[1]) for _ in range(2)]
            if pair == 0:
                found[0] = jnp.where(sublane() < count - 1, 0.0, found[0])
            both = jnp.concatenate(found, axis=0).astype(bf16)
            u_ref[pair * 2 * ROWS : (pair + 1) * 2 * ROWS, lanes] = both
            for u in tiles_of(both):
                if state is None:
                    state = [u] * modes
                else:
                    state = [factor * one + u for factor, one in zip(decay, state)]
        for mode in range(modes):
            last_scr[mode] = state[mode]
        return 0

    lax.fori_loop(0, tiles, tile, 0)
    reduce(tiles - 1)


def head_kernel(key_ref, value_ref, halo_ref, rate_ref, wide_ref, state_ref, out_ref, head_ref, *scratches, tokens, reach):
    rate_scr, column_scr, token_scr, total_scr = scratches
    modes, tiles = state_ref.shape[:2]
    pieces, piece_rows = out_ref.shape[:2]
    for group in range(modes // ROWS):
        for tile in range(tiles):
            rows = pl.ds((group * tiles + tile) * ROWS, ROWS)
            rate_scr[rows, :] = rate_ref[group * ROWS : (group + 1) * ROWS, tile * LANES : (tile + 1) * LANES]

    def some(chunk, _):
        for number in range(TILES):
            lanes = tile_lanes(chunk * TILES + number)
            halo = halo_ref[:, lanes].astype(f32)
            parts = []
            for member in range(2):
                taps = chunk_taps(wide_ref, chunk, member, number, reach + 1)
                column = column_scr.at[number, member]
                column[pl.ds(0, ROWS), :] = jnp.zeros((ROWS, LANES), f32)
                column[pl.ds(ROWS, ROWS), :] = halo[member * ROWS : (member + 1) * ROWS]
                source = (key_ref, value_ref)[member]
                column[pl.ds(2 * ROWS, ROWS), :] = source[: 2 * ROWS, lanes].astype(f32)[:ROWS]
                parts += fir(column, taps, 2 * ROWS, 1)
            u = jnp.where(sublane() < reach, rounded(parts[0] * parts[1]), 0.0)
            token_scr[pl.ds(pl.multiple_of((chunk * TILES + number) * ROWS, ROWS), ROWS), :] = u
            head_ref[:, lanes] = jnp.concatenate([u, jnp.zeros((ROWS, LANES), f32)], axis=0).astype(bf16)
        return 0

    lax.fori_loop(0, tiles // TILES, some, 0)
    signals = [token_scr[pl.ds(row, tiles, stride=ROWS), :] for row in range(reach)]
    split = pieces // modes
    for mode in range(modes):
        start = mode // ROWS * tiles * ROWS + mode % ROWS
        decay = jnp.exp(-rate_scr[pl.ds(start, tiles, stride=ROWS), :])
        head = signals[0]
        for row in range(1, reach):
            head = decay * head + signals[row]
        total_scr[mode] = state_ref[mode] + power(decay, tokens - reach) * head
        for part in range(split):
            rows = total_scr[mode, part * piece_rows : (part + 1) * piece_rows, :]
            out_ref[mode * split + part] = rows.astype(out_ref.dtype)


def gate_kernel(query_ref, halo_ref, feat_ref, u_ref, head_ref, rate_ref, coef_ref, skip_ref, gate_ref, *rest, early):
    y_ref, mid_ref, halo_buf, gate_buf, wide_scr, column, small_sem, out_sem = rest[:8]
    inner = rest[8:]
    chunks, tokens = gate_buf.shape[:2]
    count = feat_ref.shape[2]
    halo_copy = pltpu.make_async_copy(halo_ref, halo_buf, small_sem.at[0])
    halo_copy.start()
    widened(feat_ref, 0, wide_scr, 0)
    local_chunk, local_send = local_parts(u_ref, head_ref, rate_ref, coef_ref, skip_ref, y_ref, mid_ref, *inner)
    over_chunks(0, early, local_chunk, local_send)
    halo_copy.wait()
    column[pl.ds(0, ROWS), :] = jnp.zeros((ROWS, LANES), f32)

    def chunk(at):
        def tile(number, _):
            lanes = tile_lanes(number)
            all_lanes = tile_lanes(at * TILES + number)
            taps = chunk_taps(wide_scr, at, 0, number, count)
            column[pl.ds(ROWS, ROWS), :] = halo_buf[:, all_lanes].astype(f32)[2 * ROWS :]
            lay_column(column, query_ref, all_lanes)
            found = list(fir(column, taps, 2 * ROWS, tokens // ROWS))
            for pair in range(tokens // (2 * ROWS)):
                rows = slice(pair * 2 * ROWS, (pair + 1) * 2 * ROWS)
                gate_buf[at, rows, lanes] = jnp.concatenate(found[pair * 2 : pair * 2 + 2], axis=0).astype(bf16)
            return 0

        lax.fori_loop(0, TILES, tile, 0)

    give = columns_out(gate_ref, gate_buf, out_sem)
    over_chunks(0, chunks, chunk, give)
    for at in range(early):
        wait_all(local_send(at))
    for at in range(chunks):
        wait_all(give(at))


def prefix_kernel(piece_ref, rate_ref, coef_ref, out_ref, table_scr, *, tokens, axes):
    devices, piece_rows = piece_ref.shape[:2]
    split = devices // rate_ref.shape[0]
    mine = lax.axis_index(axes)
    mode, part = mine // split, mine % split
    group = pl.multiple_of(mode // ROWS * ROWS, ROWS)
    first = pl.multiple_of(part * piece_rows * LANES, LANES)

    def mine_of(ref):
        rows = ref[pl.ds(group, ROWS), pl.ds(first, piece_rows * LANES)]
        here = lax.broadcasted_iota(jnp.int32, rows.shape, 0) == mode - group
        row = jnp.sum(jnp.where(here, rows, 0.0), axis=0, keepdims=True)
        for number in range(piece_rows):
            table_scr[number : number + 1, :] = lanes_of(row, number)
        return table_scr[:piece_rows, :]

    coef = mine_of(coef_ref)
    through = jnp.exp(-float(tokens) * mine_of(rate_ref))

    def lap(number, entering):
        for step in range(4):
            source = number * 4 + step
            out_ref[source] = (coef * entering).astype(out_ref.dtype)
            entering = through * entering + piece_ref[source].astype(f32)
        return entering

    lax.fori_loop(0, devices // 4, lap, jnp.zeros((piece_rows, LANES), f32))


def local_kernel(u_ref, head_ref, rate_ref, coef_ref, skip_ref, *rest, first, last):
    chunk, send = local_parts(u_ref, head_ref, rate_ref, coef_ref, skip_ref, *rest[-8:])
    over_chunks(first, last, chunk, send)
    for at in range(first, last):
        wait_all(send(at))


def local_parts(u_ref, head_ref, rate_ref, coef_ref, skip_ref, y_ref, mid_ref, *scratches):
    y_buf, mid_buf, token_scr, sum_scr, out_sem, mid_sem = scratches
    tokens = u_ref.shape[0]
    modes = rate_ref.shape[0]
    half_groups = tokens // ROWS // 2
    give = columns_out(y_ref, y_buf, out_sem)

    def send(at):
        return give(at) + [pltpu.make_async_copy(mid_buf.at[at], mid_ref.at[at], mid_sem.at[at])]

    def chunk(at):
        for pair in range(half_groups):
            block = u_ref[pair * 2 * ROWS : (pair + 1) * 2 * ROWS, span(at)].astype(f32)
            if pair == 0:
                block = block + head_ref[:, span(at)].astype(f32)
            for part in range(2):
                group = pair * 2 + part
                half, within = group // half_groups, group % half_groups
                for tile in range(TILES):
                    piece = lanes_of(block, tile)[part * ROWS : (part + 1) * ROWS]
                    put_tile(token_scr, within, half * TILES + tile, piece)
        (skip,) = spread_rows(skip_ref, at, range(1))
        coef = spread_rows(coef_ref, at, range(modes))
        decay = [jnp.exp(-rate) for rate in spread_rows(rate_ref, at, range(modes))]

        def eight(group, state):
            state = list(state)
            for row in range(ROWS):
                u = get_row(token_scr, group, row)
                state = [factor * one + u for factor, one in zip(decay, state)]
                terms = [factor * one for factor, one in zip([skip] + coef, [u] + state)]
                sum_scr[pl.ds(group * ROWS * ROWS + row, ROWS, stride=ROWS), :] = tree(terms)
            return tuple(state)

        state = lax.fori_loop(0, half_groups, eight, (jnp.zeros((ROWS, LANES), f32),) * modes)
        for mode, (factor, one) in enumerate(zip(coef, state)):
            mid_buf[at, mode] = factor * one
        for group in range(2 * half_groups):
            half, within = group // half_groups, group % half_groups
            for tile in range(TILES):
                slot = (within * ROWS + half * TILES + tile) * ROWS
                rows = slice(group * ROWS, (group + 1) * ROWS)
                y_buf[at, rows, tile * LANES : (tile + 1) * LANES] = sum_scr[pl.ds(slot, ROWS), :]

    return chunk, send


def final_kernel(piece_ref, rate_ref, mid_ref, y_ref, gate_ref, out_ref, *scratches):
    mid_buf, y_buf, gate_buf, out_buf, total_scr, power_scr, lead_scr, in_sem, mid_sem, out_sem = scratches
    chunks, modes = mid_buf.shape[:2]
    tokens = y_buf.shape[1]
    columns = columns_in(((y_ref, y_buf), (gate_ref, gate_buf)), in_sem)

    def fetch(at):
        return columns(at) + [pltpu.make_async_copy(mid_ref.at[at], mid_buf.at[at], mid_sem.at[at])]

    begin(chunks, fetch)
    pieces, piece_rows = piece_ref.shape[:2]
    split = pieces // modes
    for mode in range(modes):
        for part in range(split):
            rows = piece_ref[mode * split + part].astype(f32)
            total_scr[mode, part * piece_rows : (part + 1) * piece_rows, :] = rows
    bits = [(sublane() >> level) % 2 == 1 for level in range(3)]

    def chunk(at):
        through = jnp.exp(-rate_ref[:, span(at)])
        for level in range(4):
            power_scr[level] = through
            through = through * through

        def tile(number, _):
            lanes = tile_lanes(number)
            state = []
            for mode in range(modes):
                rows = [wide(power_scr[level, mode : mode + 1, lanes]) for level in range(3)]
                lead = rows[0]
                for bit, row in zip(bits, rows):
                    lead = lead * jnp.where(bit, row, 1.0)
                lead_scr[mode] = lead
                state.append(lead * wide(total_scr[mode, pl.ds(at * TILES + number, 1), :]))
            decay = [wide(power_scr[3, mode : mode + 1, lanes]) for mode in range(modes)]
            for pair in range(tokens // (2 * ROWS)):
                rows = slice(pair * 2 * ROWS, (pair + 1) * 2 * ROWS)
                gates = gate_buf[at, rows, lanes].astype(f32)
                sums = []
                for part in range(2):
                    if pair == tokens // (4 * ROWS) and part == 0:
                        state = [
                            one + lead_scr[mode] * wide(mid_buf[at, mode, pl.ds(number, 1), :])
                            for mode, one in enumerate(state)
                        ]
                    here = slice((pair * 2 + part) * ROWS, (pair * 2 + part + 1) * ROWS)
                    sums.append(y_buf[at, here, lanes] + tree(state))
                    state = [factor * one for factor, one in zip(decay, state)]
                out_buf[at, rows, lanes] = (gates * rounded(jnp.concatenate(sums, axis=0))).astype(bf16)
            return 0

        lax.fori_loop(0, TILES, tile, 0)

    give = columns_out(out_ref, out_buf, out_sem)
    over_chunks(0, chunks, with_fetch(chunks, fetch, chunk), give)
    for at in range(chunks):
        wait_all(give(at))


def cost(flops, moved):
    return pl.CostEstimate(flops=int(flops), bytes_accessed=int(moved), transcendentals=0)


def local(query, key_proj, value_proj, featurizer, rates, residues, skip, *, axes):
    tokens, width = query.shape
    modes = rates.shape[0]
    members, taps, groups = featurizer.shape
    devices = math.prod(lax.axis_size(axis) for axis in axes)
    chunks = width // CHUNK
    tiles = width // LANES
    split = devices // modes
    even = devices % modes == 0 and tiles % split == 0
    vmem = pltpu.VMEM
    far = pltpu.HBM
    near = jax.ShapeDtypeStruct
    dma = pltpu.SemaphoreType.DMA
    elements = tokens * width

    def call(kernel, inputs, outputs, scratches, name, close=(), **more):
        inputs = [
            value if at in close else pltpu.with_memory_space_constraint(value, far)
            for at, value in enumerate(inputs)
        ]
        beside, there = pl.BlockSpec(memory_space=vmem), pl.BlockSpec(memory_space=far)
        return pl.pallas_call(
            kernel,
            in_specs=[beside if at in close else there for at in range(len(inputs))],
            out_specs=[beside if isinstance(one, near) else there for one in outputs],
            out_shape=outputs,
            scratch_shapes=scratches,
            compiler_params=pltpu.CompilerParams(vmem_limit_bytes=32 * 2**20),
            name=name,
            **more,
        )(*inputs)

    (packed,) = call(
        pack_kernel,
        (key_proj, value_proj, query),
        [near((members * ROWS, width), bf16)],
        [vmem((members, 2 * ROWS, width), bf16), dma((members,))],
        "pack",
    )
    halo = lax.ppermute(packed, axes, [(at, at + 1) for at in range(devices - 1)])

    feat = featurizer.reshape(members, taps, chunks, groups // chunks).transpose(2, 0, 1, 3)
    column = vmem((2 * ROWS + tokens, LANES), f32)
    half_buf, whole_buf = vmem((chunks, tokens, CHUNK), bf16), vmem((chunks, tokens, CHUNK), f32)
    u, wide_taps, state = call(
        signal_kernel,
        (key_proj, value_proj, feat, rates),
        [near((tokens, width), bf16), near((chunks, 2, ROWS, CHUNK), f32), near((modes, tiles, LANES), f32)],
        [vmem((4, modes, width), f32), vmem((modes, ROWS, LANES), f32), column, column],
        "signal",
        close=range(4),
        cost_estimate=cost(60 * elements, 10 * elements),
    )

    pieces = (modes * split, tiles // split, LANES) if even else (modes, tiles, LANES)
    left, head = call(
        functools.partial(head_kernel, tokens=tokens, reach=taps - 1),
        (key_proj, value_proj, halo, rates, wide_taps, state),
        [near(pieces, bf16), near((2 * ROWS, width), bf16)],
        [vmem((modes * tiles, LANES), f32), vmem((TILES, 2, 3 * ROWS, LANES), f32)]
        + [vmem((tiles * ROWS, LANES), f32), vmem((modes, tiles, LANES), f32)],
        "head",
        close=range(6),
    )
    left, halo_late, rates_late, skip_late = lax.optimization_barrier((left, halo, rates, skip))
    coef = residues * jnp.sqrt(-jnp.expm1(-2.0 * rates_late) / modes)
    skip_row = skip_late[None, :]
    stage = vmem((tokens // ROWS // 2 * ROWS * ROWS, LANES), f32)
    local_shapes = [far((tokens, width), f32), far((chunks, modes, ROWS, LANES), f32)]
    local_scratches = [whole_buf, vmem((chunks, modes, ROWS, LANES), f32), stage, stage]
    local_scratches += [dma((1, chunks)), dma((chunks,))]
    early = chunks * 2 // 9
    gate, y, mid = call(
        functools.partial(gate_kernel, early=early),
        (query, halo_late, feat, u, head, rates, coef, skip_row),
        [far((tokens, width), bf16)] + local_shapes,
        [vmem((members * ROWS, width), bf16), half_buf, vmem((chunks, 1, ROWS, CHUNK), f32), column]
        + [dma((1,)), dma((1, chunks))]
        + local_scratches,
        "gate",
        close=(0, 2, 3, 4, 5, 6, 7),
        cost_estimate=cost(28 * elements, 6 * elements),
    )

    def swap(value):
        return lax.all_to_all(value, axes, split_axis=0, concat_axis=0, tiled=True)

    share = modes * width // devices
    theirs = swap(left if even else left.reshape(devices, share))
    theirs, gate, coef, skip_row, y, mid = lax.optimization_barrier((theirs, gate, coef, skip_row, y, mid))
    if even:
        (entering,) = call(
            functools.partial(prefix_kernel, tokens=tokens, axes=axes),
            (theirs, rates, coef),
            [near(pieces, bf16)],
            [vmem((-(-pieces[1] // ROWS) * ROWS, LANES), f32)],
            "prefix",
            close=(0, 1, 2),
        )
    else:
        mine = lax.axis_index(axes)
        through = jnp.exp(-float(tokens) * lax.dynamic_slice_in_dim(rates.reshape(-1), mine * share, share))
        factor = lax.dynamic_slice_in_dim(coef.reshape(-1), mine * share, share)
        _, entering = lax.scan(
            lambda so_far, piece: (through * so_far + piece.astype(f32), (factor * so_far).astype(bf16)),
            jnp.zeros((share,), f32),
            theirs,
        )

    entering, y = lax.optimization_barrier((entering, y))
    entered = swap(entering).reshape(pieces)
    y, mid = call(
        functools.partial(local_kernel, first=early, last=chunks),
        (u, head, rates, coef, skip_row, y, mid),
        local_shapes,
        local_scratches,
        "within",
        close=range(5),
        cost_estimate=cost(50 * elements, 8 * elements),
        input_output_aliases={5: 0, 6: 1},
    )

    (out,) = call(
        final_kernel,
        (entered, rates, mid, y, gate),
        [far((tokens, width), bf16)],
        [vmem((chunks, modes, ROWS, LANES), f32), whole_buf, half_buf, half_buf]
        + [vmem((modes, tiles, LANES), f32), vmem((4, modes, CHUNK), f32), vmem((modes, ROWS, LANES), f32)]
        + [dma((2, chunks)), dma((chunks,)), dma((1, chunks))],
        "final",
        close=(0, 1),
        cost_estimate=cost(40 * elements, 10 * elements),
    )
    return out


def solution(mesh):
    axes = tuple(mesh.axis_names)
    placed = (P(axes, None),) * 3 + (P(),) * 4
    return jax.shard_map(
        functools.partial(local, axes=axes),
        mesh=mesh,
        in_specs=placed,
        out_specs=P(axes, None),
        check_vma=False,
    )
```

```python
import functools
import math

import jax
import jax.numpy as jnp
from jax import lax
from jax.experimental import pallas as pl
from jax.experimental.pallas import tpu as pltpu
from jax.sharding import PartitionSpec as P

LANES = 128
ROWS = 8
TILES = 4
CHUNK = TILES * LANES
AHEAD = 4
f32 = jnp.float32
bf16 = jnp.bfloat16


def put_tile(scratch, group, slot, tile):
    scratch[pl.ds((group * ROWS + slot) * ROWS, ROWS), :] = tile


def get_row(scratch, group, row):
    return scratch[pl.ds(group * ROWS * ROWS + row, ROWS, stride=ROWS), :]


def lanes_of(value, tile):
    return value[:, tile * LANES : (tile + 1) * LANES]


def tile_lanes(tile):
    return pl.ds(pl.multiple_of(tile * LANES, LANES), LANES)


def span(at):
    return pl.ds(pl.multiple_of(at * CHUNK, CHUNK), CHUNK)


def wide(row):
    return jnp.broadcast_to(row, (ROWS, LANES))


def sublane():
    return lax.broadcasted_iota(jnp.int32, (ROWS, LANES), 0)


def spread(row_of):
    slot = sublane() % TILES
    result = wide(row_of(TILES - 1))
    for tile in range(TILES - 1):
        result = jnp.where(slot == tile, wide(row_of(tile)), result)
    return result


def spread_rows(ref, at, rows):
    def one(row):
        return spread(lambda tile: ref[row : row + 1, tile_lanes(at * TILES + tile)])

    return [one(row) for row in rows]


def rounded(value):
    return value.astype(bf16).astype(f32)


def tiles_of(block):
    block = block.astype(f32)
    return [block[at : at + ROWS] for at in range(0, block.shape[0], ROWS)]


def fir(column, taps, first, count):
    half = ROWS // 2
    top = sublane() < half

    def seen(start, lags):
        return [column[pl.ds(start - lag, ROWS), :] for lag in range(lags)]

    def far_part(rows):
        total = taps[half] * rows[0]
        for lag in range(half + 1, len(taps)):
            total = total + taps[lag] * rows[lag - half]
        return pltpu.roll(total, half, 0)

    before = far_part(seen(first - ROWS, len(taps) - half))
    for start in range(first, first + count * ROWS, ROWS):
        rows = seen(start, half)
        now = far_part(rows)
        total = taps[0] * rows[0]
        for lag in range(1, half):
            total = total + taps[lag] * rows[lag]
        yield total + jnp.where(top, before, now)
        before = now


def lay_column(column, source, lanes):
    for pair in range(source.shape[0] // (2 * ROWS)):
        rows = slice(pair * 2 * ROWS, (pair + 1) * 2 * ROWS)
        column[pl.ds((pair + 1) * 2 * ROWS, 2 * ROWS), :] = source[rows, lanes].astype(f32)


def chunk_taps(wide_ref, at, member, tile, count):
    return [wide(wide_ref[at, member, lag : lag + 1, tile_lanes(tile)]) for lag in range(count)]


def widened(feat_ref, member, out_ref, position):
    chunks, _, taps, count = feat_ref.shape
    rows = [feat_ref[at, member] for at in range(chunks)]
    rows = [jnp.concatenate([row, jnp.zeros((ROWS - taps, count), f32)], axis=0) for row in rows]
    group = lax.broadcasted_iota(jnp.int32, (count, CHUNK), 0)
    lane = lax.broadcasted_iota(jnp.int32, (count, CHUNK), 1)
    pick = (group == lane // (CHUNK // count)).astype(f32).astype(bf16)
    parts, rest = [], jnp.concatenate(rows, axis=0)
    for _ in range(3):
        term = rest.astype(bf16)
        rest = rest - term.astype(f32)
        parts.append(jnp.dot(term, pick, preferred_element_type=f32))
    out_ref[:, position] = (parts[0] + parts[1] + parts[2]).reshape(chunks, ROWS, CHUNK)


def power(base, exponent):
    result = None
    while exponent:
        if exponent & 1:
            result = base if result is None else result * base
        base = base * base
        exponent >>= 1
    return result


def tree(terms):
    while len(terms) > 1:
        terms = [sum(terms[at + 1 : at + 2], terms[at]) for at in range(0, len(terms), 2)]
    return terms[0]


def start_all(copies):
    for copy in copies:
        copy.start()


def wait_all(copies):
    for copy in copies:
        copy.wait()


def begin(chunks, fetch):
    for at in range(min(AHEAD, chunks)):
        start_all(fetch(at))


def over_chunks(first, last, body, send):
    def one(at, _):
        body(at)
        start_all(send(at))
        return 0

    lax.fori_loop(first, last, one, 0)


def with_fetch(chunks, fetch, body):
    def one(at):
        @pl.when(at + AHEAD < chunks)
        def _():
            start_all(fetch(at + AHEAD))

        wait_all(fetch(at))
        body(at)

    return one


def columns_in(pairs, sem):
    def fetch(at):
        return [
            pltpu.make_async_copy(ref.at[:, span(at)], buf.at[at], sem.at[member, at])
            for member, (ref, buf) in enumerate(pairs)
        ]

    return fetch


def columns_out(ref, buf, sem):
    return lambda at: [pltpu.make_async_copy(buf.at[at], ref.at[:, span(at)], sem.at[0, at])]


def pack_kernel(key_ref, value_ref, query_ref, out_ref, in_buf, in_sem):
    tokens = key_ref.shape[0]
    copies = [
        pltpu.make_async_copy(ref.at[pl.ds(tokens - 2 * ROWS, 2 * ROWS)], in_buf.at[at], in_sem.at[at])
        for at, ref in enumerate((key_ref, value_ref, query_ref))
    ]
    start_all(copies)
    wait_all(copies)
    tails = [in_buf[at].astype(f32)[ROWS:] for at in range(len(copies))]
    out_ref[...] = jnp.concatenate(tails, axis=0).astype(bf16)


def signal_kernel(key_ref, value_ref, feat_ref, rate_ref, u_ref, wide_ref, state_ref, power_scr, last_scr, *columns):
    tokens, tiles = u_ref.shape[0], state_ref.shape[1]
    modes = rate_ref.shape[0]
    chunks = tiles // TILES
    count = feat_ref.shape[2]
    for member in range(2):
        widened(feat_ref, member + 1, wide_ref, member)
    for column in columns:
        column[pl.ds(0, 2 * ROWS), :] = jnp.zeros((2 * ROWS, LANES), f32)
    last_scr[...] = jnp.zeros(last_scr.shape, f32)

    def powers(at, _):
        through = jnp.exp(-rate_ref[:, span(at)])
        for level in range(4):
            power_scr[level, :, span(at)] = through
            through = through * through
        return 0

    lax.fori_loop(0, chunks, powers, 0)

    def reduce(number):
        lanes = tile_lanes(number)
        for mode in range(modes):
            whole = last_scr[mode]
            for level in (2, 1, 0):
                factor = wide(power_scr[level, mode : mode + 1, lanes])
                whole = factor * whole + pltpu.roll(whole, ROWS - (1 << level), 0)
            state_ref[mode, pl.ds(number, 1), :] = whole[:1]

    def tile(number, _):
        lanes = tile_lanes(number)
        reduce(jnp.maximum(number - 1, 0))
        taps = [chunk_taps(wide_ref, number // TILES, member, number % TILES, count) for member in range(2)]
        for column, ref in zip(columns, (key_ref, value_ref)):
            lay_column(column, ref, lanes)
        decay = [wide(power_scr[3, mode : mode + 1, lanes]) for mode in range(modes)]
        state = None
        parts = [fir(column, some, 2 * ROWS, tokens // ROWS) for column, some in zip(columns, taps)]
        for pair in range(tokens // (2 * ROWS)):
            found = [next(parts[0]) * next(parts[1]) for _ in range(2)]
            if pair == 0:
                found[0] = jnp.where(sublane() < count - 1, 0.0, found[0])
            both = jnp.concatenate(found, axis=0).astype(bf16)
            u_ref[pair * 2 * ROWS : (pair + 1) * 2 * ROWS, lanes] = both
            for u in tiles_of(both):
                if state is None:
                    state = [u] * modes
                else:
                    state = [factor * one + u for factor, one in zip(decay, state)]
        for mode in range(modes):
            last_scr[mode] = state[mode]
        return 0

    lax.fori_loop(0, tiles, tile, 0)
    reduce(tiles - 1)


def head_kernel(key_ref, value_ref, halo_ref, rate_ref, wide_ref, state_ref, u_ref, *rest, tokens, reach):
    out_ref, head_ref, u_out_ref, rate_scr, column_scr, token_scr, total_scr, sem = rest
    move = pltpu.make_async_copy(u_ref, u_out_ref, sem.at[0])
    move.start()
    modes, tiles = state_ref.shape[:2]
    pieces, piece_rows = out_ref.shape[:2]
    for group in range(modes // ROWS):
        for tile in range(tiles):
            rows = pl.ds((group * tiles + tile) * ROWS, ROWS)
            rate_scr[rows, :] = rate_ref[group * ROWS : (group + 1) * ROWS, tile * LANES : (tile + 1) * LANES]

    def some(chunk, _):
        for number in range(TILES):
            lanes = tile_lanes(chunk * TILES + number)
            halo = halo_ref[:, lanes].astype(f32)
            parts = []
            for member in range(2):
                taps = chunk_taps(wide_ref, chunk, member, number, reach + 1)
                column = column_scr.at[number, member]
                column[pl.ds(0, ROWS), :] = jnp.zeros((ROWS, LANES), f32)
                column[pl.ds(ROWS, ROWS), :] = halo[member * ROWS : (member + 1) * ROWS]
                source = (key_ref, value_ref)[member]
                column[pl.ds(2 * ROWS, ROWS), :] = source[: 2 * ROWS, lanes].astype(f32)[:ROWS]
                parts += fir(column, taps, 2 * ROWS, 1)
            u = jnp.where(sublane() < reach, rounded(parts[0] * parts[1]), 0.0)
            token_scr[pl.ds(pl.multiple_of((chunk * TILES + number) * ROWS, ROWS), ROWS), :] = u
            head_ref[:, lanes] = jnp.concatenate([u, jnp.zeros((ROWS, LANES), f32)], axis=0).astype(bf16)
        return 0

    lax.fori_loop(0, tiles // TILES, some, 0)
    signals = [token_scr[pl.ds(row, tiles, stride=ROWS), :] for row in range(reach)]
    split = pieces // modes
    for mode in range(modes):
        start = mode // ROWS * tiles * ROWS + mode % ROWS
        decay = jnp.exp(-rate_scr[pl.ds(start, tiles, stride=ROWS), :])
        head = signals[0]
        for row in range(1, reach):
            head = decay * head + signals[row]
        total_scr[mode] = state_ref[mode] + power(decay, tokens - reach) * head
        for part in range(split):
            rows = total_scr[mode, part * piece_rows : (part + 1) * piece_rows, :]
            out_ref[mode * split + part] = rows.astype(out_ref.dtype)
    move.wait()


def gate_kernel(query_ref, halo_ref, feat_ref, u_ref, head_ref, rate_ref, coef_ref, skip_ref, gate_ref, *rest, early):
    y_ref, mid_ref, halo_buf, gate_buf, wide_scr, column, small_sem, out_sem = rest[:8]
    inner = rest[8:]
    chunks, tokens = gate_buf.shape[:2]
    count = feat_ref.shape[2]
    halo_copy = pltpu.make_async_copy(halo_ref, halo_buf, small_sem.at[0])
    halo_copy.start()
    widened(feat_ref, 0, wide_scr, 0)
    local_chunk, local_send = local_parts(u_ref, head_ref, rate_ref, coef_ref, skip_ref, y_ref, mid_ref, *inner)
    over_chunks(0, early, local_chunk, local_send)
    halo_copy.wait()
    column[pl.ds(0, ROWS), :] = jnp.zeros((ROWS, LANES), f32)

    def chunk(at):
        def tile(number, _):
            lanes = tile_lanes(number)
            all_lanes = tile_lanes(at * TILES + number)
            taps = chunk_taps(wide_scr, at, 0, number, count)
            column[pl.ds(ROWS, ROWS), :] = halo_buf[:, all_lanes].astype(f32)[2 * ROWS :]
            lay_column(column, query_ref, all_lanes)
            found = list(fir(column, taps, 2 * ROWS, tokens // ROWS))
            for pair in range(tokens // (2 * ROWS)):
                rows = slice(pair * 2 * ROWS, (pair + 1) * 2 * ROWS)
                gate_buf[at, rows, lanes] = jnp.concatenate(found[pair * 2 : pair * 2 + 2], axis=0).astype(bf16)
            return 0

        lax.fori_loop(0, TILES, tile, 0)

    give = columns_out(gate_ref, gate_buf, out_sem)
    over_chunks(0, chunks, chunk, give)
    for at in range(early):
        wait_all(local_send(at))
    for at in range(chunks):
        wait_all(give(at))


def prefix_kernel(piece_ref, rate_ref, coef_ref, out_ref, table_scr, *, tokens, axes):
    devices, piece_rows = piece_ref.shape[:2]
    split = devices // rate_ref.shape[0]
    mine = lax.axis_index(axes)
    mode, part = mine // split, mine % split
    group = pl.multiple_of(mode // ROWS * ROWS, ROWS)
    first = pl.multiple_of(part * piece_rows * LANES, LANES)

    def mine_of(ref):
        rows = ref[pl.ds(group, ROWS), pl.ds(first, piece_rows * LANES)]
        here = lax.broadcasted_iota(jnp.int32, rows.shape, 0) == mode - group
        row = jnp.sum(jnp.where(here, rows, 0.0), axis=0, keepdims=True)
        for number in range(piece_rows):
            table_scr[number : number + 1, :] = lanes_of(row, number)
        return table_scr[:piece_rows, :]

    coef = mine_of(coef_ref)
    through = jnp.exp(-float(tokens) * mine_of(rate_ref))

    def lap(number, entering):
        for step in range(4):
            source = number * 4 + step
            out_ref[source] = (coef * entering).astype(out_ref.dtype)
            entering = through * entering + piece_ref[source].astype(f32)
        return entering

    lax.fori_loop(0, devices // 4, lap, jnp.zeros((piece_rows, LANES), f32))


def local_kernel(u_ref, head_ref, rate_ref, coef_ref, skip_ref, *rest, first, last):
    chunk, send = local_parts(u_ref, head_ref, rate_ref, coef_ref, skip_ref, *rest[-8:])
    over_chunks(first, last, chunk, send)
    for at in range(first, last):
        wait_all(send(at))


def local_parts(u_ref, head_ref, rate_ref, coef_ref, skip_ref, y_ref, mid_ref, *scratches):
    y_buf, mid_buf, token_scr, sum_scr, out_sem, mid_sem = scratches
    tokens = u_ref.shape[0]
    modes = rate_ref.shape[0]
    half_groups = tokens // ROWS // 2
    give = columns_out(y_ref, y_buf, out_sem)

    def send(at):
        return give(at) + [pltpu.make_async_copy(mid_buf.at[at], mid_ref.at[at], mid_sem.at[at])]

    def chunk(at):
        for pair in range(half_groups):
            block = u_ref[pair * 2 * ROWS : (pair + 1) * 2 * ROWS, span(at)].astype(f32)
            if pair == 0:
                block = block + head_ref[:, span(at)].astype(f32)
            for part in range(2):
                group = pair * 2 + part
                half, within = group // half_groups, group % half_groups
                for tile in range(TILES):
                    piece = lanes_of(block, tile)[part * ROWS : (part + 1) * ROWS]
                    put_tile(token_scr, within, half * TILES + tile, piece)
        (skip,) = spread_rows(skip_ref, at, range(1))
        coef = spread_rows(coef_ref, at, range(modes))
        decay = [jnp.exp(-rate) for rate in spread_rows(rate_ref, at, range(modes))]

        def eight(group, state):
            state = list(state)
            for row in range(ROWS):
                u = get_row(token_scr, group, row)
                state = [factor * one + u for factor, one in zip(decay, state)]
                terms = [factor * one for factor, one in zip([skip] + coef, [u] + state)]
                sum_scr[pl.ds(group * ROWS * ROWS + row, ROWS, stride=ROWS), :] = tree(terms)
            return tuple(state)

        state = lax.fori_loop(0, half_groups, eight, (jnp.zeros((ROWS, LANES), f32),) * modes)
        for mode, (factor, one) in enumerate(zip(coef, state)):
            mid_buf[at, mode] = factor * one
        for group in range(2 * half_groups):
            half, within = group // half_groups, group % half_groups
            for tile in range(TILES):
                slot = (within * ROWS + half * TILES + tile) * ROWS
                rows = slice(group * ROWS, (group + 1) * ROWS)
                y_buf[at, rows, tile * LANES : (tile + 1) * LANES] = sum_scr[pl.ds(slot, ROWS), :]

    return chunk, send


def final_kernel(piece_ref, rate_ref, mid_ref, y_ref, gate_ref, out_ref, *scratches):
    mid_buf, y_buf, gate_buf, out_buf, total_scr, power_scr, lead_scr, in_sem, mid_sem, out_sem = scratches
    chunks, modes = mid_buf.shape[:2]
    tokens = y_buf.shape[1]
    columns = columns_in(((y_ref, y_buf), (gate_ref, gate_buf)), in_sem)

    def fetch(at):
        return columns(at) + [pltpu.make_async_copy(mid_ref.at[at], mid_buf.at[at], mid_sem.at[at])]

    begin(chunks, fetch)
    pieces, piece_rows = piece_ref.shape[:2]
    split = pieces // modes
    for mode in range(modes):
        for part in range(split):
            rows = piece_ref[mode * split + part].astype(f32)
            total_scr[mode, part * piece_rows : (part + 1) * piece_rows, :] = rows
    bits = [(sublane() >> level) % 2 == 1 for level in range(3)]

    def chunk(at):
        through = jnp.exp(-rate_ref[:, span(at)])
        for level in range(4):
            power_scr[level] = through
            through = through * through

        def tile(number, _):
            lanes = tile_lanes(number)
            state = []
            for mode in range(modes):
                rows = [wide(power_scr[level, mode : mode + 1, lanes]) for level in range(3)]
                lead = rows[0]
                for bit, row in zip(bits, rows):
                    lead = lead * jnp.where(bit, row, 1.0)
                lead_scr[mode] = lead
                state.append(lead * wide(total_scr[mode, pl.ds(at * TILES + number, 1), :]))
            decay = [wide(power_scr[3, mode : mode + 1, lanes]) for mode in range(modes)]
            for pair in range(tokens // (2 * ROWS)):
                rows = slice(pair * 2 * ROWS, (pair + 1) * 2 * ROWS)
                gates = gate_buf[at, rows, lanes].astype(f32)
                sums = []
                for part in range(2):
                    if pair == tokens // (4 * ROWS) and part == 0:
                        state = [
                            one + lead_scr[mode] * wide(mid_buf[at, mode, pl.ds(number, 1), :])
                            for mode, one in enumerate(state)
                        ]
                    here = slice((pair * 2 + part) * ROWS, (pair * 2 + part + 1) * ROWS)
                    sums.append(y_buf[at, here, lanes] + tree(state))
                    state = [factor * one for factor, one in zip(decay, state)]
                out_buf[at, rows, lanes] = (gates * rounded(jnp.concatenate(sums, axis=0))).astype(bf16)
            return 0

        lax.fori_loop(0, TILES, tile, 0)

    give = columns_out(out_ref, out_buf, out_sem)
    over_chunks(0, chunks, with_fetch(chunks, fetch, chunk), give)
    for at in range(chunks):
        wait_all(give(at))


def cost(flops, moved):
    return pl.CostEstimate(flops=int(flops), bytes_accessed=int(moved), transcendentals=0)


def local(query, key_proj, value_proj, featurizer, rates, residues, skip, *, axes):
    tokens, width = query.shape
    modes = rates.shape[0]
    members, taps, groups = featurizer.shape
    devices = math.prod(lax.axis_size(axis) for axis in axes)
    chunks = width // CHUNK
    tiles = width // LANES
    split = devices // modes
    even = devices % modes == 0 and tiles % split == 0
    vmem = pltpu.VMEM
    far = pltpu.HBM
    near = jax.ShapeDtypeStruct
    dma = pltpu.SemaphoreType.DMA
    elements = tokens * width

    def call(kernel, inputs, outputs, scratches, name, close=(), **more):
        inputs = [
            value if at in close else pltpu.with_memory_space_constraint(value, far)
            for at, value in enumerate(inputs)
        ]
        beside, there = pl.BlockSpec(memory_space=vmem), pl.BlockSpec(memory_space=far)
        return pl.pallas_call(
            kernel,
            in_specs=[beside if at in close else there for at in range(len(inputs))],
            out_specs=[beside if isinstance(one, near) else there for one in outputs],
            out_shape=outputs,
            scratch_shapes=scratches,
            compiler_params=pltpu.CompilerParams(vmem_limit_bytes=32 * 2**20),
            name=name,
            **more,
        )(*inputs)

    (packed,) = call(
        pack_kernel,
        (key_proj, value_proj, query),
        [near((members * ROWS, width), bf16)],
        [vmem((members, 2 * ROWS, width), bf16), dma((members,))],
        "pack",
    )
    halo = lax.ppermute(packed, axes, [(at, at + 1) for at in range(devices - 1)])

    feat = featurizer.reshape(members, taps, chunks, groups // chunks).transpose(2, 0, 1, 3)
    column = vmem((2 * ROWS + tokens, LANES), f32)
    half_buf, whole_buf = vmem((chunks, tokens, CHUNK), bf16), vmem((chunks, tokens, CHUNK), f32)
    u, wide_taps, state = call(
        signal_kernel,
        (key_proj, value_proj, feat, rates),
        [near((tokens, width), bf16), near((chunks, 2, ROWS, CHUNK), f32), near((modes, tiles, LANES), f32)],
        [vmem((4, modes, width), f32), vmem((modes, ROWS, LANES), f32), column, column],
        "signal",
        close=range(4),
        cost_estimate=cost(60 * elements, 10 * elements),
    )

    pieces = (modes * split, tiles // split, LANES) if even else (modes, tiles, LANES)
    left, head, u = call(
        functools.partial(head_kernel, tokens=tokens, reach=taps - 1),
        (key_proj, value_proj, halo, rates, wide_taps, state, u),
        [near(pieces, bf16), near((2 * ROWS, width), bf16), far((tokens, width), bf16)],
        [vmem((modes * tiles, LANES), f32), vmem((TILES, 2, 3 * ROWS, LANES), f32)]
        + [vmem((tiles * ROWS, LANES), f32), vmem((modes, tiles, LANES), f32), dma((1,))],
        "head",
        close=range(7),
    )
    left, halo_late, rates_late, skip_late = lax.optimization_barrier((left, halo, rates, skip))
    coef = residues * jnp.sqrt(-jnp.expm1(-2.0 * rates_late) / modes)
    skip_row = skip_late[None, :]
    stage = vmem((tokens // ROWS // 2 * ROWS * ROWS, LANES), f32)
    local_shapes = [far((tokens, width), f32), far((chunks, modes, ROWS, LANES), f32)]
    local_scratches = [whole_buf, vmem((chunks, modes, ROWS, LANES), f32), stage, stage]
    local_scratches += [dma((1, chunks)), dma((chunks,))]
    early = chunks * 5 // 9
    gate, y, mid = call(
        functools.partial(gate_kernel, early=early),
        (query, halo_late, feat, u, head, rates, coef, skip_row),
        [far((tokens, width), bf16)] + local_shapes,
        [vmem((members * ROWS, width), bf16), half_buf, vmem((chunks, 1, ROWS, CHUNK), f32), column]
        + [dma((1,)), dma((1, chunks))]
        + local_scratches,
        "gate",
        close=(0, 2, 3, 4, 5, 6, 7),
        cost_estimate=cost(28 * elements, 6 * elements),
    )

    def swap(value):
        return lax.all_to_all(value, axes, split_axis=0, concat_axis=0, tiled=True)

    share = modes * width // devices
    theirs = swap(left if even else left.reshape(devices, share))
    theirs, gate, coef, skip_row, y, mid = lax.optimization_barrier((theirs, gate, coef, skip_row, y, mid))
    if even:
        (entering,) = call(
            functools.partial(prefix_kernel, tokens=tokens, axes=axes),
            (theirs, rates, coef),
            [near(pieces, bf16)],
            [vmem((-(-pieces[1] // ROWS) * ROWS, LANES), f32)],
            "prefix",
            close=(0, 1, 2),
        )
    else:
        mine = lax.axis_index(axes)
        through = jnp.exp(-float(tokens) * lax.dynamic_slice_in_dim(rates.reshape(-1), mine * share, share))
        factor = lax.dynamic_slice_in_dim(coef.reshape(-1), mine * share, share)
        _, entering = lax.scan(
            lambda so_far, piece: (through * so_far + piece.astype(f32), (factor * so_far).astype(bf16)),
            jnp.zeros((share,), f32),
            theirs,
        )

    entering, y = lax.optimization_barrier((entering, y))
    entered = swap(entering).reshape(pieces)
    y, mid = call(
        functools.partial(local_kernel, first=early, last=chunks),
        (u, head, rates, coef, skip_row, y, mid),
        local_shapes,
        local_scratches,
        "within",
        close=range(5),
        cost_estimate=cost(50 * elements, 8 * elements),
        input_output_aliases={5: 0, 6: 1},
    )

    (out,) = call(
        final_kernel,
        (entered, rates, mid, y, gate),
        [far((tokens, width), bf16)],
        [vmem((chunks, modes, ROWS, LANES), f32), whole_buf, half_buf, half_buf]
        + [vmem((modes, tiles, LANES), f32), vmem((4, modes, CHUNK), f32), vmem((modes, ROWS, LANES), f32)]
        + [dma((2, chunks)), dma((chunks,)), dma((1, chunks))],
        "final",
        close=(0, 1),
        cost_estimate=cost(40 * elements, 10 * elements),
    )
    return out


def solution(mesh):
    axes = tuple(mesh.axis_names)
    placed = (P(axes, None),) * 3 + (P(),) * 4
    return jax.shard_map(
        functools.partial(local, axes=axes),
        mesh=mesh,
        in_specs=placed,
        out_specs=P(axes, None),
        check_vma=False,
    )
```

```python
import functools
import math

import jax
import jax.numpy as jnp
from jax import lax
from jax.experimental import pallas as pl
from jax.experimental.pallas import tpu as pltpu
from jax.sharding import PartitionSpec as P

LANES = 128
ROWS = 8
TILES = 4
CHUNK = TILES * LANES
AHEAD = 4
f32 = jnp.float32
bf16 = jnp.bfloat16


def put_tile(scratch, group, slot, tile):
    scratch[pl.ds((group * ROWS + slot) * ROWS, ROWS), :] = tile


def get_row(scratch, group, row):
    return scratch[pl.ds(group * ROWS * ROWS + row, ROWS, stride=ROWS), :]


def lanes_of(value, tile):
    return value[:, tile * LANES : (tile + 1) * LANES]


def tile_lanes(tile):
    return pl.ds(pl.multiple_of(tile * LANES, LANES), LANES)


def span(at):
    return pl.ds(pl.multiple_of(at * CHUNK, CHUNK), CHUNK)


def wide(row):
    return jnp.broadcast_to(row, (ROWS, LANES))


def sublane():
    return lax.broadcasted_iota(jnp.int32, (ROWS, LANES), 0)


def spread(row_of):
    slot = sublane() % TILES
    result = wide(row_of(TILES - 1))
    for tile in range(TILES - 1):
        result = jnp.where(slot == tile, wide(row_of(tile)), result)
    return result


def spread_rows(ref, at, rows):
    def one(row):
        return spread(lambda tile: ref[row : row + 1, tile_lanes(at * TILES + tile)])

    return [one(row) for row in rows]


def rounded(value):
    return value.astype(bf16).astype(f32)


def tiles_of(block):
    block = block.astype(f32)
    return [block[at : at + ROWS] for at in range(0, block.shape[0], ROWS)]


def fir(column, taps, first, count):
    half = ROWS // 2
    top = sublane() < half

    def seen(start, lags):
        return [column[pl.ds(start - lag, ROWS), :] for lag in range(lags)]

    def far_part(rows):
        total = taps[half] * rows[0]
        for lag in range(half + 1, len(taps)):
            total = total + taps[lag] * rows[lag - half]
        return pltpu.roll(total, half, 0)

    before = far_part(seen(first - ROWS, len(taps) - half))
    for start in range(first, first + count * ROWS, ROWS):
        rows = seen(start, half)
        now = far_part(rows)
        total = taps[0] * rows[0]
        for lag in range(1, half):
            total = total + taps[lag] * rows[lag]
        yield total + jnp.where(top, before, now)
        before = now


def lay_column(column, source, lanes):
    for pair in range(source.shape[0] // (2 * ROWS)):
        rows = slice(pair * 2 * ROWS, (pair + 1) * 2 * ROWS)
        column[pl.ds((pair + 1) * 2 * ROWS, 2 * ROWS), :] = source[rows, lanes].astype(f32)


def chunk_taps(wide_ref, at, member, tile, count):
    return [wide(wide_ref[at, member, lag : lag + 1, tile_lanes(tile)]) for lag in range(count)]


def widened(feat_ref, member, out_ref, position):
    chunks, _, taps, count = feat_ref.shape
    rows = [feat_ref[at, member] for at in range(chunks)]
    rows = [jnp.concatenate([row, jnp.zeros((ROWS - taps, count), f32)], axis=0) for row in rows]
    group = lax.broadcasted_iota(jnp.int32, (count, CHUNK), 0)
    lane = lax.broadcasted_iota(jnp.int32, (count, CHUNK), 1)
    pick = (group == lane // (CHUNK // count)).astype(f32).astype(bf16)
    parts, rest = [], jnp.concatenate(rows, axis=0)
    for _ in range(3):
        term = rest.astype(bf16)
        rest = rest - term.astype(f32)
        parts.append(jnp.dot(term, pick, preferred_element_type=f32))
    out_ref[:, position] = (parts[0] + parts[1] + parts[2]).reshape(chunks, ROWS, CHUNK)


def power(base, exponent):
    result = None
    while exponent:
        if exponent & 1:
            result = base if result is None else result * base
        base = base * base
        exponent >>= 1
    return result


def tree(terms):
    while len(terms) > 1:
        terms = [sum(terms[at + 1 : at + 2], terms[at]) for at in range(0, len(terms), 2)]
    return terms[0]


def start_all(copies):
    for copy in copies:
        copy.start()


def wait_all(copies):
    for copy in copies:
        copy.wait()


def begin(chunks, fetch):
    for at in range(min(AHEAD, chunks)):
        start_all(fetch(at))


def over_chunks(first, last, body, send):
    def one(at, _):
        body(at)
        start_all(send(at))
        return 0

    lax.fori_loop(first, last, one, 0)


def with_fetch(chunks, fetch, body):
    def one(at):
        @pl.when(at + AHEAD < chunks)
        def _():
            start_all(fetch(at + AHEAD))

        wait_all(fetch(at))
        body(at)

    return one


def columns_in(pairs, sem):
    def fetch(at):
        return [
            pltpu.make_async_copy(ref.at[:, span(at)], buf.at[at], sem.at[member, at])
            for member, (ref, buf) in enumerate(pairs)
        ]

    return fetch


def columns_out(ref, buf, sem):
    return lambda at: [pltpu.make_async_copy(buf.at[at], ref.at[:, span(at)], sem.at[0, at])]


def pack_kernel(key_ref, value_ref, query_ref, out_ref, in_buf, in_sem):
    tokens = key_ref.shape[0]
    copies = [
        pltpu.make_async_copy(ref.at[pl.ds(tokens - 2 * ROWS, 2 * ROWS)], in_buf.at[at], in_sem.at[at])
        for at, ref in enumerate((key_ref, value_ref, query_ref))
    ]
    start_all(copies)
    wait_all(copies)
    tails = [in_buf[at].astype(f32)[ROWS:] for at in range(len(copies))]
    out_ref[...] = jnp.concatenate(tails, axis=0).astype(bf16)


def signal_kernel(key_ref, value_ref, feat_ref, rate_ref, u_ref, wide_ref, state_ref, power_scr, last_scr, *columns):
    tokens, tiles = u_ref.shape[0], u_ref.shape[1] // LANES
    modes = rate_ref.shape[0]
    chunks = tiles // TILES
    count = feat_ref.shape[2]
    for member in range(2):
        widened(feat_ref, member + 1, wide_ref, member)
    for column in columns:
        column[pl.ds(0, 2 * ROWS), :] = jnp.zeros((2 * ROWS, LANES), f32)
    last_scr[...] = jnp.zeros(last_scr.shape, f32)

    def powers(at, _):
        through = jnp.exp(-rate_ref[:, span(at)])
        for level in range(4):
            power_scr[level, :, span(at)] = through
            through = through * through
        return 0

    lax.fori_loop(0, chunks, powers, 0)

    def reduce(number):
        lanes = tile_lanes(number)
        for mode in range(modes):
            whole = last_scr[mode]
            for level in (2, 1, 0):
                factor = wide(power_scr[level, mode : mode + 1, lanes])
                whole = factor * whole + pltpu.roll(whole, ROWS - (1 << level), 0)
            state_ref[mode : mode + 1, lanes] = whole[:1]

    def tile(number, _):
        lanes = tile_lanes(number)
        reduce(jnp.maximum(number - 1, 0))
        taps = [chunk_taps(wide_ref, number // TILES, member, number % TILES, count) for member in range(2)]
        for column, ref in zip(columns, (key_ref, value_ref)):
            lay_column(column, ref, lanes)
        decay = [wide(power_scr[3, mode : mode + 1, lanes]) for mode in range(modes)]
        state = None
        parts = [fir(column, some, 2 * ROWS, tokens // ROWS) for column, some in zip(columns, taps)]
        for pair in range(tokens // (2 * ROWS)):
            found = [next(parts[0]) * next(parts[1]) for _ in range(2)]
            if pair == 0:
                found[0] = jnp.where(sublane() < count - 1, 0.0, found[0])
            both = jnp.concatenate(found, axis=0).astype(bf16)
            u_ref[pair * 2 * ROWS : (pair + 1) * 2 * ROWS, lanes] = both
            for u in tiles_of(both):
                if state is None:
                    state = [u] * modes
                else:
                    state = [factor * one + u for factor, one in zip(decay, state)]
        for mode in range(modes):
            last_scr[mode] = state[mode]
        return 0

    lax.fori_loop(0, tiles, tile, 0)
    reduce(tiles - 1)


def head_kernel(key_ref, value_ref, halo_ref, rate_ref, wide_ref, state_ref, u_ref, *rest, tokens, reach):
    out_ref, head_ref, u_out_ref, column_scr, token_scr, total_scr, sem = rest
    move = pltpu.make_async_copy(u_ref, u_out_ref, sem.at[0])
    move.start()
    modes, tiles = state_ref.shape[0], state_ref.shape[1] // LANES
    pieces, piece_modes, piece_width = out_ref.shape

    def some(chunk, _):
        for number in range(TILES):
            lanes = tile_lanes(chunk * TILES + number)
            halo = halo_ref[:, lanes].astype(f32)
            parts = []
            for member in range(2):
                taps = chunk_taps(wide_ref, chunk, member, number, reach + 1)
                column = column_scr.at[number, member]
                column[pl.ds(0, ROWS), :] = jnp.zeros((ROWS, LANES), f32)
                column[pl.ds(ROWS, ROWS), :] = halo[member * ROWS : (member + 1) * ROWS]
                source = (key_ref, value_ref)[member]
                column[pl.ds(2 * ROWS, ROWS), :] = source[: 2 * ROWS, lanes].astype(f32)[:ROWS]
                parts += fir(column, taps, 2 * ROWS, 1)
            u = jnp.where(sublane() < reach, rounded(parts[0] * parts[1]), 0.0)
            token_scr[number] = u
            for group in range(0, modes, ROWS):
                decay = jnp.exp(-rate_ref[group : group + ROWS, lanes])
                head = wide(token_scr[number, :1, :])
                for row in range(1, reach):
                    head = decay * head + wide(token_scr[number, row : row + 1, :])
                total = state_ref[group : group + ROWS, lanes] + power(decay, tokens - reach) * head
                total_scr[group : group + ROWS, lanes] = total
            head_ref[:, lanes] = jnp.concatenate([u, jnp.zeros((ROWS, LANES), f32)], axis=0).astype(bf16)
        return 0

    lax.fori_loop(0, tiles // TILES, some, 0)
    split = pieces * piece_modes // modes
    for piece in range(pieces):
        first, part = piece // split * piece_modes, piece % split
        rows = total_scr[first : first + piece_modes, part * piece_width : (part + 1) * piece_width]
        out_ref[piece] = rows.astype(out_ref.dtype)
    move.wait()


def gate_kernel(query_ref, halo_ref, feat_ref, u_ref, head_ref, rate_ref, coef_ref, skip_ref, gate_ref, *rest, early):
    y_ref, mid_ref, halo_buf, gate_buf, wide_scr, column, small_sem, out_sem = rest[:8]
    inner = rest[8:]
    chunks, tokens = gate_buf.shape[:2]
    count = feat_ref.shape[2]
    halo_copy = pltpu.make_async_copy(halo_ref, halo_buf, small_sem.at[0])
    halo_copy.start()
    widened(feat_ref, 0, wide_scr, 0)
    local_chunk, local_send = local_parts(u_ref, head_ref, rate_ref, coef_ref, skip_ref, y_ref, mid_ref, *inner)
    over_chunks(0, early, local_chunk, local_send)
    halo_copy.wait()
    column[pl.ds(0, ROWS), :] = jnp.zeros((ROWS, LANES), f32)

    def chunk(at):
        def tile(number, _):
            lanes = tile_lanes(number)
            all_lanes = tile_lanes(at * TILES + number)
            taps = chunk_taps(wide_scr, at, 0, number, count)
            column[pl.ds(ROWS, ROWS), :] = halo_buf[:, all_lanes].astype(f32)[2 * ROWS :]
            lay_column(column, query_ref, all_lanes)
            found = list(fir(column, taps, 2 * ROWS, tokens // ROWS))
            for pair in range(tokens // (2 * ROWS)):
                rows = slice(pair * 2 * ROWS, (pair + 1) * 2 * ROWS)
                gate_buf[at, rows, lanes] = jnp.concatenate(found[pair * 2 : pair * 2 + 2], axis=0).astype(bf16)
            return 0

        lax.fori_loop(0, TILES, tile, 0)

    give = columns_out(gate_ref, gate_buf, out_sem)
    over_chunks(0, chunks, chunk, give)
    for at in range(early):
        wait_all(local_send(at))
    for at in range(chunks):
        wait_all(give(at))


def prefix_kernel(piece_ref, rate_ref, coef_ref, out_ref, *, tokens, axes):
    devices, piece_modes, piece_width = piece_ref.shape
    split = devices * piece_modes // rate_ref.shape[0]
    mine = lax.axis_index(axes)
    mode, part = mine // split * piece_modes, mine % split
    group = pl.multiple_of(mode // ROWS * ROWS, ROWS)
    first = pl.multiple_of(part * piece_width, LANES)

    def mine_of(ref):
        rows = ref[pl.ds(group, ROWS), pl.ds(first, piece_width)]
        place = lax.broadcasted_iota(jnp.int32, rows.shape, 0)
        found = [
            jnp.sum(jnp.where(place == mode - group + row, rows, 0.0), axis=0, keepdims=True)
            for row in range(piece_modes)
        ]
        return jnp.concatenate(found, axis=0)

    coef = mine_of(coef_ref)
    through = jnp.exp(-float(tokens) * mine_of(rate_ref))

    def lap(number, entering):
        for step in range(4):
            source = number * 4 + step
            out_ref[source] = (coef * entering).astype(out_ref.dtype)
            entering = through * entering + piece_ref[source].astype(f32)
        return entering

    lax.fori_loop(0, devices // 4, lap, jnp.zeros((piece_modes, piece_width), f32))


def local_kernel(u_ref, head_ref, rate_ref, coef_ref, skip_ref, *rest, first, last):
    chunk, send = local_parts(u_ref, head_ref, rate_ref, coef_ref, skip_ref, *rest[-8:])
    over_chunks(first, last, chunk, send)
    for at in range(first, last):
        wait_all(send(at))


def local_parts(u_ref, head_ref, rate_ref, coef_ref, skip_ref, y_ref, mid_ref, *scratches):
    y_buf, mid_buf, token_scr, sum_scr, out_sem, mid_sem = scratches
    tokens = u_ref.shape[0]
    modes = rate_ref.shape[0]
    half_groups = tokens // ROWS // 2
    give = columns_out(y_ref, y_buf, out_sem)

    def send(at):
        return give(at) + [pltpu.make_async_copy(mid_buf.at[at], mid_ref.at[at], mid_sem.at[at])]

    def chunk(at):
        for pair in range(half_groups):
            block = u_ref[pair * 2 * ROWS : (pair + 1) * 2 * ROWS, span(at)].astype(f32)
            if pair == 0:
                block = block + head_ref[:, span(at)].astype(f32)
            for part in range(2):
                group = pair * 2 + part
                half, within = group // half_groups, group % half_groups
                for tile in range(TILES):
                    piece = lanes_of(block, tile)[part * ROWS : (part + 1) * ROWS]
                    put_tile(token_scr, within, half * TILES + tile, piece)
        (skip,) = spread_rows(skip_ref, at, range(1))
        coef = spread_rows(coef_ref, at, range(modes))
        decay = [jnp.exp(-rate) for rate in spread_rows(rate_ref, at, range(modes))]

        def eight(group, state):
            state = list(state)
            for row in range(ROWS):
                u = get_row(token_scr, group, row)
                state = [factor * one + u for factor, one in zip(decay, state)]
                terms = [factor * one for factor, one in zip([skip] + coef, [u] + state)]
                sum_scr[pl.ds(group * ROWS * ROWS + row, ROWS, stride=ROWS), :] = tree(terms)
            return tuple(state)

        state = lax.fori_loop(0, half_groups, eight, (jnp.zeros((ROWS, LANES), f32),) * modes)
        for mode, (factor, one) in enumerate(zip(coef, state)):
            mid_buf[at, mode] = factor * one
        for group in range(2 * half_groups):
            half, within = group // half_groups, group % half_groups
            for tile in range(TILES):
                slot = (within * ROWS + half * TILES + tile) * ROWS
                rows = slice(group * ROWS, (group + 1) * ROWS)
                y_buf[at, rows, tile * LANES : (tile + 1) * LANES] = sum_scr[pl.ds(slot, ROWS), :]

    return chunk, send


def final_kernel(piece_ref, rate_ref, mid_ref, y_ref, gate_ref, out_ref, *scratches):
    mid_buf, y_buf, gate_buf, out_buf, total_scr, power_scr, lead_scr, in_sem, mid_sem, out_sem = scratches
    chunks, modes = mid_buf.shape[:2]
    tokens = y_buf.shape[1]
    columns = columns_in(((y_ref, y_buf), (gate_ref, gate_buf)), in_sem)

    def fetch(at):
        return columns(at) + [pltpu.make_async_copy(mid_ref.at[at], mid_buf.at[at], mid_sem.at[at])]

    begin(chunks, fetch)
    pieces, piece_modes, piece_width = piece_ref.shape
    split = pieces * piece_modes // modes
    for piece in range(pieces):
        first, part = piece // split * piece_modes, piece % split
        lanes = slice(part * piece_width, (part + 1) * piece_width)
        total_scr[first : first + piece_modes, lanes] = piece_ref[piece].astype(f32)
    bits = [(sublane() >> level) % 2 == 1 for level in range(3)]

    def chunk(at):
        through = jnp.exp(-rate_ref[:, span(at)])
        for level in range(4):
            power_scr[level] = through
            through = through * through

        def tile(number, _):
            lanes = tile_lanes(number)
            state = []
            for mode in range(modes):
                rows = [wide(power_scr[level, mode : mode + 1, lanes]) for level in range(3)]
                lead = rows[0]
                for bit, row in zip(bits, rows):
                    lead = lead * jnp.where(bit, row, 1.0)
                lead_scr[mode] = lead
                state.append(lead * wide(total_scr[mode : mode + 1, tile_lanes(at * TILES + number)]))
            decay = [wide(power_scr[3, mode : mode + 1, lanes]) for mode in range(modes)]
            for pair in range(tokens // (2 * ROWS)):
                rows = slice(pair * 2 * ROWS, (pair + 1) * 2 * ROWS)
                gates = gate_buf[at, rows, lanes].astype(f32)
                sums = []
                for part in range(2):
                    if pair == tokens // (4 * ROWS) and part == 0:
                        state = [
                            one + lead_scr[mode] * wide(mid_buf[at, mode, pl.ds(number, 1), :])
                            for mode, one in enumerate(state)
                        ]
                    here = slice((pair * 2 + part) * ROWS, (pair * 2 + part + 1) * ROWS)
                    sums.append(y_buf[at, here, lanes] + tree(state))
                    state = [factor * one for factor, one in zip(decay, state)]
                out_buf[at, rows, lanes] = (gates * rounded(jnp.concatenate(sums, axis=0))).astype(bf16)
            return 0

        lax.fori_loop(0, TILES, tile, 0)

    give = columns_out(out_ref, out_buf, out_sem)
    over_chunks(0, chunks, with_fetch(chunks, fetch, chunk), give)
    for at in range(chunks):
        wait_all(give(at))


def cost(flops, moved):
    return pl.CostEstimate(flops=int(flops), bytes_accessed=int(moved), transcendentals=0)


def local(query, key_proj, value_proj, featurizer, rates, residues, skip, *, axes):
    tokens, width = query.shape
    modes = rates.shape[0]
    members, taps, groups = featurizer.shape
    devices = math.prod(lax.axis_size(axis) for axis in axes)
    chunks = width // CHUNK
    tiles = width // LANES
    split = devices * 2 // modes
    even = devices * 2 % modes == 0 and tiles % split == 0
    vmem = pltpu.VMEM
    far = pltpu.HBM
    near = jax.ShapeDtypeStruct
    dma = pltpu.SemaphoreType.DMA
    elements = tokens * width

    def call(kernel, inputs, outputs, scratches, name, close=(), **more):
        inputs = [
            value if at in close else pltpu.with_memory_space_constraint(value, far)
            for at, value in enumerate(inputs)
        ]
        beside, there = pl.BlockSpec(memory_space=vmem), pl.BlockSpec(memory_space=far)
        return pl.pallas_call(
            kernel,
            in_specs=[beside if at in close else there for at in range(len(inputs))],
            out_specs=[beside if isinstance(one, near) else there for one in outputs],
            out_shape=outputs,
            scratch_shapes=scratches,
            compiler_params=pltpu.CompilerParams(vmem_limit_bytes=32 * 2**20),
            name=name,
            **more,
        )(*inputs)

    (packed,) = call(
        pack_kernel,
        (key_proj, value_proj, query),
        [near((members * ROWS, width), bf16)],
        [vmem((members, 2 * ROWS, width), bf16), dma((members,))],
        "pack",
    )
    halo = lax.ppermute(packed, axes, [(at, at + 1) for at in range(devices - 1)])

    feat = featurizer.reshape(members, taps, chunks, groups // chunks).transpose(2, 0, 1, 3)
    column = vmem((2 * ROWS + tokens, LANES), f32)
    half_buf, whole_buf = vmem((chunks, tokens, CHUNK), bf16), vmem((chunks, tokens, CHUNK), f32)
    u, wide_taps, state = call(
        signal_kernel,
        (key_proj, value_proj, feat, rates),
        [near((tokens, width), bf16), near((chunks, 2, ROWS, CHUNK), f32), near((modes, width), f32)],
        [vmem((4, modes, width), f32), vmem((modes, ROWS, LANES), f32), column, column],
        "signal",
        close=range(4),
        cost_estimate=cost(60 * elements, 10 * elements),
    )

    pieces = (devices, 2, width // split) if even else (modes // 2, 2, width)
    left, head, u = call(
        functools.partial(head_kernel, tokens=tokens, reach=taps - 1),
        (key_proj, value_proj, halo, rates, wide_taps, state, u),
        [near(pieces, bf16), near((2 * ROWS, width), bf16), far((tokens, width), bf16)],
        [vmem((TILES, 2, 3 * ROWS, LANES), f32), vmem((TILES, ROWS, LANES), f32)]
        + [vmem((modes, width), f32), dma((1,))],
        "head",
        close=range(7),
    )
    left, halo_late, rates_late, skip_late = lax.optimization_barrier((left, halo, rates, skip))
    coef = residues * jnp.sqrt(-jnp.expm1(-2.0 * rates_late) / modes)
    skip_row = skip_late[None, :]
    stage = vmem((tokens // ROWS // 2 * ROWS * ROWS, LANES), f32)
    local_shapes = [far((tokens, width), f32), far((chunks, modes, ROWS, LANES), f32)]
    local_scratches = [whole_buf, vmem((chunks, modes, ROWS, LANES), f32), stage, stage]
    local_scratches += [dma((1, chunks)), dma((chunks,))]
    early = chunks // 3
    gate, y, mid = call(
        functools.partial(gate_kernel, early=early),
        (query, halo_late, feat, u, head, rates, coef, skip_row),
        [far((tokens, width), bf16)] + local_shapes,
        [vmem((members * ROWS, width), bf16), half_buf, vmem((chunks, 1, ROWS, CHUNK), f32), column]
        + [dma((1,)), dma((1, chunks))]
        + local_scratches,
        "gate",
        close=(0, 2, 3, 4, 5, 6, 7),
        cost_estimate=cost(28 * elements, 6 * elements),
    )

    def swap(value):
        return lax.all_to_all(value, axes, split_axis=0, concat_axis=0, tiled=True)

    share = modes * width // devices
    theirs = swap(left if even else left.reshape(devices, share))
    theirs, gate, coef, skip_row, y, mid = lax.optimization_barrier((theirs, gate, coef, skip_row, y, mid))
    if even:
        (entering,) = call(
            functools.partial(prefix_kernel, tokens=tokens, axes=axes),
            (theirs, rates, coef),
            [near(pieces, bf16)],
            [],
            "prefix",
            close=(0, 1, 2),
        )
    else:
        mine = lax.axis_index(axes)
        through = jnp.exp(-float(tokens) * lax.dynamic_slice_in_dim(rates.reshape(-1), mine * share, share))
        factor = lax.dynamic_slice_in_dim(coef.reshape(-1), mine * share, share)
        _, entering = lax.scan(
            lambda so_far, piece: (through * so_far + piece.astype(f32), (factor * so_far).astype(bf16)),
            jnp.zeros((share,), f32),
            theirs,
        )

    entering, y = lax.optimization_barrier((entering, y))
    entered = swap(entering).reshape(pieces)
    y, mid = call(
        functools.partial(local_kernel, first=early, last=chunks),
        (u, head, rates, coef, skip_row, y, mid),
        local_shapes,
        local_scratches,
        "within",
        close=range(5),
        cost_estimate=cost(50 * elements, 8 * elements),
        input_output_aliases={5: 0, 6: 1},
    )

    (out,) = call(
        final_kernel,
        (entered, rates, mid, y, gate),
        [far((tokens, width), bf16)],
        [vmem((chunks, modes, ROWS, LANES), f32), whole_buf, half_buf, half_buf]
        + [vmem((modes, width), f32), vmem((4, modes, CHUNK), f32), vmem((modes, ROWS, LANES), f32)]
        + [dma((2, chunks)), dma((chunks,)), dma((1, chunks))],
        "final",
        close=(0, 1),
        cost_estimate=cost(40 * elements, 10 * elements),
    )
    return out


def solution(mesh):
    axes = tuple(mesh.axis_names)
    placed = (P(axes, None),) * 3 + (P(),) * 4
    return jax.shard_map(
        functools.partial(local, axes=axes),
        mesh=mesh,
        in_specs=placed,
        out_specs=P(axes, None),
        check_vma=False,
    )
```

```python
import functools
import math

import jax
import jax.numpy as jnp
from jax import lax
from jax.experimental import pallas as pl
from jax.experimental.pallas import tpu as pltpu
from jax.sharding import PartitionSpec as P

LANES = 128
ROWS = 8
TILES = 4
CHUNK = TILES * LANES
AHEAD = 4
f32 = jnp.float32
bf16 = jnp.bfloat16


def put_tile(scratch, group, slot, tile):
    scratch[pl.ds((group * ROWS + slot) * ROWS, ROWS), :] = tile


def get_row(scratch, group, row):
    return scratch[pl.ds(group * ROWS * ROWS + row, ROWS, stride=ROWS), :]


def lanes_of(value, tile):
    return value[:, tile * LANES : (tile + 1) * LANES]


def tile_lanes(tile):
    return pl.ds(pl.multiple_of(tile * LANES, LANES), LANES)


def span(at):
    return pl.ds(pl.multiple_of(at * CHUNK, CHUNK), CHUNK)


def wide(row):
    return jnp.broadcast_to(row, (ROWS, LANES))


def sublane():
    return lax.broadcasted_iota(jnp.int32, (ROWS, LANES), 0)


def spread(row_of):
    slot = sublane() % TILES
    result = wide(row_of(TILES - 1))
    for tile in range(TILES - 1):
        result = jnp.where(slot == tile, wide(row_of(tile)), result)
    return result


def spread_rows(ref, at, rows):
    def one(row):
        return spread(lambda tile: ref[row : row + 1, tile_lanes(at * TILES + tile)])

    return [one(row) for row in rows]


def rounded(value):
    return value.astype(bf16).astype(f32)


def tiles_of(block):
    block = block.astype(f32)
    return [block[at : at + ROWS] for at in range(0, block.shape[0], ROWS)]


def fir(column, taps, first, count):
    half = ROWS // 2
    top = sublane() < half

    def seen(start, lags):
        return [column[pl.ds(start - lag, ROWS), :] for lag in range(lags)]

    def far_part(rows):
        total = taps[half] * rows[0]
        for lag in range(half + 1, len(taps)):
            total = total + taps[lag] * rows[lag - half]
        return pltpu.roll(total, half, 0)

    before = far_part(seen(first - ROWS, len(taps) - half))
    for start in range(first, first + count * ROWS, ROWS):
        rows = seen(start, half)
        now = far_part(rows)
        total = taps[0] * rows[0]
        for lag in range(1, half):
            total = total + taps[lag] * rows[lag]
        yield total + jnp.where(top, before, now)
        before = now


def lay_column(column, source, lanes):
    for pair in range(source.shape[0] // (2 * ROWS)):
        rows = slice(pair * 2 * ROWS, (pair + 1) * 2 * ROWS)
        column[pl.ds((pair + 1) * 2 * ROWS, 2 * ROWS), :] = source[rows, lanes].astype(f32)


def chunk_taps(wide_ref, at, member, tile, count):
    return [wide(wide_ref[at, member, lag : lag + 1, tile_lanes(tile)]) for lag in range(count)]


def widened(feat_ref, member, out_ref, position):
    chunks, _, taps, count = feat_ref.shape
    rows = [feat_ref[at, member] for at in range(chunks)]
    rows = [jnp.concatenate([row, jnp.zeros((ROWS - taps, count), f32)], axis=0) for row in rows]
    group = lax.broadcasted_iota(jnp.int32, (count, CHUNK), 0)
    lane = lax.broadcasted_iota(jnp.int32, (count, CHUNK), 1)
    pick = (group == lane // (CHUNK // count)).astype(f32).astype(bf16)
    parts, rest = [], jnp.concatenate(rows, axis=0)
    for _ in range(3):
        term = rest.astype(bf16)
        rest = rest - term.astype(f32)
        parts.append(jnp.dot(term, pick, preferred_element_type=f32))
    out_ref[:, position] = (parts[0] + parts[1] + parts[2]).reshape(chunks, ROWS, CHUNK)


def power(base, exponent):
    result = None
    while exponent:
        if exponent & 1:
            result = base if result is None else result * base
        base = base * base
        exponent >>= 1
    return result


def tree(terms):
    while len(terms) > 1:
        terms = [sum(terms[at + 1 : at + 2], terms[at]) for at in range(0, len(terms), 2)]
    return terms[0]


def start_all(copies):
    for copy in copies:
        copy.start()


def wait_all(copies):
    for copy in copies:
        copy.wait()


def begin(chunks, fetch):
    for at in range(min(AHEAD, chunks)):
        start_all(fetch(at))


def over_chunks(first, last, body, send):
    def one(at, _):
        body(at)
        start_all(send(at))
        return 0

    lax.fori_loop(first, last, one, 0)


def with_fetch(chunks, fetch, body):
    def one(at):
        @pl.when(at + AHEAD < chunks)
        def _():
            start_all(fetch(at + AHEAD))

        wait_all(fetch(at))
        body(at)

    return one


def columns_in(pairs, sem):
    def fetch(at):
        return [
            pltpu.make_async_copy(ref.at[:, span(at)], buf.at[at], sem.at[member, at])
            for member, (ref, buf) in enumerate(pairs)
        ]

    return fetch


def columns_out(ref, buf, sem):
    return lambda at: [pltpu.make_async_copy(buf.at[at], ref.at[:, span(at)], sem.at[0, at])]


def lay_halo(column, halo, member, lanes):
    pairs = halo.shape[0] // 3
    for pair in range(pairs):
        column[pl.ds(2 * ROWS - 2 * pairs + 2 * pair, 2), :] = halo[member * pairs + pair, :, lanes].astype(f32)


def pack_kernel(key_ref, value_ref, query_ref, out_ref, in_buf, in_sem):
    tokens = key_ref.shape[0]
    copies = [
        pltpu.make_async_copy(ref.at[pl.ds(tokens - 2 * ROWS, 2 * ROWS)], in_buf.at[at], in_sem.at[at])
        for at, ref in enumerate((key_ref, value_ref, query_ref))
    ]
    start_all(copies)
    wait_all(copies)
    pairs = out_ref.shape[0] // len(copies)
    for at in range(len(copies)):
        tail = in_buf[at].astype(f32)[2 * ROWS - 2 * pairs :]
        for pair in range(pairs):
            out_ref[at * pairs + pair] = tail[2 * pair : 2 * pair + 2].astype(bf16)


def signal_kernel(key_ref, value_ref, feat_ref, rate_ref, u_ref, wide_ref, state_ref, power_scr, last_scr, *columns):
    tokens, tiles = u_ref.shape[0], u_ref.shape[1] // LANES
    modes = rate_ref.shape[0]
    chunks = tiles // TILES
    count = feat_ref.shape[2]
    for member in range(2):
        widened(feat_ref, member + 1, wide_ref, member)
    for column in columns:
        column[pl.ds(0, 2 * ROWS), :] = jnp.zeros((2 * ROWS, LANES), f32)
    last_scr[...] = jnp.zeros(last_scr.shape, f32)

    def powers(at, _):
        through = jnp.exp(-rate_ref[:, span(at)])
        for level in range(4):
            power_scr[level, :, span(at)] = through
            through = through * through
        return 0

    lax.fori_loop(0, chunks, powers, 0)

    def reduce(number):
        lanes = tile_lanes(number)
        for mode in range(modes):
            whole = last_scr[mode]
            for level in (2, 1, 0):
                factor = wide(power_scr[level, mode : mode + 1, lanes])
                whole = factor * whole + pltpu.roll(whole, ROWS - (1 << level), 0)
            state_ref[mode : mode + 1, lanes] = whole[:1]

    def tile(number, columns):
        lanes = tile_lanes(number)
        reduce(jnp.maximum(number - 1, 0))
        taps = [chunk_taps(wide_ref, number // TILES, member, number % TILES, count) for member in range(2)]
        for column, ref in zip(columns, (key_ref, value_ref)):
            lay_column(column, ref, lanes)
        decay = [wide(power_scr[3, mode : mode + 1, lanes]) for mode in range(modes)]
        state = None
        parts = [fir(column, some, 2 * ROWS, tokens // ROWS) for column, some in zip(columns, taps)]
        for pair in range(tokens // (2 * ROWS)):
            found = [next(parts[0]) * next(parts[1]) for _ in range(2)]
            if pair == 0:
                found[0] = jnp.where(sublane() < count - 1, 0.0, found[0])
            both = jnp.concatenate(found, axis=0).astype(bf16)
            u_ref[pair * 2 * ROWS : (pair + 1) * 2 * ROWS, lanes] = both
            for u in tiles_of(both):
                if state is None:
                    state = [u] * modes
                else:
                    state = [factor * one + u for factor, one in zip(decay, state)]
        for mode in range(modes):
            last_scr[mode] = state[mode]

    def two(number, _):
        tile(2 * number, columns[:2])
        tile(2 * number + 1, columns[2:])
        return 0

    lax.fori_loop(0, tiles // 2, two, 0)
    reduce(tiles - 1)


def head_kernel(key_ref, value_ref, halo_ref, rate_ref, wide_ref, state_ref, u_ref, *rest, tokens, reach):
    out_ref, head_ref, u_out_ref, column_scr, token_scr, total_scr, sem = rest
    move = pltpu.make_async_copy(u_ref, u_out_ref, sem.at[0])
    move.start()
    modes, tiles = state_ref.shape[0], state_ref.shape[1] // LANES
    pieces, piece_modes, piece_width = out_ref.shape

    def some(chunk, _):
        for number in range(TILES):
            lanes = tile_lanes(chunk * TILES + number)
            parts = []
            for member in range(2):
                taps = chunk_taps(wide_ref, chunk, member, number, reach + 1)
                column = column_scr.at[number, member]
                column[pl.ds(0, 2 * ROWS), :] = jnp.zeros((2 * ROWS, LANES), f32)
                lay_halo(column, halo_ref, member, lanes)
                source = (key_ref, value_ref)[member]
                column[pl.ds(2 * ROWS, ROWS), :] = source[: 2 * ROWS, lanes].astype(f32)[:ROWS]
                parts += fir(column, taps, 2 * ROWS, 1)
            u = jnp.where(sublane() < reach, rounded(parts[0] * parts[1]), 0.0)
            token_scr[number] = u
            for group in range(0, modes, ROWS):
                decay = jnp.exp(-rate_ref[group : group + ROWS, lanes])
                head = wide(token_scr[number, :1, :])
                for row in range(1, reach):
                    head = decay * head + wide(token_scr[number, row : row + 1, :])
                total = state_ref[group : group + ROWS, lanes] + power(decay, tokens - reach) * head
                total_scr[group : group + ROWS, lanes] = total
            head_ref[:, lanes] = jnp.concatenate([u, jnp.zeros((ROWS, LANES), f32)], axis=0).astype(bf16)
        return 0

    lax.fori_loop(0, tiles // TILES, some, 0)
    split = pieces * piece_modes // modes
    for piece in range(pieces):
        first, part = piece // split * piece_modes, piece % split
        rows = total_scr[first : first + piece_modes, part * piece_width : (part + 1) * piece_width]
        out_ref[piece] = rows.astype(out_ref.dtype)
    move.wait()


def gate_kernel(query_ref, halo_ref, feat_ref, u_ref, head_ref, rate_ref, coef_ref, skip_ref, gate_ref, *rest, early):
    y_ref, mid_ref, halo_buf, u_buf, gate_buf, wide_scr, column, small_sem, out_sem = rest[:9]
    inner = rest[9:]
    chunks, tokens = gate_buf.shape[:2]
    count = feat_ref.shape[2]
    halo_copy = pltpu.make_async_copy(halo_ref, halo_buf, small_sem.at[0])
    halo_copy.start()
    u_copy = pltpu.make_async_copy(u_ref.at[:, pl.ds(0, early * CHUNK)], u_buf, small_sem.at[1])
    u_copy.start()
    widened(feat_ref, 0, wide_scr, 0)
    local_chunk, local_send = local_parts(u_buf, head_ref, rate_ref, coef_ref, skip_ref, y_ref, mid_ref, *inner)
    halo_copy.wait()
    column[pl.ds(0, 2 * ROWS), :] = jnp.zeros((2 * ROWS, LANES), f32)

    def chunk(at):
        def tile(number, _):
            lanes = tile_lanes(number)
            all_lanes = tile_lanes(at * TILES + number)
            taps = chunk_taps(wide_scr, at, 0, number, count)
            lay_halo(column, halo_buf, 2, all_lanes)
            lay_column(column, query_ref, all_lanes)
            found = list(fir(column, taps, 2 * ROWS, tokens // ROWS))
            for pair in range(tokens // (2 * ROWS)):
                rows = slice(pair * 2 * ROWS, (pair + 1) * 2 * ROWS)
                gate_buf[at, rows, lanes] = jnp.concatenate(found[pair * 2 : pair * 2 + 2], axis=0).astype(bf16)
            return 0

        lax.fori_loop(0, TILES, tile, 0)

    give = columns_out(gate_ref, gate_buf, out_sem)
    over_chunks(0, chunks, chunk, give)
    u_copy.wait()
    over_chunks(0, early, local_chunk, local_send)
    for at in range(early):
        wait_all(local_send(at))
    for at in range(chunks):
        wait_all(give(at))


def prefix_kernel(piece_ref, rate_ref, coef_ref, out_ref, *, tokens, axes):
    devices, piece_modes, piece_width = piece_ref.shape
    split = devices * piece_modes // rate_ref.shape[0]
    mine = devices - 1 - lax.axis_index(axes)
    mode, part = mine // split * piece_modes, mine % split
    group = pl.multiple_of(mode // ROWS * ROWS, ROWS)
    first = pl.multiple_of(part * piece_width, LANES)

    def mine_of(ref):
        rows = ref[pl.ds(group, ROWS), pl.ds(first, piece_width)]
        place = lax.broadcasted_iota(jnp.int32, rows.shape, 0)
        found = [
            jnp.sum(jnp.where(place == mode - group + row, rows, 0.0), axis=0, keepdims=True)
            for row in range(piece_modes)
        ]
        return jnp.concatenate(found, axis=0)

    coef = mine_of(coef_ref)
    through = jnp.exp(-float(tokens) * mine_of(rate_ref))

    def lap(number, entering):
        for step in range(4):
            source = devices - 1 - (number * 4 + step)
            out_ref[source] = (coef * entering).astype(out_ref.dtype)
            entering = through * entering + piece_ref[source].astype(f32)
        return entering

    lax.fori_loop(0, devices // 4, lap, jnp.zeros((piece_modes, piece_width), f32))


def local_kernel(u_ref, head_ref, rate_ref, coef_ref, skip_ref, *rest, first, last):
    chunk, send = local_parts(u_ref, head_ref, rate_ref, coef_ref, skip_ref, *rest[-8:])
    over_chunks(first, last, chunk, send)
    for at in range(first, last):
        wait_all(send(at))


def local_parts(u_ref, head_ref, rate_ref, coef_ref, skip_ref, y_ref, mid_ref, *scratches):
    y_buf, mid_buf, token_scr, sum_scr, out_sem, mid_sem = scratches
    tokens = u_ref.shape[0]
    modes = rate_ref.shape[0]
    half_groups = tokens // ROWS // 2
    give = columns_out(y_ref, y_buf, out_sem)

    def send(at):
        return give(at) + [pltpu.make_async_copy(mid_buf.at[at], mid_ref.at[at], mid_sem.at[at])]

    def chunk(at):
        for pair in range(half_groups):
            block = u_ref[pair * 2 * ROWS : (pair + 1) * 2 * ROWS, span(at)].astype(f32)
            if pair == 0:
                block = block + head_ref[:, span(at)].astype(f32)
            for part in range(2):
                group = pair * 2 + part
                half, within = group // half_groups, group % half_groups
                for tile in range(TILES):
                    piece = lanes_of(block, tile)[part * ROWS : (part + 1) * ROWS]
                    put_tile(token_scr, within, half * TILES + tile, piece)
        (skip,) = spread_rows(skip_ref, at, range(1))
        coef = spread_rows(coef_ref, at, range(modes))
        decay = [jnp.exp(-rate) for rate in spread_rows(rate_ref, at, range(modes))]

        def eight(group, state):
            state = list(state)
            for row in range(ROWS):
                u = get_row(token_scr, group, row)
                state = [factor * one + u for factor, one in zip(decay, state)]
                terms = [factor * one for factor, one in zip([skip] + coef, [u] + state)]
                sum_scr[pl.ds(group * ROWS * ROWS + row, ROWS, stride=ROWS), :] = tree(terms)
            return tuple(state)

        state = lax.fori_loop(0, half_groups, eight, (jnp.zeros((ROWS, LANES), f32),) * modes)
        for mode, (factor, one) in enumerate(zip(coef, state)):
            mid_buf[at, mode] = factor * one
        for group in range(2 * half_groups):
            half, within = group // half_groups, group % half_groups
            for tile in range(TILES):
                slot = (within * ROWS + half * TILES + tile) * ROWS
                rows = slice(group * ROWS, (group + 1) * ROWS)
                y_buf[at, rows, tile * LANES : (tile + 1) * LANES] = sum_scr[pl.ds(slot, ROWS), :]

    return chunk, send


def final_kernel(piece_ref, rate_ref, mid_ref, y_ref, gate_ref, out_ref, *scratches):
    mid_buf, y_buf, gate_buf, out_buf, total_scr, power_scr, lead_scr, in_sem, mid_sem, out_sem = scratches
    chunks, modes = mid_buf.shape[:2]
    tokens = y_buf.shape[1]
    columns = columns_in(((y_ref, y_buf), (gate_ref, gate_buf)), in_sem)

    def fetch(at):
        return columns(at) + [pltpu.make_async_copy(mid_ref.at[at], mid_buf.at[at], mid_sem.at[at])]

    begin(chunks, fetch)
    pieces, piece_modes, piece_width = piece_ref.shape
    split = pieces * piece_modes // modes
    for piece in range(pieces):
        first, part = piece // split * piece_modes, piece % split
        lanes = slice(part * piece_width, (part + 1) * piece_width)
        total_scr[first : first + piece_modes, lanes] = piece_ref[piece].astype(f32)
    bits = [(sublane() >> level) % 2 == 1 for level in range(3)]

    def chunk(at):
        through = jnp.exp(-rate_ref[:, span(at)])
        for level in range(4):
            power_scr[level] = through
            through = through * through

        def tile(number, lead_scr):
            lanes = tile_lanes(number)
            state = []
            for mode in range(modes):
                rows = [wide(power_scr[level, mode : mode + 1, lanes]) for level in range(3)]
                lead = jnp.where(bits[0], rows[1], rows[0])
                for bit, row in zip(bits[1:], rows[1:]):
                    lead = lead * jnp.where(bit, row, 1.0)
                lead_scr[mode] = lead
                state.append(lead * wide(total_scr[mode : mode + 1, tile_lanes(at * TILES + number)]))
            decay = [wide(power_scr[3, mode : mode + 1, lanes]) for mode in range(modes)]
            for pair in range(tokens // (2 * ROWS)):
                rows = slice(pair * 2 * ROWS, (pair + 1) * 2 * ROWS)
                gates = gate_buf[at, rows, lanes].astype(f32)
                sums = []
                for part in range(2):
                    if pair == tokens // (4 * ROWS) and part == 0:
                        state = [
                            one + lead_scr[mode] * wide(mid_buf[at, mode, pl.ds(number, 1), :])
                            for mode, one in enumerate(state)
                        ]
                    here = slice((pair * 2 + part) * ROWS, (pair * 2 + part + 1) * ROWS)
                    sums.append(y_buf[at, here, lanes] + tree(state))
                    state = [factor * one for factor, one in zip(decay, state)]
                out_buf[at, rows, lanes] = (gates * rounded(jnp.concatenate(sums, axis=0))).astype(bf16)

        def two(number, _):
            tile(2 * number, lead_scr.at[0])
            tile(2 * number + 1, lead_scr.at[1])
            return 0

        lax.fori_loop(0, TILES // 2, two, 0)

    give = columns_out(out_ref, out_buf, out_sem)
    over_chunks(0, chunks, with_fetch(chunks, fetch, chunk), give)
    for at in range(chunks):
        wait_all(give(at))


def cost(flops, moved):
    return pl.CostEstimate(flops=int(flops), bytes_accessed=int(moved), transcendentals=0)


def local(query, key_proj, value_proj, featurizer, rates, residues, skip, *, axes):
    tokens, width = query.shape
    modes = rates.shape[0]
    members, taps, groups = featurizer.shape
    devices = math.prod(lax.axis_size(axis) for axis in axes)
    chunks = width // CHUNK
    tiles = width // LANES
    split = devices * 2 // modes
    even = devices * 2 % modes == 0 and tiles % split == 0
    vmem = pltpu.VMEM
    far = pltpu.HBM
    near = jax.ShapeDtypeStruct
    dma = pltpu.SemaphoreType.DMA
    elements = tokens * width

    def call(kernel, inputs, outputs, scratches, name, close=(), **more):
        inputs = [
            value if at in close else pltpu.with_memory_space_constraint(value, far)
            for at, value in enumerate(inputs)
        ]
        beside, there = pl.BlockSpec(memory_space=vmem), pl.BlockSpec(memory_space=far)
        return pl.pallas_call(
            kernel,
            in_specs=[beside if at in close else there for at in range(len(inputs))],
            out_specs=[beside if isinstance(one, near) else there for one in outputs],
            out_shape=outputs,
            scratch_shapes=scratches,
            compiler_params=pltpu.CompilerParams(vmem_limit_bytes=32 * 2**20),
            name=name,
            **more,
        )(*inputs)

    halo_shape = (members * (taps - 1) // 2, 2, width)
    (packed,) = call(
        pack_kernel,
        (key_proj, value_proj, query),
        [near(halo_shape, bf16)],
        [vmem((members, 2 * ROWS, width), bf16), dma((members,))],
        "pack",
    )
    halo = lax.ppermute(packed, axes, [(at, at + 1) for at in range(devices - 1)])

    feat = featurizer.reshape(members, taps, chunks, groups // chunks).transpose(2, 0, 1, 3)
    column = vmem((2 * ROWS + tokens, LANES), f32)
    half_buf, whole_buf = vmem((chunks, tokens, CHUNK), bf16), vmem((chunks, tokens, CHUNK), f32)
    u, wide_taps, state = call(
        signal_kernel,
        (key_proj, value_proj, feat, rates),
        [near((tokens, width), bf16), near((chunks, 2, ROWS, CHUNK), f32), near((modes, width), f32)],
        [vmem((4, modes, width), f32), vmem((modes, ROWS, LANES), f32)] + [column] * 4,
        "signal",
        close=range(4),
        cost_estimate=cost(60 * elements, 10 * elements),
    )

    pieces = (devices, 2, width // split) if even else (modes // 2, 2, width)
    left, head, u = call(
        functools.partial(head_kernel, tokens=tokens, reach=taps - 1),
        (key_proj, value_proj, halo, rates, wide_taps, state, u),
        [near(pieces, bf16), near((2 * ROWS, width), bf16), far((tokens, width), bf16)],
        [vmem((TILES, 2, 3 * ROWS, LANES), f32), vmem((TILES, ROWS, LANES), f32)]
        + [vmem((modes, width), f32), dma((1,))],
        "head",
        close=range(7),
    )
    left, halo_late, rates_late, skip_late = lax.optimization_barrier((left, halo, rates, skip))
    coef = residues * jnp.sqrt(-jnp.expm1(-2.0 * rates_late) / modes)
    skip_row = skip_late[None, :]
    stage = vmem((tokens // ROWS // 2 * ROWS * ROWS, LANES), f32)
    local_shapes = [far((tokens, width), f32), far((chunks, modes, ROWS, LANES), f32)]
    local_scratches = [whole_buf, vmem((chunks, modes, ROWS, LANES), f32), stage, stage]
    local_scratches += [dma((1, chunks)), dma((chunks,))]
    early = chunks * 4 // 9
    gate, y, mid = call(
        functools.partial(gate_kernel, early=early),
        (query, halo_late, feat, u, head, rates, coef, skip_row),
        [far((tokens, width), bf16)] + local_shapes,
        [vmem(halo_shape, bf16), vmem((tokens, early * CHUNK), bf16), half_buf]
        + [vmem((chunks, 1, ROWS, CHUNK), f32), column, dma((2,)), dma((1, chunks))]
        + local_scratches,
        "gate",
        close=(0, 2, 4, 5, 6, 7),
        cost_estimate=cost(28 * elements, 6 * elements),
    )

    def swap(value):
        order = [list(range(devices))[::-1]]
        return lax.all_to_all(value, axes, split_axis=0, concat_axis=0, axis_index_groups=order, tiled=True)

    share = modes * width // devices
    theirs = swap(left if even else left.reshape(devices, share))
    theirs, gate, coef, skip_row, y, mid = lax.optimization_barrier((theirs, gate, coef, skip_row, y, mid))
    if even:
        (entering,) = call(
            functools.partial(prefix_kernel, tokens=tokens, axes=axes),
            (theirs, rates, coef),
            [near(pieces, bf16)],
            [],
            "prefix",
            close=(0, 1, 2),
        )
    else:
        mine = devices - 1 - lax.axis_index(axes)
        through = jnp.exp(-float(tokens) * lax.dynamic_slice_in_dim(rates.reshape(-1), mine * share, share))
        factor = lax.dynamic_slice_in_dim(coef.reshape(-1), mine * share, share)
        _, entering = lax.scan(
            lambda so_far, piece: (through * so_far + piece.astype(f32), (factor * so_far).astype(bf16)),
            jnp.zeros((share,), f32),
            theirs,
            reverse=True,
        )

    entering, y = lax.optimization_barrier((entering, y))
    entered = swap(entering).reshape(pieces)
    y, mid = call(
        functools.partial(local_kernel, first=early, last=chunks),
        (u, head, rates, coef, skip_row, y, mid),
        local_shapes,
        local_scratches,
        "within",
        close=range(5),
        cost_estimate=cost(50 * elements, 8 * elements),
        input_output_aliases={5: 0, 6: 1},
    )

    (out,) = call(
        final_kernel,
        (entered, rates, mid, y, gate),
        [far((tokens, width), bf16)],
        [vmem((chunks, modes, ROWS, LANES), f32), whole_buf, half_buf, half_buf]
        + [vmem((modes, width), f32), vmem((4, modes, CHUNK), f32), vmem((2, modes, ROWS, LANES), f32)]
        + [dma((2, chunks)), dma((chunks,)), dma((1, chunks))],
        "final",
        close=(0, 1),
        cost_estimate=cost(40 * elements, 10 * elements),
    )
    return out


def solution(mesh):
    axes = tuple(mesh.axis_names)
    placed = (P(axes, None),) * 3 + (P(),) * 4
    return jax.shard_map(
        functools.partial(local, axes=axes),
        mesh=mesh,
        in_specs=placed,
        out_specs=P(axes, None),
        check_vma=False,
    )
```

```python
import functools
import math

import jax
import jax.numpy as jnp
from jax import lax
from jax.experimental import pallas as pl
from jax.experimental.pallas import tpu as pltpu
from jax.sharding import PartitionSpec as P

LANES = 128
ROWS = 8
TILES = 4
CHUNK = TILES * LANES
AHEAD = 4
LAP = 4
f32 = jnp.float32
bf16 = jnp.bfloat16


def put_tile(scratch, group, slot, tile):
    scratch[pl.ds((group * ROWS + slot) * ROWS, ROWS), :] = tile


def get_row(scratch, group, row):
    return scratch[pl.ds(group * ROWS * ROWS + row, ROWS, stride=ROWS), :]


def lanes_of(value, tile):
    return value[:, tile * LANES : (tile + 1) * LANES]


def tile_lanes(tile):
    return pl.ds(pl.multiple_of(tile * LANES, LANES), LANES)


def span(at):
    return pl.ds(pl.multiple_of(at * CHUNK, CHUNK), CHUNK)


def wide(row):
    return jnp.broadcast_to(row, (ROWS, LANES))


def first_half():
    return lax.broadcasted_iota(jnp.int32, (ROWS, LANES), 0) < TILES


def sublane():
    return lax.broadcasted_iota(jnp.int32, (ROWS, LANES), 0)


def spread(row_of):
    slot = sublane() % TILES
    result = wide(row_of(TILES - 1))
    for tile in range(TILES - 1):
        result = jnp.where(slot == tile, wide(row_of(tile)), result)
    return result


def spread_rows(ref, at, rows):
    def one(row):
        return spread(lambda tile: ref[row : row + 1, tile_lanes(at * TILES + tile)])

    return [one(row) for row in rows]


def rounded(value):
    return value.astype(bf16).astype(f32)


def tiles_of(block):
    block = block.astype(f32)
    return [block[at : at + ROWS] for at in range(0, block.shape[0], ROWS)]


def fir(column, taps, first, count):
    half = ROWS // 2
    top = sublane() < half

    def seen(start, lags):
        return [column[pl.ds(start - lag, ROWS), :] for lag in range(lags)]

    def far_part(rows):
        total = taps[half] * rows[0]
        for lag in range(half + 1, len(taps)):
            total = total + taps[lag] * rows[lag - half]
        return pltpu.roll(total, half, 0)

    before = far_part(seen(first - ROWS, len(taps) - half))
    for start in range(first, first + count * ROWS, ROWS):
        rows = seen(start, half)
        now = far_part(rows)
        total = taps[0] * rows[0]
        for lag in range(1, half):
            total = total + taps[lag] * rows[lag]
        yield total + jnp.where(top, before, now)
        before = now


def lay_column(column, source, lanes):
    for pair in range(source.shape[0] // (2 * ROWS)):
        rows = slice(pair * 2 * ROWS, (pair + 1) * 2 * ROWS)
        column[pl.ds((pair + 1) * 2 * ROWS, 2 * ROWS), :] = source[rows, lanes].astype(f32)


def chunk_taps(wide_ref, at, member, tile, count):
    return [wide(wide_ref[at, member, lag : lag + 1, tile_lanes(tile)]) for lag in range(count)]


def widened(feat_ref, member, out_ref, position):
    chunks, taps = out_ref.shape[0], feat_ref.shape[1]
    count = feat_ref.shape[2] // chunks
    rows = [feat_ref[member, :, at * count : (at + 1) * count] for at in range(chunks)]
    rows = [jnp.concatenate([row, jnp.zeros((ROWS - taps, count), f32)], axis=0) for row in rows]
    group = lax.broadcasted_iota(jnp.int32, (count, CHUNK), 0)
    lane = lax.broadcasted_iota(jnp.int32, (count, CHUNK), 1)
    pick = (group == lane // (CHUNK // count)).astype(f32).astype(bf16)
    parts, rest = [], jnp.concatenate(rows, axis=0)
    for _ in range(3):
        term = rest.astype(bf16)
        rest = rest - term.astype(f32)
        parts.append(jnp.dot(term, pick, preferred_element_type=f32))
    out_ref[:, position] = (parts[0] + parts[1] + parts[2]).reshape(chunks, ROWS, CHUNK)


def power(base, exponent):
    result = None
    while exponent:
        if exponent & 1:
            result = base if result is None else result * base
        base = base * base
        exponent >>= 1
    return result


def tree(terms):
    while len(terms) > 1:
        terms = [sum(terms[at + 1 : at + 2], terms[at]) for at in range(0, len(terms), 2)]
    return terms[0]


def start_all(copies):
    for copy in copies:
        copy.start()


def wait_all(copies):
    for copy in copies:
        copy.wait()


def begin(chunks, fetch):
    for at in range(min(AHEAD, chunks)):
        start_all(fetch(at))


def over_chunks(first, last, body, send):
    def one(at, _):
        body(at)
        start_all(send(at))
        return 0

    lax.fori_loop(first, last, one, 0)


def with_fetch(chunks, fetch, body):
    def one(at):
        @pl.when(at + AHEAD < chunks)
        def _():
            start_all(fetch(at + AHEAD))

        wait_all(fetch(at))
        body(at)

    return one


def columns_in(pairs, sem):
    def fetch(at):
        return [
            pltpu.make_async_copy(ref.at[:, span(at)], buf.at[at], sem.at[member, at])
            for member, (ref, buf) in enumerate(pairs)
        ]

    return fetch


def columns_out(ref, buf, sem):
    return lambda at: [pltpu.make_async_copy(buf.at[at], ref.at[:, span(at)], sem.at[0, at])]


def lay_halo(column, halo, member, lanes):
    pairs = halo.shape[0] // 3
    for pair in range(pairs):
        column[pl.ds(2 * ROWS - 2 * pairs + 2 * pair, 2), :] = halo[member * pairs + pair, :, lanes].astype(f32)


def pack_kernel(key_ref, value_ref, query_ref, out_ref, in_buf, in_sem):
    tokens = key_ref.shape[0]
    copies = [
        pltpu.make_async_copy(ref.at[pl.ds(tokens - 2 * ROWS, 2 * ROWS)], in_buf.at[at], in_sem.at[at])
        for at, ref in enumerate((key_ref, value_ref, query_ref))
    ]
    start_all(copies)
    wait_all(copies)
    pairs = out_ref.shape[0] // len(copies)
    for at in range(len(copies)):
        tail = in_buf[at].astype(f32)[2 * ROWS - 2 * pairs :]
        for pair in range(pairs):
            out_ref[at * pairs + pair] = tail[2 * pair : 2 * pair + 2].astype(bf16)


def signal_kernel(key_ref, value_ref, feat_ref, rate_ref, u_ref, wide_ref, state_ref, power_scr, last_scr, *columns):
    tokens, tiles = u_ref.shape[0], u_ref.shape[1] // LANES
    modes = rate_ref.shape[0]
    chunks = tiles // TILES
    count = feat_ref.shape[1]
    for member in range(2):
        widened(feat_ref, member + 1, wide_ref, member)
    for column in columns:
        column[pl.ds(0, 2 * ROWS), :] = jnp.zeros((2 * ROWS, LANES), f32)
    last_scr[...] = jnp.zeros(last_scr.shape, f32)

    def powers(at, _):
        through = jnp.exp(-rate_ref[:, span(at)])
        for level in range(4):
            power_scr[level, :, span(at)] = through
            through = through * through
        return 0

    lax.fori_loop(0, chunks, powers, 0)

    def reduce(number):
        lanes = tile_lanes(number)
        for mode in range(modes):
            whole = last_scr[mode]
            for level in (2, 1, 0):
                factor = wide(power_scr[level, mode : mode + 1, lanes])
                whole = factor * whole + pltpu.roll(whole, ROWS - (1 << level), 0)
            state_ref[mode : mode + 1, lanes] = whole[:1]

    def tile(number, columns):
        lanes = tile_lanes(number)
        reduce(jnp.maximum(number - 1, 0))
        taps = [chunk_taps(wide_ref, number // TILES, member, number % TILES, count) for member in range(2)]
        for column, ref in zip(columns, (key_ref, value_ref)):
            lay_column(column, ref, lanes)
        decay = [wide(power_scr[3, mode : mode + 1, lanes]) for mode in range(modes)]
        state = None
        parts = [fir(column, some, 2 * ROWS, tokens // ROWS) for column, some in zip(columns, taps)]
        for pair in range(tokens // (2 * ROWS)):
            found = [next(parts[0]) * next(parts[1]) for _ in range(2)]
            if pair == 0:
                found[0] = jnp.where(sublane() < count - 1, 0.0, found[0])
            both = jnp.concatenate(found, axis=0).astype(bf16)
            u_ref[pair * 2 * ROWS : (pair + 1) * 2 * ROWS, lanes] = both
            for u in tiles_of(both):
                if state is None:
                    state = [u] * modes
                else:
                    state = [factor * one + u for factor, one in zip(decay, state)]
        for mode in range(modes):
            last_scr[mode] = state[mode]

    def some(number, _):
        for part in range(TILES):
            tile(TILES * number + part, columns[2 * part : 2 * part + 2])
        return 0

    lax.fori_loop(0, tiles // TILES, some, 0)
    reduce(tiles - 1)


def head_kernel(key_ref, value_ref, halo_ref, rate_ref, wide_ref, state_ref, u_ref, *rest, tokens, reach):
    out_ref, head_ref, u_out_ref, column_scr, token_scr, total_scr, sem = rest
    move = pltpu.make_async_copy(u_ref, u_out_ref, sem.at[0])
    move.start()
    modes, tiles = state_ref.shape[0], state_ref.shape[1] // LANES
    pieces, piece_modes, piece_width = out_ref.shape

    def some(chunk, _):
        for number in range(TILES):
            lanes = tile_lanes(chunk * TILES + number)
            parts = []
            for member in range(2):
                taps = chunk_taps(wide_ref, chunk, member, number, reach + 1)
                column = column_scr.at[number, member]
                column[pl.ds(0, 2 * ROWS), :] = jnp.zeros((2 * ROWS, LANES), f32)
                lay_halo(column, halo_ref, member, lanes)
                source = (key_ref, value_ref)[member]
                column[pl.ds(2 * ROWS, ROWS), :] = source[: 2 * ROWS, lanes].astype(f32)[:ROWS]
                parts += fir(column, taps, 2 * ROWS, 1)
            u = jnp.where(sublane() < reach, rounded(parts[0] * parts[1]), 0.0)
            token_scr[number] = u
            for group in range(0, modes, ROWS):
                decay = jnp.exp(-rate_ref[group : group + ROWS, lanes])
                head = wide(token_scr[number, :1, :])
                for row in range(1, reach):
                    head = decay * head + wide(token_scr[number, row : row + 1, :])
                total = state_ref[group : group + ROWS, lanes] + power(decay, tokens - reach) * head
                total_scr[group : group + ROWS, lanes] = total
            head_ref[:, lanes] = jnp.concatenate([u, jnp.zeros((ROWS, LANES), f32)], axis=0).astype(bf16)
        return 0

    lax.fori_loop(0, tiles // TILES, some, 0)
    split = pieces * piece_modes // modes
    for piece in range(pieces):
        first, part = piece // split * piece_modes, piece % split
        rows = total_scr[first : first + piece_modes, part * piece_width : (part + 1) * piece_width]
        out_ref[piece] = rows.astype(out_ref.dtype)
    move.wait()


def gate_kernel(query_ref, halo_ref, feat_ref, u_ref, head_ref, rate_ref, coef_ref, skip_ref, gate_ref, *rest, early):
    y_ref, halo_buf, u_buf, gate_buf, wide_scr, column, small_sem, out_sem = rest[:8]
    inner = rest[8:]
    chunks, tokens = gate_buf.shape[:2]
    count = feat_ref.shape[1]
    halo_copy = pltpu.make_async_copy(halo_ref, halo_buf, small_sem.at[0])
    halo_copy.start()
    u_copy = pltpu.make_async_copy(u_ref.at[:, pl.ds(0, early * CHUNK)], u_buf, small_sem.at[1])
    u_copy.start()
    widened(feat_ref, 0, wide_scr, 0)
    local_chunk, local_send = local_parts(u_buf, head_ref, rate_ref, coef_ref, skip_ref, y_ref, *inner)
    halo_copy.wait()
    column[pl.ds(0, 2 * ROWS), :] = jnp.zeros((2 * ROWS, LANES), f32)

    def chunk(at):
        def tile(number, _):
            lanes = tile_lanes(number)
            all_lanes = tile_lanes(at * TILES + number)
            taps = chunk_taps(wide_scr, at, 0, number, count)
            lay_halo(column, halo_buf, 2, all_lanes)
            lay_column(column, query_ref, all_lanes)
            found = list(fir(column, taps, 2 * ROWS, tokens // ROWS))
            for pair in range(tokens // (2 * ROWS)):
                rows = slice(pair * 2 * ROWS, (pair + 1) * 2 * ROWS)
                gate_buf[at, rows, lanes] = jnp.concatenate(found[pair * 2 : pair * 2 + 2], axis=0).astype(bf16)
            return 0

        lax.fori_loop(0, TILES, tile, 0)

    give = columns_out(gate_ref, gate_buf, out_sem)
    over_chunks(0, chunks, chunk, give)
    u_copy.wait()
    over_chunks(0, early, local_chunk, local_send)
    for at in range(early):
        wait_all(local_send(at))
    for at in range(chunks):
        wait_all(give(at))


def prefix_kernel(piece_ref, rate_ref, coef_ref, out_ref, *, tokens, axes):
    devices, piece_modes, piece_width = piece_ref.shape
    split = devices * piece_modes // rate_ref.shape[0]
    mine = devices - 1 - lax.axis_index(axes)
    mode, part = mine // split * piece_modes, mine % split
    group = pl.multiple_of(mode // ROWS * ROWS, ROWS)
    first = pl.multiple_of(part * piece_width, LANES)

    def mine_of(ref):
        rows = ref[pl.ds(group, ROWS), pl.ds(first, piece_width)]
        place = lax.broadcasted_iota(jnp.int32, rows.shape, 0)
        found = [
            jnp.sum(jnp.where(place == mode - group + row, rows, 0.0), axis=0, keepdims=True)
            for row in range(piece_modes)
        ]
        return jnp.concatenate(found, axis=0)

    coef = mine_of(coef_ref)
    through = jnp.exp(-float(tokens) * mine_of(rate_ref))

    def lap(number, entering):
        for step in range(4):
            source = devices - 1 - (number * 4 + step)
            out_ref[source] = (coef * entering).astype(out_ref.dtype)
            entering = through * entering + piece_ref[source].astype(f32)
        return entering

    lax.fori_loop(0, devices // 4, lap, jnp.zeros((piece_modes, piece_width), f32))


def local_kernel(u_ref, head_ref, rate_ref, coef_ref, skip_ref, *rest, first, last):
    chunk, send = local_parts(u_ref, head_ref, rate_ref, coef_ref, skip_ref, *rest[-5:])
    over_chunks(first, last, chunk, send)
    for at in range(first, last):
        wait_all(send(at))


def local_parts(u_ref, head_ref, rate_ref, coef_ref, skip_ref, y_ref, *scratches):
    y_buf, token_scr, sum_scr, out_sem = scratches
    tokens = u_ref.shape[0]
    modes = rate_ref.shape[0]
    half_groups = tokens // ROWS // 2
    top = first_half()

    def chunk(at):
        for pair in range(half_groups):
            block = u_ref[pair * 2 * ROWS : (pair + 1) * 2 * ROWS, span(at)].astype(f32)
            if pair == 0:
                block = block + head_ref[:, span(at)].astype(f32)
            for part in range(2):
                group = pair * 2 + part
                half, within = group // half_groups, group % half_groups
                for tile in range(TILES):
                    piece = lanes_of(block, tile)[part * ROWS : (part + 1) * ROWS]
                    put_tile(token_scr, within, half * TILES + tile, piece)
        (skip,) = spread_rows(skip_ref, at, range(1))
        coef = spread_rows(coef_ref, at, range(modes))
        decay = [jnp.exp(-rate) for rate in spread_rows(rate_ref, at, range(modes))]

        def eight(group, state):
            state = list(state)
            for row in range(ROWS):
                u = get_row(token_scr, group, row)
                state = [factor * one + u for factor, one in zip(decay, state)]
                terms = [factor * one for factor, one in zip([skip] + coef, [u] + state)]
                sum_scr[pl.ds(group * ROWS * ROWS + row, ROWS, stride=ROWS), :] = tree(terms)
            return tuple(state)

        state = lax.fori_loop(0, half_groups, eight, (jnp.zeros((ROWS, LANES), f32),) * modes)
        carried = tuple(
            jnp.where(top, 0.0, pltpu.roll(factor * one, TILES, 0)) for factor, one in zip(coef, state)
        )

        def eight_more(group, carried):
            for row in range(ROWS):
                carried = [factor * one for factor, one in zip(decay, carried)]
                place = pl.ds(group * ROWS * ROWS + row, ROWS, stride=ROWS)
                sum_scr[place, :] = sum_scr[place, :] + tree(carried)
            return tuple(carried)

        lax.fori_loop(0, half_groups, eight_more, carried)
        for group in range(2 * half_groups):
            half, within = group // half_groups, group % half_groups
            for tile in range(TILES):
                slot = (within * ROWS + half * TILES + tile) * ROWS
                rows = slice(group * ROWS, (group + 1) * ROWS)
                y_buf[at, rows, tile * LANES : (tile + 1) * LANES] = sum_scr[pl.ds(slot, ROWS), :]

    return chunk, columns_out(y_ref, y_buf, out_sem)


def final_kernel(piece_ref, rate_ref, y_ref, gate_ref, out_ref, *scratches, axes):
    y_buf, gate_buf, out_buf, total_scr, power_scr, in_sem, out_sem = scratches
    chunks, tokens = y_buf.shape[:2]
    modes = rate_ref.shape[0]
    fetch = columns_in(((y_ref, y_buf), (gate_ref, gate_buf)), in_sem)
    give = columns_out(out_ref, out_buf, out_sem)
    start_all(fetch(0))
    bits = [(sublane() >> level) % 2 == 1 for level in range(3)]
    pairs = [slice(first, first + 2 * ROWS) for first in range(0, tokens, 2 * ROWS)]

    def finish(at, rows, lanes, sums):
        gates = gate_buf[at, rows, lanes].astype(f32)
        out_buf[at, rows, lanes] = (gates * rounded(sums)).astype(bf16)

    def chunk(at):
        through = jnp.exp(-rate_ref[:, span(at)])
        for level in range(4):
            power_scr[level] = through
            through = through * through

        def tile(number):
            lanes = tile_lanes(number)
            state = []
            for mode in range(modes):
                rows = [wide(power_scr[level, mode : mode + 1, lanes]) for level in range(3)]
                lead = jnp.where(bits[0], rows[1], rows[0])
                for bit, row in zip(bits[1:], rows[1:]):
                    lead = lead * jnp.where(bit, row, 1.0)
                state.append(lead * wide(total_scr[mode : mode + 1, tile_lanes(at * TILES + number)]))
            decay = [wide(power_scr[3, mode : mode + 1, lanes]) for mode in range(modes)]
            for rows in pairs:
                sums = []
                for first in (rows.start, rows.start + ROWS):
                    sums.append(y_buf[at, first : first + ROWS, lanes] + tree(state))
                    state = [factor * one for factor, one in zip(decay, state)]
                finish(at, rows, lanes, jnp.concatenate(sums, axis=0))

        def some(number, _):
            for part in range(LAP):
                tile(number * LAP + part)
            return 0

        lax.fori_loop(0, TILES // LAP, some, 0)

    def chunk_alone(at):
        def tile(number, _):
            lanes = tile_lanes(number)
            for rows in pairs:
                finish(at, rows, lanes, y_buf[at, rows, lanes])
            return 0

        lax.fori_loop(0, TILES, tile, 0)

    def begin_others():
        for at in range(1, min(AHEAD, chunks)):
            start_all(fetch(at))

    first = lax.axis_index(axes) == 0

    @pl.when(first)
    def _():
        begin_others()
        over_chunks(0, chunks, with_fetch(chunks, fetch, chunk_alone), give)

    @pl.when(jnp.logical_not(first))
    def _():
        pieces, piece_modes, piece_width = piece_ref.shape
        split = pieces * piece_modes // modes
        for piece in range(pieces):
            row, part = piece // split * piece_modes, piece % split
            lanes = slice(part * piece_width, (part + 1) * piece_width)
            total_scr[row : row + piece_modes, lanes] = piece_ref[piece].astype(f32)
        begin_others()
        over_chunks(0, chunks, with_fetch(chunks, fetch, chunk), give)

    for at in range(chunks):
        wait_all(give(at))


def cost(flops, moved):
    return pl.CostEstimate(flops=int(flops), bytes_accessed=int(moved), transcendentals=0)


def local(query, key_proj, value_proj, featurizer, rates, residues, skip, *, axes):
    tokens, width = query.shape
    modes = rates.shape[0]
    members, taps, groups = featurizer.shape
    devices = math.prod(lax.axis_size(axis) for axis in axes)
    chunks = width // CHUNK
    tiles = width // LANES
    split = devices * 2 // modes
    even = devices * 2 % modes == 0 and tiles % split == 0
    vmem = pltpu.VMEM
    far = pltpu.HBM
    near = jax.ShapeDtypeStruct
    dma = pltpu.SemaphoreType.DMA
    elements = tokens * width

    def call(kernel, inputs, outputs, scratches, name, close=(), **more):
        inputs = [
            value if at in close else pltpu.with_memory_space_constraint(value, far)
            for at, value in enumerate(inputs)
        ]
        beside, there = pl.BlockSpec(memory_space=vmem), pl.BlockSpec(memory_space=far)
        return pl.pallas_call(
            kernel,
            in_specs=[beside if at in close else there for at in range(len(inputs))],
            out_specs=[beside if isinstance(one, near) else there for one in outputs],
            out_shape=outputs,
            scratch_shapes=scratches,
            compiler_params=pltpu.CompilerParams(vmem_limit_bytes=32 * 2**20),
            name=name,
            **more,
        )(*inputs)

    halo_shape = (members * (taps - 1) // 2, 2, width)
    (packed,) = call(
        pack_kernel,
        (key_proj, value_proj, query),
        [near(halo_shape, bf16)],
        [vmem((members, 2 * ROWS, width), bf16), dma((members,))],
        "pack",
    )
    halo = lax.ppermute(packed, axes, [(at, at + 1) for at in range(devices - 1)])

    column = vmem((2 * ROWS + tokens, LANES), f32)
    half_buf, whole_buf = vmem((chunks, tokens, CHUNK), bf16), vmem((chunks, tokens, CHUNK), f32)
    u, wide_taps, state = call(
        signal_kernel,
        (key_proj, value_proj, featurizer, rates),
        [near((tokens, width), bf16), near((chunks, 2, ROWS, CHUNK), f32), near((modes, width), f32)],
        [vmem((4, modes, width), f32), vmem((modes, ROWS, LANES), f32)] + [column] * (2 * TILES),
        "signal",
        close=range(4),
        cost_estimate=cost(60 * elements, 10 * elements),
    )

    pieces = (devices, 2, width // split) if even else (modes // 2, 2, width)
    left, head, u = call(
        functools.partial(head_kernel, tokens=tokens, reach=taps - 1),
        (key_proj, value_proj, halo, rates, wide_taps, state, u),
        [near(pieces, bf16), near((2 * ROWS, width), bf16), far((tokens, width), bf16)],
        [vmem((TILES, 2, 3 * ROWS, LANES), f32), vmem((TILES, ROWS, LANES), f32)]
        + [vmem((modes, width), f32), dma((1,))],
        "head",
        close=range(7),
    )
    left, halo_late, rates_late, skip_late = lax.optimization_barrier((left, halo, rates, skip))
    coef = residues * jnp.sqrt(-jnp.expm1(-2.0 * rates_late) / modes)
    skip_row = skip_late[None, :]
    stage = vmem((tokens // ROWS // 2 * ROWS * ROWS, LANES), f32)
    local_shapes = [far((tokens, width), f32)]
    local_scratches = [whole_buf, stage, stage, dma((1, chunks))]
    early = chunks * 4 // 9
    gate, y = call(
        functools.partial(gate_kernel, early=early),
        (query, halo_late, featurizer, u, head, rates, coef, skip_row),
        [far((tokens, width), bf16)] + local_shapes,
        [vmem(halo_shape, bf16), vmem((tokens, early * CHUNK), bf16), half_buf]
        + [vmem((chunks, 1, ROWS, CHUNK), f32), column, dma((2,)), dma((1, chunks))]
        + local_scratches,
        "gate",
        close=(0, 2, 4, 5, 6, 7),
        cost_estimate=cost(28 * elements, 6 * elements),
    )

    def swap(value):
        order = [list(range(devices))[::-1]]
        return lax.all_to_all(value, axes, split_axis=0, concat_axis=0, axis_index_groups=order, tiled=True)

    share = modes * width // devices
    theirs = swap(left if even else left.reshape(devices, share))
    theirs, gate, coef, skip_row, y = lax.optimization_barrier((theirs, gate, coef, skip_row, y))
    if even:
        (entering,) = call(
            functools.partial(prefix_kernel, tokens=tokens, axes=axes),
            (theirs, rates, coef),
            [near(pieces, bf16)],
            [],
            "prefix",
            close=(0, 1, 2),
        )
    else:
        mine = devices - 1 - lax.axis_index(axes)
        through = jnp.exp(-float(tokens) * lax.dynamic_slice_in_dim(rates.reshape(-1), mine * share, share))
        factor = lax.dynamic_slice_in_dim(coef.reshape(-1), mine * share, share)
        _, entering = lax.scan(
            lambda so_far, piece: (through * so_far + piece.astype(f32), (factor * so_far).astype(bf16)),
            jnp.zeros((share,), f32),
            theirs,
            reverse=True,
        )

    entering, y = lax.optimization_barrier((entering, y))
    entered = swap(entering).reshape(pieces)
    (y,) = call(
        functools.partial(local_kernel, first=early, last=chunks),
        (u, head, rates, coef, skip_row, y),
        local_shapes,
        local_scratches,
        "within",
        close=range(5),
        cost_estimate=cost(50 * elements, 8 * elements),
        input_output_aliases={5: 0},
    )

    (out,) = call(
        functools.partial(final_kernel, axes=axes),
        (entered, rates, y, gate),
        [far((tokens, width), bf16)],
        [whole_buf, half_buf, half_buf, vmem((modes, width), f32), vmem((4, modes, CHUNK), f32)]
        + [dma((2, chunks)), dma((1, chunks))],
        "final",
        close=(0, 1),
        cost_estimate=cost(40 * elements, 10 * elements),
    )
    return out


def solution(mesh):
    axes = tuple(mesh.axis_names)
    placed = (P(axes, None),) * 3 + (P(),) * 4
    return jax.shard_map(
        functools.partial(local, axes=axes),
        mesh=mesh,
        in_specs=placed,
        out_specs=P(axes, None),
        check_vma=False,
    )
```

```python
import functools
import math

import jax
import jax.numpy as jnp
from jax import lax
from jax.experimental import pallas as pl
from jax.experimental.pallas import tpu as pltpu
from jax.sharding import PartitionSpec as P

LANES = 128
ROWS = 8
TILES = 4
CHUNK = TILES * LANES
AHEAD = 4
LAP = 4
f32 = jnp.float32
bf16 = jnp.bfloat16


def put_tile(scratch, group, slot, tile):
    scratch[pl.ds((group * ROWS + slot) * ROWS, ROWS), :] = tile


def get_row(scratch, group, row):
    return scratch[pl.ds(group * ROWS * ROWS + row, ROWS, stride=ROWS), :]


def lanes_of(value, tile):
    return value[:, tile * LANES : (tile + 1) * LANES]


def tile_lanes(tile):
    return pl.ds(pl.multiple_of(tile * LANES, LANES), LANES)


def span(at):
    return pl.ds(pl.multiple_of(at * CHUNK, CHUNK), CHUNK)


def wide(row):
    return jnp.broadcast_to(row, (ROWS, LANES))


def first_half():
    return lax.broadcasted_iota(jnp.int32, (ROWS, LANES), 0) < TILES


def sublane():
    return lax.broadcasted_iota(jnp.int32, (ROWS, LANES), 0)


def spread(row_of):
    slot = sublane() % TILES
    result = wide(row_of(TILES - 1))
    for tile in range(TILES - 1):
        result = jnp.where(slot == tile, wide(row_of(tile)), result)
    return result


def spread_rows(ref, at, rows):
    def one(row):
        return spread(lambda tile: ref[row : row + 1, tile_lanes(at * TILES + tile)])

    return [one(row) for row in rows]


def rounded(value):
    return value.astype(bf16).astype(f32)


def tiles_of(block):
    block = block.astype(f32)
    return [block[at : at + ROWS] for at in range(0, block.shape[0], ROWS)]


def fir(column, taps, first, count):
    half = ROWS // 2
    top = sublane() < half

    def seen(start, lags):
        return [column[pl.ds(start - lag, ROWS), :] for lag in range(lags)]

    def far_part(rows):
        total = taps[half] * rows[0]
        for lag in range(half + 1, len(taps)):
            total = total + taps[lag] * rows[lag - half]
        return pltpu.roll(total, half, 0)

    before = far_part(seen(first - ROWS, len(taps) - half))
    for start in range(first, first + count * ROWS, ROWS):
        rows = seen(start, half)
        now = far_part(rows)
        total = taps[0] * rows[0]
        for lag in range(1, half):
            total = total + taps[lag] * rows[lag]
        yield total + jnp.where(top, before, now)
        before = now


def lay_column(column, source, lanes):
    for pair in range(source.shape[0] // (2 * ROWS)):
        rows = slice(pair * 2 * ROWS, (pair + 1) * 2 * ROWS)
        column[pl.ds((pair + 1) * 2 * ROWS, 2 * ROWS), :] = source[rows, lanes].astype(f32)


def chunk_taps(wide_ref, at, member, tile, count):
    return [wide(wide_ref[at, member, lag : lag + 1, tile_lanes(tile)]) for lag in range(count)]


def widened(feat_ref, member, out_ref, position):
    chunks, taps = out_ref.shape[0], feat_ref.shape[1]
    count = feat_ref.shape[2] // chunks
    rows = [feat_ref[member, :, at * count : (at + 1) * count] for at in range(chunks)]
    rows = [jnp.concatenate([row, jnp.zeros((ROWS - taps, count), f32)], axis=0) for row in rows]
    group = lax.broadcasted_iota(jnp.int32, (count, CHUNK), 0)
    lane = lax.broadcasted_iota(jnp.int32, (count, CHUNK), 1)
    pick = (group == lane // (CHUNK // count)).astype(f32).astype(bf16)
    parts, rest = [], jnp.concatenate(rows, axis=0)
    for _ in range(3):
        term = rest.astype(bf16)
        rest = rest - term.astype(f32)
        parts.append(jnp.dot(term, pick, preferred_element_type=f32))
    out_ref[:, position] = (parts[0] + parts[1] + parts[2]).reshape(chunks, ROWS, CHUNK)


def power(base, exponent):
    result = None
    while exponent:
        if exponent & 1:
            result = base if result is None else result * base
        base = base * base
        exponent >>= 1
    return result


def tree(terms):
    while len(terms) > 1:
        terms = [sum(terms[at + 1 : at + 2], terms[at]) for at in range(0, len(terms), 2)]
    return terms[0]


def start_all(copies):
    for copy in copies:
        copy.start()


def wait_all(copies):
    for copy in copies:
        copy.wait()


def begin(chunks, fetch):
    for at in range(min(AHEAD, chunks)):
        start_all(fetch(at))


def over_chunks(first, last, body, send):
    def one(at, _):
        body(at)
        start_all(send(at))
        return 0

    lax.fori_loop(first, last, one, 0)


def with_fetch(chunks, fetch, body):
    def one(at):
        @pl.when(at + AHEAD < chunks)
        def _():
            start_all(fetch(at + AHEAD))

        wait_all(fetch(at))
        body(at)

    return one


def columns_in(pairs, sem):
    def fetch(at):
        return [
            pltpu.make_async_copy(ref.at[:, span(at)], buf.at[at], sem.at[member, at])
            for member, (ref, buf) in enumerate(pairs)
        ]

    return fetch


def columns_out(ref, buf, sem):
    return lambda at: [pltpu.make_async_copy(buf.at[at], ref.at[:, span(at)], sem.at[0, at])]


def lay_halo(column, halo, member, lanes):
    pairs = halo.shape[0] // 3
    for pair in range(pairs):
        column[pl.ds(2 * ROWS - 2 * pairs + 2 * pair, 2), :] = halo[member * pairs + pair, :, lanes].astype(f32)


def pack_kernel(key_ref, value_ref, query_ref, out_ref, in_buf, in_sem):
    tokens = key_ref.shape[0]
    copies = [
        pltpu.make_async_copy(ref.at[pl.ds(tokens - 2 * ROWS, 2 * ROWS)], in_buf.at[at], in_sem.at[at])
        for at, ref in enumerate((key_ref, value_ref, query_ref))
    ]
    start_all(copies)
    wait_all(copies)
    pairs = out_ref.shape[0] // len(copies)
    for at in range(len(copies)):
        tail = in_buf[at].astype(f32)[2 * ROWS - 2 * pairs :]
        for pair in range(pairs):
            out_ref[at * pairs + pair] = tail[2 * pair : 2 * pair + 2].astype(bf16)


def signal_kernel(key_ref, value_ref, feat_ref, rate_ref, u_ref, wide_ref, state_ref, power_scr, last_scr, *columns):
    tokens, tiles = u_ref.shape[0], u_ref.shape[1] // LANES
    modes = rate_ref.shape[0]
    chunks = tiles // TILES
    count = feat_ref.shape[1]
    for member in range(2):
        widened(feat_ref, member + 1, wide_ref, member)
    for column in columns:
        column[pl.ds(0, 2 * ROWS), :] = jnp.zeros((2 * ROWS, LANES), f32)
    last_scr[...] = jnp.zeros(last_scr.shape, f32)

    def powers(at, _):
        through = jnp.exp(-rate_ref[:, span(at)])
        for level in range(4):
            power_scr[level, :, span(at)] = through
            through = through * through
        return 0

    lax.fori_loop(0, chunks, powers, 0)

    def reduce(number):
        lanes = tile_lanes(number)
        for mode in range(modes):
            whole = last_scr[mode]
            for level in (2, 1, 0):
                factor = wide(power_scr[level, mode : mode + 1, lanes])
                whole = factor * whole + pltpu.roll(whole, ROWS - (1 << level), 0)
            state_ref[mode : mode + 1, lanes] = whole[:1]

    def tile(number, columns):
        lanes = tile_lanes(number)
        reduce(jnp.maximum(number - 1, 0))
        taps = [chunk_taps(wide_ref, number // TILES, member, number % TILES, count) for member in range(2)]
        for column, ref in zip(columns, (key_ref, value_ref)):
            lay_column(column, ref, lanes)
        decay = [wide(power_scr[3, mode : mode + 1, lanes]) for mode in range(modes)]
        state = None
        parts = [fir(column, some, 2 * ROWS, tokens // ROWS) for column, some in zip(columns, taps)]
        for pair in range(tokens // (2 * ROWS)):
            found = [next(parts[0]) * next(parts[1]) for _ in range(2)]
            if pair == 0:
                found[0] = jnp.where(sublane() < count - 1, 0.0, found[0])
            both = jnp.concatenate(found, axis=0).astype(bf16)
            u_ref[pair * 2 * ROWS : (pair + 1) * 2 * ROWS, lanes] = both
            for u in tiles_of(both):
                if state is None:
                    state = [u] * modes
                else:
                    state = [factor * one + u for factor, one in zip(decay, state)]
        for mode in range(modes):
            last_scr[mode] = state[mode]

    def some(number, _):
        for part in range(TILES):
            tile(TILES * number + part, columns[2 * part : 2 * part + 2])
        return 0

    lax.fori_loop(0, tiles // TILES, some, 0)
    reduce(tiles - 1)


def head_kernel(key_ref, value_ref, halo_ref, rate_ref, wide_ref, state_ref, u_ref, *rest, tokens, reach):
    out_ref, head_ref, u_out_ref, column_scr, token_scr, total_scr, sem = rest
    move = pltpu.make_async_copy(u_ref, u_out_ref, sem.at[0])
    move.start()
    modes, tiles = state_ref.shape[0], state_ref.shape[1] // LANES
    pieces, piece_modes, piece_width = out_ref.shape

    def some(chunk, _):
        for number in range(TILES):
            lanes = tile_lanes(chunk * TILES + number)
            parts = []
            for member in range(2):
                taps = chunk_taps(wide_ref, chunk, member, number, reach + 1)
                column = column_scr.at[number, member]
                column[pl.ds(0, 2 * ROWS), :] = jnp.zeros((2 * ROWS, LANES), f32)
                lay_halo(column, halo_ref, member, lanes)
                source = (key_ref, value_ref)[member]
                column[pl.ds(2 * ROWS, ROWS), :] = source[: 2 * ROWS, lanes].astype(f32)[:ROWS]
                parts += fir(column, taps, 2 * ROWS, 1)
            u = jnp.where(sublane() < reach, rounded(parts[0] * parts[1]), 0.0)
            token_scr[number] = u
            for group in range(0, modes, ROWS):
                decay = jnp.exp(-rate_ref[group : group + ROWS, lanes])
                head = wide(token_scr[number, :1, :])
                for row in range(1, reach):
                    head = decay * head + wide(token_scr[number, row : row + 1, :])
                total = state_ref[group : group + ROWS, lanes] + power(decay, tokens - reach) * head
                total_scr[group : group + ROWS, lanes] = total
            head_ref[:, lanes] = jnp.concatenate([u, jnp.zeros((ROWS, LANES), f32)], axis=0).astype(bf16)
        return 0

    lax.fori_loop(0, tiles // TILES, some, 0)
    split = pieces * piece_modes // modes
    for piece in range(pieces):
        first, part = piece // split * piece_modes, piece % split
        rows = total_scr[first : first + piece_modes, part * piece_width : (part + 1) * piece_width]
        out_ref[piece] = rows.astype(out_ref.dtype)
    move.wait()


def gate_kernel(query_ref, halo_ref, feat_ref, u_ref, head_ref, rate_ref, coef_ref, skip_ref, gate_ref, *rest, early):
    y_ref, halo_buf, u_buf, gate_buf, wide_scr, column, small_sem, out_sem = rest[:8]
    inner = rest[8:]
    chunks, tokens = gate_buf.shape[:2]
    count = feat_ref.shape[1]
    halo_copy = pltpu.make_async_copy(halo_ref, halo_buf, small_sem.at[0])
    halo_copy.start()
    u_copy = pltpu.make_async_copy(u_ref.at[:, pl.ds(0, early * CHUNK)], u_buf, small_sem.at[1])
    u_copy.start()
    widened(feat_ref, 0, wide_scr, 0)
    local_chunk, local_send = local_parts(u_buf, head_ref, rate_ref, coef_ref, skip_ref, y_ref, *inner)
    halo_copy.wait()
    column[pl.ds(0, 2 * ROWS), :] = jnp.zeros((2 * ROWS, LANES), f32)

    def chunk(at):
        def tile(number, _):
            lanes = tile_lanes(number)
            all_lanes = tile_lanes(at * TILES + number)
            taps = chunk_taps(wide_scr, at, 0, number, count)
            lay_halo(column, halo_buf, 2, all_lanes)
            lay_column(column, query_ref, all_lanes)
            found = list(fir(column, taps, 2 * ROWS, tokens // ROWS))
            for pair in range(tokens // (2 * ROWS)):
                rows = slice(pair * 2 * ROWS, (pair + 1) * 2 * ROWS)
                gate_buf[at, rows, lanes] = jnp.concatenate(found[pair * 2 : pair * 2 + 2], axis=0).astype(bf16)
            return 0

        lax.fori_loop(0, TILES, tile, 0)

    give = columns_out(gate_ref, gate_buf, out_sem)
    over_chunks(0, chunks, chunk, give)
    u_copy.wait()
    over_chunks(0, early, local_chunk, local_send)
    for at in range(early):
        wait_all(local_send(at))
    for at in range(chunks):
        wait_all(give(at))


def prefix_kernel(piece_ref, rate_ref, coef_ref, out_ref, *, tokens, axes):
    devices, piece_modes, piece_width = piece_ref.shape
    split = devices * piece_modes // rate_ref.shape[0]
    mine = devices - 1 - lax.axis_index(axes)
    mode, part = mine // split * piece_modes, mine % split
    group = pl.multiple_of(mode // ROWS * ROWS, ROWS)
    first = pl.multiple_of(part * piece_width, LANES)

    def mine_of(ref):
        rows = ref[pl.ds(group, ROWS), pl.ds(first, piece_width)]
        place = lax.broadcasted_iota(jnp.int32, rows.shape, 0)
        found = [
            jnp.sum(jnp.where(place == mode - group + row, rows, 0.0), axis=0, keepdims=True)
            for row in range(piece_modes)
        ]
        return jnp.concatenate(found, axis=0)

    coef = mine_of(coef_ref)
    through = jnp.exp(-float(tokens) * mine_of(rate_ref))

    def lap(number, entering):
        for step in range(4):
            source = devices - 1 - (number * 4 + step)
            out_ref[source] = (coef * entering).astype(out_ref.dtype)
            entering = through * entering + piece_ref[source].astype(f32)
        return entering

    lax.fori_loop(0, devices // 4, lap, jnp.zeros((piece_modes, piece_width), f32))


def local_kernel(u_ref, head_ref, rate_ref, coef_ref, skip_ref, *rest, first, last):
    chunk, send = local_parts(u_ref, head_ref, rate_ref, coef_ref, skip_ref, *rest[-5:])
    over_chunks(first, last, chunk, send)
    for at in range(first, last):
        wait_all(send(at))


def local_parts(u_ref, head_ref, rate_ref, coef_ref, skip_ref, y_ref, *scratches):
    y_buf, token_scr, sum_scr, out_sem = scratches
    tokens = u_ref.shape[0]
    modes = rate_ref.shape[0]
    half_groups = tokens // ROWS // 2
    top = first_half()

    def chunk(at):
        for pair in range(half_groups):
            block = u_ref[pair * 2 * ROWS : (pair + 1) * 2 * ROWS, span(at)].astype(f32)
            if pair == 0:
                block = block + head_ref[:, span(at)].astype(f32)
            for part in range(2):
                group = pair * 2 + part
                half, within = group // half_groups, group % half_groups
                for tile in range(TILES):
                    piece = lanes_of(block, tile)[part * ROWS : (part + 1) * ROWS]
                    put_tile(token_scr, within, half * TILES + tile, piece)
        (skip,) = spread_rows(skip_ref, at, range(1))
        coef = spread_rows(coef_ref, at, range(modes))
        decay = [jnp.exp(-rate) for rate in spread_rows(rate_ref, at, range(modes))]

        def eight(group, state):
            state = list(state)
            for row in range(ROWS):
                u = get_row(token_scr, group, row)
                state = [factor * one + u for factor, one in zip(decay, state)]
                terms = [factor * one for factor, one in zip([skip] + coef, [u] + state)]
                sum_scr[pl.ds(group * ROWS * ROWS + row, ROWS, stride=ROWS), :] = tree(terms)
            return tuple(state)

        state = lax.fori_loop(0, half_groups, eight, (jnp.zeros((ROWS, LANES), f32),) * modes)
        carried = tuple(
            jnp.where(top, 0.0, pltpu.roll(factor * one, TILES, 0)) for factor, one in zip(coef, state)
        )

        def eight_more(group, carried):
            for row in range(ROWS):
                carried = [factor * one for factor, one in zip(decay, carried)]
                place = pl.ds(group * ROWS * ROWS + row, ROWS, stride=ROWS)
                sum_scr[place, :] = sum_scr[place, :] + tree(carried)
            return tuple(carried)

        lax.fori_loop(0, half_groups, eight_more, carried)
        for group in range(2 * half_groups):
            half, within = group // half_groups, group % half_groups
            for tile in range(TILES):
                slot = (within * ROWS + half * TILES + tile) * ROWS
                rows = slice(group * ROWS, (group + 1) * ROWS)
                y_buf[at, rows, tile * LANES : (tile + 1) * LANES] = sum_scr[pl.ds(slot, ROWS), :]

    return chunk, columns_out(y_ref, y_buf, out_sem)


def final_kernel(piece_ref, rate_ref, y_ref, gate_ref, out_ref, *scratches, axes):
    y_buf, gate_buf, out_buf, total_scr, power_scr, in_sem, out_sem = scratches
    chunks, tokens = y_buf.shape[:2]
    modes = rate_ref.shape[0]
    fetch = columns_in(((y_ref, y_buf), (gate_ref, gate_buf)), in_sem)
    give = columns_out(out_ref, out_buf, out_sem)
    start_all(fetch(0))
    bits = [(sublane() >> level) % 2 == 1 for level in range(3)]
    pairs = [slice(first, first + 2 * ROWS) for first in range(0, tokens, 2 * ROWS)]

    def finish(at, rows, lanes, sums):
        gates = gate_buf[at, rows, lanes].astype(f32)
        out_buf[at, rows, lanes] = (gates * rounded(sums)).astype(bf16)

    def chunk(at):
        through = jnp.exp(-rate_ref[:, span(at)])
        for level in range(4):
            power_scr[level] = through
            through = through * through

        def tile(number):
            lanes = tile_lanes(number)
            state = []
            for mode in range(modes):
                rows = [wide(power_scr[level, mode : mode + 1, lanes]) for level in range(3)]
                lead = jnp.where(bits[0], rows[1], rows[0])
                for bit, row in zip(bits[1:], rows[1:]):
                    lead = lead * jnp.where(bit, row, 1.0)
                state.append(lead * wide(total_scr[mode : mode + 1, tile_lanes(at * TILES + number)]))
            decay = [wide(power_scr[3, mode : mode + 1, lanes]) for mode in range(modes)]
            for rows in pairs:
                sums = []
                for first in (rows.start, rows.start + ROWS):
                    sums.append(y_buf[at, first : first + ROWS, lanes] + tree(state))
                    state = [factor * one for factor, one in zip(decay, state)]
                finish(at, rows, lanes, jnp.concatenate(sums, axis=0))

        def some(number, _):
            for part in range(LAP):
                tile(number * LAP + part)
            return 0

        lax.fori_loop(0, TILES // LAP, some, 0)

    def chunk_alone(at):
        def tile(number, _):
            lanes = tile_lanes(number)
            for rows in pairs:
                finish(at, rows, lanes, y_buf[at, rows, lanes])
            return 0

        lax.fori_loop(0, TILES, tile, 0)

    def begin_others():
        for at in range(1, min(AHEAD, chunks)):
            start_all(fetch(at))

    first = lax.axis_index(axes) == 0

    @pl.when(first)
    def _():
        begin_others()
        over_chunks(0, chunks, with_fetch(chunks, fetch, chunk_alone), give)

    @pl.when(jnp.logical_not(first))
    def _():
        pieces, piece_modes, piece_width = piece_ref.shape
        split = pieces * piece_modes // modes
        for piece in range(pieces):
            row, part = piece // split * piece_modes, piece % split
            lanes = slice(part * piece_width, (part + 1) * piece_width)
            total_scr[row : row + piece_modes, lanes] = piece_ref[piece].astype(f32)
        begin_others()
        over_chunks(0, chunks, with_fetch(chunks, fetch, chunk), give)

    for at in range(chunks):
        wait_all(give(at))


def cost(flops, moved):
    return pl.CostEstimate(flops=int(flops), bytes_accessed=int(moved), transcendentals=0)


def local(query, key_proj, value_proj, featurizer, rates, residues, skip, *, axes):
    tokens, width = query.shape
    modes = rates.shape[0]
    members, taps, groups = featurizer.shape
    devices = math.prod(lax.axis_size(axis) for axis in axes)
    chunks = width // CHUNK
    tiles = width // LANES
    split = devices * 2 // modes
    even = devices * 2 % modes == 0 and tiles % split == 0
    vmem = pltpu.VMEM
    far = pltpu.HBM
    near = jax.ShapeDtypeStruct
    dma = pltpu.SemaphoreType.DMA
    elements = tokens * width

    def call(kernel, inputs, outputs, scratches, name, close=(), **more):
        inputs = [
            value if at in close else pltpu.with_memory_space_constraint(value, far)
            for at, value in enumerate(inputs)
        ]
        beside, there = pl.BlockSpec(memory_space=vmem), pl.BlockSpec(memory_space=far)
        return pl.pallas_call(
            kernel,
            in_specs=[beside if at in close else there for at in range(len(inputs))],
            out_specs=[beside if isinstance(one, near) else there for one in outputs],
            out_shape=outputs,
            scratch_shapes=scratches,
            compiler_params=pltpu.CompilerParams(vmem_limit_bytes=32 * 2**20),
            name=name,
            **more,
        )(*inputs)

    halo_shape = (members * (taps - 1) // 2, 2, width)
    (packed,) = call(
        pack_kernel,
        (key_proj, value_proj, query),
        [near(halo_shape, bf16)],
        [vmem((members, 2 * ROWS, width), bf16), dma((members,))],
        "pack",
    )
    halo = lax.ppermute(packed, axes, [(at, at + 1) for at in range(devices - 1)])

    column = vmem((2 * ROWS + tokens, LANES), f32)
    half_buf, whole_buf = vmem((chunks, tokens, CHUNK), bf16), vmem((chunks, tokens, CHUNK), f32)
    u, wide_taps, state = call(
        signal_kernel,
        (key_proj, value_proj, featurizer, rates),
        [near((tokens, width), bf16), near((chunks, 2, ROWS, CHUNK), f32), near((modes, width), f32)],
        [vmem((4, modes, width), f32), vmem((modes, ROWS, LANES), f32)] + [column] * (2 * TILES),
        "signal",
        close=range(4),
        cost_estimate=cost(60 * elements, 10 * elements),
    )

    pieces = (devices, 2, width // split) if even else (modes // 2, 2, width)
    left, head, u = call(
        functools.partial(head_kernel, tokens=tokens, reach=taps - 1),
        (key_proj, value_proj, halo, rates, wide_taps, state, u),
        [near(pieces, bf16), near((2 * ROWS, width), bf16), far((tokens, width), bf16)],
        [vmem((TILES, 2, 3 * ROWS, LANES), f32), vmem((TILES, ROWS, LANES), f32)]
        + [vmem((modes, width), f32), dma((1,))],
        "head",
        close=range(7),
    )
    left, halo_late, rates_late, skip_late = lax.optimization_barrier((left, halo, rates, skip))
    coef = residues * jnp.sqrt(-jnp.expm1(-2.0 * rates_late) / modes)
    skip_row = skip_late[None, :]
    stage = vmem((tokens // ROWS // 2 * ROWS * ROWS, LANES), f32)
    local_shapes = [far((tokens, width), f32)]
    local_scratches = [whole_buf, stage, stage, dma((1, chunks))]
    early = chunks * 2 // 9
    gate, y = call(
        functools.partial(gate_kernel, early=early),
        (query, halo_late, featurizer, u, head, rates, coef, skip_row),
        [far((tokens, width), bf16)] + local_shapes,
        [vmem(halo_shape, bf16), vmem((tokens, early * CHUNK), bf16), half_buf]
        + [vmem((chunks, 1, ROWS, CHUNK), f32), column, dma((2,)), dma((1, chunks))]
        + local_scratches,
        "gate",
        close=(0, 2, 4, 5, 6, 7),
        cost_estimate=cost(28 * elements, 6 * elements),
    )

    def swap(value):
        order = [list(range(devices))[::-1]]
        return lax.all_to_all(value, axes, split_axis=0, concat_axis=0, axis_index_groups=order, tiled=True)

    share = modes * width // devices
    theirs = swap(left if even else left.reshape(devices, share))
    theirs, gate, coef, skip_row, y = lax.optimization_barrier((theirs, gate, coef, skip_row, y))
    if even:
        (entering,) = call(
            functools.partial(prefix_kernel, tokens=tokens, axes=axes),
            (theirs, rates, coef),
            [near(pieces, bf16)],
            [],
            "prefix",
            close=(0, 1, 2),
        )
    else:
        mine = devices - 1 - lax.axis_index(axes)
        through = jnp.exp(-float(tokens) * lax.dynamic_slice_in_dim(rates.reshape(-1), mine * share, share))
        factor = lax.dynamic_slice_in_dim(coef.reshape(-1), mine * share, share)
        _, entering = lax.scan(
            lambda so_far, piece: (through * so_far + piece.astype(f32), (factor * so_far).astype(bf16)),
            jnp.zeros((share,), f32),
            theirs,
            reverse=True,
        )

    entering, y = lax.optimization_barrier((entering, y))
    entered = swap(entering).reshape(pieces)
    (y,) = call(
        functools.partial(local_kernel, first=early, last=chunks),
        (u, head, rates, coef, skip_row, y),
        local_shapes,
        local_scratches,
        "within",
        close=range(5),
        cost_estimate=cost(50 * elements, 8 * elements),
        input_output_aliases={5: 0},
    )

    (out,) = call(
        functools.partial(final_kernel, axes=axes),
        (entered, rates, y, gate),
        [far((tokens, width), bf16)],
        [whole_buf, half_buf, half_buf, vmem((modes, width), f32), vmem((4, modes, CHUNK), f32)]
        + [dma((2, chunks)), dma((1, chunks))],
        "final",
        close=(0, 1),
        cost_estimate=cost(40 * elements, 10 * elements),
    )
    return out


def solution(mesh):
    axes = tuple(mesh.axis_names)
    placed = (P(axes, None),) * 3 + (P(),) * 4
    return jax.shard_map(
        functools.partial(local, axes=axes),
        mesh=mesh,
        in_specs=placed,
        out_specs=P(axes, None),
        check_vma=False,
    )
```

```python
import functools
import math

import jax
import jax.numpy as jnp
from jax import lax
from jax.experimental import pallas as pl
from jax.experimental.pallas import tpu as pltpu
from jax.sharding import PartitionSpec as P

LANES = 128
ROWS = 8
TILES = 4
CHUNK = TILES * LANES
AHEAD = 4
LAP = 4
f32 = jnp.float32
bf16 = jnp.bfloat16


def put_tile(scratch, group, slot, tile):
    scratch[pl.ds((group * ROWS + slot) * ROWS, ROWS), :] = tile


def get_row(scratch, group, row):
    return scratch[pl.ds(group * ROWS * ROWS + row, ROWS, stride=ROWS), :]


def lanes_of(value, tile):
    return value[:, tile * LANES : (tile + 1) * LANES]


def tile_lanes(tile):
    return pl.ds(pl.multiple_of(tile * LANES, LANES), LANES)


def span(at):
    return pl.ds(pl.multiple_of(at * CHUNK, CHUNK), CHUNK)


def wide(row):
    return jnp.broadcast_to(row, (ROWS, LANES))


def first_half():
    return lax.broadcasted_iota(jnp.int32, (ROWS, LANES), 0) < TILES


def sublane():
    return lax.broadcasted_iota(jnp.int32, (ROWS, LANES), 0)


def spread(row_of):
    slot = sublane() % TILES
    result = wide(row_of(TILES - 1))
    for tile in range(TILES - 1):
        result = jnp.where(slot == tile, wide(row_of(tile)), result)
    return result


def spread_rows(ref, at, rows):
    def one(row):
        return spread(lambda tile: ref[row : row + 1, tile_lanes(at * TILES + tile)])

    return [one(row) for row in rows]


def rounded(value):
    return value.astype(bf16).astype(f32)


def tiles_of(block):
    block = block.astype(f32)
    return [block[at : at + ROWS] for at in range(0, block.shape[0], ROWS)]


def fir(column, taps, first, count):
    half = ROWS // 2
    top = sublane() < half

    def seen(start, lags):
        return [column[pl.ds(start - lag, ROWS), :] for lag in range(lags)]

    def far_part(rows):
        total = taps[half] * rows[0]
        for lag in range(half + 1, len(taps)):
            total = total + taps[lag] * rows[lag - half]
        return pltpu.roll(total, half, 0)

    before = far_part(seen(first - ROWS, len(taps) - half))
    for start in range(first, first + count * ROWS, ROWS):
        rows = seen(start, half)
        now = far_part(rows)
        total = taps[0] * rows[0]
        for lag in range(1, half):
            total = total + taps[lag] * rows[lag]
        yield total + jnp.where(top, before, now)
        before = now


def fir_loads(column, taps, first):
    total = taps[0] * column[pl.ds(first, ROWS), :]
    for lag in range(1, len(taps)):
        total = total + taps[lag] * column[pl.ds(first - lag, ROWS), :]
    return total


def lay_column(column, source, lanes):
    for pair in range(source.shape[0] // (2 * ROWS)):
        rows = slice(pair * 2 * ROWS, (pair + 1) * 2 * ROWS)
        column[pl.ds((pair + 1) * 2 * ROWS, 2 * ROWS), :] = source[rows, lanes].astype(f32)


def chunk_taps(wide_ref, at, member, tile, count):
    return [wide(wide_ref[at, member, lag : lag + 1, tile_lanes(tile)]) for lag in range(count)]


def widened(feat_ref, member, out_ref, position):
    chunks, taps = out_ref.shape[0], feat_ref.shape[1]
    count = feat_ref.shape[2] // chunks
    rows = [feat_ref[member, :, at * count : (at + 1) * count] for at in range(chunks)]
    rows = [jnp.concatenate([row, jnp.zeros((ROWS - taps, count), f32)], axis=0) for row in rows]
    group = lax.broadcasted_iota(jnp.int32, (count, CHUNK), 0)
    lane = lax.broadcasted_iota(jnp.int32, (count, CHUNK), 1)
    pick = (group == lane // (CHUNK // count)).astype(f32).astype(bf16)
    parts, rest = [], jnp.concatenate(rows, axis=0)
    for _ in range(3):
        term = rest.astype(bf16)
        rest = rest - term.astype(f32)
        parts.append(jnp.dot(term, pick, preferred_element_type=f32))
    out_ref[:, position] = (parts[0] + parts[1] + parts[2]).reshape(chunks, ROWS, CHUNK)


def power(base, exponent):
    result = None
    while exponent:
        if exponent & 1:
            result = base if result is None else result * base
        base = base * base
        exponent >>= 1
    return result


def tree(terms):
    while len(terms) > 1:
        terms = [sum(terms[at + 1 : at + 2], terms[at]) for at in range(0, len(terms), 2)]
    return terms[0]


def start_all(copies):
    for copy in copies:
        copy.start()


def wait_all(copies):
    for copy in copies:
        copy.wait()


def begin(chunks, fetch):
    for at in range(min(AHEAD, chunks)):
        start_all(fetch(at))


def over_chunks(first, last, body, send):
    def one(at, _):
        body(at)
        start_all(send(at))
        return 0

    lax.fori_loop(first, last, one, 0)


def with_fetch(chunks, fetch, body):
    def one(at):
        @pl.when(at + AHEAD < chunks)
        def _():
            start_all(fetch(at + AHEAD))

        wait_all(fetch(at))
        body(at)

    return one


def columns_in(pairs, sem):
    def fetch(at):
        return [
            pltpu.make_async_copy(ref.at[:, span(at)], buf.at[at], sem.at[member, at])
            for member, (ref, buf) in enumerate(pairs)
        ]

    return fetch


def columns_out(ref, buf, sem):
    return lambda at: [pltpu.make_async_copy(buf.at[at], ref.at[:, span(at)], sem.at[0, at])]


def lay_halo(column, halo, member, lanes):
    pairs = halo.shape[0] // 3
    for pair in range(pairs):
        column[pl.ds(2 * ROWS - 2 * pairs + 2 * pair, 2), :] = halo[member * pairs + pair, :, lanes].astype(f32)


def pack_kernel(key_ref, value_ref, query_ref, out_ref, in_buf, in_sem):
    tokens = key_ref.shape[0]
    copies = [
        pltpu.make_async_copy(ref.at[pl.ds(tokens - 2 * ROWS, 2 * ROWS)], in_buf.at[at], in_sem.at[at])
        for at, ref in enumerate((key_ref, value_ref, query_ref))
    ]
    start_all(copies)
    wait_all(copies)
    pairs = out_ref.shape[0] // len(copies)
    for at in range(len(copies)):
        tail = in_buf[at].astype(f32)[2 * ROWS - 2 * pairs :]
        for pair in range(pairs):
            out_ref[at * pairs + pair] = tail[2 * pair : 2 * pair + 2].astype(bf16)


def signal_kernel(key_ref, value_ref, feat_ref, rate_ref, u_ref, u_out_ref, wide_ref, state_ref, *scratches):
    power_scr, last_scr, *columns, out_sem = scratches
    tokens, tiles = u_ref.shape[0], u_ref.shape[1] // LANES
    modes = rate_ref.shape[0]
    chunks = tiles // TILES
    count = feat_ref.shape[1]
    for member in range(2):
        widened(feat_ref, member + 1, wide_ref, member)
    for column in columns:
        column[pl.ds(0, 2 * ROWS), :] = jnp.zeros((2 * ROWS, LANES), f32)
    last_scr[...] = jnp.zeros(last_scr.shape, f32)

    def powers(at, _):
        through = jnp.exp(-rate_ref[:, span(at)])
        for level in range(4):
            power_scr[level, :, span(at)] = through
            through = through * through
        return 0

    lax.fori_loop(0, chunks, powers, 0)

    def reduce(number):
        lanes = tile_lanes(number)
        for mode in range(modes):
            whole = last_scr[mode]
            for level in (2, 1, 0):
                factor = wide(power_scr[level, mode : mode + 1, lanes])
                whole = factor * whole + pltpu.roll(whole, ROWS - (1 << level), 0)
            state_ref[mode : mode + 1, lanes] = whole[:1]

    def tile(number, columns):
        lanes = tile_lanes(number)
        reduce(jnp.maximum(number - 1, 0))
        taps = [chunk_taps(wide_ref, number // TILES, member, number % TILES, count) for member in range(2)]
        for column, ref in zip(columns, (key_ref, value_ref)):
            lay_column(column, ref, lanes)
        decay = [wide(power_scr[3, mode : mode + 1, lanes]) for mode in range(modes)]
        state = None
        for pair in range(tokens // (2 * ROWS)):
            found = []
            for first in (pair * 2 * ROWS + 2 * ROWS, pair * 2 * ROWS + 3 * ROWS):
                found.append(fir_loads(columns[0], taps[0], first) * fir_loads(columns[1], taps[1], first))
            if pair == 0:
                found[0] = jnp.where(sublane() < count - 1, 0.0, found[0])
            both = jnp.concatenate(found, axis=0).astype(bf16)
            u_ref[pair * 2 * ROWS : (pair + 1) * 2 * ROWS, lanes] = both
            for u in tiles_of(both):
                if state is None:
                    state = [u] * modes
                else:
                    state = [factor * one + u for factor, one in zip(decay, state)]
        for mode in range(modes):
            last_scr[mode] = state[mode]

    def send(at):
        return pltpu.make_async_copy(u_ref.at[:, span(at)], u_out_ref.at[:, span(at)], out_sem.at[at])

    def chunk(at, _):
        for part in range(TILES):
            tile(TILES * at + part, columns[2 * part : 2 * part + 2])

        @pl.when(at < chunks - 1)
        def _():
            send(at).start()

        return 0

    lax.fori_loop(0, chunks, chunk, 0)
    reduce(tiles - 1)
    for at in range(chunks - 1):
        send(at).wait()


def head_kernel(key_ref, value_ref, halo_ref, rate_ref, wide_ref, state_ref, u_ref, _, *rest, tokens, reach):
    out_ref, head_ref, u_out_ref, column_scr, token_scr, total_scr, sem = rest
    modes, tiles = state_ref.shape[0], state_ref.shape[1] // LANES
    last = span(tiles // TILES - 1)
    move = pltpu.make_async_copy(u_ref.at[:, last], u_out_ref.at[:, last], sem.at[0])
    move.start()
    pieces, piece_modes, piece_width = out_ref.shape

    def some(chunk, _):
        for number in range(TILES):
            lanes = tile_lanes(chunk * TILES + number)
            parts = []
            for member in range(2):
                taps = chunk_taps(wide_ref, chunk, member, number, reach + 1)
                column = column_scr.at[number, member]
                column[pl.ds(0, 2 * ROWS), :] = jnp.zeros((2 * ROWS, LANES), f32)
                lay_halo(column, halo_ref, member, lanes)
                source = (key_ref, value_ref)[member]
                column[pl.ds(2 * ROWS, ROWS), :] = source[: 2 * ROWS, lanes].astype(f32)[:ROWS]
                parts += fir(column, taps, 2 * ROWS, 1)
            u = jnp.where(sublane() < reach, rounded(parts[0] * parts[1]), 0.0)
            token_scr[number] = u
            for group in range(0, modes, ROWS):
                decay = jnp.exp(-rate_ref[group : group + ROWS, lanes])
                head = wide(token_scr[number, :1, :])
                for row in range(1, reach):
                    head = decay * head + wide(token_scr[number, row : row + 1, :])
                total = state_ref[group : group + ROWS, lanes] + power(decay, tokens - reach) * head
                total_scr[group : group + ROWS, lanes] = total
            head_ref[:, lanes] = jnp.concatenate([u, jnp.zeros((ROWS, LANES), f32)], axis=0).astype(bf16)
        return 0

    lax.fori_loop(0, tiles // TILES, some, 0)
    split = pieces * piece_modes // modes
    for piece in range(pieces):
        first, part = piece // split * piece_modes, piece % split
        rows = total_scr[first : first + piece_modes, part * piece_width : (part + 1) * piece_width]
        out_ref[piece] = rows.astype(out_ref.dtype)
    move.wait()


def gate_kernel(query_ref, halo_ref, feat_ref, u_ref, head_ref, rate_ref, coef_ref, skip_ref, gate_ref, *rest, early):
    y_ref, halo_buf, u_buf, gate_buf, wide_scr, column, small_sem, out_sem = rest[:8]
    inner = rest[8:]
    chunks, tokens = gate_buf.shape[:2]
    count = feat_ref.shape[1]
    halo_copy = pltpu.make_async_copy(halo_ref, halo_buf, small_sem.at[0])
    halo_copy.start()
    u_copy = pltpu.make_async_copy(u_ref.at[:, pl.ds(0, early * CHUNK)], u_buf, small_sem.at[1])
    u_copy.start()
    widened(feat_ref, 0, wide_scr, 0)
    local_chunk, local_send = local_parts(u_buf, head_ref, rate_ref, coef_ref, skip_ref, y_ref, *inner)
    halo_copy.wait()
    column[pl.ds(0, 2 * ROWS), :] = jnp.zeros((2 * ROWS, LANES), f32)

    def chunk(at):
        def tile(number, _):
            lanes = tile_lanes(number)
            all_lanes = tile_lanes(at * TILES + number)
            taps = chunk_taps(wide_scr, at, 0, number, count)
            lay_halo(column, halo_buf, 2, all_lanes)
            lay_column(column, query_ref, all_lanes)
            found = list(fir(column, taps, 2 * ROWS, tokens // ROWS))
            for pair in range(tokens // (2 * ROWS)):
                rows = slice(pair * 2 * ROWS, (pair + 1) * 2 * ROWS)
                gate_buf[at, rows, lanes] = jnp.concatenate(found[pair * 2 : pair * 2 + 2], axis=0).astype(bf16)
            return 0

        lax.fori_loop(0, TILES, tile, 0)

    give = columns_out(gate_ref, gate_buf, out_sem)
    over_chunks(0, chunks, chunk, give)
    u_copy.wait()
    over_chunks(0, early, local_chunk, local_send)
    for at in range(early):
        wait_all(local_send(at))
    for at in range(chunks):
        wait_all(give(at))


def prefix_kernel(piece_ref, rate_ref, coef_ref, out_ref, *, tokens, axes):
    devices, piece_modes, piece_width = piece_ref.shape
    split = devices * piece_modes // rate_ref.shape[0]
    mine = devices - 1 - lax.axis_index(axes)
    mode, part = mine // split * piece_modes, mine % split
    group = pl.multiple_of(mode // ROWS * ROWS, ROWS)
    first = pl.multiple_of(part * piece_width, LANES)

    def mine_of(ref):
        rows = ref[pl.ds(group, ROWS), pl.ds(first, piece_width)]
        place = lax.broadcasted_iota(jnp.int32, rows.shape, 0)
        found = [
            jnp.sum(jnp.where(place == mode - group + row, rows, 0.0), axis=0, keepdims=True)
            for row in range(piece_modes)
        ]
        return jnp.concatenate(found, axis=0)

    coef = mine_of(coef_ref)
    through = jnp.exp(-float(tokens) * mine_of(rate_ref))

    def lap(number, entering):
        for step in range(4):
            source = devices - 1 - (number * 4 + step)
            out_ref[source] = (coef * entering).astype(out_ref.dtype)
            entering = through * entering + piece_ref[source].astype(f32)
        return entering

    lax.fori_loop(0, devices // 4, lap, jnp.zeros((piece_modes, piece_width), f32))


def local_kernel(u_ref, head_ref, rate_ref, coef_ref, skip_ref, *rest, first, last):
    chunk, send = local_parts(u_ref, head_ref, rate_ref, coef_ref, skip_ref, *rest[-5:])
    over_chunks(first, last, chunk, send)
    for at in range(first, last):
        wait_all(send(at))


def local_parts(u_ref, head_ref, rate_ref, coef_ref, skip_ref, y_ref, *scratches):
    y_buf, token_scr, sum_scr, out_sem = scratches
    tokens = u_ref.shape[0]
    modes = rate_ref.shape[0]
    half_groups = tokens // ROWS // 2
    top = first_half()

    def chunk(at):
        for pair in range(half_groups):
            block = u_ref[pair * 2 * ROWS : (pair + 1) * 2 * ROWS, span(at)].astype(f32)
            if pair == 0:
                block = block + head_ref[:, span(at)].astype(f32)
            for part in range(2):
                group = pair * 2 + part
                half, within = group // half_groups, group % half_groups
                for tile in range(TILES):
                    piece = lanes_of(block, tile)[part * ROWS : (part + 1) * ROWS]
                    put_tile(token_scr, within, half * TILES + tile, piece)
        (skip,) = spread_rows(skip_ref, at, range(1))
        coef = spread_rows(coef_ref, at, range(modes))
        decay = [jnp.exp(-rate) for rate in spread_rows(rate_ref, at, range(modes))]

        def eight(group, state):
            state = list(state)
            for row in range(ROWS):
                u = get_row(token_scr, group, row)
                state = [factor * one + u for factor, one in zip(decay, state)]
                terms = [factor * one for factor, one in zip([skip] + coef, [u] + state)]
                sum_scr[pl.ds(group * ROWS * ROWS + row, ROWS, stride=ROWS), :] = tree(terms)
            return tuple(state)

        state = lax.fori_loop(0, half_groups, eight, (jnp.zeros((ROWS, LANES), f32),) * modes)
        carried = tuple(
            jnp.where(top, 0.0, pltpu.roll(factor * one, TILES, 0)) for factor, one in zip(coef, state)
        )

        def eight_more(group, carried):
            for row in range(ROWS):
                carried = [factor * one for factor, one in zip(decay, carried)]
                place = pl.ds(group * ROWS * ROWS + row, ROWS, stride=ROWS)
                sum_scr[place, :] = sum_scr[place, :] + tree(carried)
            return tuple(carried)

        lax.fori_loop(0, half_groups, eight_more, carried)
        for group in range(2 * half_groups):
            half, within = group // half_groups, group % half_groups
            for tile in range(TILES):
                slot = (within * ROWS + half * TILES + tile) * ROWS
                rows = slice(group * ROWS, (group + 1) * ROWS)
                y_buf[at, rows, tile * LANES : (tile + 1) * LANES] = sum_scr[pl.ds(slot, ROWS), :]

    return chunk, columns_out(y_ref, y_buf, out_sem)


def final_kernel(piece_ref, rate_ref, y_ref, gate_ref, out_ref, *scratches, axes):
    y_buf, gate_buf, out_buf, total_scr, power_scr, in_sem, out_sem = scratches
    chunks, tokens = y_buf.shape[:2]
    modes = rate_ref.shape[0]
    fetch = columns_in(((y_ref, y_buf), (gate_ref, gate_buf)), in_sem)
    give = columns_out(out_ref, out_buf, out_sem)
    start_all(fetch(0))
    bits = [(sublane() >> level) % 2 == 1 for level in range(3)]
    pairs = [slice(first, first + 2 * ROWS) for first in range(0, tokens, 2 * ROWS)]

    def finish(at, rows, lanes, sums):
        gates = gate_buf[at, rows, lanes].astype(f32)
        out_buf[at, rows, lanes] = (gates * rounded(sums)).astype(bf16)

    def chunk(at):
        through = jnp.exp(-rate_ref[:, span(at)])
        for level in range(4):
            power_scr[level] = through
            through = through * through

        def tile(number):
            lanes = tile_lanes(number)
            state = []
            for mode in range(modes):
                rows = [wide(power_scr[level, mode : mode + 1, lanes]) for level in range(3)]
                lead = jnp.where(bits[0], rows[1], rows[0])
                for bit, row in zip(bits[1:], rows[1:]):
                    lead = lead * jnp.where(bit, row, 1.0)
                state.append(lead * wide(total_scr[mode : mode + 1, tile_lanes(at * TILES + number)]))
            decay = [wide(power_scr[3, mode : mode + 1, lanes]) for mode in range(modes)]
            for rows in pairs:
                sums = []
                for first in (rows.start, rows.start + ROWS):
                    sums.append(y_buf[at, first : first + ROWS, lanes] + tree(state))
                    state = [factor * one for factor, one in zip(decay, state)]
                finish(at, rows, lanes, jnp.concatenate(sums, axis=0))

        def some(number, _):
            for part in range(LAP):
                tile(number * LAP + part)
            return 0

        lax.fori_loop(0, TILES // LAP, some, 0)

    def chunk_alone(at):
        def tile(number, _):
            lanes = tile_lanes(number)
            for rows in pairs:
                finish(at, rows, lanes, y_buf[at, rows, lanes])
            return 0

        lax.fori_loop(0, TILES, tile, 0)

    def begin_others():
        for at in range(1, min(AHEAD, chunks)):
            start_all(fetch(at))

    first = lax.axis_index(axes) == 0

    @pl.when(first)
    def _():
        begin_others()
        over_chunks(0, chunks, with_fetch(chunks, fetch, chunk_alone), give)

    @pl.when(jnp.logical_not(first))
    def _():
        pieces, piece_modes, piece_width = piece_ref.shape
        split = pieces * piece_modes // modes
        for piece in range(pieces):
            row, part = piece // split * piece_modes, piece % split
            lanes = slice(part * piece_width, (part + 1) * piece_width)
            total_scr[row : row + piece_modes, lanes] = piece_ref[piece].astype(f32)
        begin_others()
        over_chunks(0, chunks, with_fetch(chunks, fetch, chunk), give)

    for at in range(chunks):
        wait_all(give(at))


def cost(flops, moved):
    return pl.CostEstimate(flops=int(flops), bytes_accessed=int(moved), transcendentals=0)


def local(query, key_proj, value_proj, featurizer, rates, residues, skip, *, axes):
    tokens, width = query.shape
    modes = rates.shape[0]
    members, taps, groups = featurizer.shape
    devices = math.prod(lax.axis_size(axis) for axis in axes)
    chunks = width // CHUNK
    tiles = width // LANES
    split = devices * 2 // modes
    even = devices * 2 % modes == 0 and tiles % split == 0
    vmem = pltpu.VMEM
    far = pltpu.HBM
    near = jax.ShapeDtypeStruct
    dma = pltpu.SemaphoreType.DMA
    elements = tokens * width

    def call(kernel, inputs, outputs, scratches, name, close=(), **more):
        inputs = [
            value if at in close else pltpu.with_memory_space_constraint(value, far)
            for at, value in enumerate(inputs)
        ]
        beside, there = pl.BlockSpec(memory_space=vmem), pl.BlockSpec(memory_space=far)
        return pl.pallas_call(
            kernel,
            in_specs=[beside if at in close else there for at in range(len(inputs))],
            out_specs=[beside if isinstance(one, near) else there for one in outputs],
            out_shape=outputs,
            scratch_shapes=scratches,
            compiler_params=pltpu.CompilerParams(vmem_limit_bytes=32 * 2**20),
            name=name,
            **more,
        )(*inputs)

    halo_shape = (members * (taps - 1) // 2, 2, width)
    (packed,) = call(
        pack_kernel,
        (key_proj, value_proj, query),
        [near(halo_shape, bf16)],
        [vmem((members, 2 * ROWS, width), bf16), dma((members,))],
        "pack",
    )
    halo = lax.ppermute(packed, axes, [(at, at + 1) for at in range(devices - 1)])

    column = vmem((2 * ROWS + tokens, LANES), f32)
    half_buf, whole_buf = vmem((chunks, tokens, CHUNK), bf16), vmem((chunks, tokens, CHUNK), f32)
    u, u_far, wide_taps, state = call(
        signal_kernel,
        (key_proj, value_proj, featurizer, rates),
        [near((tokens, width), bf16), far((tokens, width), bf16)]
        + [near((chunks, 2, ROWS, CHUNK), f32), near((modes, width), f32)],
        [vmem((4, modes, width), f32), vmem((modes, ROWS, LANES), f32)] + [column] * (2 * TILES)
        + [dma((chunks,))],
        "signal",
        close=range(4),
        cost_estimate=cost(60 * elements, 10 * elements),
    )

    pieces = (devices, 2, width // split) if even else (modes // 2, 2, width)
    left, head, u = call(
        functools.partial(head_kernel, tokens=tokens, reach=taps - 1),
        (key_proj, value_proj, halo, rates, wide_taps, state, u, u_far),
        [near(pieces, bf16), near((2 * ROWS, width), bf16), far((tokens, width), bf16)],
        [vmem((TILES, 2, 3 * ROWS, LANES), f32), vmem((TILES, ROWS, LANES), f32)]
        + [vmem((modes, width), f32), dma((1,))],
        "head",
        close=range(7),
        input_output_aliases={7: 2},
    )
    left, halo_late, rates_late, skip_late = lax.optimization_barrier((left, halo, rates, skip))
    coef = residues * jnp.sqrt(-jnp.expm1(-2.0 * rates_late) / modes)
    skip_row = skip_late[None, :]
    stage = vmem((tokens // ROWS // 2 * ROWS * ROWS, LANES), f32)
    local_shapes = [far((tokens, width), f32)]
    local_scratches = [whole_buf, stage, stage, dma((1, chunks))]
    early = chunks * 2 // 9
    gate, y = call(
        functools.partial(gate_kernel, early=early),
        (query, halo_late, featurizer, u, head, rates, coef, skip_row),
        [far((tokens, width), bf16)] + local_shapes,
        [vmem(halo_shape, bf16), vmem((tokens, early * CHUNK), bf16), half_buf]
        + [vmem((chunks, 1, ROWS, CHUNK), f32), column, dma((2,)), dma((1, chunks))]
        + local_scratches,
        "gate",
        close=(0, 2, 4, 5, 6, 7),
        cost_estimate=cost(28 * elements, 6 * elements),
    )

    def swap(value):
        order = [list(range(devices))[::-1]]
        return lax.all_to_all(value, axes, split_axis=0, concat_axis=0, axis_index_groups=order, tiled=True)

    share = modes * width // devices
    theirs = swap(left if even else left.reshape(devices, share))
    theirs, gate, coef, skip_row, y = lax.optimization_barrier((theirs, gate, coef, skip_row, y))
    if even:
        (entering,) = call(
            functools.partial(prefix_kernel, tokens=tokens, axes=axes),
            (theirs, rates, coef),
            [near(pieces, bf16)],
            [],
            "prefix",
            close=(0, 1, 2),
        )
    else:
        mine = devices - 1 - lax.axis_index(axes)
        through = jnp.exp(-float(tokens) * lax.dynamic_slice_in_dim(rates.reshape(-1), mine * share, share))
        factor = lax.dynamic_slice_in_dim(coef.reshape(-1), mine * share, share)
        _, entering = lax.scan(
            lambda so_far, piece: (through * so_far + piece.astype(f32), (factor * so_far).astype(bf16)),
            jnp.zeros((share,), f32),
            theirs,
            reverse=True,
        )

    entering, y = lax.optimization_barrier((entering, y))
    entered = swap(entering).reshape(pieces)
    (y,) = call(
        functools.partial(local_kernel, first=early, last=chunks),
        (u, head, rates, coef, skip_row, y),
        local_shapes,
        local_scratches,
        "within",
        close=range(5),
        cost_estimate=cost(50 * elements, 8 * elements),
        input_output_aliases={5: 0},
    )

    (out,) = call(
        functools.partial(final_kernel, axes=axes),
        (entered, rates, y, gate),
        [far((tokens, width), bf16)],
        [whole_buf, half_buf, half_buf, vmem((modes, width), f32), vmem((4, modes, CHUNK), f32)]
        + [dma((2, chunks)), dma((1, chunks))],
        "final",
        close=(0, 1),
        cost_estimate=cost(40 * elements, 10 * elements),
    )
    return out


def solution(mesh):
    axes = tuple(mesh.axis_names)
    placed = (P(axes, None),) * 3 + (P(),) * 4
    return jax.shard_map(
        functools.partial(local, axes=axes),
        mesh=mesh,
        in_specs=placed,
        out_specs=P(axes, None),
        check_vma=False,
    )
```

```python
import functools
import math

import jax
import jax.numpy as jnp
from jax import lax
from jax.experimental import pallas as pl
from jax.experimental.pallas import tpu as pltpu
from jax.sharding import PartitionSpec as P

LANES = 128
ROWS = 8
TILES = 4
CHUNK = TILES * LANES
AHEAD = 4
LAP = 4
f32 = jnp.float32
bf16 = jnp.bfloat16


def put_tile(scratch, group, slot, tile):
    scratch[pl.ds((group * ROWS + slot) * ROWS, ROWS), :] = tile


def get_row(scratch, group, row):
    return scratch[pl.ds(group * ROWS * ROWS + row, ROWS, stride=ROWS), :]


def lanes_of(value, tile):
    return value[:, tile * LANES : (tile + 1) * LANES]


def tile_lanes(tile):
    return pl.ds(pl.multiple_of(tile * LANES, LANES), LANES)


def span(at):
    return pl.ds(pl.multiple_of(at * CHUNK, CHUNK), CHUNK)


def wide(row):
    return jnp.broadcast_to(row, (ROWS, LANES))


def first_half():
    return lax.broadcasted_iota(jnp.int32, (ROWS, LANES), 0) < TILES


def sublane():
    return lax.broadcasted_iota(jnp.int32, (ROWS, LANES), 0)


def spread(row_of):
    slot = sublane() % TILES
    result = wide(row_of(TILES - 1))
    for tile in range(TILES - 1):
        result = jnp.where(slot == tile, wide(row_of(tile)), result)
    return result


def spread_rows(ref, at, rows):
    def one(row):
        return spread(lambda tile: ref[row : row + 1, tile_lanes(at * TILES + tile)])

    return [one(row) for row in rows]


def rounded(value):
    return value.astype(bf16).astype(f32)


def tiles_of(block):
    block = block.astype(f32)
    return [block[at : at + ROWS] for at in range(0, block.shape[0], ROWS)]


def fir(column, taps, first, count):
    half = ROWS // 2
    top = sublane() < half

    def seen(start, lags):
        return [column[pl.ds(start - lag, ROWS), :] for lag in range(lags)]

    def far_part(rows):
        total = taps[half] * rows[0]
        for lag in range(half + 1, len(taps)):
            total = total + taps[lag] * rows[lag - half]
        return pltpu.roll(total, half, 0)

    before = far_part(seen(first - ROWS, len(taps) - half))
    for start in range(first, first + count * ROWS, ROWS):
        rows = seen(start, half)
        now = far_part(rows)
        total = taps[0] * rows[0]
        for lag in range(1, half):
            total = total + taps[lag] * rows[lag]
        yield total + jnp.where(top, before, now)
        before = now


def fir_loads(column, taps, first):
    total = taps[0] * column[pl.ds(first, ROWS), :]
    for lag in range(1, len(taps)):
        total = total + taps[lag] * column[pl.ds(first - lag, ROWS), :]
    return total


def lay_column(column, source, lanes):
    for pair in range(source.shape[0] // (2 * ROWS)):
        rows = slice(pair * 2 * ROWS, (pair + 1) * 2 * ROWS)
        column[pl.ds((pair + 1) * 2 * ROWS, 2 * ROWS), :] = source[rows, lanes].astype(f32)


def chunk_taps(wide_ref, at, member, tile, count):
    return [wide(wide_ref[at, member, lag : lag + 1, tile_lanes(tile)]) for lag in range(count)]


def widened(feat_ref, member, out_ref, position):
    chunks, taps = out_ref.shape[0], feat_ref.shape[1]
    count = feat_ref.shape[2] // chunks
    rows = [feat_ref[member, :, at * count : (at + 1) * count] for at in range(chunks)]
    rows = [jnp.concatenate([row, jnp.zeros((ROWS - taps, count), f32)], axis=0) for row in rows]
    group = lax.broadcasted_iota(jnp.int32, (count, CHUNK), 0)
    lane = lax.broadcasted_iota(jnp.int32, (count, CHUNK), 1)
    pick = (group == lane // (CHUNK // count)).astype(f32).astype(bf16)
    parts, rest = [], jnp.concatenate(rows, axis=0)
    for _ in range(3):
        term = rest.astype(bf16)
        rest = rest - term.astype(f32)
        parts.append(jnp.dot(term, pick, preferred_element_type=f32))
    out_ref[:, position] = (parts[0] + parts[1] + parts[2]).reshape(chunks, ROWS, CHUNK)


def power(base, exponent):
    result = None
    while exponent:
        if exponent & 1:
            result = base if result is None else result * base
        base = base * base
        exponent >>= 1
    return result


def tree(terms):
    while len(terms) > 1:
        terms = [sum(terms[at + 1 : at + 2], terms[at]) for at in range(0, len(terms), 2)]
    return terms[0]


def start_all(copies):
    for copy in copies:
        copy.start()


def wait_all(copies):
    for copy in copies:
        copy.wait()


def begin(chunks, fetch):
    for at in range(min(AHEAD, chunks)):
        start_all(fetch(at))


def over_chunks(first, last, body, send):
    def one(at, _):
        body(at)
        start_all(send(at))
        return 0

    lax.fori_loop(first, last, one, 0)


def with_fetch(chunks, fetch, body):
    def one(at):
        @pl.when(at + AHEAD < chunks)
        def _():
            start_all(fetch(at + AHEAD))

        wait_all(fetch(at))
        body(at)

    return one


def columns_in(pairs, sem):
    def fetch(at):
        return [
            pltpu.make_async_copy(ref.at[:, span(at)], buf.at[at], sem.at[member, at])
            for member, (ref, buf) in enumerate(pairs)
        ]

    return fetch


def columns_out(ref, buf, sem):
    return lambda at: [pltpu.make_async_copy(buf.at[at], ref.at[:, span(at)], sem.at[0, at])]


def lay_halo(column, halo, member, lanes):
    pairs = halo.shape[0] // 3
    for pair in range(pairs):
        column[pl.ds(2 * ROWS - 2 * pairs + 2 * pair, 2), :] = halo[member * pairs + pair, :, lanes].astype(f32)


def pack_kernel(key_ref, value_ref, query_ref, out_ref, in_buf, in_sem):
    tokens = key_ref.shape[0]
    copies = [
        pltpu.make_async_copy(ref.at[pl.ds(tokens - 2 * ROWS, 2 * ROWS)], in_buf.at[at], in_sem.at[at])
        for at, ref in enumerate((key_ref, value_ref, query_ref))
    ]
    start_all(copies)
    wait_all(copies)
    pairs = out_ref.shape[0] // len(copies)
    for at in range(len(copies)):
        tail = in_buf[at].astype(f32)[2 * ROWS - 2 * pairs :]
        for pair in range(pairs):
            out_ref[at * pairs + pair] = tail[2 * pair : 2 * pair + 2].astype(bf16)


def signal_kernel(key_ref, value_ref, feat_ref, rate_ref, u_ref, u_out_ref, wide_ref, state_ref, *scratches):
    power_scr, last_scr, *columns, out_sem = scratches
    tokens, tiles = u_ref.shape[0], u_ref.shape[1] // LANES
    modes = rate_ref.shape[0]
    chunks = tiles // TILES
    count = feat_ref.shape[1]
    for member in range(2):
        widened(feat_ref, member + 1, wide_ref, member)
    for column in columns:
        column[pl.ds(0, 2 * ROWS), :] = jnp.zeros((2 * ROWS, LANES), f32)
    last_scr[...] = jnp.zeros(last_scr.shape, f32)

    def powers(at, _):
        through = jnp.exp(-rate_ref[:, span(at)])
        for level in range(4):
            power_scr[level, :, span(at)] = through
            through = through * through
        return 0

    lax.fori_loop(0, chunks, powers, 0)

    def reduce(number):
        lanes = tile_lanes(number)
        for mode in range(modes):
            whole = last_scr[mode]
            for level in (2, 1, 0):
                factor = wide(power_scr[level, mode : mode + 1, lanes])
                whole = factor * whole + pltpu.roll(whole, ROWS - (1 << level), 0)
            state_ref[mode : mode + 1, lanes] = whole[:1]

    def tile(number, columns):
        lanes = tile_lanes(number)
        reduce(jnp.maximum(number - 1, 0))
        taps = [chunk_taps(wide_ref, number // TILES, member, number % TILES, count) for member in range(2)]
        for column, ref in zip(columns, (key_ref, value_ref)):
            lay_column(column, ref, lanes)
        decay = [wide(power_scr[3, mode : mode + 1, lanes]) for mode in range(modes)]
        state = None
        for pair in range(tokens // (2 * ROWS)):
            found = []
            for first in (pair * 2 * ROWS + 2 * ROWS, pair * 2 * ROWS + 3 * ROWS):
                found.append(fir_loads(columns[0], taps[0], first) * fir_loads(columns[1], taps[1], first))
            if pair == 0:
                found[0] = jnp.where(sublane() < count - 1, 0.0, found[0])
            both = jnp.concatenate(found, axis=0).astype(bf16)
            u_ref[pair * 2 * ROWS : (pair + 1) * 2 * ROWS, lanes] = both
            for u in tiles_of(both):
                if state is None:
                    state = [u] * modes
                else:
                    state = [factor * one + u for factor, one in zip(decay, state)]
        for mode in range(modes):
            last_scr[mode] = state[mode]

    def send(at):
        return pltpu.make_async_copy(u_ref.at[:, span(at)], u_out_ref.at[:, span(at)], out_sem.at[at])

    def chunk(at, _):
        for part in range(TILES):
            tile(TILES * at + part, columns[2 * part : 2 * part + 2])

        @pl.when(at < chunks - 1)
        def _():
            send(at).start()

        return 0

    lax.fori_loop(0, chunks, chunk, 0)
    reduce(tiles - 1)
    for at in range(chunks - 1):
        send(at).wait()


def head_kernel(key_ref, value_ref, halo_ref, rate_ref, wide_ref, state_ref, u_ref, _, *rest, tokens, reach):
    out_ref, head_ref, u_out_ref, column_scr, token_scr, total_scr, sem = rest
    modes, tiles = state_ref.shape[0], state_ref.shape[1] // LANES
    last = span(tiles // TILES - 1)
    move = pltpu.make_async_copy(u_ref.at[:, last], u_out_ref.at[:, last], sem.at[0])
    move.start()
    pieces, piece_modes, piece_width = out_ref.shape

    def some(chunk, _):
        for number in range(TILES):
            lanes = tile_lanes(chunk * TILES + number)
            parts = []
            for member in range(2):
                taps = chunk_taps(wide_ref, chunk, member, number, reach + 1)
                column = column_scr.at[number, member]
                column[pl.ds(0, 2 * ROWS), :] = jnp.zeros((2 * ROWS, LANES), f32)
                lay_halo(column, halo_ref, member, lanes)
                source = (key_ref, value_ref)[member]
                column[pl.ds(2 * ROWS, ROWS), :] = source[: 2 * ROWS, lanes].astype(f32)[:ROWS]
                parts.append(fir_loads(column, taps, 2 * ROWS))
            u = jnp.where(sublane() < reach, rounded(parts[0] * parts[1]), 0.0)
            token_scr[number] = u
            for group in range(0, modes, ROWS):
                decay = jnp.exp(-rate_ref[group : group + ROWS, lanes])
                head = wide(token_scr[number, :1, :])
                for row in range(1, reach):
                    head = decay * head + wide(token_scr[number, row : row + 1, :])
                total = state_ref[group : group + ROWS, lanes] + power(decay, tokens - reach) * head
                total_scr[group : group + ROWS, lanes] = total
            head_ref[:, lanes] = jnp.concatenate([u, jnp.zeros((ROWS, LANES), f32)], axis=0).astype(bf16)
        return 0

    lax.fori_loop(0, tiles // TILES, some, 0)
    split = pieces * piece_modes // modes
    for piece in range(pieces):
        first, part = piece // split * piece_modes, piece % split
        rows = total_scr[first : first + piece_modes, part * piece_width : (part + 1) * piece_width]
        out_ref[piece] = rows.astype(out_ref.dtype)
    move.wait()


def gate_kernel(query_ref, halo_ref, feat_ref, u_ref, head_ref, rate_ref, coef_ref, skip_ref, gate_ref, *rest, early):
    y_ref, halo_buf, u_buf, gate_buf, wide_scr, column, small_sem, out_sem = rest[:8]
    inner = rest[8:]
    chunks, tokens = gate_buf.shape[:2]
    count = feat_ref.shape[1]
    halo_copy = pltpu.make_async_copy(halo_ref, halo_buf, small_sem.at[0])
    halo_copy.start()
    u_copy = pltpu.make_async_copy(u_ref.at[:, pl.ds(0, early * CHUNK)], u_buf, small_sem.at[1])
    u_copy.start()
    widened(feat_ref, 0, wide_scr, 0)
    local_chunk, local_send = local_parts(u_buf, head_ref, rate_ref, coef_ref, skip_ref, y_ref, *inner)
    halo_copy.wait()
    column[pl.ds(0, 2 * ROWS), :] = jnp.zeros((2 * ROWS, LANES), f32)

    def chunk(at):
        def tile(number, _):
            lanes = tile_lanes(number)
            all_lanes = tile_lanes(at * TILES + number)
            taps = chunk_taps(wide_scr, at, 0, number, count)
            lay_halo(column, halo_buf, 2, all_lanes)
            lay_column(column, query_ref, all_lanes)
            found = list(fir(column, taps, 2 * ROWS, tokens // ROWS))
            for pair in range(tokens // (2 * ROWS)):
                rows = slice(pair * 2 * ROWS, (pair + 1) * 2 * ROWS)
                gate_buf[at, rows, lanes] = jnp.concatenate(found[pair * 2 : pair * 2 + 2], axis=0).astype(bf16)
            return 0

        lax.fori_loop(0, TILES, tile, 0)

    give = columns_out(gate_ref, gate_buf, out_sem)
    over_chunks(0, chunks, chunk, give)
    u_copy.wait()
    over_chunks(0, early, local_chunk, local_send)
    for at in range(early):
        wait_all(local_send(at))
    for at in range(chunks):
        wait_all(give(at))


def prefix_kernel(piece_ref, rate_ref, coef_ref, out_ref, *, tokens, axes):
    devices, piece_modes, piece_width = piece_ref.shape
    split = devices * piece_modes // rate_ref.shape[0]
    mine = devices - 1 - lax.axis_index(axes)
    mode, part = mine // split * piece_modes, mine % split
    group = pl.multiple_of(mode // ROWS * ROWS, ROWS)
    first = pl.multiple_of(part * piece_width, LANES)

    def mine_of(ref):
        rows = ref[pl.ds(group, ROWS), pl.ds(first, piece_width)]
        return pltpu.roll(rows, lax.rem(ROWS - (mode - group), ROWS), 0)[:piece_modes]

    coef = mine_of(coef_ref)
    through = jnp.exp(-float(tokens) * mine_of(rate_ref))

    def lap(number, entering):
        for step in range(4):
            source = devices - 1 - (number * 4 + step)
            out_ref[source] = (coef * entering).astype(out_ref.dtype)
            entering = through * entering + piece_ref[source].astype(f32)
        return entering

    lax.fori_loop(0, devices // 4, lap, jnp.zeros((piece_modes, piece_width), f32))


def local_kernel(u_ref, head_ref, rate_ref, coef_ref, skip_ref, gate_ref, _, y_ref, y_last_ref, gate_last_ref, *scratches, first):
    *inner, sem = scratches
    last = u_ref.shape[1] // CHUNK - 1
    take = pltpu.make_async_copy(gate_ref.at[:, span(last)], gate_last_ref, sem.at[0])
    take.start()
    chunk, send = local_parts(u_ref, head_ref, rate_ref, coef_ref, skip_ref, y_ref, *inner)
    over_chunks(first, last, chunk, send)
    chunk(last)
    y_last_ref[...] = inner[0][last]
    for at in range(first, last):
        wait_all(send(at))
    take.wait()


def local_parts(u_ref, head_ref, rate_ref, coef_ref, skip_ref, y_ref, *scratches):
    y_buf, token_scr, sum_scr, out_sem = scratches
    tokens = u_ref.shape[0]
    modes = rate_ref.shape[0]
    half_groups = tokens // ROWS // 2
    top = first_half()

    def chunk(at):
        for pair in range(half_groups):
            block = u_ref[pair * 2 * ROWS : (pair + 1) * 2 * ROWS, span(at)].astype(f32)
            if pair == 0:
                block = block + head_ref[:, span(at)].astype(f32)
            for part in range(2):
                group = pair * 2 + part
                half, within = group // half_groups, group % half_groups
                for tile in range(TILES):
                    piece = lanes_of(block, tile)[part * ROWS : (part + 1) * ROWS]
                    put_tile(token_scr, within, half * TILES + tile, piece)
        (skip,) = spread_rows(skip_ref, at, range(1))
        coef = spread_rows(coef_ref, at, range(modes))
        decay = [jnp.exp(-rate) for rate in spread_rows(rate_ref, at, range(modes))]

        def eight(group, state):
            state = list(state)
            for row in range(ROWS):
                u = get_row(token_scr, group, row)
                state = [factor * one + u for factor, one in zip(decay, state)]
                terms = [factor * one for factor, one in zip([skip] + coef, [u] + state)]
                sum_scr[pl.ds(group * ROWS * ROWS + row, ROWS, stride=ROWS), :] = tree(terms)
            return tuple(state)

        state = lax.fori_loop(0, half_groups, eight, (jnp.zeros((ROWS, LANES), f32),) * modes)
        carried = tuple(
            jnp.where(top, 0.0, pltpu.roll(factor * one, TILES, 0)) for factor, one in zip(coef, state)
        )

        def eight_more(group, carried):
            for row in range(ROWS):
                carried = [factor * one for factor, one in zip(decay, carried)]
                place = pl.ds(group * ROWS * ROWS + row, ROWS, stride=ROWS)
                sum_scr[place, :] = sum_scr[place, :] + tree(carried)
            return tuple(carried)

        lax.fori_loop(0, half_groups, eight_more, carried)
        for group in range(2 * half_groups):
            half, within = group // half_groups, group % half_groups
            for tile in range(TILES):
                slot = (within * ROWS + half * TILES + tile) * ROWS
                rows = slice(group * ROWS, (group + 1) * ROWS)
                y_buf[at, rows, tile * LANES : (tile + 1) * LANES] = sum_scr[pl.ds(slot, ROWS), :]

    return chunk, columns_out(y_ref, y_buf, out_sem)


def final_kernel(piece_ref, rate_ref, y_last_ref, gate_last_ref, y_ref, gate_ref, out_ref, *scratches, axes):
    y_buf, gate_buf, out_buf, total_scr, power_scr, in_sem, out_sem = scratches
    chunks, tokens = y_buf.shape[:2]
    modes = rate_ref.shape[0]
    fetch = columns_in(((y_ref, y_buf), (gate_ref, gate_buf)), in_sem)
    give = columns_out(out_ref, out_buf, out_sem)
    begin(chunks - 1, fetch)
    bits = [(sublane() >> level) % 2 == 1 for level in range(3)]
    pairs = [slice(first, first + 2 * ROWS) for first in range(0, tokens, 2 * ROWS)]

    def finish(at, rows, lanes, sums):
        gates = gate_buf[at, rows, lanes].astype(f32)
        out_buf[at, rows, lanes] = (gates * rounded(sums)).astype(bf16)

    def chunk(at):
        through = jnp.exp(-rate_ref[:, span(at)])
        for level in range(4):
            power_scr[level] = through
            through = through * through

        def tile(number):
            lanes = tile_lanes(number)
            state = []
            for mode in range(modes):
                rows = [wide(power_scr[level, mode : mode + 1, lanes]) for level in range(3)]
                lead = jnp.where(bits[0], rows[1], rows[0])
                for bit, row in zip(bits[1:], rows[1:]):
                    lead = lead * jnp.where(bit, row, 1.0)
                state.append(lead * wide(total_scr[mode : mode + 1, tile_lanes(at * TILES + number)]))
            decay = [wide(power_scr[3, mode : mode + 1, lanes]) for mode in range(modes)]
            for rows in pairs:
                sums = []
                for first in (rows.start, rows.start + ROWS):
                    sums.append(y_buf[at, first : first + ROWS, lanes] + tree(state))
                    state = [factor * one for factor, one in zip(decay, state)]
                finish(at, rows, lanes, jnp.concatenate(sums, axis=0))

        def some(number, _):
            for part in range(LAP):
                tile(number * LAP + part)
            return 0

        lax.fori_loop(0, TILES // LAP, some, 0)

    def chunk_alone(at):
        def tile(number, _):
            lanes = tile_lanes(number)
            for rows in pairs:
                finish(at, rows, lanes, y_buf[at, rows, lanes])
            return 0

        lax.fori_loop(0, TILES, tile, 0)

    def all_chunks(body):
        last = chunks - 1
        y_buf[last] = y_last_ref[...]
        gate_buf[last] = gate_last_ref[...]
        body(last)
        start_all(give(last))
        over_chunks(0, last, with_fetch(last, fetch, body), give)

    first = lax.axis_index(axes) == 0

    @pl.when(first)
    def _():
        all_chunks(chunk_alone)

    @pl.when(jnp.logical_not(first))
    def _():
        pieces, piece_modes, piece_width = piece_ref.shape
        split = pieces * piece_modes // modes
        for piece in range(pieces):
            row, part = piece // split * piece_modes, piece % split
            lanes = slice(part * piece_width, (part + 1) * piece_width)
            total_scr[row : row + piece_modes, lanes] = piece_ref[piece].astype(f32)
        all_chunks(chunk)

    for at in range(chunks):
        wait_all(give(at))


def cost(flops, moved):
    return pl.CostEstimate(flops=int(flops), bytes_accessed=int(moved), transcendentals=0)


def local(query, key_proj, value_proj, featurizer, rates, residues, skip, *, axes):
    tokens, width = query.shape
    modes = rates.shape[0]
    members, taps, groups = featurizer.shape
    devices = math.prod(lax.axis_size(axis) for axis in axes)
    chunks = width // CHUNK
    tiles = width // LANES
    split = devices * 2 // modes
    even = devices * 2 % modes == 0 and tiles % split == 0
    vmem = pltpu.VMEM
    far = pltpu.HBM
    near = jax.ShapeDtypeStruct
    dma = pltpu.SemaphoreType.DMA
    elements = tokens * width

    def call(kernel, inputs, outputs, scratches, name, close=(), **more):
        inputs = [
            value if at in close else pltpu.with_memory_space_constraint(value, far)
            for at, value in enumerate(inputs)
        ]
        beside, there = pl.BlockSpec(memory_space=vmem), pl.BlockSpec(memory_space=far)
        return pl.pallas_call(
            kernel,
            in_specs=[beside if at in close else there for at in range(len(inputs))],
            out_specs=[beside if isinstance(one, near) else there for one in outputs],
            out_shape=outputs,
            scratch_shapes=scratches,
            compiler_params=pltpu.CompilerParams(vmem_limit_bytes=32 * 2**20),
            name=name,
            **more,
        )(*inputs)

    halo_shape = (members * (taps - 1) // 2, 2, width)
    (packed,) = call(
        pack_kernel,
        (key_proj, value_proj, query),
        [near(halo_shape, bf16)],
        [vmem((members, 2 * ROWS, width), bf16), dma((members,))],
        "pack",
    )
    halo = lax.ppermute(packed, axes, [(at, at + 1) for at in range(devices - 1)])

    column = vmem((2 * ROWS + tokens, LANES), f32)
    half_buf, whole_buf = vmem((chunks, tokens, CHUNK), bf16), vmem((chunks, tokens, CHUNK), f32)
    u, u_far, wide_taps, state = call(
        signal_kernel,
        (key_proj, value_proj, featurizer, rates),
        [near((tokens, width), bf16), far((tokens, width), bf16)]
        + [near((chunks, 2, ROWS, CHUNK), f32), near((modes, width), f32)],
        [vmem((4, modes, width), f32), vmem((modes, ROWS, LANES), f32)] + [column] * (2 * TILES)
        + [dma((chunks,))],
        "signal",
        close=range(4),
        cost_estimate=cost(60 * elements, 10 * elements),
    )

    pieces = (devices, 2, width // split) if even else (modes // 2, 2, width)
    left, head, u = call(
        functools.partial(head_kernel, tokens=tokens, reach=taps - 1),
        (key_proj, value_proj, halo, rates, wide_taps, state, u, u_far),
        [near(pieces, bf16), near((2 * ROWS, width), bf16), far((tokens, width), bf16)],
        [vmem((TILES, 2, 3 * ROWS, LANES), f32), vmem((TILES, ROWS, LANES), f32)]
        + [vmem((modes, width), f32), dma((1,))],
        "head",
        close=range(7),
        input_output_aliases={7: 2},
    )
    left, halo_late, rates_late, skip_late = lax.optimization_barrier((left, halo, rates, skip))
    coef = residues * jnp.sqrt(-jnp.expm1(-2.0 * rates_late) / modes)
    skip_row = skip_late[None, :]
    stage = vmem((tokens // ROWS // 2 * ROWS * ROWS, LANES), f32)
    local_shapes = [far((tokens, width), f32)]
    local_scratches = [whole_buf, stage, stage, dma((1, chunks))]
    early = chunks * 2 // 9
    gate, y = call(
        functools.partial(gate_kernel, early=early),
        (query, halo_late, featurizer, u, head, rates, coef, skip_row),
        [far((tokens, width), bf16)] + local_shapes,
        [vmem(halo_shape, bf16), vmem((tokens, early * CHUNK), bf16), half_buf]
        + [vmem((chunks, 1, ROWS, CHUNK), f32), column, dma((2,)), dma((1, chunks))]
        + local_scratches,
        "gate",
        close=(0, 2, 4, 5, 6, 7),
        cost_estimate=cost(28 * elements, 6 * elements),
    )

    def swap(value):
        order = [list(range(devices))[::-1]]
        return lax.all_to_all(value, axes, split_axis=0, concat_axis=0, axis_index_groups=order, tiled=True)

    share = modes * width // devices
    theirs = swap(left if even else left.reshape(devices, share))
    theirs, gate, coef, skip_row, y = lax.optimization_barrier((theirs, gate, coef, skip_row, y))
    if even:
        (entering,) = call(
            functools.partial(prefix_kernel, tokens=tokens, axes=axes),
            (theirs, rates, coef),
            [near(pieces, bf16)],
            [],
            "prefix",
            close=(0, 1, 2),
        )
    else:
        mine = devices - 1 - lax.axis_index(axes)
        through = jnp.exp(-float(tokens) * lax.dynamic_slice_in_dim(rates.reshape(-1), mine * share, share))
        factor = lax.dynamic_slice_in_dim(coef.reshape(-1), mine * share, share)
        _, entering = lax.scan(
            lambda so_far, piece: (through * so_far + piece.astype(f32), (factor * so_far).astype(bf16)),
            jnp.zeros((share,), f32),
            theirs,
            reverse=True,
        )

    entering, y = lax.optimization_barrier((entering, y))
    entered = swap(entering).reshape(pieces)
    y, y_last, gate_last = call(
        functools.partial(local_kernel, first=early),
        (u, head, rates, coef, skip_row, gate, y),
        local_shapes + [near((tokens, CHUNK), f32), near((tokens, CHUNK), bf16)],
        local_scratches + [dma((1,))],
        "within",
        close=range(5),
        cost_estimate=cost(50 * elements, 8 * elements),
        input_output_aliases={6: 0},
    )

    (out,) = call(
        functools.partial(final_kernel, axes=axes),
        (entered, rates, y_last, gate_last, y, gate),
        [far((tokens, width), bf16)],
        [whole_buf, half_buf, half_buf, vmem((modes, width), f32), vmem((4, modes, CHUNK), f32)]
        + [dma((2, chunks)), dma((1, chunks))],
        "final",
        close=range(4),
        cost_estimate=cost(40 * elements, 10 * elements),
    )
    return out


def solution(mesh):
    axes = tuple(mesh.axis_names)
    placed = (P(axes, None),) * 3 + (P(),) * 4
    return jax.shard_map(
        functools.partial(local, axes=axes),
        mesh=mesh,
        in_specs=placed,
        out_specs=P(axes, None),
        check_vma=False,
    )
```

```python
import functools
import math

import jax
import jax.numpy as jnp
from jax import lax
from jax.experimental import pallas as pl
from jax.experimental.pallas import tpu as pltpu
from jax.sharding import PartitionSpec as P

LANES = 128
ROWS = 8
TILES = 4
CHUNK = TILES * LANES
AHEAD = 4
LAP = 4
f32 = jnp.float32
bf16 = jnp.bfloat16


def put_tile(scratch, group, slot, tile):
    scratch[pl.ds((group * ROWS + slot) * ROWS, ROWS), :] = tile


def get_row(scratch, group, row):
    return scratch[pl.ds(group * ROWS * ROWS + row, ROWS, stride=ROWS), :]


def lanes_of(value, tile):
    return value[:, tile * LANES : (tile + 1) * LANES]


def tile_lanes(tile):
    return pl.ds(pl.multiple_of(tile * LANES, LANES), LANES)


def span(at):
    return pl.ds(pl.multiple_of(at * CHUNK, CHUNK), CHUNK)


def wide(row):
    return jnp.broadcast_to(row, (ROWS, LANES))


def first_half():
    return lax.broadcasted_iota(jnp.int32, (ROWS, LANES), 0) < TILES


def sublane():
    return lax.broadcasted_iota(jnp.int32, (ROWS, LANES), 0)


def spread(row_of):
    slot = sublane() % TILES
    result = wide(row_of(TILES - 1))
    for tile in range(TILES - 1):
        result = jnp.where(slot == tile, wide(row_of(tile)), result)
    return result


def spread_rows(ref, at, rows):
    def one(row):
        return spread(lambda tile: ref[row : row + 1, tile_lanes(at * TILES + tile)])

    return [one(row) for row in rows]


def rounded(value):
    return value.astype(bf16).astype(f32)


def tiles_of(block):
    block = block.astype(f32)
    return [block[at : at + ROWS] for at in range(0, block.shape[0], ROWS)]


def fir(column, taps, first, count):
    half = ROWS // 2
    top = sublane() < half

    def seen(start, lags):
        return [column[pl.ds(start - lag, ROWS), :] for lag in range(lags)]

    def far_part(rows):
        total = taps[half] * rows[0]
        for lag in range(half + 1, len(taps)):
            total = total + taps[lag] * rows[lag - half]
        return pltpu.roll(total, half, 0)

    before = far_part(seen(first - ROWS, len(taps) - half))
    for start in range(first, first + count * ROWS, ROWS):
        rows = seen(start, half)
        now = far_part(rows)
        total = taps[0] * rows[0]
        for lag in range(1, half):
            total = total + taps[lag] * rows[lag]
        yield total + jnp.where(top, before, now)
        before = now


def fir_loads(column, taps, first):
    total = taps[0] * column[pl.ds(first, ROWS), :]
    for lag in range(1, len(taps)):
        total = total + taps[lag] * column[pl.ds(first - lag, ROWS), :]
    return total


def lay_column(column, source, lanes):
    for pair in range(source.shape[0] // (2 * ROWS)):
        rows = slice(pair * 2 * ROWS, (pair + 1) * 2 * ROWS)
        column[pl.ds((pair + 1) * 2 * ROWS, 2 * ROWS), :] = source[rows, lanes].astype(f32)


def chunk_taps(wide_ref, at, member, tile, count):
    return [wide(wide_ref[at, member, lag : lag + 1, tile_lanes(tile)]) for lag in range(count)]


def widened(feat_ref, member, out_ref, position):
    chunks, taps = out_ref.shape[0], feat_ref.shape[1]
    count = feat_ref.shape[2] // chunks
    rows = [feat_ref[member, :, at * count : (at + 1) * count] for at in range(chunks)]
    rows = [jnp.concatenate([row, jnp.zeros((ROWS - taps, count), f32)], axis=0) for row in rows]
    group = lax.broadcasted_iota(jnp.int32, (count, CHUNK), 0)
    lane = lax.broadcasted_iota(jnp.int32, (count, CHUNK), 1)
    pick = (group == lane // (CHUNK // count)).astype(f32).astype(bf16)
    parts, rest = [], jnp.concatenate(rows, axis=0)
    for _ in range(3):
        term = rest.astype(bf16)
        rest = rest - term.astype(f32)
        parts.append(jnp.dot(term, pick, preferred_element_type=f32))
    out_ref[:, position] = (parts[0] + parts[1] + parts[2]).reshape(chunks, ROWS, CHUNK)


def power(base, exponent):
    result = None
    while exponent:
        if exponent & 1:
            result = base if result is None else result * base
        base = base * base
        exponent >>= 1
    return result


def tree(terms):
    while len(terms) > 1:
        terms = [sum(terms[at + 1 : at + 2], terms[at]) for at in range(0, len(terms), 2)]
    return terms[0]


def start_all(copies):
    for copy in copies:
        copy.start()


def wait_all(copies):
    for copy in copies:
        copy.wait()


def begin(chunks, fetch):
    for at in range(min(AHEAD, chunks)):
        start_all(fetch(at))


def over_chunks(first, last, body, send):
    def one(at, _):
        body(at)
        start_all(send(at))
        return 0

    lax.fori_loop(first, last, one, 0)


def with_fetch(chunks, fetch, body):
    def one(at):
        @pl.when(at + AHEAD < chunks)
        def _():
            start_all(fetch(at + AHEAD))

        wait_all(fetch(at))
        body(at)

    return one


def columns_in(pairs, sem):
    def fetch(at):
        return [
            pltpu.make_async_copy(ref.at[:, span(at)], buf.at[at], sem.at[member, at])
            for member, (ref, buf) in enumerate(pairs)
        ]

    return fetch


def columns_out(ref, buf, sem):
    return lambda at: [pltpu.make_async_copy(buf.at[at], ref.at[:, span(at)], sem.at[0, at])]


def lay_halo(column, halo, member, lanes):
    pairs = halo.shape[0] // 3
    for pair in range(pairs):
        column[pl.ds(2 * ROWS - 2 * pairs + 2 * pair, 2), :] = halo[member * pairs + pair, :, lanes].astype(f32)


def pack_kernel(key_ref, value_ref, query_ref, out_ref, in_buf, in_sem):
    tokens = key_ref.shape[0]
    copies = [
        pltpu.make_async_copy(ref.at[pl.ds(tokens - 2 * ROWS, 2 * ROWS)], in_buf.at[at], in_sem.at[at])
        for at, ref in enumerate((key_ref, value_ref, query_ref))
    ]
    start_all(copies)
    wait_all(copies)
    pairs = out_ref.shape[0] // len(copies)
    for at in range(len(copies)):
        tail = in_buf[at].astype(f32)[2 * ROWS - 2 * pairs :]
        for pair in range(pairs):
            out_ref[at * pairs + pair] = tail[2 * pair : 2 * pair + 2].astype(bf16)


def signal_kernel(key_ref, value_ref, feat_ref, rate_ref, u_ref, u_out_ref, wide_ref, state_ref, *scratches):
    power_scr, last_scr, *columns, out_sem = scratches
    tokens, tiles = u_ref.shape[0], u_ref.shape[1] // LANES
    modes = rate_ref.shape[0]
    chunks = tiles // TILES
    count = feat_ref.shape[1]
    for member in range(2):
        widened(feat_ref, member + 1, wide_ref, member)
    for column in columns:
        column[pl.ds(0, 2 * ROWS), :] = jnp.zeros((2 * ROWS, LANES), f32)
    last_scr[...] = jnp.zeros(last_scr.shape, f32)

    def powers(at, _):
        through = jnp.exp(-rate_ref[:, span(at)])
        for level in range(4):
            power_scr[level, :, span(at)] = through
            through = through * through
        return 0

    lax.fori_loop(0, chunks, powers, 0)

    def reduce(number):
        lanes = tile_lanes(number)
        for mode in range(modes):
            whole = last_scr[mode]
            for level in (2, 1, 0):
                factor = wide(power_scr[level, mode : mode + 1, lanes])
                whole = factor * whole + pltpu.roll(whole, ROWS - (1 << level), 0)
            state_ref[mode : mode + 1, lanes] = whole[:1]

    def tile(number, columns):
        lanes = tile_lanes(number)
        reduce(jnp.maximum(number - 1, 0))
        taps = [chunk_taps(wide_ref, number // TILES, member, number % TILES, count) for member in range(2)]
        for column, ref in zip(columns, (key_ref, value_ref)):
            lay_column(column, ref, lanes)
        decay = [wide(power_scr[3, mode : mode + 1, lanes]) for mode in range(modes)]
        state = None
        for pair in range(tokens // (2 * ROWS)):
            found = []
            for first in (pair * 2 * ROWS + 2 * ROWS, pair * 2 * ROWS + 3 * ROWS):
                found.append(fir_loads(columns[0], taps[0], first) * fir_loads(columns[1], taps[1], first))
            if pair == 0:
                found[0] = jnp.where(sublane() < count - 1, 0.0, found[0])
            both = jnp.concatenate(found, axis=0).astype(bf16)
            u_ref[pair * 2 * ROWS : (pair + 1) * 2 * ROWS, lanes] = both
            for u in tiles_of(both):
                if state is None:
                    state = [u] * modes
                else:
                    state = [factor * one + u for factor, one in zip(decay, state)]
        for mode in range(modes):
            last_scr[mode] = state[mode]

    def send(at):
        return pltpu.make_async_copy(u_ref.at[:, span(at)], u_out_ref.at[:, span(at)], out_sem.at[at])

    def chunk(at, _):
        for part in range(TILES):
            tile(TILES * at + part, columns[2 * part : 2 * part + 2])

        @pl.when(at < chunks - 1)
        def _():
            send(at).start()

        return 0

    lax.fori_loop(0, chunks, chunk, 0)
    reduce(tiles - 1)
    for at in range(chunks - 1):
        send(at).wait()


def head_kernel(key_ref, value_ref, halo_ref, rate_ref, wide_ref, state_ref, u_ref, _, *rest, tokens, reach):
    out_ref, head_ref, u_out_ref, column_scr, token_scr, total_scr, sem = rest
    modes, tiles = state_ref.shape[0], state_ref.shape[1] // LANES
    last = span(tiles // TILES - 1)
    move = pltpu.make_async_copy(u_ref.at[:, last], u_out_ref.at[:, last], sem.at[0])
    move.start()
    pieces, piece_modes, piece_width = out_ref.shape

    lap = column_scr.shape[0]

    def some(chunk, _):
        for number in range(lap):
            lanes = tile_lanes(chunk * lap + number)
            parts = []
            for member in range(2):
                place = chunk * (lap // TILES) + number // TILES
                taps = chunk_taps(wide_ref, place, member, number % TILES, reach + 1)
                column = column_scr.at[number, member]
                column[pl.ds(0, 2 * ROWS), :] = jnp.zeros((2 * ROWS, LANES), f32)
                lay_halo(column, halo_ref, member, lanes)
                source = (key_ref, value_ref)[member]
                column[pl.ds(2 * ROWS, ROWS), :] = source[: 2 * ROWS, lanes].astype(f32)[:ROWS]
                parts.append(fir_loads(column, taps, 2 * ROWS))
            u = jnp.where(sublane() < reach, rounded(parts[0] * parts[1]), 0.0)
            token_scr[number] = u
            for group in range(0, modes, ROWS):
                decay = jnp.exp(-rate_ref[group : group + ROWS, lanes])
                head = wide(token_scr[number, :1, :])
                for row in range(1, reach):
                    head = decay * head + wide(token_scr[number, row : row + 1, :])
                total = state_ref[group : group + ROWS, lanes] + power(decay, tokens - reach) * head
                total_scr[group : group + ROWS, lanes] = total
            head_ref[:, lanes] = jnp.concatenate([u, jnp.zeros((ROWS, LANES), f32)], axis=0).astype(bf16)
        return 0

    lax.fori_loop(0, tiles // lap, some, 0)
    split = pieces * piece_modes // modes
    for piece in range(pieces):
        first, part = piece // split * piece_modes, piece % split
        rows = total_scr[first : first + piece_modes, part * piece_width : (part + 1) * piece_width]
        out_ref[piece] = rows.astype(out_ref.dtype)
    move.wait()


def gate_kernel(query_ref, halo_ref, feat_ref, u_ref, head_ref, rate_ref, coef_ref, skip_ref, gate_ref, *rest, early):
    y_ref, halo_buf, u_buf, gate_buf, wide_scr, column, small_sem, out_sem = rest[:8]
    inner = rest[8:]
    chunks, tokens = gate_buf.shape[:2]
    count = feat_ref.shape[1]
    halo_copy = pltpu.make_async_copy(halo_ref, halo_buf, small_sem.at[0])
    halo_copy.start()
    u_copy = pltpu.make_async_copy(u_ref.at[:, pl.ds(0, early * CHUNK)], u_buf, small_sem.at[1])
    u_copy.start()
    widened(feat_ref, 0, wide_scr, 0)
    local_chunk, local_send = local_parts(u_buf, head_ref, rate_ref, coef_ref, skip_ref, y_ref, *inner)
    halo_copy.wait()
    column[pl.ds(0, 2 * ROWS), :] = jnp.zeros((2 * ROWS, LANES), f32)

    def chunk(at):
        def tile(number, _):
            lanes = tile_lanes(number)
            all_lanes = tile_lanes(at * TILES + number)
            taps = chunk_taps(wide_scr, at, 0, number, count)
            lay_halo(column, halo_buf, 2, all_lanes)
            lay_column(column, query_ref, all_lanes)
            found = list(fir(column, taps, 2 * ROWS, tokens // ROWS))
            for pair in range(tokens // (2 * ROWS)):
                rows = slice(pair * 2 * ROWS, (pair + 1) * 2 * ROWS)
                gate_buf[at, rows, lanes] = jnp.concatenate(found[pair * 2 : pair * 2 + 2], axis=0).astype(bf16)
            return 0

        lax.fori_loop(0, TILES, tile, 0)

    give = columns_out(gate_ref, gate_buf, out_sem)
    over_chunks(0, chunks, chunk, give)
    u_copy.wait()
    over_chunks(0, early, local_chunk, local_send)
    for at in range(early):
        wait_all(local_send(at))
    for at in range(chunks):
        wait_all(give(at))


def prefix_kernel(piece_ref, rate_ref, coef_ref, out_ref, *, tokens, axes):
    devices, piece_modes, piece_width = piece_ref.shape
    split = devices * piece_modes // rate_ref.shape[0]
    mine = devices - 1 - lax.axis_index(axes)
    mode, part = mine // split * piece_modes, mine % split
    group = pl.multiple_of(mode // ROWS * ROWS, ROWS)
    first = pl.multiple_of(part * piece_width, LANES)

    def mine_of(ref):
        rows = ref[pl.ds(group, ROWS), pl.ds(first, piece_width)]
        return pltpu.roll(rows, lax.rem(ROWS - (mode - group), ROWS), 0)[:piece_modes]

    coef = mine_of(coef_ref)
    through = jnp.exp(-float(tokens) * mine_of(rate_ref))

    entering = jnp.zeros((piece_modes, piece_width), f32)
    for source in reversed(range(devices)):
        out_ref[source] = (coef * entering).astype(out_ref.dtype)
        entering = through * entering + piece_ref[source].astype(f32)


def local_kernel(u_ref, head_ref, rate_ref, coef_ref, skip_ref, gate_ref, _, y_ref, y_last_ref, gate_last_ref, *scratches, first):
    *inner, sem = scratches
    last = u_ref.shape[1] // CHUNK - 1
    take = pltpu.make_async_copy(gate_ref.at[:, span(last)], gate_last_ref, sem.at[0])
    take.start()
    chunk, send = local_parts(u_ref, head_ref, rate_ref, coef_ref, skip_ref, y_ref, *inner)
    over_chunks(first, last, chunk, send)
    chunk(last)
    y_last_ref[...] = inner[0][last]
    for at in range(first, last):
        wait_all(send(at))
    take.wait()


def local_parts(u_ref, head_ref, rate_ref, coef_ref, skip_ref, y_ref, *scratches):
    y_buf, token_scr, sum_scr, out_sem = scratches
    tokens = u_ref.shape[0]
    modes = rate_ref.shape[0]
    half_groups = tokens // ROWS // 2
    top = first_half()

    def chunk(at):
        for pair in range(half_groups):
            block = u_ref[pair * 2 * ROWS : (pair + 1) * 2 * ROWS, span(at)].astype(f32)
            if pair == 0:
                block = block + head_ref[:, span(at)].astype(f32)
            for part in range(2):
                group = pair * 2 + part
                half, within = group // half_groups, group % half_groups
                for tile in range(TILES):
                    piece = lanes_of(block, tile)[part * ROWS : (part + 1) * ROWS]
                    put_tile(token_scr, within, half * TILES + tile, piece)
        (skip,) = spread_rows(skip_ref, at, range(1))
        coef = spread_rows(coef_ref, at, range(modes))
        decay = [jnp.exp(-rate) for rate in spread_rows(rate_ref, at, range(modes))]

        def eight(group, state):
            state = list(state)
            for row in range(ROWS):
                u = get_row(token_scr, group, row)
                state = [factor * one + u for factor, one in zip(decay, state)]
                terms = [factor * one for factor, one in zip([skip] + coef, [u] + state)]
                sum_scr[pl.ds(group * ROWS * ROWS + row, ROWS, stride=ROWS), :] = tree(terms)
            return tuple(state)

        state = lax.fori_loop(0, half_groups, eight, (jnp.zeros((ROWS, LANES), f32),) * modes)
        carried = tuple(
            jnp.where(top, 0.0, pltpu.roll(factor * one, TILES, 0)) for factor, one in zip(coef, state)
        )

        def eight_more(group, carried):
            for row in range(ROWS):
                carried = [factor * one for factor, one in zip(decay, carried)]
                place = pl.ds(group * ROWS * ROWS + row, ROWS, stride=ROWS)
                sum_scr[place, :] = sum_scr[place, :] + tree(carried)
            return tuple(carried)

        lax.fori_loop(0, half_groups, eight_more, carried)
        for group in range(2 * half_groups):
            half, within = group // half_groups, group % half_groups
            for tile in range(TILES):
                slot = (within * ROWS + half * TILES + tile) * ROWS
                rows = slice(group * ROWS, (group + 1) * ROWS)
                y_buf[at, rows, tile * LANES : (tile + 1) * LANES] = sum_scr[pl.ds(slot, ROWS), :]

    return chunk, columns_out(y_ref, y_buf, out_sem)


def final_kernel(piece_ref, rate_ref, y_last_ref, gate_last_ref, y_ref, gate_ref, out_ref, *scratches, axes):
    y_buf, gate_buf, out_buf, total_scr, power_scr, in_sem, out_sem = scratches
    pieces, piece_modes, piece_width = piece_ref.shape
    chunks, tokens = y_buf.shape[:2]
    modes = rate_ref.shape[0]
    fetch = columns_in(((y_ref, y_buf), (gate_ref, gate_buf)), in_sem)
    give = columns_out(out_ref, out_buf, out_sem)
    begin(chunks - 1, fetch)
    split, piece_tiles = pieces * piece_modes // modes, piece_width // LANES
    bits = [(sublane() >> level) % 2 == 1 for level in range(3)]
    pairs = [slice(first, first + 2 * ROWS) for first in range(0, tokens, 2 * ROWS)]

    def finish(at, rows, lanes, sums):
        gates = gate_buf[at, rows, lanes].astype(f32)
        out_buf[at, rows, lanes] = (gates * rounded(sums)).astype(bf16)

    def chunk(at):
        through = jnp.exp(-rate_ref[:, span(at)])
        for level in range(4):
            power_scr[level] = through
            through = through * through

        def tile(number):
            lanes = tile_lanes(number)
            part, within = (at * TILES + number) // piece_tiles, (at * TILES + number) % piece_tiles
            state = []
            for mode in range(modes):
                rows = [wide(power_scr[level, mode : mode + 1, lanes]) for level in range(3)]
                lead = jnp.where(bits[0], rows[1], rows[0])
                for bit, row in zip(bits[1:], rows[1:]):
                    lead = lead * jnp.where(bit, row, 1.0)
                piece, row = mode // piece_modes * split + part, mode % piece_modes
                state.append(lead * wide(total_scr[piece, row : row + 1, tile_lanes(within)]))
            decay = [wide(power_scr[3, mode : mode + 1, lanes]) for mode in range(modes)]
            for rows in pairs:
                sums = []
                for first in (rows.start, rows.start + ROWS):
                    sums.append(y_buf[at, first : first + ROWS, lanes] + tree(state))
                    state = [factor * one for factor, one in zip(decay, state)]
                finish(at, rows, lanes, jnp.concatenate(sums, axis=0))

        def some(number, _):
            for part in range(LAP):
                tile(number * LAP + part)
            return 0

        lax.fori_loop(0, TILES // LAP, some, 0)

    def chunk_alone(at):
        def tile(number, _):
            lanes = tile_lanes(number)
            for rows in pairs:
                finish(at, rows, lanes, y_buf[at, rows, lanes])
            return 0

        lax.fori_loop(0, TILES, tile, 0)

    def all_chunks(body):
        last = chunks - 1
        y_buf[last] = y_last_ref[...]
        gate_buf[last] = gate_last_ref[...]
        body(last)
        start_all(give(last))
        over_chunks(0, last, with_fetch(last, fetch, body), give)

    first = lax.axis_index(axes) == 0

    @pl.when(first)
    def _():
        all_chunks(chunk_alone)

    @pl.when(jnp.logical_not(first))
    def _():
        total_scr[...] = piece_ref[...].astype(f32)
        all_chunks(chunk)

    for at in range(chunks):
        wait_all(give(at))


def cost(flops, moved):
    return pl.CostEstimate(flops=int(flops), bytes_accessed=int(moved), transcendentals=0)


def local(query, key_proj, value_proj, featurizer, rates, residues, skip, *, axes):
    tokens, width = query.shape
    modes = rates.shape[0]
    members, taps, groups = featurizer.shape
    devices = math.prod(lax.axis_size(axis) for axis in axes)
    chunks = width // CHUNK
    tiles = width // LANES
    split = devices * 2 // modes
    even = devices * 2 % modes == 0 and tiles % split == 0
    vmem = pltpu.VMEM
    far = pltpu.HBM
    near = jax.ShapeDtypeStruct
    dma = pltpu.SemaphoreType.DMA
    elements = tokens * width

    def call(kernel, inputs, outputs, scratches, name, close=(), **more):
        inputs = [
            value if at in close else pltpu.with_memory_space_constraint(value, far)
            for at, value in enumerate(inputs)
        ]
        beside, there = pl.BlockSpec(memory_space=vmem), pl.BlockSpec(memory_space=far)
        return pl.pallas_call(
            kernel,
            in_specs=[beside if at in close else there for at in range(len(inputs))],
            out_specs=[beside if isinstance(one, near) else there for one in outputs],
            out_shape=outputs,
            scratch_shapes=scratches,
            compiler_params=pltpu.CompilerParams(vmem_limit_bytes=32 * 2**20),
            name=name,
            **more,
        )(*inputs)

    halo_shape = (members * (taps - 1) // 2, 2, width)
    (packed,) = call(
        pack_kernel,
        (key_proj, value_proj, query),
        [near(halo_shape, bf16)],
        [vmem((members, 2 * ROWS, width), bf16), dma((members,))],
        "pack",
    )
    halo = lax.ppermute(packed, axes, [(at, at + 1) for at in range(devices - 1)])

    column = vmem((2 * ROWS + tokens, LANES), f32)
    half_buf, whole_buf = vmem((chunks, tokens, CHUNK), bf16), vmem((chunks, tokens, CHUNK), f32)
    u, u_far, wide_taps, state = call(
        signal_kernel,
        (key_proj, value_proj, featurizer, rates),
        [near((tokens, width), bf16), far((tokens, width), bf16)]
        + [near((chunks, 2, ROWS, CHUNK), f32), near((modes, width), f32)],
        [vmem((4, modes, width), f32), vmem((modes, ROWS, LANES), f32)] + [column] * (2 * TILES)
        + [dma((chunks,))],
        "signal",
        close=range(4),
        cost_estimate=cost(60 * elements, 10 * elements),
    )

    pieces = (devices, 2, width // split) if even else (modes // 2, 2, width)
    lap = TILES * (3 if chunks % 3 == 0 else 1)
    left, head, u = call(
        functools.partial(head_kernel, tokens=tokens, reach=taps - 1),
        (key_proj, value_proj, halo, rates, wide_taps, state, u, u_far),
        [near(pieces, bf16), near((2 * ROWS, width), bf16), far((tokens, width), bf16)],
        [vmem((lap, 2, 3 * ROWS, LANES), f32), vmem((lap, ROWS, LANES), f32)]
        + [vmem((modes, width), f32), dma((1,))],
        "head",
        close=range(7),
        input_output_aliases={7: 2},
    )
    left, halo_late, rates_late, skip_late = lax.optimization_barrier((left, halo, rates, skip))
    coef = residues * jnp.sqrt(-jnp.expm1(-2.0 * rates_late) / modes)
    skip_row = skip_late[None, :]
    stage = vmem((tokens // ROWS // 2 * ROWS * ROWS, LANES), f32)
    local_shapes = [far((tokens, width), f32)]
    local_scratches = [whole_buf, stage, stage, dma((1, chunks))]
    early = chunks // 9
    gate, y = call(
        functools.partial(gate_kernel, early=early),
        (query, halo_late, featurizer, u, head, rates, coef, skip_row),
        [far((tokens, width), bf16)] + local_shapes,
        [vmem(halo_shape, bf16), vmem((tokens, early * CHUNK), bf16), half_buf]
        + [vmem((chunks, 1, ROWS, CHUNK), f32), column, dma((2,)), dma((1, chunks))]
        + local_scratches,
        "gate",
        close=(0, 2, 4, 5, 6, 7),
        cost_estimate=cost(28 * elements, 6 * elements),
    )

    def swap(value):
        order = [list(range(devices))[::-1]]
        return lax.all_to_all(value, axes, split_axis=0, concat_axis=0, axis_index_groups=order, tiled=True)

    share = modes * width // devices
    theirs = swap(left if even else left.reshape(devices, share))
    theirs, gate, coef, skip_row, y = lax.optimization_barrier((theirs, gate, coef, skip_row, y))
    if even:
        (entering,) = call(
            functools.partial(prefix_kernel, tokens=tokens, axes=axes),
            (theirs, rates, coef),
            [near(pieces, bf16)],
            [],
            "prefix",
            close=(0, 1, 2),
        )
    else:
        mine = devices - 1 - lax.axis_index(axes)
        through = jnp.exp(-float(tokens) * lax.dynamic_slice_in_dim(rates.reshape(-1), mine * share, share))
        factor = lax.dynamic_slice_in_dim(coef.reshape(-1), mine * share, share)
        _, entering = lax.scan(
            lambda so_far, piece: (through * so_far + piece.astype(f32), (factor * so_far).astype(bf16)),
            jnp.zeros((share,), f32),
            theirs,
            reverse=True,
        )

    entering, y = lax.optimization_barrier((entering, y))
    entered = swap(entering).reshape(pieces)
    y, y_last, gate_last = call(
        functools.partial(local_kernel, first=early),
        (u, head, rates, coef, skip_row, gate, y),
        local_shapes + [near((tokens, CHUNK), f32), near((tokens, CHUNK), bf16)],
        local_scratches + [dma((1,))],
        "within",
        close=range(5),
        cost_estimate=cost(50 * elements, 8 * elements),
        input_output_aliases={6: 0},
    )

    (out,) = call(
        functools.partial(final_kernel, axes=axes),
        (entered, rates, y_last, gate_last, y, gate),
        [far((tokens, width), bf16)],
        [whole_buf, half_buf, half_buf, vmem(pieces, f32), vmem((4, modes, CHUNK), f32)]
        + [dma((2, chunks)), dma((1, chunks))],
        "final",
        close=range(4),
        cost_estimate=cost(40 * elements, 10 * elements),
    )
    return out


def solution(mesh):
    axes = tuple(mesh.axis_names)
    placed = (P(axes, None),) * 3 + (P(),) * 4
    return jax.shard_map(
        functools.partial(local, axes=axes),
        mesh=mesh,
        in_specs=placed,
        out_specs=P(axes, None),
        check_vma=False,
    )
```

```python
import functools
import math

import jax
import jax.numpy as jnp
from jax import lax
from jax.experimental import pallas as pl
from jax.experimental.pallas import tpu as pltpu
from jax.sharding import PartitionSpec as P

LANES = 128
ROWS = 8
TILES = 4
CHUNK = TILES * LANES
AHEAD = 4
LAP = 4
f32 = jnp.float32
bf16 = jnp.bfloat16


def put_tile(scratch, group, slot, tile):
    scratch[pl.ds((group * ROWS + slot) * ROWS, ROWS), :] = tile


def get_row(scratch, group, row):
    return scratch[pl.ds(group * ROWS * ROWS + row, ROWS, stride=ROWS), :]


def lanes_of(value, tile):
    return value[:, tile * LANES : (tile + 1) * LANES]


def tile_lanes(tile):
    return pl.ds(pl.multiple_of(tile * LANES, LANES), LANES)


def span(at):
    return pl.ds(pl.multiple_of(at * CHUNK, CHUNK), CHUNK)


def wide(row):
    return jnp.broadcast_to(row, (ROWS, LANES))


def first_half():
    return lax.broadcasted_iota(jnp.int32, (ROWS, LANES), 0) < TILES


def sublane():
    return lax.broadcasted_iota(jnp.int32, (ROWS, LANES), 0)


def spread(row_of):
    slot = sublane() % TILES
    result = wide(row_of(TILES - 1))
    for tile in range(TILES - 1):
        result = jnp.where(slot == tile, wide(row_of(tile)), result)
    return result


def spread_rows(ref, at, rows):
    def one(row):
        return spread(lambda tile: ref[row : row + 1, tile_lanes(at * TILES + tile)])

    return [one(row) for row in rows]


def rounded(value):
    return value.astype(bf16).astype(f32)


def tiles_of(block):
    block = block.astype(f32)
    return [block[at : at + ROWS] for at in range(0, block.shape[0], ROWS)]


def fir(column, taps, first, count):
    half = ROWS // 2
    top = sublane() < half

    def seen(start, lags):
        return [column[pl.ds(start - lag, ROWS), :] for lag in range(lags)]

    def far_part(rows):
        total = taps[half] * rows[0]
        for lag in range(half + 1, len(taps)):
            total = total + taps[lag] * rows[lag - half]
        return pltpu.roll(total, half, 0)

    before = far_part(seen(first - ROWS, len(taps) - half))
    for start in range(first, first + count * ROWS, ROWS):
        rows = seen(start, half)
        now = far_part(rows)
        total = taps[0] * rows[0]
        for lag in range(1, half):
            total = total + taps[lag] * rows[lag]
        yield total + jnp.where(top, before, now)
        before = now


def fir_loads(column, taps, first):
    total = taps[0] * column[pl.ds(first, ROWS), :]
    for lag in range(1, len(taps)):
        total = total + taps[lag] * column[pl.ds(first - lag, ROWS), :]
    return total


def lay_column(column, source, lanes):
    for pair in range(source.shape[0] // (2 * ROWS)):
        rows = slice(pair * 2 * ROWS, (pair + 1) * 2 * ROWS)
        column[pl.ds((pair + 1) * 2 * ROWS, 2 * ROWS), :] = source[rows, lanes].astype(f32)


def chunk_taps(wide_ref, at, member, tile, count):
    return [wide(wide_ref[at, member, lag : lag + 1, tile_lanes(tile)]) for lag in range(count)]


def widened(feat_ref, member, out_ref, position):
    chunks, taps = out_ref.shape[0], feat_ref.shape[1]
    count = feat_ref.shape[2] // chunks
    rows = [feat_ref[member, :, at * count : (at + 1) * count] for at in range(chunks)]
    rows = [jnp.concatenate([row, jnp.zeros((ROWS - taps, count), f32)], axis=0) for row in rows]
    group = lax.broadcasted_iota(jnp.int32, (count, CHUNK), 0)
    lane = lax.broadcasted_iota(jnp.int32, (count, CHUNK), 1)
    pick = (group == lane // (CHUNK // count)).astype(f32).astype(bf16)
    parts, rest = [], jnp.concatenate(rows, axis=0)
    for _ in range(3):
        term = rest.astype(bf16)
        rest = rest - term.astype(f32)
        parts.append(jnp.dot(term, pick, preferred_element_type=f32))
    out_ref[:, position] = (parts[0] + parts[1] + parts[2]).reshape(chunks, ROWS, CHUNK)


def power(base, exponent):
    result = None
    while exponent:
        if exponent & 1:
            result = base if result is None else result * base
        base = base * base
        exponent >>= 1
    return result


def tree(terms):
    while len(terms) > 1:
        terms = [sum(terms[at + 1 : at + 2], terms[at]) for at in range(0, len(terms), 2)]
    return terms[0]


def start_all(copies):
    for copy in copies:
        copy.start()


def wait_all(copies):
    for copy in copies:
        copy.wait()


def begin(chunks, fetch):
    for at in range(min(AHEAD, chunks)):
        start_all(fetch(at))


def over_chunks(first, last, body, send):
    def one(at, _):
        body(at)
        start_all(send(at))
        return 0

    lax.fori_loop(first, last, one, 0)


def with_fetch(chunks, fetch, body):
    def one(at):
        @pl.when(at + AHEAD < chunks)
        def _():
            start_all(fetch(at + AHEAD))

        wait_all(fetch(at))
        body(at)

    return one


def columns_in(pairs, sem):
    def fetch(at):
        return [
            pltpu.make_async_copy(ref.at[:, span(at)], buf.at[at], sem.at[member, at])
            for member, (ref, buf) in enumerate(pairs)
        ]

    return fetch


def columns_out(ref, buf, sem):
    return lambda at: [pltpu.make_async_copy(buf.at[at], ref.at[:, span(at)], sem.at[0, at])]


def lay_halo(column, halo, member, lanes):
    pairs = halo.shape[0] // 3
    for pair in range(pairs):
        column[pl.ds(2 * ROWS - 2 * pairs + 2 * pair, 2), :] = halo[member * pairs + pair, :, lanes].astype(f32)


def pack_kernel(key_ref, value_ref, query_ref, out_ref, in_buf, in_sem):
    tokens = key_ref.shape[0]
    copies = [
        pltpu.make_async_copy(ref.at[pl.ds(tokens - 2 * ROWS, 2 * ROWS)], in_buf.at[at], in_sem.at[at])
        for at, ref in enumerate((key_ref, value_ref, query_ref))
    ]
    start_all(copies)
    wait_all(copies)
    pairs = out_ref.shape[0] // len(copies)
    for at in range(len(copies)):
        tail = in_buf[at].astype(f32)[2 * ROWS - 2 * pairs :]
        for pair in range(pairs):
            out_ref[at * pairs + pair] = tail[2 * pair : 2 * pair + 2].astype(bf16)


def signal_kernel(key_ref, value_ref, feat_ref, rate_ref, u_ref, u_out_ref, wide_ref, state_ref, *scratches):
    power_scr, last_scr, *columns, out_sem = scratches
    tokens, tiles = u_ref.shape[0], u_ref.shape[1] // LANES
    modes = rate_ref.shape[0]
    chunks = tiles // TILES
    count = feat_ref.shape[1]
    for member in range(2):
        widened(feat_ref, member + 1, wide_ref, member)
    for column in columns:
        column[pl.ds(0, 2 * ROWS), :] = jnp.zeros((2 * ROWS, LANES), f32)
    last_scr[...] = jnp.zeros(last_scr.shape, f32)

    def powers(at, _):
        through = jnp.exp(-rate_ref[:, span(at)])
        for level in range(4):
            power_scr[level, :, span(at)] = through
            through = through * through
        return 0

    lax.fori_loop(0, chunks, powers, 0)

    def reduce(number):
        lanes = tile_lanes(number)
        for mode in range(modes):
            whole = last_scr[mode]
            for level in (2, 1, 0):
                factor = wide(power_scr[level, mode : mode + 1, lanes])
                whole = factor * whole + pltpu.roll(whole, ROWS - (1 << level), 0)
            state_ref[mode : mode + 1, lanes] = whole[:1]

    def tile(number, columns):
        lanes = tile_lanes(number)
        reduce(jnp.maximum(number - 1, 0))
        taps = [chunk_taps(wide_ref, number // TILES, member, number % TILES, count) for member in range(2)]
        for column, ref in zip(columns, (key_ref, value_ref)):
            lay_column(column, ref, lanes)
        decay = [wide(power_scr[3, mode : mode + 1, lanes]) for mode in range(modes)]
        state = None
        for pair in range(tokens // (2 * ROWS)):
            found = []
            for first in (pair * 2 * ROWS + 2 * ROWS, pair * 2 * ROWS + 3 * ROWS):
                found.append(fir_loads(columns[0], taps[0], first) * fir_loads(columns[1], taps[1], first))
            if pair == 0:
                found[0] = jnp.where(sublane() < count - 1, 0.0, found[0])
            both = jnp.concatenate(found, axis=0).astype(bf16)
            u_ref[pair * 2 * ROWS : (pair + 1) * 2 * ROWS, lanes] = both
            for u in tiles_of(both):
                if state is None:
                    state = [u] * modes
                else:
                    state = [factor * one + u for factor, one in zip(decay, state)]
        for mode in range(modes):
            last_scr[mode] = state[mode]

    def send(at):
        return pltpu.make_async_copy(u_ref.at[:, span(at)], u_out_ref.at[:, span(at)], out_sem.at[at])

    def chunk(at, _):
        for part in range(TILES):
            tile(TILES * at + part, columns[2 * part : 2 * part + 2])

        @pl.when(at < chunks - 1)
        def _():
            send(at).start()

        return 0

    lax.fori_loop(0, chunks, chunk, 0)
    reduce(tiles - 1)
    for at in range(chunks - 1):
        send(at).wait()


def head_kernel(key_ref, value_ref, halo_ref, rate_ref, wide_ref, state_ref, u_ref, _, *rest, tokens, reach):
    out_ref, head_ref, u_out_ref, column_scr, token_scr, total_scr, sem = rest
    modes, tiles = state_ref.shape[0], state_ref.shape[1] // LANES
    last = span(tiles // TILES - 1)
    move = pltpu.make_async_copy(u_ref.at[:, last], u_out_ref.at[:, last], sem.at[0])
    move.start()
    pieces, piece_modes, piece_width = out_ref.shape

    lap = column_scr.shape[0]

    def some(chunk, _):
        for number in range(lap):
            lanes = tile_lanes(chunk * lap + number)
            parts = []
            for member in range(2):
                place = chunk * (lap // TILES) + number // TILES
                taps = chunk_taps(wide_ref, place, member, number % TILES, reach + 1)
                column = column_scr.at[number, member]
                column[pl.ds(0, 2 * ROWS), :] = jnp.zeros((2 * ROWS, LANES), f32)
                lay_halo(column, halo_ref, member, lanes)
                source = (key_ref, value_ref)[member]
                column[pl.ds(2 * ROWS, ROWS), :] = source[: 2 * ROWS, lanes].astype(f32)[:ROWS]
                parts.append(fir_loads(column, taps, 2 * ROWS))
            u = jnp.where(sublane() < reach, rounded(parts[0] * parts[1]), 0.0)
            token_scr[number] = u
            for group in range(0, modes, ROWS):
                decay = jnp.exp(-rate_ref[group : group + ROWS, lanes])
                head = wide(token_scr[number, :1, :])
                for row in range(1, reach):
                    head = decay * head + wide(token_scr[number, row : row + 1, :])
                total = state_ref[group : group + ROWS, lanes] + power(decay, tokens - reach) * head
                total_scr[group : group + ROWS, lanes] = total
            head_ref[:, lanes] = jnp.concatenate([u, jnp.zeros((ROWS, LANES), f32)], axis=0).astype(bf16)
        return 0

    lax.fori_loop(0, tiles // lap, some, 0)
    split = pieces * piece_modes // modes
    for piece in range(pieces):
        first, part = piece // split * piece_modes, piece % split
        rows = total_scr[first : first + piece_modes, part * piece_width : (part + 1) * piece_width]
        out_ref[piece] = rows.astype(out_ref.dtype)
    move.wait()


def gate_kernel(query_ref, halo_ref, feat_ref, u_ref, head_ref, rate_ref, coef_ref, skip_ref, gate_ref, *rest, early):
    y_ref, halo_buf, u_buf, gate_buf, wide_scr, column, small_sem, out_sem = rest[:8]
    inner = rest[8:]
    chunks, tokens = gate_buf.shape[:2]
    count = feat_ref.shape[1]
    halo_copy = pltpu.make_async_copy(halo_ref, halo_buf, small_sem.at[0])
    halo_copy.start()
    u_copy = pltpu.make_async_copy(u_ref.at[:, pl.ds(0, early * CHUNK)], u_buf, small_sem.at[1])
    u_copy.start()
    widened(feat_ref, 0, wide_scr, 0)
    local_chunk, local_send = local_parts(u_buf, head_ref, rate_ref, coef_ref, skip_ref, y_ref, *inner)
    halo_copy.wait()
    column[pl.ds(0, 2 * ROWS), :] = jnp.zeros((2 * ROWS, LANES), f32)

    def chunk(at):
        def tile(number, _):
            lanes = tile_lanes(number)
            all_lanes = tile_lanes(at * TILES + number)
            taps = chunk_taps(wide_scr, at, 0, number, count)
            lay_halo(column, halo_buf, 2, all_lanes)
            lay_column(column, query_ref, all_lanes)
            found = list(fir(column, taps, 2 * ROWS, tokens // ROWS))
            for pair in range(tokens // (2 * ROWS)):
                rows = slice(pair * 2 * ROWS, (pair + 1) * 2 * ROWS)
                gate_buf[at, rows, lanes] = jnp.concatenate(found[pair * 2 : pair * 2 + 2], axis=0).astype(bf16)
            return 0

        lax.fori_loop(0, TILES, tile, 0)

    give = columns_out(gate_ref, gate_buf, out_sem)
    over_chunks(0, chunks, chunk, give)
    u_copy.wait()
    over_chunks(0, early, local_chunk, local_send)
    for at in range(early):
        wait_all(local_send(at))
    for at in range(chunks):
        wait_all(give(at))


def prefix_kernel(piece_ref, rate_ref, coef_ref, out_ref, *, tokens, axes):
    devices, piece_modes, piece_width = piece_ref.shape
    split = devices * piece_modes // rate_ref.shape[0]
    mine = devices - 1 - lax.axis_index(axes)
    mode, part = mine // split * piece_modes, mine % split
    group = pl.multiple_of(mode // ROWS * ROWS, ROWS)
    first = pl.multiple_of(part * piece_width, LANES)

    def mine_of(ref):
        rows = ref[pl.ds(group, ROWS), pl.ds(first, piece_width)]
        return pltpu.roll(rows, lax.rem(ROWS - (mode - group), ROWS), 0)[:piece_modes]

    coef = mine_of(coef_ref)
    through = jnp.exp(-float(tokens) * mine_of(rate_ref))

    entering = jnp.zeros((piece_modes, piece_width), f32)
    for source in reversed(range(devices)):
        out_ref[source] = (coef * entering).astype(out_ref.dtype)
        entering = through * entering + piece_ref[source].astype(f32)


def local_kernel(u_ref, head_ref, rate_ref, coef_ref, skip_ref, gate_ref, _, y_ref, y_last_ref, gate_last_ref, *scratches, first):
    *inner, sem = scratches
    last = u_ref.shape[1] // CHUNK - 1
    take = pltpu.make_async_copy(gate_ref.at[:, span(last)], gate_last_ref, sem.at[0])
    take.start()
    chunk, send = local_parts(u_ref, head_ref, rate_ref, coef_ref, skip_ref, y_ref, *inner)
    over_chunks(first, last, chunk, send)
    chunk(last)
    y_last_ref[...] = inner[0][last]
    for at in range(first, last):
        wait_all(send(at))
    take.wait()


def local_parts(u_ref, head_ref, rate_ref, coef_ref, skip_ref, y_ref, *scratches):
    y_buf, token_scr, sum_scr, out_sem = scratches
    tokens = u_ref.shape[0]
    modes = rate_ref.shape[0]
    half_groups = tokens // ROWS // 2
    top = first_half()

    def chunk(at):
        for pair in range(half_groups):
            block = u_ref[pair * 2 * ROWS : (pair + 1) * 2 * ROWS, span(at)].astype(f32)
            if pair == 0:
                block = block + head_ref[:, span(at)].astype(f32)
            for part in range(2):
                group = pair * 2 + part
                half, within = group // half_groups, group % half_groups
                for tile in range(TILES):
                    piece = lanes_of(block, tile)[part * ROWS : (part + 1) * ROWS]
                    put_tile(token_scr, within, half * TILES + tile, piece)
        (skip,) = spread_rows(skip_ref, at, range(1))
        coef = spread_rows(coef_ref, at, range(modes))
        decay = [jnp.exp(-rate) for rate in spread_rows(rate_ref, at, range(modes))]

        def eight(group, state):
            state = list(state)
            for row in range(ROWS):
                u = get_row(token_scr, group, row)
                state = [factor * one + u for factor, one in zip(decay, state)]
                terms = [factor * one for factor, one in zip([skip] + coef, [u] + state)]
                sum_scr[pl.ds(group * ROWS * ROWS + row, ROWS, stride=ROWS), :] = tree(terms)
            return tuple(state)

        state = lax.fori_loop(0, half_groups, eight, (jnp.zeros((ROWS, LANES), f32),) * modes)
        carried = tuple(
            jnp.where(top, 0.0, pltpu.roll(factor * one, TILES, 0)) for factor, one in zip(coef, state)
        )

        def eight_more(group, carried):
            for row in range(ROWS):
                carried = [factor * one for factor, one in zip(decay, carried)]
                place = pl.ds(group * ROWS * ROWS + row, ROWS, stride=ROWS)
                sum_scr[place, :] = sum_scr[place, :] + tree(carried)
            return tuple(carried)

        lax.fori_loop(0, half_groups, eight_more, carried)
        for group in range(2 * half_groups):
            half, within = group // half_groups, group % half_groups
            for tile in range(TILES):
                slot = (within * ROWS + half * TILES + tile) * ROWS
                rows = slice(group * ROWS, (group + 1) * ROWS)
                y_buf[at, rows, tile * LANES : (tile + 1) * LANES] = sum_scr[pl.ds(slot, ROWS), :]

    return chunk, columns_out(y_ref, y_buf, out_sem)


def final_kernel(piece_ref, rate_ref, y_last_ref, gate_last_ref, y_ref, gate_ref, out_ref, *scratches, axes):
    y_buf, gate_buf, out_buf, total_scr, power_scr, in_sem, out_sem = scratches
    pieces, piece_modes, piece_width = piece_ref.shape
    chunks, tokens = y_buf.shape[:2]
    modes = rate_ref.shape[0]
    fetch = columns_in(((y_ref, y_buf), (gate_ref, gate_buf)), in_sem)
    give = columns_out(out_ref, out_buf, out_sem)
    begin(chunks - 1, fetch)
    split, piece_tiles = pieces * piece_modes // modes, piece_width // LANES
    bits = [(sublane() >> level) % 2 == 1 for level in range(3)]
    pairs = [slice(first, first + 2 * ROWS) for first in range(0, tokens, 2 * ROWS)]

    def finish(at, gates, rows, lanes, sums):
        out_buf[at, rows, lanes] = gates[rows, lanes] * sums.astype(bf16)

    def chunk(at, y, gates):
        through = jnp.exp(-rate_ref[:, span(at)])
        for level in range(4):
            power_scr[level] = through
            through = through * through

        def tile(number):
            lanes = tile_lanes(number)
            part, within = (at * TILES + number) // piece_tiles, (at * TILES + number) % piece_tiles
            state = []
            for mode in range(modes):
                rows = [wide(power_scr[level, mode : mode + 1, lanes]) for level in range(3)]
                lead = jnp.where(bits[0], rows[1], rows[0])
                for bit, row in zip(bits[1:], rows[1:]):
                    lead = lead * jnp.where(bit, row, 1.0)
                piece, row = mode // piece_modes * split + part, mode % piece_modes
                state.append(lead * wide(total_scr[piece, row : row + 1, tile_lanes(within)]))
            decay = [wide(power_scr[3, mode : mode + 1, lanes]) for mode in range(modes)]
            for rows in pairs:
                sums = []
                for first in (rows.start, rows.start + ROWS):
                    sums.append(y[first : first + ROWS, lanes] + tree(state))
                    state = [factor * one for factor, one in zip(decay, state)]
                finish(at, gates, rows, lanes, jnp.concatenate(sums, axis=0))

        def some(number, _):
            for part in range(LAP):
                tile(number * LAP + part)
            return 0

        lax.fori_loop(0, TILES // LAP, some, 0)

    def chunk_alone(at, y, gates):
        def tile(number, _):
            lanes = tile_lanes(number)
            for rows in pairs:
                finish(at, gates, rows, lanes, y[rows, lanes])
            return 0

        lax.fori_loop(0, TILES, tile, 0)

    def all_chunks(body):
        last = chunks - 1
        body(last, y_last_ref, gate_last_ref)
        start_all(give(last))
        over_chunks(0, last, with_fetch(last, fetch, lambda at: body(at, y_buf.at[at], gate_buf.at[at])), give)

    first = lax.axis_index(axes) == 0

    @pl.when(first)
    def _():
        all_chunks(chunk_alone)

    @pl.when(jnp.logical_not(first))
    def _():
        total_scr[...] = piece_ref[...].astype(f32)
        all_chunks(chunk)

    for at in range(chunks):
        wait_all(give(at))


def cost(flops, moved):
    return pl.CostEstimate(flops=int(flops), bytes_accessed=int(moved), transcendentals=0)


def local(query, key_proj, value_proj, featurizer, rates, residues, skip, *, axes):
    tokens, width = query.shape
    modes = rates.shape[0]
    members, taps, groups = featurizer.shape
    devices = math.prod(lax.axis_size(axis) for axis in axes)
    chunks = width // CHUNK
    tiles = width // LANES
    split = devices * 2 // modes
    even = devices * 2 % modes == 0 and tiles % split == 0
    vmem = pltpu.VMEM
    far = pltpu.HBM
    near = jax.ShapeDtypeStruct
    dma = pltpu.SemaphoreType.DMA
    elements = tokens * width

    def call(kernel, inputs, outputs, scratches, name, close=(), **more):
        inputs = [
            value if at in close else pltpu.with_memory_space_constraint(value, far)
            for at, value in enumerate(inputs)
        ]
        beside, there = pl.BlockSpec(memory_space=vmem), pl.BlockSpec(memory_space=far)
        return pl.pallas_call(
            kernel,
            in_specs=[beside if at in close else there for at in range(len(inputs))],
            out_specs=[beside if isinstance(one, near) else there for one in outputs],
            out_shape=outputs,
            scratch_shapes=scratches,
            compiler_params=pltpu.CompilerParams(vmem_limit_bytes=32 * 2**20),
            name=name,
            **more,
        )(*inputs)

    halo_shape = (members * (taps - 1) // 2, 2, width)
    (packed,) = call(
        pack_kernel,
        (key_proj, value_proj, query),
        [near(halo_shape, bf16)],
        [vmem((members, 2 * ROWS, width), bf16), dma((members,))],
        "pack",
    )
    halo = lax.ppermute(packed, axes, [(at, at + 1) for at in range(devices - 1)])

    column = vmem((2 * ROWS + tokens, LANES), f32)
    half_buf, whole_buf = vmem((chunks, tokens, CHUNK), bf16), vmem((chunks, tokens, CHUNK), f32)
    u, u_far, wide_taps, state = call(
        signal_kernel,
        (key_proj, value_proj, featurizer, rates),
        [near((tokens, width), bf16), far((tokens, width), bf16)]
        + [near((chunks, 2, ROWS, CHUNK), f32), near((modes, width), f32)],
        [vmem((4, modes, width), f32), vmem((modes, ROWS, LANES), f32)] + [column] * (2 * TILES)
        + [dma((chunks,))],
        "signal",
        close=range(4),
        cost_estimate=cost(60 * elements, 10 * elements),
    )

    pieces = (devices, 2, width // split) if even else (modes // 2, 2, width)
    lap = TILES * (3 if chunks % 3 == 0 else 1)
    left, head, u = call(
        functools.partial(head_kernel, tokens=tokens, reach=taps - 1),
        (key_proj, value_proj, halo, rates, wide_taps, state, u, u_far),
        [near(pieces, bf16), near((2 * ROWS, width), bf16), far((tokens, width), bf16)],
        [vmem((lap, 2, 3 * ROWS, LANES), f32), vmem((lap, ROWS, LANES), f32)]
        + [vmem((modes, width), f32), dma((1,))],
        "head",
        close=range(7),
        input_output_aliases={7: 2},
    )
    left, halo_late, rates_late, skip_late = lax.optimization_barrier((left, halo, rates, skip))
    coef = residues * jnp.sqrt(-jnp.expm1(-2.0 * rates_late) / modes)
    skip_row = skip_late[None, :]
    stage = vmem((tokens // ROWS // 2 * ROWS * ROWS, LANES), f32)
    local_shapes = [far((tokens, width), f32)]
    local_scratches = [whole_buf, stage, stage, dma((1, chunks))]
    early = chunks // 9
    gate, y = call(
        functools.partial(gate_kernel, early=early),
        (query, halo_late, featurizer, u, head, rates, coef, skip_row),
        [far((tokens, width), bf16)] + local_shapes,
        [vmem(halo_shape, bf16), vmem((tokens, early * CHUNK), bf16), half_buf]
        + [vmem((chunks, 1, ROWS, CHUNK), f32), column, dma((2,)), dma((1, chunks))]
        + local_scratches,
        "gate",
        close=(0, 2, 4, 5, 6, 7),
        cost_estimate=cost(28 * elements, 6 * elements),
    )

    def swap(value):
        order = [list(range(devices))[::-1]]
        return lax.all_to_all(value, axes, split_axis=0, concat_axis=0, axis_index_groups=order, tiled=True)

    share = modes * width // devices
    theirs = swap(left if even else left.reshape(devices, share))
    theirs, gate, coef, skip_row, y = lax.optimization_barrier((theirs, gate, coef, skip_row, y))
    if even:
        (entering,) = call(
            functools.partial(prefix_kernel, tokens=tokens, axes=axes),
            (theirs, rates, coef),
            [near(pieces, bf16)],
            [],
            "prefix",
            close=(0, 1, 2),
        )
    else:
        mine = devices - 1 - lax.axis_index(axes)
        through = jnp.exp(-float(tokens) * lax.dynamic_slice_in_dim(rates.reshape(-1), mine * share, share))
        factor = lax.dynamic_slice_in_dim(coef.reshape(-1), mine * share, share)
        _, entering = lax.scan(
            lambda so_far, piece: (through * so_far + piece.astype(f32), (factor * so_far).astype(bf16)),
            jnp.zeros((share,), f32),
            theirs,
            reverse=True,
        )

    entering, y = lax.optimization_barrier((entering, y))
    entered = swap(entering).reshape(pieces)
    y, y_last, gate_last = call(
        functools.partial(local_kernel, first=early),
        (u, head, rates, coef, skip_row, gate, y),
        local_shapes + [near((tokens, CHUNK), f32), near((tokens, CHUNK), bf16)],
        local_scratches + [dma((1,))],
        "within",
        close=range(5),
        cost_estimate=cost(50 * elements, 8 * elements),
        input_output_aliases={6: 0},
    )

    (out,) = call(
        functools.partial(final_kernel, axes=axes),
        (entered, rates, y_last, gate_last, y, gate),
        [far((tokens, width), bf16)],
        [whole_buf, half_buf, half_buf, vmem(pieces, f32), vmem((4, modes, CHUNK), f32)]
        + [dma((2, chunks)), dma((1, chunks))],
        "final",
        close=range(4),
        cost_estimate=cost(40 * elements, 10 * elements),
    )
    return out


def solution(mesh):
    axes = tuple(mesh.axis_names)
    placed = (P(axes, None),) * 3 + (P(),) * 4
    return jax.shard_map(
        functools.partial(local, axes=axes),
        mesh=mesh,
        in_specs=placed,
        out_specs=P(axes, None),
        check_vma=False,
    )
```

```python
import functools
import math

import jax
import jax.numpy as jnp
from jax import lax
from jax.experimental import pallas as pl
from jax.experimental.pallas import tpu as pltpu
from jax.sharding import PartitionSpec as P

LANES = 128
ROWS = 8
TILES = 4
CHUNK = TILES * LANES
AHEAD = 4
LAP = 4
f32 = jnp.float32
bf16 = jnp.bfloat16


def put_tile(scratch, group, slot, tile):
    scratch[pl.ds((group * ROWS + slot) * ROWS, ROWS), :] = tile


def get_row(scratch, group, row):
    return scratch[pl.ds(group * ROWS * ROWS + row, ROWS, stride=ROWS), :]


def lanes_of(value, tile):
    return value[:, tile * LANES : (tile + 1) * LANES]


def tile_lanes(tile):
    return pl.ds(pl.multiple_of(tile * LANES, LANES), LANES)


def span(at):
    return pl.ds(pl.multiple_of(at * CHUNK, CHUNK), CHUNK)


def wide(row):
    return jnp.broadcast_to(row, (ROWS, LANES))


def first_half():
    return lax.broadcasted_iota(jnp.int32, (ROWS, LANES), 0) < TILES


def sublane():
    return lax.broadcasted_iota(jnp.int32, (ROWS, LANES), 0)


def spread(row_of):
    slot = sublane() % TILES
    result = wide(row_of(TILES - 1))
    for tile in range(TILES - 1):
        result = jnp.where(slot == tile, wide(row_of(tile)), result)
    return result


def spread_rows(ref, at, rows):
    def one(row):
        return spread(lambda tile: ref[row : row + 1, tile_lanes(at * TILES + tile)])

    return [one(row) for row in rows]


def rounded(value):
    return value.astype(bf16).astype(f32)


def tiles_of(block):
    block = block.astype(f32)
    return [block[at : at + ROWS] for at in range(0, block.shape[0], ROWS)]


def fir(column, taps, first, count):
    half = ROWS // 2
    top = sublane() < half

    def seen(start, lags):
        return [column[pl.ds(start - lag, ROWS), :] for lag in range(lags)]

    def far_part(rows):
        total = taps[half] * rows[0]
        for lag in range(half + 1, len(taps)):
            total = total + taps[lag] * rows[lag - half]
        return pltpu.roll(total, half, 0)

    before = far_part(seen(first - ROWS, len(taps) - half))
    for start in range(first, first + count * ROWS, ROWS):
        rows = seen(start, half)
        now = far_part(rows)
        total = taps[0] * rows[0]
        for lag in range(1, half):
            total = total + taps[lag] * rows[lag]
        yield total + jnp.where(top, before, now)
        before = now


def fir_loads(column, taps, first):
    total = taps[0] * column[pl.ds(first, ROWS), :]
    for lag in range(1, len(taps)):
        total = total + taps[lag] * column[pl.ds(first - lag, ROWS), :]
    return total


def lay_column(column, source, lanes):
    for pair in range(source.shape[0] // (2 * ROWS)):
        rows = slice(pair * 2 * ROWS, (pair + 1) * 2 * ROWS)
        column[pl.ds((pair + 1) * 2 * ROWS, 2 * ROWS), :] = source[rows, lanes].astype(f32)


def chunk_taps(wide_ref, at, member, tile, count):
    return [wide(wide_ref[at, member, lag : lag + 1, tile_lanes(tile)]) for lag in range(count)]


def widened(feat_ref, member, out_ref, position):
    chunks, taps = out_ref.shape[0], feat_ref.shape[1]
    count = feat_ref.shape[2] // chunks
    rows = [feat_ref[member, :, at * count : (at + 1) * count] for at in range(chunks)]
    rows = [jnp.concatenate([row, jnp.zeros((ROWS - taps, count), f32)], axis=0) for row in rows]
    group = lax.broadcasted_iota(jnp.int32, (count, CHUNK), 0)
    lane = lax.broadcasted_iota(jnp.int32, (count, CHUNK), 1)
    pick = (group == lane // (CHUNK // count)).astype(f32).astype(bf16)
    parts, rest = [], jnp.concatenate(rows, axis=0)
    for _ in range(3):
        term = rest.astype(bf16)
        rest = rest - term.astype(f32)
        parts.append(jnp.dot(term, pick, preferred_element_type=f32))
    out_ref[:, position] = (parts[0] + parts[1] + parts[2]).reshape(chunks, ROWS, CHUNK)


def power(base, exponent):
    result = None
    while exponent:
        if exponent & 1:
            result = base if result is None else result * base
        base = base * base
        exponent >>= 1
    return result


def tree(terms):
    while len(terms) > 1:
        terms = [sum(terms[at + 1 : at + 2], terms[at]) for at in range(0, len(terms), 2)]
    return terms[0]


def start_all(copies):
    for copy in copies:
        copy.start()


def wait_all(copies):
    for copy in copies:
        copy.wait()


def begin(chunks, fetch):
    for at in range(min(AHEAD, chunks)):
        start_all(fetch(at))


def over_chunks(first, last, body, send):
    def one(at, _):
        body(at)
        start_all(send(at))
        return 0

    lax.fori_loop(first, last, one, 0)


def with_fetch(chunks, fetch, body):
    def one(at):
        @pl.when(at + AHEAD < chunks)
        def _():
            start_all(fetch(at + AHEAD))

        wait_all(fetch(at))
        body(at)

    return one


def columns_in(pairs, sem):
    def fetch(at):
        return [
            pltpu.make_async_copy(ref.at[:, span(at)], buf.at[at], sem.at[member, at])
            for member, (ref, buf) in enumerate(pairs)
        ]

    return fetch


def columns_out(ref, buf, sem):
    return lambda at: [pltpu.make_async_copy(buf.at[at], ref.at[:, span(at)], sem.at[0, at])]


def lay_halo(column, halo, member, lanes):
    pairs = halo.shape[0] // 3
    for pair in range(pairs):
        column[pl.ds(2 * ROWS - 2 * pairs + 2 * pair, 2), :] = halo[member * pairs + pair, :, lanes].astype(f32)


def decay_powers(rate_ref, power_scr):
    for first in range(0, rate_ref.shape[1], CHUNK):
        lanes = slice(first, first + CHUNK)
        through = jnp.exp(-rate_ref[:, lanes])
        for level in range(power_scr.shape[0]):
            power_scr[level, :, lanes] = through
            through = through * through


def pack_kernel(key_ref, value_ref, query_ref, out_ref, in_buf, in_sem):
    tokens = key_ref.shape[0]
    copies = [
        pltpu.make_async_copy(ref.at[pl.ds(tokens - 2 * ROWS, 2 * ROWS)], in_buf.at[at], in_sem.at[at])
        for at, ref in enumerate((key_ref, value_ref, query_ref))
    ]
    start_all(copies)
    wait_all(copies)
    pairs = out_ref.shape[0] // len(copies)
    for at in range(len(copies)):
        tail = in_buf[at].astype(f32)[2 * ROWS - 2 * pairs :]
        for pair in range(pairs):
            out_ref[at * pairs + pair] = tail[2 * pair : 2 * pair + 2].astype(bf16)


def signal_kernel(key_ref, value_ref, feat_ref, rate_ref, u_ref, u_out_ref, wide_ref, state_ref, *scratches):
    power_scr, last_scr, *columns, out_sem = scratches
    tokens, tiles = u_ref.shape[0], u_ref.shape[1] // LANES
    modes = rate_ref.shape[0]
    chunks = tiles // TILES
    count = feat_ref.shape[1]
    for member in range(2):
        widened(feat_ref, member + 1, wide_ref, member)
    for column in columns:
        column[pl.ds(0, 2 * ROWS), :] = jnp.zeros((2 * ROWS, LANES), f32)
    last_scr[...] = jnp.zeros(last_scr.shape, f32)

    decay_powers(rate_ref, power_scr)

    def reduce(number):
        lanes = tile_lanes(number)
        for mode in range(modes):
            whole = last_scr[mode]
            for level in (2, 1, 0):
                factor = wide(power_scr[level, mode : mode + 1, lanes])
                whole = factor * whole + pltpu.roll(whole, ROWS - (1 << level), 0)
            state_ref[mode : mode + 1, lanes] = whole[:1]

    def tile(number, columns):
        lanes = tile_lanes(number)
        reduce(jnp.maximum(number - 1, 0))
        taps = [chunk_taps(wide_ref, number // TILES, member, number % TILES, count) for member in range(2)]
        for column, ref in zip(columns, (key_ref, value_ref)):
            lay_column(column, ref, lanes)
        decay = [wide(power_scr[3, mode : mode + 1, lanes]) for mode in range(modes)]
        state = None
        for pair in range(tokens // (2 * ROWS)):
            found = []
            for first in (pair * 2 * ROWS + 2 * ROWS, pair * 2 * ROWS + 3 * ROWS):
                found.append(fir_loads(columns[0], taps[0], first) * fir_loads(columns[1], taps[1], first))
            if pair == 0:
                found[0] = jnp.where(sublane() < count - 1, 0.0, found[0])
            both = jnp.concatenate(found, axis=0).astype(bf16)
            u_ref[pair * 2 * ROWS : (pair + 1) * 2 * ROWS, lanes] = both
            for u in tiles_of(both):
                if state is None:
                    state = [u] * modes
                else:
                    state = [factor * one + u for factor, one in zip(decay, state)]
        for mode in range(modes):
            last_scr[mode] = state[mode]

    def send(at):
        return pltpu.make_async_copy(u_ref.at[:, span(at)], u_out_ref.at[:, span(at)], out_sem.at[at])

    def chunk(at, _):
        for part in range(TILES):
            tile(TILES * at + part, columns[2 * part : 2 * part + 2])

        @pl.when(at < chunks - 1)
        def _():
            send(at).start()

        return 0

    lax.fori_loop(0, chunks, chunk, 0)
    reduce(tiles - 1)
    for at in range(chunks - 1):
        send(at).wait()


def head_kernel(key_ref, value_ref, halo_ref, rate_ref, wide_ref, state_ref, u_ref, _, *rest, tokens, reach):
    out_ref, head_ref, u_out_ref, column_scr, token_scr, total_scr, sem = rest
    modes, tiles = state_ref.shape[0], state_ref.shape[1] // LANES
    last = span(tiles // TILES - 1)
    move = pltpu.make_async_copy(u_ref.at[:, last], u_out_ref.at[:, last], sem.at[0])
    move.start()
    pieces, piece_modes, piece_width = out_ref.shape

    lap = column_scr.shape[0]

    def some(chunk, _):
        for number in range(lap):
            lanes = tile_lanes(chunk * lap + number)
            parts = []
            for member in range(2):
                place = chunk * (lap // TILES) + number // TILES
                taps = chunk_taps(wide_ref, place, member, number % TILES, reach + 1)
                column = column_scr.at[number, member]
                column[pl.ds(0, 2 * ROWS), :] = jnp.zeros((2 * ROWS, LANES), f32)
                lay_halo(column, halo_ref, member, lanes)
                source = (key_ref, value_ref)[member]
                column[pl.ds(2 * ROWS, ROWS), :] = source[: 2 * ROWS, lanes].astype(f32)[:ROWS]
                parts.append(fir_loads(column, taps, 2 * ROWS))
            u = jnp.where(sublane() < reach, rounded(parts[0] * parts[1]), 0.0)
            token_scr[number] = u
            for group in range(0, modes, ROWS):
                decay = jnp.exp(-rate_ref[group : group + ROWS, lanes])
                head = wide(token_scr[number, :1, :])
                for row in range(1, reach):
                    head = decay * head + wide(token_scr[number, row : row + 1, :])
                total = state_ref[group : group + ROWS, lanes] + power(decay, tokens - reach) * head
                total_scr[group : group + ROWS, lanes] = total
            head_ref[:, lanes] = jnp.concatenate([u, jnp.zeros((ROWS, LANES), f32)], axis=0).astype(bf16)
        return 0

    lax.fori_loop(0, tiles // lap, some, 0)
    split = pieces * piece_modes // modes
    for piece in range(pieces):
        first, part = piece // split * piece_modes, piece % split
        rows = total_scr[first : first + piece_modes, part * piece_width : (part + 1) * piece_width]
        out_ref[piece] = rows.astype(out_ref.dtype)
    move.wait()


def gate_kernel(query_ref, halo_ref, feat_ref, u_ref, head_ref, rate_ref, coef_ref, skip_ref, gate_ref, *rest, early):
    y_ref, halo_buf, u_buf, gate_buf, wide_scr, column, small_sem, out_sem = rest[:8]
    inner = rest[8:]
    chunks, tokens = gate_buf.shape[:2]
    count = feat_ref.shape[1]
    halo_copy = pltpu.make_async_copy(halo_ref, halo_buf, small_sem.at[0])
    halo_copy.start()
    u_copy = pltpu.make_async_copy(u_ref.at[:, pl.ds(0, early * CHUNK)], u_buf, small_sem.at[1])
    u_copy.start()
    widened(feat_ref, 0, wide_scr, 0)
    local_chunk, local_send = local_parts(u_buf, head_ref, rate_ref, coef_ref, skip_ref, y_ref, *inner)
    halo_copy.wait()
    column[pl.ds(0, 2 * ROWS), :] = jnp.zeros((2 * ROWS, LANES), f32)

    def chunk(at):
        def tile(number, _):
            lanes = tile_lanes(number)
            all_lanes = tile_lanes(at * TILES + number)
            taps = chunk_taps(wide_scr, at, 0, number, count)
            lay_halo(column, halo_buf, 2, all_lanes)
            lay_column(column, query_ref, all_lanes)
            found = list(fir(column, taps, 2 * ROWS, tokens // ROWS))
            for pair in range(tokens // (2 * ROWS)):
                rows = slice(pair * 2 * ROWS, (pair + 1) * 2 * ROWS)
                gate_buf[at, rows, lanes] = jnp.concatenate(found[pair * 2 : pair * 2 + 2], axis=0).astype(bf16)
            return 0

        lax.fori_loop(0, TILES, tile, 0)

    give = columns_out(gate_ref, gate_buf, out_sem)
    over_chunks(0, chunks, chunk, give)
    u_copy.wait()
    over_chunks(0, early, local_chunk, local_send)
    for at in range(early):
        wait_all(local_send(at))
    for at in range(chunks):
        wait_all(give(at))


def prefix_kernel(piece_ref, rate_ref, coef_ref, out_ref, *, tokens, axes):
    devices, piece_modes, piece_width = piece_ref.shape
    split = devices * piece_modes // rate_ref.shape[0]
    mine = devices - 1 - lax.axis_index(axes)
    mode, part = mine // split * piece_modes, mine % split
    group = pl.multiple_of(mode // ROWS * ROWS, ROWS)
    first = pl.multiple_of(part * piece_width, LANES)

    def mine_of(ref):
        rows = ref[pl.ds(group, ROWS), pl.ds(first, piece_width)]
        return pltpu.roll(rows, lax.rem(ROWS - (mode - group), ROWS), 0)[:piece_modes]

    coef = mine_of(coef_ref)
    through = jnp.exp(-float(tokens) * mine_of(rate_ref))

    entering = jnp.zeros((piece_modes, piece_width), f32)
    for source in reversed(range(devices)):
        out_ref[source] = (coef * entering).astype(out_ref.dtype)
        entering = through * entering + piece_ref[source].astype(f32)


def local_kernel(u_ref, head_ref, rate_ref, coef_ref, skip_ref, gate_ref, _, y_ref, y_last_ref, gate_last_ref, *scratches, first):
    *inner, sem = scratches
    last = u_ref.shape[1] // CHUNK - 1
    take = pltpu.make_async_copy(gate_ref.at[:, span(last)], gate_last_ref, sem.at[0])
    take.start()
    chunk, send = local_parts(u_ref, head_ref, rate_ref, coef_ref, skip_ref, y_ref, *inner)
    over_chunks(first, last, chunk, send)
    chunk(last)
    y_last_ref[...] = inner[0][last]
    for at in range(first, last):
        wait_all(send(at))
    take.wait()


def local_parts(u_ref, head_ref, rate_ref, coef_ref, skip_ref, y_ref, *scratches):
    y_buf, token_scr, sum_scr, out_sem = scratches
    tokens = u_ref.shape[0]
    modes = rate_ref.shape[0]
    half_groups = tokens // ROWS // 2
    top = first_half()

    def chunk(at):
        for pair in range(half_groups):
            block = u_ref[pair * 2 * ROWS : (pair + 1) * 2 * ROWS, span(at)].astype(f32)
            if pair == 0:
                block = block + head_ref[:, span(at)].astype(f32)
            for part in range(2):
                group = pair * 2 + part
                half, within = group // half_groups, group % half_groups
                for tile in range(TILES):
                    piece = lanes_of(block, tile)[part * ROWS : (part + 1) * ROWS]
                    put_tile(token_scr, within, half * TILES + tile, piece)
        (skip,) = spread_rows(skip_ref, at, range(1))
        coef = spread_rows(coef_ref, at, range(modes))
        decay = [jnp.exp(-rate) for rate in spread_rows(rate_ref, at, range(modes))]

        def eight(group, state):
            state = list(state)
            for row in range(ROWS):
                u = get_row(token_scr, group, row)
                state = [factor * one + u for factor, one in zip(decay, state)]
                terms = [factor * one for factor, one in zip([skip] + coef, [u] + state)]
                sum_scr[pl.ds(group * ROWS * ROWS + row, ROWS, stride=ROWS), :] = tree(terms)
            return tuple(state)

        state = lax.fori_loop(0, half_groups, eight, (jnp.zeros((ROWS, LANES), f32),) * modes)
        carried = tuple(
            jnp.where(top, 0.0, pltpu.roll(factor * one, TILES, 0)) for factor, one in zip(coef, state)
        )

        def eight_more(group, carried):
            for row in range(ROWS):
                carried = [factor * one for factor, one in zip(decay, carried)]
                place = pl.ds(group * ROWS * ROWS + row, ROWS, stride=ROWS)
                sum_scr[place, :] = sum_scr[place, :] + tree(carried)
            return tuple(carried)

        lax.fori_loop(0, half_groups, eight_more, carried)
        for group in range(2 * half_groups):
            half, within = group // half_groups, group % half_groups
            for tile in range(TILES):
                slot = (within * ROWS + half * TILES + tile) * ROWS
                rows = slice(group * ROWS, (group + 1) * ROWS)
                y_buf[at, rows, tile * LANES : (tile + 1) * LANES] = sum_scr[pl.ds(slot, ROWS), :]

    return chunk, columns_out(y_ref, y_buf, out_sem)


def final_kernel(piece_ref, rate_ref, y_last_ref, gate_last_ref, y_ref, gate_ref, out_ref, *scratches, axes):
    y_buf, gate_buf, out_buf, total_scr, power_scr, in_sem, out_sem = scratches
    pieces, piece_modes, piece_width = piece_ref.shape
    chunks, tokens = y_buf.shape[:2]
    modes = rate_ref.shape[0]
    fetch = columns_in(((y_ref, y_buf), (gate_ref, gate_buf)), in_sem)
    give = columns_out(out_ref, out_buf, out_sem)
    begin(chunks - 1, fetch)
    split, piece_tiles = pieces * piece_modes // modes, piece_width // LANES
    bits = [(sublane() >> level) % 2 == 1 for level in range(3)]
    pairs = [slice(first, first + 2 * ROWS) for first in range(0, tokens, 2 * ROWS)]

    def finish(at, gates, rows, lanes, sums):
        out_buf[at, rows, lanes] = gates[rows, lanes] * sums.astype(bf16)

    def chunk(at, y, gates):
        def tile(number):
            lanes, all_lanes = tile_lanes(number), tile_lanes(at * TILES + number)
            part, within = (at * TILES + number) // piece_tiles, (at * TILES + number) % piece_tiles
            state = []
            for mode in range(modes):
                rows = [wide(power_scr[level, mode : mode + 1, all_lanes]) for level in range(3)]
                lead = jnp.where(bits[0], rows[1], rows[0])
                for bit, row in zip(bits[1:], rows[1:]):
                    lead = lead * jnp.where(bit, row, 1.0)
                piece, row = mode // piece_modes * split + part, mode % piece_modes
                state.append(lead * wide(total_scr[piece, row : row + 1, tile_lanes(within)]))
            decay = [wide(power_scr[3, mode : mode + 1, all_lanes]) for mode in range(modes)]
            for rows in pairs:
                sums = []
                for first in (rows.start, rows.start + ROWS):
                    sums.append(y[first : first + ROWS, lanes] + tree(state))
                    state = [factor * one for factor, one in zip(decay, state)]
                finish(at, gates, rows, lanes, jnp.concatenate(sums, axis=0))

        def some(number, _):
            for part in range(LAP):
                tile(number * LAP + part)
            return 0

        lax.fori_loop(0, TILES // LAP, some, 0)

    def chunk_alone(at, y, gates):
        def tile(number, _):
            lanes = tile_lanes(number)
            for rows in pairs:
                finish(at, gates, rows, lanes, y[rows, lanes])
            return 0

        lax.fori_loop(0, TILES, tile, 0)

    def all_chunks(body):
        last = chunks - 1
        body(last, y_last_ref, gate_last_ref)
        start_all(give(last))
        over_chunks(0, last, with_fetch(last, fetch, lambda at: body(at, y_buf.at[at], gate_buf.at[at])), give)

    first = lax.axis_index(axes) == 0

    @pl.when(first)
    def _():
        all_chunks(chunk_alone)

    @pl.when(jnp.logical_not(first))
    def _():
        decay_powers(rate_ref, power_scr)
        total_scr[...] = piece_ref[...].astype(f32)
        all_chunks(chunk)

    for at in range(chunks):
        wait_all(give(at))


def cost(flops, moved):
    return pl.CostEstimate(flops=int(flops), bytes_accessed=int(moved), transcendentals=0)


def local(query, key_proj, value_proj, featurizer, rates, residues, skip, *, axes):
    tokens, width = query.shape
    modes = rates.shape[0]
    members, taps, groups = featurizer.shape
    devices = math.prod(lax.axis_size(axis) for axis in axes)
    chunks = width // CHUNK
    tiles = width // LANES
    split = devices * 2 // modes
    even = devices * 2 % modes == 0 and tiles % split == 0
    vmem = pltpu.VMEM
    far = pltpu.HBM
    near = jax.ShapeDtypeStruct
    dma = pltpu.SemaphoreType.DMA
    elements = tokens * width

    def call(kernel, inputs, outputs, scratches, name, close=(), **more):
        inputs = [
            value if at in close else pltpu.with_memory_space_constraint(value, far)
            for at, value in enumerate(inputs)
        ]
        beside, there = pl.BlockSpec(memory_space=vmem), pl.BlockSpec(memory_space=far)
        return pl.pallas_call(
            kernel,
            in_specs=[beside if at in close else there for at in range(len(inputs))],
            out_specs=[beside if isinstance(one, near) else there for one in outputs],
            out_shape=outputs,
            scratch_shapes=scratches,
            compiler_params=pltpu.CompilerParams(vmem_limit_bytes=32 * 2**20),
            name=name,
            **more,
        )(*inputs)

    halo_shape = (members * (taps - 1) // 2, 2, width)
    (packed,) = call(
        pack_kernel,
        (key_proj, value_proj, query),
        [near(halo_shape, bf16)],
        [vmem((members, 2 * ROWS, width), bf16), dma((members,))],
        "pack",
    )
    halo = lax.ppermute(packed, axes, [(at, at + 1) for at in range(devices - 1)])

    column = vmem((2 * ROWS + tokens, LANES), f32)
    half_buf, whole_buf = vmem((chunks, tokens, CHUNK), bf16), vmem((chunks, tokens, CHUNK), f32)
    u, u_far, wide_taps, state = call(
        signal_kernel,
        (key_proj, value_proj, featurizer, rates),
        [near((tokens, width), bf16), far((tokens, width), bf16)]
        + [near((chunks, 2, ROWS, CHUNK), f32), near((modes, width), f32)],
        [vmem((4, modes, width), f32), vmem((modes, ROWS, LANES), f32)] + [column] * (2 * TILES)
        + [dma((chunks,))],
        "signal",
        close=range(4),
        cost_estimate=cost(60 * elements, 10 * elements),
    )

    pieces = (devices, 2, width // split) if even else (modes // 2, 2, width)
    lap = TILES * (3 if chunks % 3 == 0 else 1)
    left, head, u = call(
        functools.partial(head_kernel, tokens=tokens, reach=taps - 1),
        (key_proj, value_proj, halo, rates, wide_taps, state, u, u_far),
        [near(pieces, bf16), near((2 * ROWS, width), bf16), far((tokens, width), bf16)],
        [vmem((lap, 2, 3 * ROWS, LANES), f32), vmem((lap, ROWS, LANES), f32)]
        + [vmem((modes, width), f32), dma((1,))],
        "head",
        close=range(7),
        input_output_aliases={7: 2},
    )
    left, halo_late, rates_late, skip_late = lax.optimization_barrier((left, halo, rates, skip))
    coef = residues * jnp.sqrt(-jnp.expm1(-2.0 * rates_late) / modes)
    skip_row = skip_late[None, :]
    stage = vmem((tokens // ROWS // 2 * ROWS * ROWS, LANES), f32)
    local_shapes = [far((tokens, width), f32)]
    local_scratches = [whole_buf, stage, stage, dma((1, chunks))]
    early = chunks // 9
    gate, y = call(
        functools.partial(gate_kernel, early=early),
        (query, halo_late, featurizer, u, head, rates, coef, skip_row),
        [far((tokens, width), bf16)] + local_shapes,
        [vmem(halo_shape, bf16), vmem((tokens, early * CHUNK), bf16), half_buf]
        + [vmem((chunks, 1, ROWS, CHUNK), f32), column, dma((2,)), dma((1, chunks))]
        + local_scratches,
        "gate",
        close=(0, 2, 4, 5, 6, 7),
        cost_estimate=cost(28 * elements, 6 * elements),
    )

    def swap(value):
        order = [list(range(devices))[::-1]]
        return lax.all_to_all(value, axes, split_axis=0, concat_axis=0, axis_index_groups=order, tiled=True)

    share = modes * width // devices
    theirs = swap(left if even else left.reshape(devices, share))
    theirs, gate, coef, skip_row, y = lax.optimization_barrier((theirs, gate, coef, skip_row, y))
    if even:
        (entering,) = call(
            functools.partial(prefix_kernel, tokens=tokens, axes=axes),
            (theirs, rates, coef),
            [near(pieces, bf16)],
            [],
            "prefix",
            close=(0, 1, 2),
        )
    else:
        mine = devices - 1 - lax.axis_index(axes)
        through = jnp.exp(-float(tokens) * lax.dynamic_slice_in_dim(rates.reshape(-1), mine * share, share))
        factor = lax.dynamic_slice_in_dim(coef.reshape(-1), mine * share, share)
        _, entering = lax.scan(
            lambda so_far, piece: (through * so_far + piece.astype(f32), (factor * so_far).astype(bf16)),
            jnp.zeros((share,), f32),
            theirs,
            reverse=True,
        )

    entering, y = lax.optimization_barrier((entering, y))
    entered = swap(entering).reshape(pieces)
    y, y_last, gate_last = call(
        functools.partial(local_kernel, first=early),
        (u, head, rates, coef, skip_row, gate, y),
        local_shapes + [near((tokens, CHUNK), f32), near((tokens, CHUNK), bf16)],
        local_scratches + [dma((1,))],
        "within",
        close=range(5),
        cost_estimate=cost(50 * elements, 8 * elements),
        input_output_aliases={6: 0},
    )

    (out,) = call(
        functools.partial(final_kernel, axes=axes),
        (entered, rates, y_last, gate_last, y, gate),
        [far((tokens, width), bf16)],
        [whole_buf, half_buf, half_buf, vmem(pieces, f32), vmem((4, modes, width), f32)]
        + [dma((2, chunks)), dma((1, chunks))],
        "final",
        close=range(4),
        cost_estimate=cost(40 * elements, 10 * elements),
    )
    return out


def solution(mesh):
    axes = tuple(mesh.axis_names)
    placed = (P(axes, None),) * 3 + (P(),) * 4
    return jax.shard_map(
        functools.partial(local, axes=axes),
        mesh=mesh,
        in_specs=placed,
        out_specs=P(axes, None),
        check_vma=False,
    )
```

```python
import functools
import math

import jax
import jax.numpy as jnp
from jax import lax
from jax.experimental import pallas as pl
from jax.experimental.pallas import tpu as pltpu
from jax.sharding import PartitionSpec as P

LANES = 128
ROWS = 8
TILES = 4
CHUNK = TILES * LANES
AHEAD = 4
LAP = 4
f32 = jnp.float32
bf16 = jnp.bfloat16


def put_tile(scratch, group, slot, tile):
    scratch[pl.ds((group * ROWS + slot) * ROWS, ROWS), :] = tile


def get_row(scratch, group, row):
    return scratch[pl.ds(group * ROWS * ROWS + row, ROWS, stride=ROWS), :]


def lanes_of(value, tile):
    return value[:, tile * LANES : (tile + 1) * LANES]


def tile_lanes(tile):
    return pl.ds(pl.multiple_of(tile * LANES, LANES), LANES)


def span(at):
    return pl.ds(pl.multiple_of(at * CHUNK, CHUNK), CHUNK)


def wide(row):
    return jnp.broadcast_to(row, (ROWS, LANES))


def first_half():
    return lax.broadcasted_iota(jnp.int32, (ROWS, LANES), 0) < TILES


def sublane():
    return lax.broadcasted_iota(jnp.int32, (ROWS, LANES), 0)


def spread(row_of):
    slot = sublane() % TILES
    result = wide(row_of(TILES - 1))
    for tile in range(TILES - 1):
        result = jnp.where(slot == tile, wide(row_of(tile)), result)
    return result


def spread_rows(ref, at, rows):
    def one(row):
        return spread(lambda tile: ref[row : row + 1, tile_lanes(at * TILES + tile)])

    return [one(row) for row in rows]


def rounded(value):
    return value.astype(bf16).astype(f32)


def tiles_of(block):
    block = block.astype(f32)
    return [block[at : at + ROWS] for at in range(0, block.shape[0], ROWS)]


def fir(column, taps, first, count):
    half = ROWS // 2
    top = sublane() < half

    def seen(start, lags):
        return [column[pl.ds(start - lag, ROWS), :] for lag in range(lags)]

    def far_part(rows):
        total = taps[half] * rows[0]
        for lag in range(half + 1, len(taps)):
            total = total + taps[lag] * rows[lag - half]
        return pltpu.roll(total, half, 0)

    before = far_part(seen(first - ROWS, len(taps) - half))
    for start in range(first, first + count * ROWS, ROWS):
        rows = seen(start, half)
        now = far_part(rows)
        total = taps[0] * rows[0]
        for lag in range(1, half):
            total = total + taps[lag] * rows[lag]
        yield total + jnp.where(top, before, now)
        before = now


def fir_loads(column, taps, first):
    total = taps[0] * column[pl.ds(first, ROWS), :]
    for lag in range(1, len(taps)):
        total = total + taps[lag] * column[pl.ds(first - lag, ROWS), :]
    return total


def lay_column(column, source, lanes):
    for pair in range(source.shape[0] // (2 * ROWS)):
        rows = slice(pair * 2 * ROWS, (pair + 1) * 2 * ROWS)
        column[pl.ds((pair + 1) * 2 * ROWS, 2 * ROWS), :] = source[rows, lanes].astype(f32)


def chunk_taps(wide_ref, at, member, tile, count):
    return [wide(wide_ref[at, member, lag : lag + 1, tile_lanes(tile)]) for lag in range(count)]


def widened(feat_ref, member, out_ref, position):
    chunks, taps = out_ref.shape[0], feat_ref.shape[1]
    count = feat_ref.shape[2] // chunks
    rows = [feat_ref[member, :, at * count : (at + 1) * count] for at in range(chunks)]
    rows = [jnp.concatenate([row, jnp.zeros((ROWS - taps, count), f32)], axis=0) for row in rows]
    group = lax.broadcasted_iota(jnp.int32, (count, CHUNK), 0)
    lane = lax.broadcasted_iota(jnp.int32, (count, CHUNK), 1)
    pick = (group == lane // (CHUNK // count)).astype(f32).astype(bf16)
    parts, rest = [], jnp.concatenate(rows, axis=0)
    for _ in range(3):
        term = rest.astype(bf16)
        rest = rest - term.astype(f32)
        parts.append(jnp.dot(term, pick, preferred_element_type=f32))
    out_ref[:, position] = (parts[0] + parts[1] + parts[2]).reshape(chunks, ROWS, CHUNK)


def power(base, exponent):
    result = None
    while exponent:
        if exponent & 1:
            result = base if result is None else result * base
        base = base * base
        exponent >>= 1
    return result


def tree(terms):
    while len(terms) > 1:
        terms = [sum(terms[at + 1 : at + 2], terms[at]) for at in range(0, len(terms), 2)]
    return terms[0]


def start_all(copies):
    for copy in copies:
        copy.start()


def wait_all(copies):
    for copy in copies:
        copy.wait()


def begin(chunks, fetch):
    for at in range(min(AHEAD, chunks)):
        start_all(fetch(at))


def over_chunks(first, last, body, send):
    def one(at, _):
        body(at)
        start_all(send(at))
        return 0

    lax.fori_loop(first, last, one, 0)


def with_fetch(chunks, fetch, body):
    def one(at):
        @pl.when(at + AHEAD < chunks)
        def _():
            start_all(fetch(at + AHEAD))

        wait_all(fetch(at))
        body(at)

    return one


def columns_in(pairs, sem):
    def fetch(at):
        return [
            pltpu.make_async_copy(ref.at[:, span(at)], buf.at[at], sem.at[member, at])
            for member, (ref, buf) in enumerate(pairs)
        ]

    return fetch


def columns_out(ref, buf, sem):
    return lambda at: [pltpu.make_async_copy(buf.at[at], ref.at[:, span(at)], sem.at[0, at])]


def lay_halo(column, halo, member, lanes):
    pairs = halo.shape[0] // 3
    for pair in range(pairs):
        column[pl.ds(2 * ROWS - 2 * pairs + 2 * pair, 2), :] = halo[member * pairs + pair, :, lanes].astype(f32)


def decay_powers(rate_ref, power_scr):
    for first in range(0, rate_ref.shape[1], CHUNK):
        lanes = slice(first, first + CHUNK)
        through = jnp.exp(-rate_ref[:, lanes])
        for level in range(power_scr.shape[0]):
            power_scr[level, :, lanes] = through
            through = through * through


def pack_kernel(key_ref, value_ref, query_ref, out_ref, in_buf, in_sem):
    tokens = key_ref.shape[0]
    copies = [
        pltpu.make_async_copy(ref.at[pl.ds(tokens - 2 * ROWS, 2 * ROWS)], in_buf.at[at], in_sem.at[at])
        for at, ref in enumerate((key_ref, value_ref, query_ref))
    ]
    start_all(copies)
    wait_all(copies)
    pairs = out_ref.shape[0] // len(copies)
    for at in range(len(copies)):
        tail = in_buf[at].astype(f32)[2 * ROWS - 2 * pairs :]
        for pair in range(pairs):
            out_ref[at * pairs + pair] = tail[2 * pair : 2 * pair + 2].astype(bf16)


def signal_kernel(key_ref, value_ref, feat_ref, rate_ref, u_ref, u_out_ref, wide_ref, state_ref, *scratches):
    power_scr, last_scr, *columns, out_sem = scratches
    tokens, tiles = u_ref.shape[0], u_ref.shape[1] // LANES
    modes = rate_ref.shape[0]
    chunks = tiles // TILES
    count = feat_ref.shape[1]
    for member in range(2):
        widened(feat_ref, member + 1, wide_ref, member)
    for column in columns:
        column[pl.ds(0, 2 * ROWS), :] = jnp.zeros((2 * ROWS, LANES), f32)
    last_scr[...] = jnp.zeros(last_scr.shape, f32)

    decay_powers(rate_ref, power_scr)

    def reduce(number):
        lanes = tile_lanes(number)
        for mode in range(modes):
            whole = last_scr[mode]
            for level in (2, 1, 0):
                factor = wide(power_scr[level, mode : mode + 1, lanes])
                whole = factor * whole + pltpu.roll(whole, ROWS - (1 << level), 0)
            state_ref[mode : mode + 1, lanes] = whole[:1]

    def tile(number, columns):
        lanes = tile_lanes(number)
        reduce(jnp.maximum(number - 1, 0))
        taps = [chunk_taps(wide_ref, number // TILES, member, number % TILES, count) for member in range(2)]
        for column, ref in zip(columns, (key_ref, value_ref)):
            lay_column(column, ref, lanes)
        decay = [wide(power_scr[3, mode : mode + 1, lanes]) for mode in range(modes)]
        state = None
        for pair in range(tokens // (2 * ROWS)):
            found = []
            for first in (pair * 2 * ROWS + 2 * ROWS, pair * 2 * ROWS + 3 * ROWS):
                found.append(fir_loads(columns[0], taps[0], first) * fir_loads(columns[1], taps[1], first))
            if pair == 0:
                found[0] = jnp.where(sublane() < count - 1, 0.0, found[0])
            both = jnp.concatenate(found, axis=0).astype(bf16)
            u_ref[pair * 2 * ROWS : (pair + 1) * 2 * ROWS, lanes] = both
            for u in tiles_of(both):
                if state is None:
                    state = [u] * modes
                else:
                    state = [factor * one + u for factor, one in zip(decay, state)]
        for mode in range(modes):
            last_scr[mode] = state[mode]

    def send(at):
        return pltpu.make_async_copy(u_ref.at[:, span(at)], u_out_ref.at[:, span(at)], out_sem.at[at])

    def chunk(at, _):
        for part in range(TILES):
            tile(TILES * at + part, columns[2 * part : 2 * part + 2])

        @pl.when(at < chunks - 1)
        def _():
            send(at).start()

        return 0

    lax.fori_loop(0, chunks, chunk, 0)
    reduce(tiles - 1)
    for at in range(chunks - 1):
        send(at).wait()


def head_kernel(key_ref, value_ref, halo_ref, rate_ref, wide_ref, state_ref, u_ref, _, *rest, tokens, reach):
    out_ref, head_ref, u_out_ref, column_scr, token_scr, total_scr, sem = rest
    modes, tiles = state_ref.shape[0], state_ref.shape[1] // LANES
    last = span(tiles // TILES - 1)
    move = pltpu.make_async_copy(u_ref.at[:, last], u_out_ref.at[:, last], sem.at[0])
    move.start()
    pieces, piece_modes, piece_width = out_ref.shape

    lap = column_scr.shape[0]

    def some(chunk, _):
        for number in range(lap):
            lanes = tile_lanes(chunk * lap + number)
            parts = []
            for member in range(2):
                place = chunk * (lap // TILES) + number // TILES
                taps = chunk_taps(wide_ref, place, member, number % TILES, reach + 1)
                column = column_scr.at[number, member]
                column[pl.ds(0, 2 * ROWS), :] = jnp.zeros((2 * ROWS, LANES), f32)
                lay_halo(column, halo_ref, member, lanes)
                source = (key_ref, value_ref)[member]
                column[pl.ds(2 * ROWS, ROWS), :] = source[: 2 * ROWS, lanes].astype(f32)[:ROWS]
                parts.append(fir_loads(column, taps, 2 * ROWS))
            u = jnp.where(sublane() < reach, rounded(parts[0] * parts[1]), 0.0)
            token_scr[number] = u
            for group in range(0, modes, ROWS):
                decay = jnp.exp(-rate_ref[group : group + ROWS, lanes])
                head = wide(token_scr[number, :1, :])
                for row in range(1, reach):
                    head = decay * head + wide(token_scr[number, row : row + 1, :])
                total = state_ref[group : group + ROWS, lanes] + power(decay, tokens - reach) * head
                total_scr[group : group + ROWS, lanes] = total
            head_ref[:, lanes] = jnp.concatenate([u, jnp.zeros((ROWS, LANES), f32)], axis=0).astype(bf16)
        return 0

    lax.fori_loop(0, tiles // lap, some, 0)
    split = pieces * piece_modes // modes
    for piece in range(pieces):
        first, part = piece // split * piece_modes, piece % split
        rows = total_scr[first : first + piece_modes, part * piece_width : (part + 1) * piece_width]
        out_ref[piece] = rows.astype(out_ref.dtype)
    move.wait()


def gate_kernel(query_ref, halo_ref, feat_ref, u_ref, head_ref, rate_ref, coef_ref, skip_ref, gate_ref, *rest, early):
    y_ref, halo_buf, u_buf, gate_buf, wide_scr, column, small_sem, out_sem = rest[:8]
    inner = rest[8:]
    chunks, tokens = gate_buf.shape[:2]
    count = feat_ref.shape[1]
    halo_copy = pltpu.make_async_copy(halo_ref, halo_buf, small_sem.at[0])
    halo_copy.start()
    u_copy = pltpu.make_async_copy(u_ref.at[:, pl.ds(0, early * CHUNK)], u_buf, small_sem.at[1])
    u_copy.start()
    widened(feat_ref, 0, wide_scr, 0)
    local_chunk, local_send = local_parts(u_buf, head_ref, rate_ref, coef_ref, skip_ref, y_ref, *inner)
    halo_copy.wait()
    column[pl.ds(0, 2 * ROWS), :] = jnp.zeros((2 * ROWS, LANES), f32)

    def chunk(at):
        def tile(number, _):
            lanes = tile_lanes(number)
            all_lanes = tile_lanes(at * TILES + number)
            taps = chunk_taps(wide_scr, at, 0, number, count)
            lay_halo(column, halo_buf, 2, all_lanes)
            lay_column(column, query_ref, all_lanes)
            found = list(fir(column, taps, 2 * ROWS, tokens // ROWS))
            for pair in range(tokens // (2 * ROWS)):
                rows = slice(pair * 2 * ROWS, (pair + 1) * 2 * ROWS)
                gate_buf[at, rows, lanes] = jnp.concatenate(found[pair * 2 : pair * 2 + 2], axis=0).astype(bf16)
            return 0

        lax.fori_loop(0, TILES, tile, 0)

    give = columns_out(gate_ref, gate_buf, out_sem)
    over_chunks(0, chunks, chunk, give)
    u_copy.wait()
    over_chunks(0, early, local_chunk, local_send)
    for at in range(early):
        wait_all(local_send(at))
    for at in range(chunks):
        wait_all(give(at))


def prefix_kernel(piece_ref, rate_ref, coef_ref, out_ref, *, tokens, axes):
    devices, piece_modes, piece_width = piece_ref.shape
    split = devices * piece_modes // rate_ref.shape[0]
    mine = devices - 1 - lax.axis_index(axes)
    mode, part = mine // split * piece_modes, mine % split
    group = pl.multiple_of(mode // ROWS * ROWS, ROWS)
    first = pl.multiple_of(part * piece_width, LANES)

    def mine_of(ref):
        rows = ref[pl.ds(group, ROWS), pl.ds(first, piece_width)]
        return pltpu.roll(rows, lax.rem(ROWS - (mode - group), ROWS), 0)[:piece_modes]

    coef = mine_of(coef_ref)
    through = jnp.exp(-float(tokens) * mine_of(rate_ref))

    entering = jnp.zeros((piece_modes, piece_width), f32)
    for source in reversed(range(devices)):
        out_ref[source] = (coef * entering).astype(out_ref.dtype)
        entering = through * entering + piece_ref[source].astype(f32)


def local_kernel(u_ref, head_ref, rate_ref, coef_ref, skip_ref, gate_ref, _, y_ref, y_last_ref, gate_last_ref, *scratches, first):
    *inner, sem = scratches
    last = u_ref.shape[1] // CHUNK - 1
    take = pltpu.make_async_copy(gate_ref.at[:, span(last)], gate_last_ref, sem.at[0])
    take.start()
    chunk, send = local_parts(u_ref, head_ref, rate_ref, coef_ref, skip_ref, y_ref, *inner)
    over_chunks(first, last, chunk, send)
    chunk(last)
    y_last_ref[...] = inner[0][last]
    for at in range(first, last):
        wait_all(send(at))
    take.wait()


def local_parts(u_ref, head_ref, rate_ref, coef_ref, skip_ref, y_ref, *scratches):
    y_buf, token_scr, sum_scr, out_sem = scratches
    tokens = u_ref.shape[0]
    modes = rate_ref.shape[0]
    half_groups = tokens // ROWS // 2
    top = first_half()

    def chunk(at):
        for pair in range(half_groups):
            block = u_ref[pair * 2 * ROWS : (pair + 1) * 2 * ROWS, span(at)].astype(f32)
            if pair == 0:
                block = block + head_ref[:, span(at)].astype(f32)
            for part in range(2):
                group = pair * 2 + part
                half, within = group // half_groups, group % half_groups
                for tile in range(TILES):
                    piece = lanes_of(block, tile)[part * ROWS : (part + 1) * ROWS]
                    put_tile(token_scr, within, half * TILES + tile, piece)
        (skip,) = spread_rows(skip_ref, at, range(1))
        coef = spread_rows(coef_ref, at, range(modes))
        decay = [jnp.exp(-rate) for rate in spread_rows(rate_ref, at, range(modes))]

        def eight(group, state):
            state = list(state)
            for row in range(ROWS):
                u = get_row(token_scr, group, row)
                state = [factor * one + u for factor, one in zip(decay, state)]
                terms = [factor * one for factor, one in zip([skip] + coef, [u] + state)]
                sum_scr[pl.ds(group * ROWS * ROWS + row, ROWS, stride=ROWS), :] = tree(terms)
            return tuple(state)

        state = lax.fori_loop(0, half_groups, eight, (jnp.zeros((ROWS, LANES), f32),) * modes)
        carried = tuple(
            jnp.where(top, 0.0, pltpu.roll(factor * one, TILES, 0)) for factor, one in zip(coef, state)
        )

        def eight_more(group, carried):
            for row in range(ROWS):
                carried = [factor * one for factor, one in zip(decay, carried)]
                place = pl.ds(group * ROWS * ROWS + row, ROWS, stride=ROWS)
                sum_scr[place, :] = sum_scr[place, :] + tree(carried)
            return tuple(carried)

        lax.fori_loop(0, half_groups, eight_more, carried)
        for group in range(2 * half_groups):
            half, within = group // half_groups, group % half_groups
            for tile in range(TILES):
                slot = (within * ROWS + half * TILES + tile) * ROWS
                rows = slice(group * ROWS, (group + 1) * ROWS)
                y_buf[at, rows, tile * LANES : (tile + 1) * LANES] = sum_scr[pl.ds(slot, ROWS), :]

    return chunk, columns_out(y_ref, y_buf, out_sem)


def final_kernel(piece_ref, rate_ref, y_last_ref, gate_last_ref, y_ref, gate_ref, out_ref, *scratches, axes):
    y_buf, gate_buf, out_buf, total_scr, power_scr, in_sem, out_sem = scratches
    pieces, piece_modes, piece_width = piece_ref.shape
    chunks, tokens = y_buf.shape[:2]
    modes = rate_ref.shape[0]
    fetch = columns_in(((y_ref, y_buf), (gate_ref, gate_buf)), in_sem)
    give = columns_out(out_ref, out_buf, out_sem)
    begin(chunks - 1, fetch)
    split, piece_tiles = pieces * piece_modes // modes, piece_width // LANES
    bits = [(sublane() >> level) % 2 == 1 for level in range(3)]
    pairs = [slice(first, first + 2 * ROWS) for first in range(0, tokens, 2 * ROWS)]

    def finish(at, gates, rows, lanes, sums):
        out_buf[at, rows, lanes] = gates[rows, lanes] * sums.astype(bf16)

    def chunk(at, y, gates):
        def tile(number):
            lanes, all_lanes = tile_lanes(number), tile_lanes(at * TILES + number)
            part, within = (at * TILES + number) // piece_tiles, (at * TILES + number) % piece_tiles
            state = []
            for mode in range(modes):
                rows = [wide(power_scr[level, mode : mode + 1, all_lanes]) for level in range(3)]
                lead = jnp.where(bits[0], rows[1], rows[0])
                for bit, row in zip(bits[1:], rows[1:]):
                    lead = lead * jnp.where(bit, row, 1.0)
                piece, row = mode // piece_modes * split + part, mode % piece_modes
                state.append(lead * wide(total_scr[piece, row : row + 1, tile_lanes(within)]))
            decay = [wide(power_scr[3, mode : mode + 1, all_lanes]) for mode in range(modes)]
            for rows in pairs:
                sums = []
                for first in (rows.start, rows.start + ROWS):
                    sums.append(y[first : first + ROWS, lanes] + tree(state))
                    state = [factor * one for factor, one in zip(decay, state)]
                finish(at, gates, rows, lanes, jnp.concatenate(sums, axis=0))

        def some(number, _):
            for part in range(LAP):
                tile(number * LAP + part)
            return 0

        lax.fori_loop(0, TILES // LAP, some, 0)

    def chunk_alone(at, y, gates):
        def tile(number, _):
            lanes = tile_lanes(number)
            for rows in pairs:
                finish(at, gates, rows, lanes, y[rows, lanes])
            return 0

        lax.fori_loop(0, TILES, tile, 0)

    def all_chunks(body):
        last = chunks - 1
        body(last, y_last_ref, gate_last_ref)
        start_all(give(last))
        over_chunks(0, last, with_fetch(last, fetch, lambda at: body(at, y_buf.at[at], gate_buf.at[at])), give)

    first = lax.axis_index(axes) == 0

    @pl.when(first)
    def _():
        all_chunks(chunk_alone)

    @pl.when(jnp.logical_not(first))
    def _():
        decay_powers(rate_ref, power_scr)
        total_scr[...] = piece_ref[...].astype(f32)
        all_chunks(chunk)

    for at in range(chunks):
        wait_all(give(at))


def cost(flops, moved):
    return pl.CostEstimate(flops=int(flops), bytes_accessed=int(moved), transcendentals=0)


def local(query, key_proj, value_proj, featurizer, rates, residues, skip, *, axes):
    tokens, width = query.shape
    modes = rates.shape[0]
    members, taps, groups = featurizer.shape
    devices = math.prod(lax.axis_size(axis) for axis in axes)
    chunks = width // CHUNK
    tiles = width // LANES
    split = devices * 2 // modes
    even = devices * 2 % modes == 0 and tiles % split == 0
    vmem = pltpu.VMEM
    far = pltpu.HBM
    near = jax.ShapeDtypeStruct
    dma = pltpu.SemaphoreType.DMA
    elements = tokens * width

    def call(kernel, inputs, outputs, scratches, name, close=(), **more):
        inputs = [
            value if at in close else pltpu.with_memory_space_constraint(value, far)
            for at, value in enumerate(inputs)
        ]
        beside, there = pl.BlockSpec(memory_space=vmem), pl.BlockSpec(memory_space=far)
        return pl.pallas_call(
            kernel,
            in_specs=[beside if at in close else there for at in range(len(inputs))],
            out_specs=[beside if isinstance(one, near) else there for one in outputs],
            out_shape=outputs,
            scratch_shapes=scratches,
            compiler_params=pltpu.CompilerParams(vmem_limit_bytes=32 * 2**20),
            name=name,
            **more,
        )(*inputs)

    halo_shape = (members * (taps - 1) // 2, 2, width)
    (packed,) = call(
        pack_kernel,
        (key_proj, value_proj, query),
        [near(halo_shape, bf16)],
        [vmem((members, 2 * ROWS, width), bf16), dma((members,))],
        "pack",
    )
    halo = lax.ppermute(packed, axes, [(at, at + 1) for at in range(devices - 1)])

    column = vmem((2 * ROWS + tokens, LANES), f32)
    half_buf, whole_buf = vmem((chunks, tokens, CHUNK), bf16), vmem((chunks, tokens, CHUNK), f32)
    u, u_far, wide_taps, state = call(
        signal_kernel,
        (key_proj, value_proj, featurizer, rates),
        [near((tokens, width), bf16), far((tokens, width), bf16)]
        + [near((chunks, 2, ROWS, CHUNK), f32), near((modes, width), f32)],
        [vmem((4, modes, width), f32), vmem((modes, ROWS, LANES), f32)] + [column] * (2 * TILES)
        + [dma((chunks,))],
        "signal",
        close=range(4),
        cost_estimate=cost(60 * elements, 10 * elements),
    )

    pieces = (devices, 2, width // split) if even else (modes // 2, 2, width)
    lap = TILES * (3 if chunks % 3 == 0 else 1)
    left, head, u = call(
        functools.partial(head_kernel, tokens=tokens, reach=taps - 1),
        (key_proj, value_proj, halo, rates, wide_taps, state, u, u_far),
        [near(pieces, bf16), near((2 * ROWS, width), bf16), far((tokens, width), bf16)],
        [vmem((lap, 2, 3 * ROWS, LANES), f32), vmem((lap, ROWS, LANES), f32)]
        + [vmem((modes, width), f32), dma((1,))],
        "head",
        close=range(7),
        input_output_aliases={7: 2},
    )
    left, halo_late, rates_late, skip_late = lax.optimization_barrier((left, halo, rates, skip))
    coef = residues * jnp.sqrt(-jnp.expm1(-2.0 * rates_late) / modes)
    skip_row = skip_late[None, :]
    stage = vmem((tokens // ROWS // 2 * ROWS * ROWS + ROWS, LANES), f32)
    local_shapes = [far((tokens, width), f32)]
    local_scratches = [whole_buf, stage, stage, dma((1, chunks))]
    early = chunks // 9
    gate, y = call(
        functools.partial(gate_kernel, early=early),
        (query, halo_late, featurizer, u, head, rates, coef, skip_row),
        [far((tokens, width), bf16)] + local_shapes,
        [vmem(halo_shape, bf16), vmem((tokens, early * CHUNK), bf16), half_buf]
        + [vmem((chunks, 1, ROWS, CHUNK), f32), column, dma((2,)), dma((1, chunks))]
        + local_scratches,
        "gate",
        close=(0, 2, 4, 5, 6, 7),
        cost_estimate=cost(28 * elements, 6 * elements),
    )

    def swap(value):
        order = [list(range(devices))[::-1]]
        return lax.all_to_all(value, axes, split_axis=0, concat_axis=0, axis_index_groups=order, tiled=True)

    share = modes * width // devices
    theirs = swap(left if even else left.reshape(devices, share))
    theirs, gate, coef, skip_row, y = lax.optimization_barrier((theirs, gate, coef, skip_row, y))
    if even:
        (entering,) = call(
            functools.partial(prefix_kernel, tokens=tokens, axes=axes),
            (theirs, rates, coef),
            [near(pieces, bf16)],
            [],
            "prefix",
            close=(0, 1, 2),
        )
    else:
        mine = devices - 1 - lax.axis_index(axes)
        through = jnp.exp(-float(tokens) * lax.dynamic_slice_in_dim(rates.reshape(-1), mine * share, share))
        factor = lax.dynamic_slice_in_dim(coef.reshape(-1), mine * share, share)
        _, entering = lax.scan(
            lambda so_far, piece: (through * so_far + piece.astype(f32), (factor * so_far).astype(bf16)),
            jnp.zeros((share,), f32),
            theirs,
            reverse=True,
        )

    entering, y = lax.optimization_barrier((entering, y))
    entered = swap(entering).reshape(pieces)
    y, y_last, gate_last = call(
        functools.partial(local_kernel, first=early),
        (u, head, rates, coef, skip_row, gate, y),
        local_shapes + [near((tokens, CHUNK), f32), near((tokens, CHUNK), bf16)],
        local_scratches + [dma((1,))],
        "within",
        close=range(5),
        cost_estimate=cost(50 * elements, 8 * elements),
        input_output_aliases={6: 0},
    )

    (out,) = call(
        functools.partial(final_kernel, axes=axes),
        (entered, rates, y_last, gate_last, y, gate),
        [far((tokens, width), bf16)],
        [whole_buf, half_buf, half_buf, vmem(pieces, f32), vmem((4, modes, width), f32)]
        + [dma((2, chunks)), dma((1, chunks))],
        "final",
        close=range(4),
        cost_estimate=cost(40 * elements, 10 * elements),
    )
    return out


def solution(mesh):
    axes = tuple(mesh.axis_names)
    placed = (P(axes, None),) * 3 + (P(),) * 4
    return jax.shard_map(
        functools.partial(local, axes=axes),
        mesh=mesh,
        in_specs=placed,
        out_specs=P(axes, None),
        check_vma=False,
    )
```

```python
import functools
import math

import jax
import jax.numpy as jnp
from jax import lax
from jax.experimental import pallas as pl
from jax.experimental.pallas import tpu as pltpu
from jax.sharding import PartitionSpec as P

LANES = 128
ROWS = 8
TILES = 4
CHUNK = TILES * LANES
AHEAD = 4
LAP = 4
f32 = jnp.float32
bf16 = jnp.bfloat16


def put_tile(scratch, group, slot, tile):
    scratch[pl.ds((group * ROWS + slot) * ROWS, ROWS), :] = tile


def get_row(scratch, group, row):
    return scratch[pl.ds(group * ROWS * ROWS + row, ROWS, stride=ROWS), :]


def lanes_of(value, tile):
    return value[:, tile * LANES : (tile + 1) * LANES]


def tile_lanes(tile):
    return pl.ds(pl.multiple_of(tile * LANES, LANES), LANES)


def span(at):
    return pl.ds(pl.multiple_of(at * CHUNK, CHUNK), CHUNK)


def wide(row):
    return jnp.broadcast_to(row, (ROWS, LANES))


def first_half():
    return lax.broadcasted_iota(jnp.int32, (ROWS, LANES), 0) < TILES


def sublane():
    return lax.broadcasted_iota(jnp.int32, (ROWS, LANES), 0)


def spread(row_of):
    slot = sublane() % TILES
    result = wide(row_of(TILES - 1))
    for tile in range(TILES - 1):
        result = jnp.where(slot == tile, wide(row_of(tile)), result)
    return result


def spread_rows(ref, at, rows):
    def one(row):
        return spread(lambda tile: ref[row : row + 1, tile_lanes(at * TILES + tile)])

    return [one(row) for row in rows]


def rounded(value):
    return value.astype(bf16).astype(f32)


def tiles_of(block):
    block = block.astype(f32)
    return [block[at : at + ROWS] for at in range(0, block.shape[0], ROWS)]


def fir(column, taps, first, count):
    half = ROWS // 2
    top = sublane() < half

    def seen(start, lags):
        return [column[pl.ds(start - lag, ROWS), :] for lag in range(lags)]

    def far_part(rows):
        total = taps[half] * rows[0]
        for lag in range(half + 1, len(taps)):
            total = total + taps[lag] * rows[lag - half]
        return pltpu.roll(total, half, 0)

    before = far_part(seen(first - ROWS, len(taps) - half))
    for start in range(first, first + count * ROWS, ROWS):
        rows = seen(start, half)
        now = far_part(rows)
        total = taps[0] * rows[0]
        for lag in range(1, half):
            total = total + taps[lag] * rows[lag]
        yield total + jnp.where(top, before, now)
        before = now


def fir_loads(column, taps, first):
    total = taps[0] * column[pl.ds(first, ROWS), :]
    for lag in range(1, len(taps)):
        total = total + taps[lag] * column[pl.ds(first - lag, ROWS), :]
    return total


def lay_column(column, source, lanes):
    for pair in range(source.shape[0] // (2 * ROWS)):
        rows = slice(pair * 2 * ROWS, (pair + 1) * 2 * ROWS)
        column[pl.ds((pair + 1) * 2 * ROWS, 2 * ROWS), :] = source[rows, lanes].astype(f32)


def chunk_taps(wide_ref, at, member, tile, count):
    return [wide(wide_ref[at, member, lag : lag + 1, tile_lanes(tile)]) for lag in range(count)]


def widened(feat_ref, member, out_ref, position):
    chunks, taps = out_ref.shape[0], feat_ref.shape[1]
    count = feat_ref.shape[2] // chunks
    rows = [feat_ref[member, :, at * count : (at + 1) * count] for at in range(chunks)]
    rows = [jnp.concatenate([row, jnp.zeros((ROWS - taps, count), f32)], axis=0) for row in rows]
    group = lax.broadcasted_iota(jnp.int32, (count, CHUNK), 0)
    lane = lax.broadcasted_iota(jnp.int32, (count, CHUNK), 1)
    pick = (group == lane // (CHUNK // count)).astype(f32).astype(bf16)
    parts, rest = [], jnp.concatenate(rows, axis=0)
    for _ in range(3):
        term = rest.astype(bf16)
        rest = rest - term.astype(f32)
        parts.append(jnp.dot(term, pick, preferred_element_type=f32))
    out_ref[:, position] = (parts[0] + parts[1] + parts[2]).reshape(chunks, ROWS, CHUNK)


def power(base, exponent):
    result = None
    while exponent:
        if exponent & 1:
            result = base if result is None else result * base
        base = base * base
        exponent >>= 1
    return result


def tree(terms):
    while len(terms) > 1:
        terms = [sum(terms[at + 1 : at + 2], terms[at]) for at in range(0, len(terms), 2)]
    return terms[0]


def start_all(copies):
    for copy in copies:
        copy.start()


def wait_all(copies):
    for copy in copies:
        copy.wait()


def begin(chunks, fetch):
    for at in range(min(AHEAD, chunks)):
        start_all(fetch(at))


def over_chunks(first, last, body, send):
    def one(at, _):
        body(at)
        start_all(send(at))
        return 0

    lax.fori_loop(first, last, one, 0)


def with_fetch(chunks, fetch, body):
    def one(at):
        @pl.when(at + AHEAD < chunks)
        def _():
            start_all(fetch(at + AHEAD))

        wait_all(fetch(at))
        body(at)

    return one


def columns_in(pairs, sem):
    def fetch(at):
        return [
            pltpu.make_async_copy(ref.at[:, span(at)], buf.at[at], sem.at[member, at])
            for member, (ref, buf) in enumerate(pairs)
        ]

    return fetch


def columns_out(ref, buf, sem):
    return lambda at: [pltpu.make_async_copy(buf.at[at], ref.at[:, span(at)], sem.at[0, at])]


def lay_halo(column, halo, member, lanes):
    pairs = halo.shape[0] // 3
    for pair in range(pairs):
        column[pl.ds(2 * ROWS - 2 * pairs + 2 * pair, 2), :] = halo[member * pairs + pair, :, lanes].astype(f32)


def decay_powers(rate_ref, power_scr):
    for first in range(0, rate_ref.shape[1], CHUNK):
        lanes = slice(first, first + CHUNK)
        through = jnp.exp(-rate_ref[:, lanes])
        for level in range(power_scr.shape[0]):
            power_scr[level, :, lanes] = through
            through = through * through


def pack_kernel(key_ref, value_ref, query_ref, out_ref, in_buf, in_sem):
    tokens = key_ref.shape[0]
    copies = [
        pltpu.make_async_copy(ref.at[pl.ds(tokens - 2 * ROWS, 2 * ROWS)], in_buf.at[at], in_sem.at[at])
        for at, ref in enumerate((key_ref, value_ref, query_ref))
    ]
    start_all(copies)
    wait_all(copies)
    pairs = out_ref.shape[0] // len(copies)
    for at in range(len(copies)):
        tail = in_buf[at].astype(f32)[2 * ROWS - 2 * pairs :]
        for pair in range(pairs):
            out_ref[at * pairs + pair] = tail[2 * pair : 2 * pair + 2].astype(bf16)


def signal_kernel(key_ref, value_ref, feat_ref, rate_ref, u_ref, u_out_ref, wide_ref, state_ref, *scratches):
    power_scr, last_scr, *columns, out_sem = scratches
    tokens, tiles = u_ref.shape[0], u_ref.shape[1] // LANES
    modes = rate_ref.shape[0]
    chunks = tiles // TILES
    count = feat_ref.shape[1]
    for member in range(2):
        widened(feat_ref, member + 1, wide_ref, member)
    for column in columns:
        column[pl.ds(0, 2 * ROWS), :] = jnp.zeros((2 * ROWS, LANES), f32)
    last_scr[...] = jnp.zeros(last_scr.shape, f32)

    decay_powers(rate_ref, power_scr)

    def reduce(number):
        lanes = tile_lanes(number)
        for mode in range(modes):
            whole = last_scr[mode]
            for level in (2, 1, 0):
                factor = wide(power_scr[level, mode : mode + 1, lanes])
                whole = factor * whole + pltpu.roll(whole, ROWS - (1 << level), 0)
            state_ref[mode : mode + 1, lanes] = whole[:1]

    def tile(number, columns):
        lanes = tile_lanes(number)
        reduce(jnp.maximum(number - 1, 0))
        taps = [chunk_taps(wide_ref, number // TILES, member, number % TILES, count) for member in range(2)]
        for column, ref in zip(columns, (key_ref, value_ref)):
            lay_column(column, ref, lanes)
        decay = [wide(power_scr[3, mode : mode + 1, lanes]) for mode in range(modes)]
        state = None
        for pair in range(tokens // (2 * ROWS)):
            found = []
            for first in (pair * 2 * ROWS + 2 * ROWS, pair * 2 * ROWS + 3 * ROWS):
                found.append(fir_loads(columns[0], taps[0], first) * fir_loads(columns[1], taps[1], first))
            if pair == 0:
                found[0] = jnp.where(sublane() < count - 1, 0.0, found[0])
            both = jnp.concatenate(found, axis=0).astype(bf16)
            u_ref[pair * 2 * ROWS : (pair + 1) * 2 * ROWS, lanes] = both
            for u in tiles_of(both):
                if state is None:
                    state = [u] * modes
                else:
                    state = [factor * one + u for factor, one in zip(decay, state)]
        for mode in range(modes):
            last_scr[mode] = state[mode]

    def send(at):
        return pltpu.make_async_copy(u_ref.at[:, span(at)], u_out_ref.at[:, span(at)], out_sem.at[at])

    def chunk(at, _):
        for part in range(TILES):
            tile(TILES * at + part, columns[2 * part : 2 * part + 2])

        @pl.when(at < chunks - 1)
        def _():
            send(at).start()

        return 0

    lax.fori_loop(0, chunks, chunk, 0)
    reduce(tiles - 1)
    for at in range(chunks - 1):
        send(at).wait()


def head_kernel(key_ref, value_ref, halo_ref, rate_ref, wide_ref, state_ref, u_ref, _, *rest, tokens, reach):
    out_ref, head_ref, u_out_ref, column_scr, token_scr, total_scr, sem = rest
    modes, tiles = state_ref.shape[0], state_ref.shape[1] // LANES
    last = span(tiles // TILES - 1)
    move = pltpu.make_async_copy(u_ref.at[:, last], u_out_ref.at[:, last], sem.at[0])
    move.start()
    pieces, piece_modes, piece_width = out_ref.shape

    lap = column_scr.shape[0]

    def some(chunk, _):
        for number in range(lap):
            lanes = tile_lanes(chunk * lap + number)
            parts = []
            for member in range(2):
                place = chunk * (lap // TILES) + number // TILES
                taps = chunk_taps(wide_ref, place, member, number % TILES, reach + 1)
                column = column_scr.at[number, member]
                lay_halo(column, halo_ref, member, lanes)
                source = (key_ref, value_ref)[member]
                column[pl.ds(2 * ROWS, ROWS), :] = source[: 2 * ROWS, lanes].astype(f32)[:ROWS]
                parts.append(fir_loads(column, taps, 2 * ROWS))
            u = jnp.where(sublane() < reach, rounded(parts[0] * parts[1]), 0.0)
            token_scr[number] = u
            for group in range(0, modes, ROWS):
                decay = jnp.exp(-rate_ref[group : group + ROWS, lanes])
                head = wide(token_scr[number, :1, :])
                for row in range(1, reach):
                    head = decay * head + wide(token_scr[number, row : row + 1, :])
                total = state_ref[group : group + ROWS, lanes] + jnp.exp(-float(tokens - reach) * rate_ref[group : group + ROWS, lanes]) * head
                total_scr[group : group + ROWS, lanes] = total
            head_ref[:, lanes] = jnp.concatenate([u, jnp.zeros((ROWS, LANES), f32)], axis=0).astype(bf16)
        return 0

    lax.fori_loop(0, tiles // lap, some, 0)
    split = pieces * piece_modes // modes
    for piece in range(pieces):
        first, part = piece // split * piece_modes, piece % split
        rows = total_scr[first : first + piece_modes, part * piece_width : (part + 1) * piece_width]
        out_ref[piece] = rows.astype(out_ref.dtype)
    move.wait()


def gate_kernel(query_ref, halo_ref, feat_ref, u_ref, head_ref, rate_ref, coef_ref, skip_ref, gate_ref, *rest, early):
    y_ref, halo_buf, u_buf, gate_buf, wide_scr, column, small_sem, out_sem = rest[:8]
    inner = rest[8:]
    chunks, tokens = gate_buf.shape[:2]
    count = feat_ref.shape[1]
    halo_copy = pltpu.make_async_copy(halo_ref, halo_buf, small_sem.at[0])
    halo_copy.start()
    u_copy = pltpu.make_async_copy(u_ref.at[:, pl.ds(0, early * CHUNK)], u_buf, small_sem.at[1])
    u_copy.start()
    widened(feat_ref, 0, wide_scr, 0)
    local_chunk, local_send = local_parts(u_buf, head_ref, rate_ref, coef_ref, skip_ref, y_ref, *inner)
    halo_copy.wait()
    column[pl.ds(0, 2 * ROWS), :] = jnp.zeros((2 * ROWS, LANES), f32)

    def chunk(at):
        def tile(number, _):
            lanes = tile_lanes(number)
            all_lanes = tile_lanes(at * TILES + number)
            taps = chunk_taps(wide_scr, at, 0, number, count)
            lay_halo(column, halo_buf, 2, all_lanes)
            lay_column(column, query_ref, all_lanes)
            found = list(fir(column, taps, 2 * ROWS, tokens // ROWS))
            for pair in range(tokens // (2 * ROWS)):
                rows = slice(pair * 2 * ROWS, (pair + 1) * 2 * ROWS)
                gate_buf[at, rows, lanes] = jnp.concatenate(found[pair * 2 : pair * 2 + 2], axis=0).astype(bf16)
            return 0

        lax.fori_loop(0, TILES, tile, 0)

    give = columns_out(gate_ref, gate_buf, out_sem)
    over_chunks(0, chunks, chunk, give)
    u_copy.wait()
    over_chunks(0, early, local_chunk, local_send)
    for at in range(early):
        wait_all(local_send(at))
    for at in range(chunks):
        wait_all(give(at))


def prefix_kernel(piece_ref, rate_ref, coef_ref, out_ref, *, tokens, axes):
    devices, piece_modes, piece_width = piece_ref.shape
    split = devices * piece_modes // rate_ref.shape[0]
    mine = devices - 1 - lax.axis_index(axes)
    mode, part = mine // split * piece_modes, mine % split
    group = pl.multiple_of(mode // ROWS * ROWS, ROWS)
    first = pl.multiple_of(part * piece_width, LANES)

    def mine_of(ref):
        rows = ref[pl.ds(group, ROWS), pl.ds(first, piece_width)]
        return pltpu.roll(rows, lax.rem(ROWS - (mode - group), ROWS), 0)[:piece_modes]

    coef = mine_of(coef_ref)
    through = jnp.exp(-float(tokens) * mine_of(rate_ref))

    entering = jnp.zeros((piece_modes, piece_width), f32)
    for source in reversed(range(devices)):
        out_ref[source] = (coef * entering).astype(out_ref.dtype)
        entering = through * entering + piece_ref[source].astype(f32)


def local_kernel(u_ref, head_ref, rate_ref, coef_ref, skip_ref, gate_ref, _, y_ref, y_last_ref, gate_last_ref, *scratches, first):
    *inner, sem = scratches
    last = u_ref.shape[1] // CHUNK - 1
    take = pltpu.make_async_copy(gate_ref.at[:, span(last)], gate_last_ref, sem.at[0])
    take.start()
    chunk, send = local_parts(u_ref, head_ref, rate_ref, coef_ref, skip_ref, y_ref, *inner)
    over_chunks(first, last, chunk, send)
    chunk(last)
    y_last_ref[...] = inner[0][last]
    for at in range(first, last):
        wait_all(send(at))
    take.wait()


def local_parts(u_ref, head_ref, rate_ref, coef_ref, skip_ref, y_ref, *scratches):
    y_buf, token_scr, sum_scr, out_sem = scratches
    tokens = u_ref.shape[0]
    modes = rate_ref.shape[0]
    half_groups = tokens // ROWS // 2
    top = first_half()

    def chunk(at):
        for pair in range(half_groups):
            block = u_ref[pair * 2 * ROWS : (pair + 1) * 2 * ROWS, span(at)].astype(f32)
            if pair == 0:
                block = block + head_ref[:, span(at)].astype(f32)
            for part in range(2):
                group = pair * 2 + part
                half, within = group // half_groups, group % half_groups
                for tile in range(TILES):
                    piece = lanes_of(block, tile)[part * ROWS : (part + 1) * ROWS]
                    put_tile(token_scr, within, half * TILES + tile, piece)
        (skip,) = spread_rows(skip_ref, at, range(1))
        coef = spread_rows(coef_ref, at, range(modes))
        decay = [jnp.exp(-rate) for rate in spread_rows(rate_ref, at, range(modes))]

        def eight(group, state):
            state = list(state)
            for row in range(ROWS):
                u = get_row(token_scr, group, row)
                state = [factor * one + u for factor, one in zip(decay, state)]
                terms = [factor * one for factor, one in zip([skip] + coef, [u] + state)]
                sum_scr[pl.ds(group * ROWS * ROWS + row, ROWS, stride=ROWS), :] = tree(terms)
            return tuple(state)

        state = lax.fori_loop(0, half_groups, eight, (jnp.zeros((ROWS, LANES), f32),) * modes)
        carried = tuple(
            jnp.where(top, 0.0, pltpu.roll(factor * one, TILES, 0)) for factor, one in zip(coef, state)
        )

        def eight_more(group, carried):
            for row in range(ROWS):
                carried = [factor * one for factor, one in zip(decay, carried)]
                place = pl.ds(group * ROWS * ROWS + row, ROWS, stride=ROWS)
                sum_scr[place, :] = sum_scr[place, :] + tree(carried)
            return tuple(carried)

        lax.fori_loop(0, half_groups, eight_more, carried)
        for group in range(2 * half_groups):
            half, within = group // half_groups, group % half_groups
            for tile in range(TILES):
                slot = (within * ROWS + half * TILES + tile) * ROWS
                rows = slice(group * ROWS, (group + 1) * ROWS)
                y_buf[at, rows, tile * LANES : (tile + 1) * LANES] = sum_scr[pl.ds(slot, ROWS), :]

    return chunk, columns_out(y_ref, y_buf, out_sem)


def final_kernel(piece_ref, rate_ref, y_last_ref, gate_last_ref, y_ref, gate_ref, out_ref, *scratches, axes):
    y_buf, gate_buf, out_buf, total_scr, power_scr, in_sem, out_sem = scratches
    pieces, piece_modes, piece_width = piece_ref.shape
    chunks, tokens = y_buf.shape[:2]
    modes = rate_ref.shape[0]
    fetch = columns_in(((y_ref, y_buf), (gate_ref, gate_buf)), in_sem)
    give = columns_out(out_ref, out_buf, out_sem)
    begin(chunks - 1, fetch)
    split, piece_tiles = pieces * piece_modes // modes, piece_width // LANES
    bits = [(sublane() >> level) % 2 == 1 for level in range(3)]
    pairs = [slice(first, first + 2 * ROWS) for first in range(0, tokens, 2 * ROWS)]

    def finish(at, gates, rows, lanes, sums):
        out_buf[at, rows, lanes] = gates[rows, lanes] * sums.astype(bf16)

    def chunk(at, y, gates):
        def tile(number):
            lanes, all_lanes = tile_lanes(number), tile_lanes(at * TILES + number)
            part, within = (at * TILES + number) // piece_tiles, (at * TILES + number) % piece_tiles
            state = []
            for mode in range(modes):
                rows = [wide(power_scr[level, mode : mode + 1, all_lanes]) for level in range(3)]
                lead = jnp.where(bits[0], rows[1], rows[0])
                for bit, row in zip(bits[1:], rows[1:]):
                    lead = lead * jnp.where(bit, row, 1.0)
                piece, row = mode // piece_modes * split + part, mode % piece_modes
                state.append(lead * wide(total_scr[piece, row : row + 1, tile_lanes(within)]))
            decay = [wide(power_scr[3, mode : mode + 1, all_lanes]) for mode in range(modes)]
            for rows in pairs:
                sums = []
                for first in (rows.start, rows.start + ROWS):
                    sums.append(y[first : first + ROWS, lanes] + tree(state))
                    state = [factor * one for factor, one in zip(decay, state)]
                finish(at, gates, rows, lanes, jnp.concatenate(sums, axis=0))

        def some(number, _):
            for part in range(LAP):
                tile(number * LAP + part)
            return 0

        lax.fori_loop(0, TILES // LAP, some, 0)

    def chunk_alone(at, y, gates):
        def tile(number, _):
            lanes = tile_lanes(number)
            for rows in pairs:
                finish(at, gates, rows, lanes, y[rows, lanes])
            return 0

        lax.fori_loop(0, TILES, tile, 0)

    def all_chunks(body):
        last = chunks - 1
        body(last, y_last_ref, gate_last_ref)
        start_all(give(last))
        over_chunks(0, last, with_fetch(last, fetch, lambda at: body(at, y_buf.at[at], gate_buf.at[at])), give)

    first = lax.axis_index(axes) == 0

    @pl.when(first)
    def _():
        all_chunks(chunk_alone)

    @pl.when(jnp.logical_not(first))
    def _():
        decay_powers(rate_ref, power_scr)
        total_scr[...] = piece_ref[...].astype(f32)
        all_chunks(chunk)

    for at in range(chunks):
        wait_all(give(at))


def cost(flops, moved):
    return pl.CostEstimate(flops=int(flops), bytes_accessed=int(moved), transcendentals=0)


def local(query, key_proj, value_proj, featurizer, rates, residues, skip, *, axes):
    tokens, width = query.shape
    modes = rates.shape[0]
    members, taps, groups = featurizer.shape
    devices = math.prod(lax.axis_size(axis) for axis in axes)
    chunks = width // CHUNK
    tiles = width // LANES
    split = devices * 2 // modes
    even = devices * 2 % modes == 0 and tiles % split == 0
    vmem = pltpu.VMEM
    far = pltpu.HBM
    near = jax.ShapeDtypeStruct
    dma = pltpu.SemaphoreType.DMA
    elements = tokens * width

    def call(kernel, inputs, outputs, scratches, name, close=(), **more):
        inputs = [
            value if at in close else pltpu.with_memory_space_constraint(value, far)
            for at, value in enumerate(inputs)
        ]
        beside, there = pl.BlockSpec(memory_space=vmem), pl.BlockSpec(memory_space=far)
        return pl.pallas_call(
            kernel,
            in_specs=[beside if at in close else there for at in range(len(inputs))],
            out_specs=[beside if isinstance(one, near) else there for one in outputs],
            out_shape=outputs,
            scratch_shapes=scratches,
            compiler_params=pltpu.CompilerParams(vmem_limit_bytes=32 * 2**20),
            name=name,
            **more,
        )(*inputs)

    halo_shape = (members * (taps - 1) // 2, 2, width)
    (packed,) = call(
        pack_kernel,
        (key_proj, value_proj, query),
        [near(halo_shape, bf16)],
        [vmem((members, 2 * ROWS, width), bf16), dma((members,))],
        "pack",
    )
    halo = lax.ppermute(packed, axes, [(at, at + 1) for at in range(devices - 1)])

    column = vmem((2 * ROWS + tokens, LANES), f32)
    half_buf, whole_buf = vmem((chunks, tokens, CHUNK), bf16), vmem((chunks, tokens, CHUNK), f32)
    u, u_far, wide_taps, state = call(
        signal_kernel,
        (key_proj, value_proj, featurizer, rates),
        [near((tokens, width), bf16), far((tokens, width), bf16)]
        + [near((chunks, 2, ROWS, CHUNK), f32), near((modes, width), f32)],
        [vmem((4, modes, width), f32), vmem((modes, ROWS, LANES), f32)] + [column] * (2 * TILES)
        + [dma((chunks,))],
        "signal",
        close=range(4),
        cost_estimate=cost(60 * elements, 10 * elements),
    )

    pieces = (devices, 2, width // split) if even else (modes // 2, 2, width)
    lap = TILES * (3 if chunks % 3 == 0 else 1)
    left, head, u = call(
        functools.partial(head_kernel, tokens=tokens, reach=taps - 1),
        (key_proj, value_proj, halo, rates, wide_taps, state, u, u_far),
        [near(pieces, bf16), near((2 * ROWS, width), bf16), far((tokens, width), bf16)],
        [vmem((lap, 2, 3 * ROWS, LANES), f32), vmem((lap, ROWS, LANES), f32)]
        + [vmem((modes, width), f32), dma((1,))],
        "head",
        close=range(7),
        input_output_aliases={7: 2},
    )
    left, halo_late, rates_late, skip_late = lax.optimization_barrier((left, halo, rates, skip))
    coef = residues * jnp.sqrt(-jnp.expm1(-2.0 * rates_late) / modes)
    skip_row = skip_late[None, :]
    stage = vmem((tokens // ROWS // 2 * ROWS * ROWS + ROWS, LANES), f32)
    local_shapes = [far((tokens, width), f32)]
    local_scratches = [whole_buf, stage, stage, dma((1, chunks))]
    early = chunks // 9
    gate, y = call(
        functools.partial(gate_kernel, early=early),
        (query, halo_late, featurizer, u, head, rates, coef, skip_row),
        [far((tokens, width), bf16)] + local_shapes,
        [vmem(halo_shape, bf16), vmem((tokens, early * CHUNK), bf16), half_buf]
        + [vmem((chunks, 1, ROWS, CHUNK), f32), column, dma((2,)), dma((1, chunks))]
        + local_scratches,
        "gate",
        close=(0, 2, 4, 5, 6, 7),
        cost_estimate=cost(28 * elements, 6 * elements),
    )

    def swap(value):
        order = [list(range(devices))[::-1]]
        return lax.all_to_all(value, axes, split_axis=0, concat_axis=0, axis_index_groups=order, tiled=True)

    share = modes * width // devices
    theirs = swap(left if even else left.reshape(devices, share))
    theirs, gate, coef, skip_row, y = lax.optimization_barrier((theirs, gate, coef, skip_row, y))
    if even:
        (entering,) = call(
            functools.partial(prefix_kernel, tokens=tokens, axes=axes),
            (theirs, rates, coef),
            [near(pieces, bf16)],
            [],
            "prefix",
            close=(0, 1, 2),
        )
    else:
        mine = devices - 1 - lax.axis_index(axes)
        through = jnp.exp(-float(tokens) * lax.dynamic_slice_in_dim(rates.reshape(-1), mine * share, share))
        factor = lax.dynamic_slice_in_dim(coef.reshape(-1), mine * share, share)
        _, entering = lax.scan(
            lambda so_far, piece: (through * so_far + piece.astype(f32), (factor * so_far).astype(bf16)),
            jnp.zeros((share,), f32),
            theirs,
            reverse=True,
        )

    entering, y = lax.optimization_barrier((entering, y))
    entered = swap(entering).reshape(pieces)
    y, y_last, gate_last = call(
        functools.partial(local_kernel, first=early),
        (u, head, rates, coef, skip_row, gate, y),
        local_shapes + [near((tokens, CHUNK), f32), near((tokens, CHUNK), bf16)],
        local_scratches + [dma((1,))],
        "within",
        close=range(5),
        cost_estimate=cost(50 * elements, 8 * elements),
        input_output_aliases={6: 0},
    )

    (out,) = call(
        functools.partial(final_kernel, axes=axes),
        (entered, rates, y_last, gate_last, y, gate),
        [far((tokens, width), bf16)],
        [whole_buf, half_buf, half_buf, vmem(pieces, f32), vmem((4, modes, width), f32)]
        + [dma((2, chunks)), dma((1, chunks))],
        "final",
        close=range(4),
        cost_estimate=cost(40 * elements, 10 * elements),
    )
    return out


def solution(mesh):
    axes = tuple(mesh.axis_names)
    placed = (P(axes, None),) * 3 + (P(),) * 4
    return jax.shard_map(
        functools.partial(local, axes=axes),
        mesh=mesh,
        in_specs=placed,
        out_specs=P(axes, None),
        check_vma=False,
    )
```
